32 devices in a mesh: group: 2 (over x), slab: 4 (over y, core), inner: 4 (over z).
Axes of the slice: x: 2, y: 2, z: 4, core: 2. Of those that a mesh axis runs over, the one named last changes fastest.
Arguments:
- populations: float32 [19, 32, 32, 256], P(None, ('group', 'slab'), 'inner'), parts along dimension 1, may hold values from 0 to 1, as said below
- relaxation: float32 [32, 32, 256], P(('group', 'slab'), 'inner'), parts along dimension 0, may hold values from 0.7 to 1.8
- node_flags: int32 [32, 32, 256], P(('group', 'slab'), 'inner'), parts along dimension 0, may hold values from 0 to 3, as said below
- displacement: float32 [3, 65536], P(None, ('group', 'slab', 'inner')), parts along dimension 1, may hold values from -0.04 to 0.04
- elements: int32 [3, 131072], P(None, ('group', 'slab', 'inner')), parts along dimension 1, may hold values from 0 to 4095, as said below
- shape_inverse: float32 [3, 131072], P(None, ('group', 'slab', 'inner')), parts along dimension 1, may hold values from -0.5 to 2
- stiffness: float32 [131072], P(('group', 'slab', 'inner')), parts along dimension 0, may hold values from 5 to 50
- block_source: int32 [8, 4, 8], P(('group', 'slab'), 'inner'), parts along dimension 0, may hold values from 0 to 63
- block_target: int32 [8, 4, 8], P(('group', 'slab'), 'inner'), parts along dimension 0, may hold values from 0 to 3, as said below
- block_node: int32 [8, 4, 8], P(('group', 'slab'), 'inner'), parts along dimension 0, may hold values from 0 to 15
- block_count: int32 [8, 4], P(('group', 'slab'), 'inner'), parts along dimension 0, may hold values from 4 to 8, as said below
Outputs:
- populations_out: float32 [19, 32, 32, 256], P(None, ('group', 'slab'), 'inner'), parts along dimension 1
- wall_force: float32 [3, 65536], P(None, ('group', 'slab', 'inner')), parts along dimension 1
- wall_motion: float32 [8, 4, 8, 3, 128], P(('group', 'slab'), 'inner'), parts along dimension 0
The draws below stay inside these ranges and needn't reach their ends.
There are 2 independent parts, one for each index of `group`. The reference program is written for one: setup_inputs(seed, part) draws one part's arguments, and reference() takes and returns one part's arrays. A program takes and returns all parts, laid end to end along the dimension named above; each array names one. Nothing has to cross between parts.
Inputs may be any that keep to these rules, and one draw needn't show every extreme that they name: `node_flags`: 0 fluid, 1 wall, 2 inlet, 3 outlet; the planes y = 0 and y = 31 are wall, x = 0 is inlet and x = 15 outlet except wall cells. Positive populations. `elements`: numbers below 4096 on devices of the last slab index below 2048. `block_target`: at most 3 of one device's blocks name one inner index, and every device names some inner index exactly 3 times among its live blocks. `block_count`: some device has 8 live blocks and some has half as many.
All inputs are finite; a program needn't handle non-finite values.
Results may differ from the reference program's by a relative error of at most 0.0003.
Values sent between devices are 32-bit elements; how exact they have to be, the bound alone decides.
No kernel may reach another device: no remote copies, remote signals or barrier semaphores. Data moves between devices by JAX's collectives and lax.ppermute only.
A program may use at most 64 MiB of HBM per device.

```python
import math
import jax
import jax.numpy as jnp
from jax import lax

Q = 19
PL = 4
CY = 8
NZ = 256
NODE_DEV = 2048
BLK = 128
CAP = 3
NX = 16
NY = 32
NB = 8
NNB = 16
NCB = 64
ELEM_DEV = 4096
NODES = 32768
ELEMS = 65536
N_SLAB = 4
N_INNER = 4


DRAW_VELOCITIES = ((0, 0, 0), (1, 0, 0), (-1, 0, 0), (0, 1, 0), (0, -1, 0), (0, 0, 1), (0, 0, -1), (1, 1, 0), (-1, -1, 0), (1, -1, 0), (-1, 1, 0), (1, 0, 1), (-1, 0, -1), (1, 0, -1), (-1, 0, 1), (0, 1, 1), (0, -1, -1), (0, 1, -1), (0, -1, 1))


DRAW_WEIGHTS = (1.0 / 3.0,) + (1.0 / 18.0,) * 6 + (1.0 / 36.0,) * 12


DRAW_SPEED = 0.04


def draw_populations(key, part):
    key = jax.random.fold_in(key, 11)
    extent = (Q, NX, NY, NZ)
    resting = []
    for velocity in range(Q):
        project_x = DRAW_VELOCITIES[velocity][0] * DRAW_SPEED
        resting.append(DRAW_WEIGHTS[velocity] * (1.0 + 3.0 * project_x + 4.5 * project_x * project_x - 1.5 * DRAW_SPEED * DRAW_SPEED))
    resting = jnp.asarray(resting, jnp.float32)[:, None, None, None]
    jitter = jnp.clip(0.1 * jax.random.normal(key, extent, jnp.float32), -0.3, 0.3)
    return resting * (1.0 + jitter)


def draw_node_flags(key, part):
    key = jax.random.fold_in(key, 12)
    extent = (NX, NY, NZ)
    plaque_cells = jax.random.randint(key, extent, 0, 100) < 8
    pos_x = lax.broadcasted_iota(jnp.int32, extent, 0)
    pos_y = lax.broadcasted_iota(jnp.int32, extent, 1)
    kinds = jnp.zeros(extent, jnp.int32)
    kinds = jnp.where(pos_x == 0, 2, kinds)
    kinds = jnp.where(pos_x == NX - 1, 3, kinds)
    kinds = jnp.where(plaque_cells | (pos_y == 0) | (pos_y == NY - 1), 1, kinds)
    return kinds


def draw_elements(key, part):
    key = jax.random.fold_in(key, 13)
    picked_nodes = jax.random.randint(key, (3, ELEMS), 0, 2 * NODE_DEV)
    owner_rank = lax.broadcasted_iota(jnp.int32, (3, ELEMS), 1) // ELEM_DEV
    last_slab = owner_rank // N_INNER == N_SLAB - 1
    return jnp.where(last_slab, picked_nodes % NODE_DEV, picked_nodes)


def draw_shape_inverse(key, part):
    key = jax.random.fold_in(key, 14)
    first, second, third = jax.random.split(key, 3)
    diag_a = jnp.exp(jax.random.uniform(first, (ELEMS,), jnp.float32, math.log(0.5), math.log(2.0)))
    diag_c = jnp.exp(jax.random.uniform(second, (ELEMS,), jnp.float32, math.log(0.5), math.log(2.0)))
    skew_b = jax.random.uniform(third, (ELEMS,), jnp.float32, -0.5, 0.5)
    return jnp.stack([jnp.clip(diag_a, 0.5, 2.0), skew_b, jnp.clip(diag_c, 0.5, 2.0)])


def draw_block_target(key, part):
    key = jax.random.fold_in(key, 15)
    first, second, third = jax.random.split(key, 3)
    start = jax.random.randint(first, (N_SLAB, N_INNER, 1), 0, N_INNER)
    stride = 2 * jax.random.randint(second, (N_SLAB, N_INNER, 1), 0, max(N_INNER // 2, 1)) + 1
    offset = jax.random.randint(third, (N_SLAB, N_INNER, 1), 0, 2)
    rows = lax.broadcasted_iota(jnp.int32, (N_SLAB, N_INNER, NB), 2)
    group_ids = jnp.where(rows < CAP, 0, 1 + (rows - CAP + offset) // 2)
    return (start + stride * group_ids) % N_INNER


def draw_block_count(key, part):
    key = jax.random.fold_in(key, 16)
    first, second, third = jax.random.split(key, 3)
    total = N_SLAB * N_INNER
    counts = jax.random.randint(first, (total,), N_INNER, 2 * N_INNER + 1)
    fullest = jax.random.randint(second, (), 0, total)
    lightest = (fullest + 1 + jax.random.randint(third, (), 0, total - 1)) % total
    ranks = jnp.arange(total, dtype=jnp.int32)
    counts = jnp.where(ranks == fullest, 2 * N_INNER, counts)
    counts = jnp.where(ranks == lightest, N_INNER, counts)
    return counts.reshape(N_SLAB, N_INNER)


def with_ends(array, own_key, low, high):
    longest = array.shape.index(max(array.shape))
    spots = []
    for shift in (0, 1):
        where = [jax.random.randint(jax.random.fold_in(own_key, axis), (), 0, length) for axis, length in enumerate(array.shape)]
        where[longest] = (where[longest] + shift) % array.shape[longest]
        spots.append(tuple(where))
    return array.at[spots[0]].set(low).at[spots[1]].set(high)


def shard_levels(stream_key, shape, cuts, low, top_value):
    level = 1.0
    for axis_at, parts in cuts:
        heights = jax.random.uniform(jax.random.fold_in(jax.random.fold_in(stream_key, 6), axis_at), (parts,), jnp.float32, low / len(cuts), top_value / len(cuts))
        level = level * jnp.repeat(jnp.exp(heights), shape[axis_at] // parts).reshape((-1,) + (1,) * (len(shape) - 1 - axis_at))
    return level


def noise(own_key, shape, spread, bound, pieces=(), kind=jnp.bfloat16):
    values = spread * jax.random.normal(own_key, shape, jnp.float32)
    if pieces:
        values = values * shard_levels(own_key, shape, pieces, -0.22, 0.18)
    return jnp.clip(values, -bound, bound).astype(kind)


def setup_inputs(seed: int = 0, part: int = 0) -> dict:
    streams_of = jax.random.split(jax.random.key(seed), 12)
    part_splits = jax.random.split(jax.random.fold_in(streams_of[11], part), 12)
    return {
        "populations": draw_populations(jax.random.fold_in(jax.random.fold_in(streams_of[11], part), 71), part),
        "relaxation": jnp.clip(0.7 + 1.09999996 * jax.random.uniform(part_splits[1], (NX, NY, NZ), jnp.float32) ** shard_levels(part_splits[1], (NX, NY, NZ), ((0, 4), (1, 4)), -0.2, 0.2), 0.7, 1.8),
        "node_flags": draw_node_flags(jax.random.fold_in(jax.random.fold_in(streams_of[11], part), 71), part),
        "displacement": noise(part_splits[3], (3, NODES), 0.01, 0.04, ((1, 16),), jnp.float32),
        "elements": draw_elements(jax.random.fold_in(jax.random.fold_in(streams_of[11], part), 71), part),
        "shape_inverse": draw_shape_inverse(jax.random.fold_in(jax.random.fold_in(streams_of[11], part), 71), part),
        "stiffness": jnp.clip(jnp.exp(math.log(50.0) - 2.3025851 * jax.random.uniform(part_splits[6], (ELEMS,), jnp.float32) ** shard_levels(part_splits[6], (ELEMS,), ((0, 16),), -0.2, 0.2)), 5.0, 50.0),
        "block_source": with_ends(jax.random.randint(part_splits[7], (N_SLAB, N_INNER, NB), 0, NCB), jax.random.fold_in(part_splits[7], 1), 0, NCB - 1).astype(jnp.int32),
        "block_target": draw_block_target(jax.random.fold_in(jax.random.fold_in(streams_of[11], part), 71), part),
        "block_node": with_ends(jax.random.randint(part_splits[9], (N_SLAB, N_INNER, NB), 0, NNB), jax.random.fold_in(part_splits[9], 1), 0, NNB - 1).astype(jnp.int32),
        "block_count": draw_block_count(jax.random.fold_in(jax.random.fold_in(streams_of[11], part), 71), part),
    }


VELOCITIES = ((0, 0, 0), (1, 0, 0), (-1, 0, 0), (0, 1, 0), (0, -1, 0), (0, 0, 1), (0, 0, -1),
              (1, 1, 0), (-1, -1, 0), (1, -1, 0), (-1, 1, 0), (1, 0, 1), (-1, 0, -1), (1, 0, -1), (-1, 0, 1),
              (0, 1, 1), (0, -1, -1), (0, 1, -1), (0, -1, 1))
WEIGHTS = (1.0 / 3.0,) + (1.0 / 18.0,) * 6 + (1.0 / 36.0,) * 12
OPPOSITE = (0, 2, 1, 4, 3, 6, 5, 8, 7, 10, 9, 12, 11, 14, 13, 16, 15, 18, 17)
INLET_SPEED = 0.04
LOAD_SCALE = 25.0
COMPLIANCE = 0.5
LAME_RATIO = 2.0


def moments(values):
    density = jnp.sum(values, axis=0)
    flows = []
    for axis_num in range(3):
        total = None
        for velocity in range(19):
            factor = VELOCITIES[velocity][axis_num]
            if factor != 0:
                term = values[velocity] if factor > 0 else -values[velocity]
                total = term if total is None else total + term
        flows.append(total)
    return density, flows[0], flows[1], flows[2]


def equilibrium(density, vel_x, vel_y, vel_z):
    speed_sq = vel_x * vel_x + vel_y * vel_y + vel_z * vel_z
    result = []
    for velocity in range(19):
        project = 0.0
        for factor, component in zip(VELOCITIES[velocity], (vel_x, vel_y, vel_z)):
            if factor != 0:
                project = project + factor * component
        result.append(WEIGHTS[velocity] * density * (1.0 + 3.0 * project + 4.5 * project * project - 1.5 * speed_sq))
    return jnp.stack(result)


def collide(values, relaxation, node_flags, inside):
    density, flow_x, flow_y, flow_z = moments(values)
    if inside is not None:
        density = jnp.where(inside, density, 1.0)
    vel_x = flow_x / density
    vel_y = flow_y / density
    vel_z = flow_z / density
    balance = equilibrium(density, vel_x, vel_y, vel_z)
    relaxed = values - relaxation[None] * (values - balance)
    bounced = jnp.stack([values[other] for other in OPPOSITE])
    unity = jnp.ones_like(density)
    nothing = jnp.zeros_like(density)
    inflow = equilibrium(unity, jnp.full_like(density, INLET_SPEED), nothing, nothing)
    outflow = equilibrium(unity, vel_x, vel_y, vel_z)
    kinds = node_flags[None]
    collided = jnp.where(kinds == 0, relaxed, jnp.where(kinds == 1, bounced, jnp.where(kinds == 2, inflow, outflow)))
    if inside is not None:
        collided = jnp.where(inside[None], collided, 0.0)
    return collided


def pull(padded, rows_x, rows_y):
    moved = []
    for velocity in range(19):
        step_x, step_y, step_z = VELOCITIES[velocity]
        piece = padded[velocity, 1 - step_x:1 - step_x + rows_x, 1 - step_y:1 - step_y + rows_y, :]
        moved.append(jnp.roll(piece, step_z, axis=2))
    return jnp.stack(moved)


def element_forces(first, second, third, shape_inverse, stiffness):
    diag_a = shape_inverse[0]
    skew_b = shape_inverse[1]
    diag_c = shape_inverse[2]
    edge_one = second - first
    edge_two = third - first
    grad_one = diag_a * edge_one
    grad_two = skew_b * edge_one + diag_c * edge_two
    column_one = jnp.stack([grad_one[0] + 1.0, grad_one[1], grad_one[2]])
    column_two = jnp.stack([grad_two[0], grad_two[1] + 1.0, grad_two[2]])
    metric_aa = jnp.sum(column_one * column_one, axis=0)
    metric_ab = jnp.sum(column_one * column_two, axis=0)
    metric_bb = jnp.sum(column_two * column_two, axis=0)
    determinant = metric_aa * metric_bb - metric_ab * metric_ab
    inverse_aa = metric_bb / determinant
    inverse_ab = -metric_ab / determinant
    inverse_bb = metric_aa / determinant
    pulled_one = column_one * inverse_aa + column_two * inverse_ab
    pulled_two = column_one * inverse_ab + column_two * inverse_bb
    log_volume = 0.5 * jnp.log(determinant)
    stress_one = stiffness * (column_one - pulled_one + LAME_RATIO * log_volume * pulled_one)
    stress_two = stiffness * (column_two - pulled_two + LAME_RATIO * log_volume * pulled_two)
    force_one = diag_a * stress_one + skew_b * stress_two
    force_two = diag_c * stress_two
    return -(force_one + force_two), force_one, force_two


def reference(populations, relaxation, node_flags, displacement, elements, shape_inverse, stiffness, block_source, block_target, block_node, block_count):
    values = populations
    for sweep in range(2):
        collided = collide(values, relaxation, node_flags, None)
        padded = jnp.pad(collided, ((0, 0), (1, 1), (1, 1), (0, 0)))
        values = pull(padded, NX, NY)
    density, flow_x, flow_y, flow_z = moments(values)
    loads = LOAD_SCALE * jnp.stack([flow_x, flow_y + (density - 1.0) / 3.0, flow_z])
    per_device = loads.reshape(3, N_SLAB, PL, N_INNER, CY, NZ).transpose(1, 3, 0, 2, 4, 5)
    per_device = per_device.reshape(N_SLAB, N_INNER, 3, NCB, BLK).transpose(0, 1, 3, 2, 4)
    chosen = jnp.broadcast_to(block_source[:, :, :, None, None], (N_SLAB, N_INNER, NB, 3, BLK))
    blocks = jnp.take_along_axis(per_device, chosen, axis=2)
    active = jnp.arange(NB, dtype=jnp.int32)[None, None, :] < block_count[:, :, None]
    slab_ids = jnp.arange(N_SLAB, dtype=jnp.int32)[:, None, None]
    owners = N_SLAB * N_INNER * NNB
    target = (slab_ids * N_INNER + block_target) * NNB + block_node
    target = jnp.where(active, target, owners)
    summed = jax.ops.segment_sum(blocks.reshape(-1, 3, BLK), target.reshape(-1), num_segments=owners + 1)[:owners]
    external = summed.reshape(N_SLAB * N_INNER, NNB, 3, BLK).transpose(2, 0, 1, 3).reshape(3, NODES)
    owner_rank = jnp.arange(ELEMS, dtype=jnp.int32) // ELEM_DEV
    neighbour = jnp.minimum(owner_rank + N_INNER, N_SLAB * N_INNER - 1)
    global_ids = jnp.where(elements < NODE_DEV, owner_rank * NODE_DEV + elements, neighbour * NODE_DEV + elements - NODE_DEV)
    nodal = element_forces(displacement[:, global_ids[0]], displacement[:, global_ids[1]], displacement[:, global_ids[2]], shape_inverse, stiffness)
    internal = jnp.zeros((3, NODES), jnp.float32)
    for corner in range(3):
        internal = internal.at[:, global_ids[corner]].add(nodal[corner])
    residual = external - internal
    by_block = residual.reshape(3, owners, BLK).transpose(1, 0, 2)
    picked = by_block[jnp.minimum(target, owners - 1)]
    motion = jnp.where(active[:, :, :, None, None], COMPLIANCE * picked, 0.0)
    return values, residual, motion
```

```python
import functools

import jax
import jax.numpy as jnp
from jax import lax
from jax.experimental import pallas as pl
from jax.experimental.pallas import tpu as pltpu
from jax.sharding import PartitionSpec as P

BLK = 128
VELOCITIES = (
    (0, 0, 0),
    (1, 0, 0),
    (-1, 0, 0),
    (0, 1, 0),
    (0, -1, 0),
    (0, 0, 1),
    (0, 0, -1),
    (1, 1, 0),
    (-1, -1, 0),
    (1, -1, 0),
    (-1, 1, 0),
    (1, 0, 1),
    (-1, 0, -1),
    (1, 0, -1),
    (-1, 0, 1),
    (0, 1, 1),
    (0, -1, -1),
    (0, 1, -1),
    (0, -1, 1),
)
WEIGHTS = (1.0 / 3.0,) + (1.0 / 18.0,) * 6 + (1.0 / 36.0,) * 12
OPPOSITE = (0, 2, 1, 4, 3, 6, 5, 8, 7, 10, 9, 12, 11, 14, 13, 16, 15, 18, 17)
INLET_SPEED = 0.04
LOAD_SCALE = 25.0
COMPLIANCE = 0.5
LAME_RATIO = 2.0
Q = 19
FLAG_SLOT = 19
RATE_SLOT = 20
SLOTS = 21
F32 = jnp.float32
VMEM_BYTES = 48 * 1024 * 1024


def moments(values):
    sums = [values[q] + values[q + 1] for q in range(1, Q, 2)]
    diffs = [values[q] - values[q + 1] for q in range(1, Q, 2)]
    density = values[0]
    for term in sums:
        density = density + term
    flows = []
    for axis in range(3):
        total = None
        for k, q in enumerate(range(1, Q, 2)):
            factor = VELOCITIES[q][axis]
            if factor == 0:
                continue
            if total is None:
                total = diffs[k] if factor > 0 else -diffs[k]
            else:
                total = total + diffs[k] if factor > 0 else total - diffs[k]
        flows.append(total)
    return density, flows[0], flows[1], flows[2]


def collide(values, rate, kind):
    density, flow_x, flow_y, flow_z = moments(values)
    inverse = 1.0 / density
    wall = kind == 1
    inlet = kind == 2
    fluid = kind == 0
    vel = (
        jnp.where(inlet, INLET_SPEED, flow_x * inverse),
        jnp.where(inlet, 0.0, flow_y * inverse),
        jnp.where(inlet, 0.0, flow_z * inverse),
    )
    scale = jnp.where(fluid, density, 1.0)
    rate = jnp.where(fluid, rate, 1.0)
    base = 1.0 - 1.5 * (vel[0] * vel[0] + vel[1] * vel[1] + vel[2] * vel[2])
    weighted = {w: w * scale for w in set(WEIGHTS)}
    out = [None] * Q
    relaxed = values[0] + rate * (weighted[WEIGHTS[0]] * base - values[0])
    out[0] = jnp.where(wall, values[0], relaxed)
    for q in range(1, Q, 2):
        project = None
        for factor, component in zip(VELOCITIES[q], vel):
            if factor == 0:
                continue
            if project is None:
                project = component
            else:
                project = project + component if factor > 0 else project - component
        even = base + 4.5 * (project * project)
        odd = 3.0 * project
        w = weighted[WEIGHTS[q]]
        forward = values[q] + rate * (w * (even + odd) - values[q])
        backward = values[q + 1] + rate * (w * (even - odd) - values[q + 1])
        out[q] = jnp.where(wall, values[q + 1], forward)
        out[q + 1] = jnp.where(wall, values[q], backward)
    return out


def roll_by(block, step, axis):
    if step == 0:
        return block
    return pltpu.roll(block, step % block.shape[axis], axis)


def face_slots(axis, sign):
    picks = []
    for q in range(Q):
        if VELOCITIES[q][axis] * sign >= 0:
            picks.append((q, 0))
        else:
            picks.append((OPPOSITE[q], 1))
    return picks


def first_kernel(pops, rate, flags, c1, up, down):
    planes = pops.shape[1]

    def plane(x, carry):
        values = [pops[q, x] for q in range(Q)]
        result = collide(values, rate[x], flags[x])
        for q in range(Q):
            c1[q, x] = roll_by(result[q], VELOCITIES[q][2], 1)
        return carry

    lax.fori_loop(0, planes, plane, 0)
    for slot, (q, depth) in enumerate(face_slots(0, 1)):
        up[slot] = c1[q, planes - 1 - depth]
    for slot, (q, depth) in enumerate(face_slots(0, -1)):
        down[slot] = c1[q, depth]
    up[FLAG_SLOT] = flags[planes - 1].astype(F32)
    up[RATE_SLOT] = rate[planes - 1]
    down[FLAG_SLOT] = flags[0].astype(F32)
    down[RATE_SLOT] = rate[0]


def pack_kernel(c1, rate, flags, below, above, top, bottom):
    planes = c1.shape[1]
    last = c1.shape[2] - 1
    for out, sign in ((top, 1), (bottom, -1)):
        for slot, (q, depth) in enumerate(face_slots(1, sign)):
            y = last - depth if sign > 0 else depth
            row = slice(y, y + 1)
            out[slot, 0:1] = below[OPPOSITE[q], row]
            out[slot, 1:2] = below[q, row]
            for x in range(planes):
                out[slot, x + 2 : x + 3] = c1[q, x, row]
            out[slot, planes + 2 : planes + 3] = above[q, row]
            out[slot, planes + 3 : planes + 4] = above[OPPOSITE[q], row]
        y = last if sign > 0 else 0
        row = slice(y, y + 1)
        for slot in (FLAG_SLOT, RATE_SLOT):
            out[slot, 0:1] = below[slot, row]
            out[slot, 1:2] = below[slot, row]
            for x in range(planes):
                if slot == FLAG_SLOT:
                    out[slot, x + 2 : x + 3] = flags[x, row].astype(F32)
                else:
                    out[slot, x + 2 : x + 3] = rate[x, row]
            out[slot, planes + 2 : planes + 3] = above[slot, row]
            out[slot, planes + 3 : planes + 4] = above[slot, row]


def second_kernel(
    block_source,
    block_target,
    block_node,
    block_count,
    c1,
    rate,
    flags,
    below,
    above,
    top,
    bottom,
    behind,
    ahead,
    internal_own,
    internal_other,
    out,
    message,
    extended,
    kinds,
    rates,
    second,
    edge_low,
    edge_high,
    loads,
):
    planes, rows, length = c1.shape[1:]
    half = length // BLK
    slots = block_source.shape[2]
    slab = lax.axis_index("slab")
    inner = lax.axis_index("inner")
    slab_end = lax.axis_size("slab") - 1
    inner_end = lax.axis_size("inner") - 1

    for q in range(Q):
        for x in range(planes):
            extended[q, x + 2] = c1[q, x]
        extended[q, 1] = below[q]
        extended[q, planes + 2] = above[q]
        if VELOCITIES[q][0] > 0:
            extended[q, 0] = below[OPPOSITE[q]]
        if VELOCITIES[q][0] < 0:
            extended[q, planes + 3] = above[OPPOSITE[q]]
    kinds[0] = below[FLAG_SLOT]
    rates[0] = below[RATE_SLOT]
    kinds[planes + 1] = above[FLAG_SLOT]
    rates[planes + 1] = above[RATE_SLOT]
    for x in range(planes):
        kinds[x + 1] = flags[x].astype(F32)
        rates[x + 1] = rate[x]

    sub = lax.broadcasted_iota(jnp.int32, (rows, length), 0)
    is_first = sub == 0
    is_last = sub == rows - 1

    def plane_one(at, carry):
        values = []
        for q in range(Q):
            step_x, step_y, _ = VELOCITIES[q]
            block = extended[q, at + 1 - step_x]
            if step_y > 0:
                edge = behind[q, pl.ds(at + 1 - step_x, 1)]
                block = jnp.where(is_first, edge, roll_by(block, 1, 0))
            if step_y < 0:
                edge = ahead[q, pl.ds(at + 1 - step_x, 1)]
                block = jnp.where(is_last, edge, roll_by(block, -1, 0))
            values.append(block)
        result = collide(values, rates[at], kinds[at])
        for q in range(Q):
            second[q, at] = roll_by(result[q], VELOCITIES[q][2], 1)
        return carry

    lax.fori_loop(0, planes + 2, plane_one, 0)

    @pl.when(slab == 0)
    def _():
        for q in range(Q):
            if VELOCITIES[q][0] > 0:
                second[q, 0] = jnp.zeros((rows, length), F32)

    @pl.when(slab == slab_end)
    def _():
        for q in range(Q):
            if VELOCITIES[q][0] < 0:
                second[q, planes + 1] = jnp.zeros((rows, length), F32)

    across = lax.broadcasted_iota(jnp.int32, (planes + 4, length), 0)
    hidden = ((across <= 1) & (slab == 0)) | ((across >= planes + 2) & (slab == slab_end))
    for sign, received, sent, edge, outside in (
        (1, behind, bottom, edge_low, inner == 0),
        (-1, ahead, top, edge_high, inner == inner_end),
    ):
        values = []
        for q in range(Q):
            step_x, step_y, _ = VELOCITIES[q]
            if step_y == 0:
                block = received[q]
            elif step_y == sign:
                block = received[OPPOSITE[q]]
            else:
                block = sent[q]
            values.append(roll_by(block, step_x, 0))
        result = collide(values, received[RATE_SLOT], received[FLAG_SLOT])
        place = 0
        for q in range(Q):
            if VELOCITIES[q][1] == sign:
                kept = jnp.where(hidden | outside, 0.0, result[q])
                edge[place] = roll_by(kept, VELOCITIES[q][2], 1)
                place += 1

    def plane_two(x, carry):
        values = []
        places = {1: 0, -1: 0}
        for q in range(Q):
            step_x, step_y, _ = VELOCITIES[q]
            block = second[q, x + 1 - step_x]
            if step_y > 0:
                edge = edge_low[places[1], pl.ds(x + 2 - step_x, 1)]
                places[1] += 1
                block = jnp.where(is_first, edge, roll_by(block, 1, 0))
            if step_y < 0:
                edge = edge_high[places[-1], pl.ds(x + 2 - step_x, 1)]
                places[-1] += 1
                block = jnp.where(is_last, edge, roll_by(block, -1, 0))
            values.append(block)
            out[q, x] = block
        density, flow_x, flow_y, flow_z = moments(values)
        parts = (
            LOAD_SCALE * flow_x,
            LOAD_SCALE * (flow_y + (density - 1.0) / 3.0),
            LOAD_SCALE * flow_z,
        )
        for part in range(3):
            for piece in range(half):
                loads[x * half + piece, part] = parts[part][:, piece * BLK : (piece + 1) * BLK]
        return carry

    lax.fori_loop(0, planes, plane_two, 0)

    node_blocks = internal_own.shape[1]
    live = block_count[0, 0]
    for k in range(slots):
        run = block_source[0, 0, k]
        x = run // (rows * half)
        left = run - x * (rows * half)
        y = left // half
        piece = left - y * half
        for part in range(3):
            message[4 * k + part : 4 * k + part + 1] = loads[x * half + piece, part, pl.ds(y, 1)]
        key = jnp.where(k < live, block_target[0, 0, k] * node_blocks + block_node[0, 0, k], -1)
        message[4 * k + 3 : 4 * k + 4] = jnp.broadcast_to(key, (1, BLK)).astype(F32)
    for part in range(3):
        start = 4 * slots + part * node_blocks
        message[start : start + node_blocks] = internal_own[part] + internal_other[part]


def shell_kernel(
    elements,
    displacement,
    next_nodes,
    shape_inverse,
    stiffness,
    own,
    other,
    ids,
    shapes,
    forces,
):
    node_dev = displacement.shape[1]
    node_blocks = node_dev // BLK
    runs = elements.shape[1] // BLK
    groups = runs // 8
    for j in range(runs):
        lanes = slice(j * BLK, (j + 1) * BLK)
        for row in range(3):
            ids[row, j : j + 1] = elements[row : row + 1, lanes]
            shapes[row, j : j + 1] = shape_inverse[row : row + 1, lanes]

    def compute(group, carry):
        rows = pl.ds(pl.multiple_of(group * 8, 8), 8)
        low = [ids[corner, rows] & (BLK - 1) for corner in range(3)]
        high = [ids[corner, rows] >> 7 for corner in range(3)]
        nodes = [[jnp.zeros((8, BLK), F32)] * 3 for _ in range(3)]
        for block in range(2 * node_blocks):
            source = displacement if block < node_blocks else next_nodes
            start = (block % node_blocks) * BLK
            table = [
                jnp.broadcast_to(source[part : part + 1, start : start + BLK], (8, BLK))
                for part in range(3)
            ]
            for corner in range(3):
                here = high[corner] == block
                for part in range(3):
                    picked = jnp.take_along_axis(
                        table[part], low[corner], axis=1, mode="promise_in_bounds"
                    )
                    nodes[corner][part] = jnp.where(here, picked, nodes[corner][part])
        diag_a = shapes[0, rows]
        skew_b = shapes[1, rows]
        diag_c = shapes[2, rows]
        stiff = stiffness[rows]
        first, second, third = nodes
        edge_one = [second[p] - first[p] for p in range(3)]
        edge_two = [third[p] - first[p] for p in range(3)]
        one = [diag_a * edge_one[p] for p in range(3)]
        two = [skew_b * edge_one[p] + diag_c * edge_two[p] for p in range(3)]
        one[0] = one[0] + 1.0
        two[1] = two[1] + 1.0
        aa = one[0] * one[0] + one[1] * one[1] + one[2] * one[2]
        ab = one[0] * two[0] + one[1] * two[1] + one[2] * two[2]
        bb = two[0] * two[0] + two[1] * two[1] + two[2] * two[2]
        determinant = aa * bb - ab * ab
        inverse_aa = bb / determinant
        inverse_ab = -ab / determinant
        inverse_bb = aa / determinant
        pressure = LAME_RATIO * (0.5 * jnp.log(determinant))
        for p in range(3):
            pulled_one = one[p] * inverse_aa + two[p] * inverse_ab
            pulled_two = one[p] * inverse_ab + two[p] * inverse_bb
            stress_one = stiff * (one[p] - pulled_one + pressure * pulled_one)
            stress_two = stiff * (two[p] - pulled_two + pressure * pulled_two)
            force_one = diag_a * stress_one + skew_b * stress_two
            force_two = diag_c * stress_two
            for corner, force in enumerate((-(force_one + force_two), force_one, force_two)):
                rest = force
                for part in range(3):
                    piece = rest.astype(jnp.bfloat16).astype(F32)
                    rest = rest - piece
                    forces[part * 3 + p, corner, rows] = piece
        return carry

    lax.fori_loop(0, groups, compute, 0)

    slots = 2 * node_blocks
    slot_ids = lax.broadcasted_iota(jnp.int32, (slots, BLK), 0)
    lane_ids = lax.broadcasted_iota(jnp.int32, (BLK, BLK), 0)

    def spread(group, total):
        corner = group // groups
        base = (group - corner * groups) * 8
        left = [[] for _ in range(9)]
        right = []
        for j in range(8):
            row = pl.ds(base + j, 1)
            numbers = ids[corner, row]
            here = slot_ids == (numbers >> 7)
            right.append(jnp.where(lane_ids == (numbers & (BLK - 1)), 1.0, 0.0).astype(jnp.bfloat16))
            for part in range(9):
                left[part].append(
                    jnp.where(here, forces[part, corner, row], 0.0).astype(jnp.bfloat16)
                )
        tall = jnp.concatenate([jnp.concatenate(part, axis=1) for part in left], axis=0)
        wide = jnp.concatenate(right, axis=1)
        return total + lax.dot_general(
            tall, wide, (((1,), (1,)), ((), ())), preferred_element_type=F32
        )

    total = lax.fori_loop(0, 3 * groups, spread, jnp.zeros((9 * slots, BLK), F32))
    for p in range(3):
        summed = (
            total[p * slots : (p + 1) * slots]
            + total[(3 + p) * slots : (4 + p) * slots]
            + total[(6 + p) * slots : (7 + p) * slots]
        )
        own[p] = summed[:node_blocks]
        other[p] = summed[node_blocks:]


def final_kernel(*refs):
    messages = refs[:-3]
    residual, motion, keys = refs[-3:]
    slots = keys.shape[0]
    node_blocks = residual.shape[1] // BLK
    count = len(messages)
    inner = lax.axis_index("inner")
    mine = messages[0]
    for k in range(slots):
        keys[k : k + 1] = mine[4 * k + 3 : 4 * k + 4]
    wanted = keys[...]
    node_ids = lax.broadcasted_iota(jnp.int32, (node_blocks, BLK), 0)
    own_ids = (node_ids + inner * node_blocks).astype(F32)
    external = [jnp.zeros((node_blocks, BLK), F32)] * 3
    moved = [jnp.zeros((slots, BLK), F32)] * 3
    for message in messages:
        for k in range(slots):
            key = message[4 * k + 3 : 4 * k + 4]
            here = own_ids == key
            same = wanted == key
            for part in range(3):
                row = message[4 * k + part : 4 * k + part + 1]
                external[part] = external[part] + jnp.where(here, row, 0.0)
                moved[part] = moved[part] + jnp.where(same, row, 0.0)
    for distance, message in enumerate(messages):
        sender = lax.rem(inner - distance + count, count)
        for b in range(node_blocks):
            key = jnp.broadcast_to(sender * node_blocks + b, (1, BLK)).astype(F32)
            same = wanted == key
            for part in range(3):
                at = 4 * slots + part * node_blocks + b
                moved[part] = moved[part] - jnp.where(same, message[at : at + 1], 0.0)
    live = wanted >= 0.0
    for part in range(3):
        start = 4 * slots + part * node_blocks
        left = external[part] - mine[start : start + node_blocks]
        for b in range(node_blocks):
            residual[part : part + 1, b * BLK : (b + 1) * BLK] = left[b : b + 1]
        shown = jnp.where(live, COMPLIANCE * moved[part], 0.0)
        for k in range(slots):
            motion[0, 0, k, part : part + 1] = shown[k : k + 1]


def call(kernel, outs, scratch=(), scalars=0, inputs=0):
    return pl.pallas_call(
        kernel,
        out_shape=outs,
        in_specs=[pl.BlockSpec(memory_space=pltpu.SMEM)] * scalars
        + [pl.BlockSpec(memory_space=pltpu.VMEM)] * inputs,
        out_specs=jax.tree.map(lambda _: pl.BlockSpec(memory_space=pltpu.VMEM), outs),
        scratch_shapes=list(scratch),
        compiler_params=pltpu.CompilerParams(vmem_limit_bytes=VMEM_BYTES),
    )


def shift(block, axis, step):
    count = lax.axis_size(axis)
    route = [(i, i + step) for i in range(count) if 0 <= i + step < count]
    return lax.ppermute(block, axis, route)


def around(block, axis, step):
    count = lax.axis_size(axis)
    return lax.ppermute(block, axis, [(i, (i + step) % count) for i in range(count)])


def shards(
    populations,
    relaxation,
    node_flags,
    displacement,
    elements,
    shape_inverse,
    stiffness,
    block_source,
    block_target,
    block_node,
    block_count,
):
    planes, rows, length = populations.shape[1:]
    half = length // BLK
    node_dev = displacement.shape[1]
    node_blocks = node_dev // BLK
    runs = stiffness.shape[0] // BLK
    slots = block_source.shape[2]
    count = lax.axis_size("inner")
    shape = lambda *dims: jax.ShapeDtypeStruct(dims, F32)

    next_nodes = shift(displacement, "slab", -1)
    face = shape(SLOTS, rows, length)
    c1, up, down = call(first_kernel, (shape(*populations.shape), face, face), inputs=3)(
        populations, relaxation, node_flags
    )
    below = shift(up, "slab", 1)
    above = shift(down, "slab", -1)
    own, other = call(
        shell_kernel,
        (shape(3, node_blocks, BLK), shape(3, node_blocks, BLK)),
        scratch=(
            pltpu.VMEM((3, runs, BLK), jnp.int32),
            pltpu.VMEM((3, runs, BLK), F32),
            pltpu.VMEM((9, 3, runs, BLK), F32),
        ),
        inputs=5,
    )(elements, displacement, next_nodes, shape_inverse, stiffness.reshape(runs, BLK))
    arrived = shift(other, "slab", 1)
    side = shape(SLOTS, planes + 4, length)
    top, bottom = call(pack_kernel, (side, side), inputs=5)(
        c1, relaxation, node_flags, below, above
    )
    behind = shift(top, "inner", 1)
    ahead = shift(bottom, "inner", -1)
    lines = 4 * slots + 3 * node_blocks
    values, message = call(
        second_kernel,
        (shape(*populations.shape), shape(lines, BLK)),
        scratch=(
            pltpu.VMEM((Q, planes + 4, rows, length), F32),
            pltpu.VMEM((planes + 2, rows, length), F32),
            pltpu.VMEM((planes + 2, rows, length), F32),
            pltpu.VMEM((Q, planes + 2, rows, length), F32),
            pltpu.VMEM((5, planes + 4, length), F32),
            pltpu.VMEM((5, planes + 4, length), F32),
            pltpu.VMEM((planes * half, 3, rows, BLK), F32),
        ),
        scalars=4,
        inputs=11,
    )(
        block_source,
        block_target,
        block_node,
        block_count,
        c1,
        relaxation,
        node_flags,
        below,
        above,
        top,
        bottom,
        behind,
        ahead,
        own,
        arrived,
    )
    messages = [message] + [around(message, "inner", step) for step in range(1, count)]
    residual, motion = call(
        final_kernel,
        (shape(3, node_dev), shape(1, 1, slots, 3, BLK)),
        scratch=(pltpu.VMEM((slots, BLK), F32),),
        inputs=count,
    )(*messages)
    return values, residual, motion


def solution(mesh):
    return jax.shard_map(
        shards,
        mesh=mesh,
        in_specs=(
            P(None, ("group", "slab"), "inner", None),
            P(("group", "slab"), "inner", None),
            P(("group", "slab"), "inner", None),
            P(None, ("group", "slab", "inner")),
            P(None, ("group", "slab", "inner")),
            P(None, ("group", "slab", "inner")),
            P(("group", "slab", "inner")),
            P(("group", "slab"), "inner", None),
            P(("group", "slab"), "inner", None),
            P(("group", "slab"), "inner", None),
            P(("group", "slab"), "inner"),
        ),
        out_specs=(
            P(None, ("group", "slab"), "inner", None),
            P(None, ("group", "slab", "inner")),
            P(("group", "slab"), "inner", None, None, None),
        ),
        check_vma=False,
    )
```

```python
import functools

import jax
import jax.numpy as jnp
from jax import lax
from jax.experimental import pallas as pl
from jax.experimental.pallas import tpu as pltpu
from jax.sharding import PartitionSpec as P

BLK = 128
VELOCITIES = (
    (0, 0, 0),
    (1, 0, 0),
    (-1, 0, 0),
    (0, 1, 0),
    (0, -1, 0),
    (0, 0, 1),
    (0, 0, -1),
    (1, 1, 0),
    (-1, -1, 0),
    (1, -1, 0),
    (-1, 1, 0),
    (1, 0, 1),
    (-1, 0, -1),
    (1, 0, -1),
    (-1, 0, 1),
    (0, 1, 1),
    (0, -1, -1),
    (0, 1, -1),
    (0, -1, 1),
)
WEIGHTS = (1.0 / 3.0,) + (1.0 / 18.0,) * 6 + (1.0 / 36.0,) * 12
OPPOSITE = (0, 2, 1, 4, 3, 6, 5, 8, 7, 10, 9, 12, 11, 14, 13, 16, 15, 18, 17)
INLET_SPEED = 0.04
LOAD_SCALE = 25.0
COMPLIANCE = 0.5
LAME_RATIO = 2.0
Q = 19
FLAG_SLOT = 19
RATE_SLOT = 20
SLOTS = 21
FORCE_SLOT = SLOTS + 6
MESSAGE_SLOTS = FORCE_SLOT + 3
PIECES = 2
F32 = jnp.float32
VMEM_BYTES = 48 * 1024 * 1024


def moments(values):
    sums = [values[q] + values[q + 1] for q in range(1, Q, 2)]
    diffs = [values[q] - values[q + 1] for q in range(1, Q, 2)]
    density = values[0]
    for term in sums:
        density = density + term
    flows = []
    for axis in range(3):
        total = None
        for k, q in enumerate(range(1, Q, 2)):
            factor = VELOCITIES[q][axis]
            if factor == 0:
                continue
            if total is None:
                total = diffs[k] if factor > 0 else -diffs[k]
            else:
                total = total + diffs[k] if factor > 0 else total - diffs[k]
        flows.append(total)
    return density, flows[0], flows[1], flows[2]


def collide(values, rate, kind):
    density, flow_x, flow_y, flow_z = moments(values)
    inverse = 1.0 / density
    wall = kind == 1
    inlet = kind == 2
    fluid = kind == 0
    vel = (
        jnp.where(inlet, INLET_SPEED, flow_x * inverse),
        jnp.where(inlet, 0.0, flow_y * inverse),
        jnp.where(inlet, 0.0, flow_z * inverse),
    )
    scale = jnp.where(fluid, density, 1.0)
    rate = jnp.where(fluid, rate, 1.0)
    base = 1.0 - 1.5 * (vel[0] * vel[0] + vel[1] * vel[1] + vel[2] * vel[2])
    weighted = {w: w * scale for w in set(WEIGHTS)}
    out = [None] * Q
    relaxed = values[0] + rate * (weighted[WEIGHTS[0]] * base - values[0])
    out[0] = jnp.where(wall, values[0], relaxed)
    for q in range(1, Q, 2):
        project = None
        for factor, component in zip(VELOCITIES[q], vel):
            if factor == 0:
                continue
            if project is None:
                project = component
            else:
                project = project + component if factor > 0 else project - component
        even = base + 4.5 * (project * project)
        odd = 3.0 * project
        w = weighted[WEIGHTS[q]]
        forward = values[q] + rate * (w * (even + odd) - values[q])
        backward = values[q + 1] + rate * (w * (even - odd) - values[q + 1])
        out[q] = jnp.where(wall, values[q + 1], forward)
        out[q + 1] = jnp.where(wall, values[q], backward)
    return out


def roll_by(block, step, axis):
    if step == 0:
        return block
    return pltpu.roll(block, step % block.shape[axis], axis)


def face_slots(axis, sign):
    picks = []
    for q in range(Q):
        if VELOCITIES[q][axis] * sign >= 0:
            picks.append((q, 0))
        else:
            picks.append((OPPOSITE[q], 1))
    return picks


def mirror(q, axis):
    flipped = tuple(-c if k == axis else c for k, c in enumerate(VELOCITIES[q]))
    return VELOCITIES.index(flipped)


def corner_rows(sign_x, sign_y):
    rows = []
    for q, depth in face_slots(0, sign_x):
        if VELOCITIES[q][1] * sign_y >= 0:
            rows.append((q, depth))
        else:
            rows.append((OPPOSITE[mirror(q, 1)], depth))
    return rows


def first_kernel(pops_hbm, rate_hbm, flags_hbm, c1, fixed, near, far, pops, rate, flags, sems):
    planes, rows = c1.shape[1], c1.shape[2]
    inner = lax.axis_index("inner")
    even = lax.rem(inner, 2) == 0
    copies = [
        pltpu.make_async_copy(rate_hbm, rate, sems.at[planes]),
        pltpu.make_async_copy(flags_hbm, flags, sems.at[planes + 1]),
    ]
    loads = [
        pltpu.make_async_copy(pops_hbm.at[:, x], pops.at[x], sems.at[x]) for x in range(planes)
    ]
    for copy in loads[:1] + copies + loads[1:]:
        copy.start()
    for copy in copies:
        copy.wait()

    def plane(x, carry):
        pltpu.make_async_copy(pops_hbm.at[:, x], pops.at[x], sems.at[x]).wait()
        kind = flags[x]
        values = [pops[x, q] for q in range(Q)]
        result = collide(values, rate[x], kind)
        for q in range(Q):
            c1[q, x] = roll_by(result[q], VELOCITIES[q][2], 1)
        fixed[0, x] = kind.astype(F32)
        fixed[1, x] = rate[x]
        return carry

    lax.fori_loop(0, planes, plane, 0)

    def pack(out, sign, outside):
        def line(x, carry):
            for slot, (q, depth) in enumerate(face_slots(1, sign)):
                y = rows - 1 - depth if sign > 0 else depth
                out[slot, pl.ds(x, 1)] = c1[q, x, y : y + 1]
            y = rows - 1 if sign > 0 else 0
            for k, slot in enumerate((FLAG_SLOT, RATE_SLOT)):
                out[slot, pl.ds(x, 1)] = fixed[k, x, y : y + 1]
            return carry

        lax.fori_loop(0, planes, line, 0)

        @pl.when(outside)
        def _():
            out[...] = jnp.zeros(out.shape, F32)

    first_row, last_row = inner == 0, inner == lax.axis_size("inner") - 1

    @pl.when(even)
    def _():
        pack(near, 1, last_row)
        pack(far, -1, first_row)

    @pl.when(jnp.logical_not(even))
    def _():
        pack(near, -1, first_row)
        pack(far, 1, last_row)


def gather_both(near, far, both, axis):
    odd = lax.rem(lax.axis_index(axis), 2)
    for slot in range(both.shape[1]):
        both[1 - odd, slot] = near[slot]
        both[odd, slot] = far[slot]


def pack_kernel(c1, fixed, near, far, other, up_or_down, down_or_up, both):
    planes, rows = c1.shape[1], c1.shape[2]
    gather_both(near, far, both, "inner")
    slab = lax.axis_index("slab")
    even = lax.rem(slab, 2) == 0

    def pack(out, sign, outside):
        for slot, (q, depth) in enumerate(face_slots(0, sign)):
            out[slot] = c1[q, planes - 1 - depth if sign > 0 else depth]
        end = planes - 1 if sign > 0 else 0
        out[FLAG_SLOT] = fixed[0, end]
        out[RATE_SLOT] = fixed[1, end]
        for side, sign_y in enumerate((1, -1)):
            picks = corner_rows(sign, sign_y) + [(FLAG_SLOT, 0), (RATE_SLOT, 0)]
            for row, (slot, depth) in enumerate(picks):
                x = planes - 1 - depth if sign > 0 else depth
                at = SLOTS + 3 * side + row // 8
                out[at, row % 8 : row % 8 + 1] = both[side, slot, x : x + 1]
        for part in range(3):
            out[FORCE_SLOT + part] = other[part]

        @pl.when(outside)
        def _():
            out[...] = jnp.zeros(out.shape, F32)

    first_plane, last_plane = slab == 0, slab == lax.axis_size("slab") - 1

    @pl.when(even)
    def _():
        pack(up_or_down, 1, last_plane)
        pack(down_or_up, -1, first_plane)

    @pl.when(jnp.logical_not(even))
    def _():
        pack(up_or_down, -1, first_plane)
        pack(down_or_up, 1, last_plane)


def second_kernel(
    block_source,
    block_target,
    block_node,
    block_count,
    c1,
    fixed,
    near_y,
    far_y,
    near_x,
    far_x,
    internal_own,
    out,
    message,
    both_y,
    both_x,
    extended,
    walls,
    crossing,
    second,
    edges,
    loads,
):
    planes, rows, length = c1.shape[1:]
    half = length // BLK
    slots = block_source.shape[2]
    wide = planes + 4
    slab = lax.axis_index("slab")
    inner = lax.axis_index("inner")
    slab_end = lax.axis_size("slab") - 1
    inner_end = lax.axis_size("inner") - 1
    gather_both(near_y, far_y, both_y, "inner")
    gather_both(near_x, far_x, both_x, "slab")

    for q in range(Q):
        for x in range(planes):
            extended[q, x + 2] = c1[q, x]
        extended[q, 1] = both_x[0, q]
        extended[q, planes + 2] = both_x[1, q]
        if VELOCITIES[q][0] > 0:
            extended[q, 0] = both_x[0, OPPOSITE[q]]
        if VELOCITIES[q][0] < 0:
            extended[q, planes + 3] = both_x[1, OPPOSITE[q]]

    for side, sign in enumerate((1, -1)):
        y = 0 if sign > 0 else rows - 1
        own_row = slice(y, y + 1)
        place = 0
        for slot in range(SLOTS):
            walls[side, slot, 2 : planes + 2] = both_y[side, slot]
        for end, sign_x in enumerate((1, -1)):
            for row, (slot, depth) in enumerate(corner_rows(sign_x, sign)):
                at = (1 - depth) if sign_x > 0 else planes + 2 + depth
                source = SLOTS + 3 * side + row // 8
                walls[side, slot, at : at + 1] = both_x[end, source, row % 8 : row % 8 + 1]
            at = 1 if sign_x > 0 else planes + 2
            for row in (FLAG_SLOT, RATE_SLOT):
                source = SLOTS + 3 * side + row // 8
                walls[side, row, at : at + 1] = both_x[end, source, row % 8 : row % 8 + 1]
        for q in range(Q):
            if VELOCITIES[q][1] != -sign:
                continue
            for x in range(wide):
                crossing[side, place, x : x + 1] = extended[q, x, own_row]
            place += 1

    sub = lax.broadcasted_iota(jnp.int32, (rows, length), 0)
    is_first = sub == 0
    is_last = sub == rows - 1

    def with_edge(block, step_y, edge):
        if step_y > 0:
            return jnp.where(is_first, edge, roll_by(block, 1, 0))
        return jnp.where(is_last, edge, roll_by(block, -1, 0))

    def store_plane(at, rate, kind):
        values = []
        for q in range(Q):
            step_x, step_y, _ = VELOCITIES[q]
            block = extended[q, at + 1 - step_x]
            if step_y != 0:
                edge = walls[0 if step_y > 0 else 1, q, pl.ds(at + 1 - step_x, 1)]
                block = with_edge(block, step_y, edge)
            values.append(block)
        result = collide(values, rate, kind)
        for q in range(Q):
            second[q, at] = roll_by(result[q], VELOCITIES[q][2], 1)

    def inside_plane(x, carry):
        store_plane(x + 1, fixed[1, x], fixed[0, x])
        return carry

    def outside_plane(end, carry):
        store_plane(end * (planes + 1), both_x[end, RATE_SLOT], both_x[end, FLAG_SLOT])
        return carry

    lax.fori_loop(0, planes, inside_plane, 0)
    lax.fori_loop(0, 2, outside_plane, 0)

    @pl.when(slab == 0)
    def _():
        for q in range(Q):
            if VELOCITIES[q][0] > 0:
                second[q, 0] = jnp.zeros((rows, length), F32)

    @pl.when(slab == slab_end)
    def _():
        for q in range(Q):
            if VELOCITIES[q][0] < 0:
                second[q, planes + 1] = jnp.zeros((rows, length), F32)

    across = lax.broadcasted_iota(jnp.int32, (wide, length), 0)
    hidden = ((across <= 1) & (slab == 0)) | ((across >= planes + 2) & (slab == slab_end))
    for side, sign, outside in ((0, 1, inner == 0), (1, -1, inner == inner_end)):
        values = []
        place = 0
        for q in range(Q):
            step_x, step_y, _ = VELOCITIES[q]
            if step_y == 0:
                block = walls[side, q]
            elif step_y == sign:
                block = walls[side, OPPOSITE[q]]
            else:
                block = crossing[side, place]
                place += 1
            values.append(roll_by(block, step_x, 0))
        result = collide(values, walls[side, RATE_SLOT], walls[side, FLAG_SLOT])
        place = 0
        for q in range(Q):
            if VELOCITIES[q][1] == sign:
                kept = jnp.where(hidden | outside, 0.0, result[q])
                edges[side, place] = roll_by(kept, VELOCITIES[q][2], 1)
                place += 1

    def plane_two(x, carry):
        values = []
        places = {1: 0, -1: 0}
        for q in range(Q):
            step_x, step_y, _ = VELOCITIES[q]
            block = second[q, x + 1 - step_x]
            if step_y != 0:
                edge = edges[0 if step_y > 0 else 1, places[step_y], pl.ds(x + 2 - step_x, 1)]
                places[step_y] += 1
                block = with_edge(block, step_y, edge)
            values.append(block)
            out[q, x] = block
        density, flow_x, flow_y, flow_z = moments(values)
        parts = (
            LOAD_SCALE * flow_x,
            LOAD_SCALE * (flow_y + (density - 1.0) / 3.0),
            LOAD_SCALE * flow_z,
        )
        for part in range(3):
            for piece in range(half):
                loads[x * half + piece, part] = parts[part][:, piece * BLK : (piece + 1) * BLK]
        return carry

    lax.fori_loop(0, planes, plane_two, 0)

    node_blocks = internal_own.shape[1]
    live = block_count[0, 0]
    for k in range(slots):
        run = block_source[0, 0, k]
        x = run // (rows * half)
        left = run - x * (rows * half)
        y = left // half
        piece = left - y * half
        for part in range(3):
            message[4 * k + part : 4 * k + part + 1] = loads[x * half + piece, part, pl.ds(y, 1)]
        key = jnp.where(k < live, block_target[0, 0, k] * node_blocks + block_node[0, 0, k], -1)
        message[4 * k + 3 : 4 * k + 4] = jnp.broadcast_to(key, (1, BLK)).astype(F32)
    for part in range(3):
        start = 4 * slots + part * node_blocks
        for piece in range(half):
            at = piece * rows
            message[start + at : start + at + rows] = (
                internal_own[part, at : at + rows]
                + both_x[0, FORCE_SLOT + part, :, piece * BLK : (piece + 1) * BLK]
            )


def element_kernel(
    elements, displacement, next_nodes, shape_inverse, stiffness, low_ids, high_ids, forces, shapes
):
    node_dev = displacement.shape[1]
    node_blocks = node_dev // BLK
    runs = elements.shape[1] // BLK
    groups = runs // 8
    for j in range(runs):
        lanes = slice(j * BLK, (j + 1) * BLK)
        for row in range(3):
            number = elements[row : row + 1, lanes]
            low_ids[row, j : j + 1] = number & (BLK - 1)
            high_ids[row, j : j + 1] = number >> 7
            shapes[row, j : j + 1] = shape_inverse[row : row + 1, lanes]

    def compute(group, carry):
        rows = pl.ds(pl.multiple_of(group * 8, 8), 8)
        low = [low_ids[corner, rows] for corner in range(3)]
        high = [high_ids[corner, rows] for corner in range(3)]
        nodes = [[jnp.zeros((8, BLK), F32)] * 3 for _ in range(3)]
        for block in range(2 * node_blocks):
            source = displacement if block < node_blocks else next_nodes
            start = (block % node_blocks) * BLK
            table = [
                jnp.broadcast_to(source[part : part + 1, start : start + BLK], (8, BLK))
                for part in range(3)
            ]
            for corner in range(3):
                here = high[corner] == block
                for part in range(3):
                    picked = jnp.take_along_axis(
                        table[part], low[corner], axis=1, mode="promise_in_bounds"
                    )
                    nodes[corner][part] = jnp.where(here, picked, nodes[corner][part])
        diag_a = shapes[0, rows]
        skew_b = shapes[1, rows]
        diag_c = shapes[2, rows]
        stiff = stiffness[rows]
        first, second, third = nodes
        edge_one = [second[p] - first[p] for p in range(3)]
        edge_two = [third[p] - first[p] for p in range(3)]
        one = [diag_a * edge_one[p] for p in range(3)]
        two = [skew_b * edge_one[p] + diag_c * edge_two[p] for p in range(3)]
        one[0] = one[0] + 1.0
        two[1] = two[1] + 1.0
        aa = one[0] * one[0] + one[1] * one[1] + one[2] * one[2]
        ab = one[0] * two[0] + one[1] * two[1] + one[2] * two[2]
        bb = two[0] * two[0] + two[1] * two[1] + two[2] * two[2]
        determinant = aa * bb - ab * ab
        inverse_aa = bb / determinant
        inverse_ab = -ab / determinant
        inverse_bb = aa / determinant
        pressure = LAME_RATIO * (0.5 * jnp.log(determinant))
        for p in range(3):
            pulled_one = one[p] * inverse_aa + two[p] * inverse_ab
            pulled_two = one[p] * inverse_ab + two[p] * inverse_bb
            stress_one = stiff * (one[p] - pulled_one + pressure * pulled_one)
            stress_two = stiff * (two[p] - pulled_two + pressure * pulled_two)
            force_one = diag_a * stress_one + skew_b * stress_two
            force_two = diag_c * stress_two
            for corner, force in enumerate((-(force_one + force_two), force_one, force_two)):
                rest = force
                for part in range(PIECES):
                    piece = rest.astype(jnp.bfloat16).astype(F32)
                    rest = rest - piece
                    forces[part * 3 + p, corner, rows] = piece
        return carry

    lax.fori_loop(0, groups, compute, 0)


def spread_kernel(low_ids, high_ids, forces, own, other):
    node_blocks = own.shape[1]
    groups = low_ids.shape[1] // 8
    slots = 2 * node_blocks
    slot_ids = lax.broadcasted_iota(jnp.int32, (slots, BLK), 0)
    lane_ids = lax.broadcasted_iota(jnp.int32, (BLK, BLK), 0)

    def spread(group, total):
        corner = group // groups
        base = (group - corner * groups) * 8
        left = [[] for _ in range(3 * PIECES)]
        right = []
        for j in range(8):
            row = pl.ds(base + j, 1)
            here = slot_ids == high_ids[corner, row]
            right.append(jnp.where(lane_ids == low_ids[corner, row], 1.0, 0.0).astype(jnp.bfloat16))
            for part in range(3 * PIECES):
                left[part].append(
                    jnp.where(here, forces[part, corner, row], 0.0).astype(jnp.bfloat16)
                )
        tall = jnp.concatenate([jnp.concatenate(part, axis=1) for part in left], axis=0)
        wide = jnp.concatenate(right, axis=1)
        return total + lax.dot_general(
            tall, wide, (((1,), (1,)), ((), ())), preferred_element_type=F32
        )

    total = lax.fori_loop(0, 3 * groups, spread, jnp.zeros((3 * PIECES * slots, BLK), F32))
    half = other.shape[2] // BLK
    rows = other.shape[1]
    for p in range(3):
        summed = total[p * slots : (p + 1) * slots]
        for part in range(1, PIECES):
            start = (3 * part + p) * slots
            summed = summed + total[start : start + slots]
        own[p] = summed[:node_blocks]
        for piece in range(half):
            at = node_blocks + piece * rows
            other[p, :, piece * BLK : (piece + 1) * BLK] = summed[at : at + rows]


def final_kernel(count, *refs):
    messages = refs[:count]
    values, out_hbm, residual, motion, keys, sem = refs[count:]
    store = pltpu.make_async_copy(values, out_hbm, sem)
    store.start()
    slots = keys.shape[0]
    node_blocks = residual.shape[1] // BLK
    inner = lax.axis_index("inner")
    mine = messages[0]
    for k in range(slots):
        keys[k : k + 1] = mine[4 * k + 3 : 4 * k + 4]
    wanted = keys[...]
    node_ids = lax.broadcasted_iota(jnp.int32, (node_blocks, BLK), 0)
    own_ids = (node_ids + inner * node_blocks).astype(F32)
    external = [jnp.zeros((node_blocks, BLK), F32)] * 3
    moved = [jnp.zeros((slots, BLK), F32)] * 3
    for message in messages:
        for k in range(slots):
            key = message[4 * k + 3 : 4 * k + 4]
            here = own_ids == key
            same = wanted == key
            for part in range(3):
                row = message[4 * k + part : 4 * k + part + 1]
                external[part] = external[part] + jnp.where(here, row, 0.0)
                moved[part] = moved[part] + jnp.where(same, row, 0.0)
    for distance, message in enumerate(messages):
        sender = lax.rem(inner - distance + count, count)
        for b in range(node_blocks):
            key = jnp.broadcast_to(sender * node_blocks + b, (1, BLK)).astype(F32)
            same = wanted == key
            for part in range(3):
                at = 4 * slots + part * node_blocks + b
                moved[part] = moved[part] - jnp.where(same, message[at : at + 1], 0.0)
    live = wanted >= 0.0
    for part in range(3):
        start = 4 * slots + part * node_blocks
        left = external[part] - mine[start : start + node_blocks]
        for b in range(node_blocks):
            residual[part : part + 1, b * BLK : (b + 1) * BLK] = left[b : b + 1]
        motion[part] = jnp.where(live, COMPLIANCE * moved[part], 0.0)
    store.wait()


def call(kernel, outs, operands, spaces, scratch=(), out_spaces=None, micros=1.0):
    spec = lambda space: pl.BlockSpec(memory_space=space)
    out_spaces = out_spaces or (pltpu.VMEM,) * len(outs)
    return pl.pallas_call(
        kernel,
        out_shape=outs,
        in_specs=[spec(space) for space in spaces],
        out_specs=tuple(spec(space) for space in out_spaces),
        scratch_shapes=list(scratch),
        compiler_params=pltpu.CompilerParams(vmem_limit_bytes=VMEM_BYTES),
        cost_estimate=pl.CostEstimate(
            flops=0, bytes_accessed=int(micros * 3.6e6), transcendentals=0
        ),
    )(*operands)


def shift(block, axis, step):
    count = lax.axis_size(axis)
    route = [(i, i + step) for i in range(count) if 0 <= i + step < count]
    return lax.ppermute(block, axis, route)


def around(block, axis, step):
    count = lax.axis_size(axis)
    return lax.ppermute(block, axis, [(i, (i + step) % count) for i in range(count)])


def swap(near, far, axis):
    count = lax.axis_size(axis)
    outcome = []
    for block, start in ((near, 0), (far, 1)):
        partner = list(range(count))
        for i in range(start, count - 1, 2):
            partner[i], partner[i + 1] = i + 1, i
        outcome.append(lax.ppermute(block, axis, list(enumerate(partner))))
    return outcome


def shards(
    populations,
    relaxation,
    node_flags,
    displacement,
    elements,
    shape_inverse,
    stiffness,
    block_source,
    block_target,
    block_node,
    block_count,
):
    planes, rows, length = populations.shape[1:]
    half = length // BLK
    node_dev = displacement.shape[1]
    node_blocks = node_dev // BLK
    runs = stiffness.shape[0] // BLK
    slots = block_source.shape[2]
    count = lax.axis_size("inner")
    shape = lambda *dims: jax.ShapeDtypeStruct(dims, F32)
    whole = shape(*populations.shape)
    vmem, hbm, smem = pltpu.VMEM, pltpu.HBM, pltpu.SMEM

    next_nodes = shift(displacement, "slab", -1)
    face_y = shape(SLOTS, planes, length)
    c1, fixed, near, far = call(
        first_kernel,
        (whole, shape(2, planes, rows, length), face_y, face_y),
        (populations, relaxation, node_flags),
        (hbm,) * 3,
        scratch=(
            pltpu.VMEM((planes, Q, rows, length), F32),
            pltpu.VMEM((planes, rows, length), F32),
            pltpu.VMEM((planes, rows, length), jnp.int32),
            pltpu.SemaphoreType.DMA((planes + 2,)),
        ),
        micros=1.5,
    )
    near_y, far_y = swap(near, far, "inner")
    numbers = jax.ShapeDtypeStruct((3, runs, BLK), jnp.int32)
    low_ids, high_ids, forces = call(
        element_kernel,
        (numbers, numbers, shape(3 * PIECES, 3, runs, BLK)),
        (elements, displacement, next_nodes, shape_inverse, stiffness.reshape(runs, BLK)),
        (vmem,) * 5,
        scratch=(pltpu.VMEM((3, runs, BLK), F32),),
        micros=3.0,
    )
    own, other = call(
        spread_kernel,
        (shape(3, node_blocks, BLK), shape(3, node_blocks // half, length)),
        (low_ids, high_ids, forces),
        (vmem,) * 3,
        micros=3.0,
    )
    face_x = shape(MESSAGE_SLOTS, rows, length)
    near, far = call(
        pack_kernel,
        (face_x, face_x),
        (c1, fixed, near_y, far_y, other),
        (vmem,) * 5,
        scratch=(pltpu.VMEM((2, SLOTS, planes, length), F32),),
        micros=0.3,
    )
    near_x, far_x = swap(near, far, "slab")
    lines = 4 * slots + 3 * node_blocks
    values, message = call(
        second_kernel,
        (whole, shape(lines, BLK)),
        (
            block_source,
            block_target,
            block_node,
            block_count,
            c1,
            fixed,
            near_y,
            far_y,
            near_x,
            far_x,
            own,
        ),
        (smem,) * 4 + (vmem,) * 7,
        scratch=(
            pltpu.VMEM((2, SLOTS, planes, length), F32),
            pltpu.VMEM((2, MESSAGE_SLOTS, rows, length), F32),
            pltpu.VMEM((Q, planes + 4, rows, length), F32),
            pltpu.VMEM((2, SLOTS, planes + 4, length), F32),
            pltpu.VMEM((2, 5, planes + 4, length), F32),
            pltpu.VMEM((Q, planes + 2, rows, length), F32),
            pltpu.VMEM((2, 5, planes + 4, length), F32),
            pltpu.VMEM((planes * half, 3, rows, BLK), F32),
        ),
        micros=2.5,
    )
    messages = [message] + [around(message, "inner", step) for step in range(1, count)]
    populations_out, residual, motion = call(
        functools.partial(final_kernel, count),
        (whole, shape(3, node_dev), shape(3, slots, BLK)),
        (*messages, values),
        (vmem,) * (count + 1),
        out_spaces=(hbm, vmem, vmem),
        scratch=(pltpu.VMEM((slots, BLK), F32), pltpu.SemaphoreType.DMA(())),
        micros=0.8,
    )
    return populations_out, residual, motion.transpose(1, 0, 2)[None, None]


def solution(mesh):
    return jax.shard_map(
        shards,
        mesh=mesh,
        in_specs=(
            P(None, ("group", "slab"), "inner", None),
            P(("group", "slab"), "inner", None),
            P(("group", "slab"), "inner", None),
            P(None, ("group", "slab", "inner")),
            P(None, ("group", "slab", "inner")),
            P(None, ("group", "slab", "inner")),
            P(("group", "slab", "inner")),
            P(("group", "slab"), "inner", None),
            P(("group", "slab"), "inner", None),
            P(("group", "slab"), "inner", None),
            P(("group", "slab"), "inner"),
        ),
        out_specs=(
            P(None, ("group", "slab"), "inner", None),
            P(None, ("group", "slab", "inner")),
            P(("group", "slab"), "inner", None, None, None),
        ),
        check_vma=False,
    )
```

```python
import functools

import jax
import jax.numpy as jnp
from jax import lax
from jax.experimental import pallas as pl
from jax.experimental.pallas import tpu as pltpu
from jax.sharding import PartitionSpec as P

BLK = 128
VELOCITIES = (
    (0, 0, 0),
    (1, 0, 0),
    (-1, 0, 0),
    (0, 1, 0),
    (0, -1, 0),
    (0, 0, 1),
    (0, 0, -1),
    (1, 1, 0),
    (-1, -1, 0),
    (1, -1, 0),
    (-1, 1, 0),
    (1, 0, 1),
    (-1, 0, -1),
    (1, 0, -1),
    (-1, 0, 1),
    (0, 1, 1),
    (0, -1, -1),
    (0, 1, -1),
    (0, -1, 1),
)
WEIGHTS = (1.0 / 3.0,) + (1.0 / 18.0,) * 6 + (1.0 / 36.0,) * 12
OPPOSITE = (0, 2, 1, 4, 3, 6, 5, 8, 7, 10, 9, 12, 11, 14, 13, 16, 15, 18, 17)
INLET_SPEED = 0.04
LOAD_SCALE = 25.0
COMPLIANCE = 0.5
LAME_RATIO = 2.0
Q = 19
FLAG_SLOT = 19
RATE_SLOT = 20
SLOTS = 21
FORCE_SLOT = SLOTS + 6
MESSAGE_SLOTS = FORCE_SLOT + 3
PIECES = 2
F32 = jnp.float32
VMEM_BYTES = 48 * 1024 * 1024


def moments(values):
    sums = [values[q] + values[q + 1] for q in range(1, Q, 2)]
    diffs = [values[q] - values[q + 1] for q in range(1, Q, 2)]
    density = values[0]
    for term in sums:
        density = density + term
    flows = []
    for axis in range(3):
        total = None
        for k, q in enumerate(range(1, Q, 2)):
            factor = VELOCITIES[q][axis]
            if factor == 0:
                continue
            if total is None:
                total = diffs[k] if factor > 0 else -diffs[k]
            else:
                total = total + diffs[k] if factor > 0 else total - diffs[k]
        flows.append(total)
    return density, flows[0], flows[1], flows[2]


def collide(values, rate, kind):
    density, flow_x, flow_y, flow_z = moments(values)
    inverse = 1.0 / density
    wall = kind == 1
    inlet = kind == 2
    fluid = kind == 0
    vel = (
        jnp.where(inlet, INLET_SPEED, flow_x * inverse),
        jnp.where(inlet, 0.0, flow_y * inverse),
        jnp.where(inlet, 0.0, flow_z * inverse),
    )
    scale = jnp.where(fluid, density, 1.0)
    rate = jnp.where(fluid, rate, 1.0)
    base = 1.0 - 1.5 * (vel[0] * vel[0] + vel[1] * vel[1] + vel[2] * vel[2])
    weighted = {w: w * scale for w in set(WEIGHTS)}
    out = [None] * Q
    relaxed = values[0] + rate * (weighted[WEIGHTS[0]] * base - values[0])
    out[0] = jnp.where(wall, values[0], relaxed)
    for q in range(1, Q, 2):
        project = None
        for factor, component in zip(VELOCITIES[q], vel):
            if factor == 0:
                continue
            if project is None:
                project = component
            else:
                project = project + component if factor > 0 else project - component
        even = base + 4.5 * (project * project)
        odd = 3.0 * project
        w = weighted[WEIGHTS[q]]
        forward = values[q] + rate * (w * (even + odd) - values[q])
        backward = values[q + 1] + rate * (w * (even - odd) - values[q + 1])
        out[q] = jnp.where(wall, values[q + 1], forward)
        out[q + 1] = jnp.where(wall, values[q], backward)
    return out


def roll_by(block, step, axis):
    if step == 0:
        return block
    return pltpu.roll(block, step % block.shape[axis], axis)


def face_slots(axis, sign):
    picks = []
    for q in range(Q):
        if VELOCITIES[q][axis] * sign >= 0:
            picks.append((q, 0))
        else:
            picks.append((OPPOSITE[q], 1))
    return picks


def mirror(q, axis):
    flipped = tuple(-c if k == axis else c for k, c in enumerate(VELOCITIES[q]))
    return VELOCITIES.index(flipped)


def corner_rows(sign_x, sign_y):
    rows = []
    for q, depth in face_slots(0, sign_x):
        if VELOCITIES[q][1] * sign_y >= 0:
            rows.append((q, depth))
        else:
            rows.append((OPPOSITE[mirror(q, 1)], depth))
    return rows


def first_kernel(pops_hbm, rate_hbm, flags_hbm, c1, fixed, pops, rate, flags, sems):
    planes = c1.shape[1]
    copies = [
        pltpu.make_async_copy(rate_hbm, rate, sems.at[planes]),
        pltpu.make_async_copy(flags_hbm, flags, sems.at[planes + 1]),
    ]
    loads = [
        pltpu.make_async_copy(pops_hbm.at[:, x], pops.at[x], sems.at[x]) for x in range(planes)
    ]
    for copy in loads[:1] + copies + loads[1:]:
        copy.start()
    for copy in copies:
        copy.wait()

    def plane(x, carry):
        pltpu.make_async_copy(pops_hbm.at[:, x], pops.at[x], sems.at[x]).wait()
        kind = flags[x]
        values = [pops[x, q] for q in range(Q)]
        result = collide(values, rate[x], kind)
        for q in range(Q):
            c1[q, x] = roll_by(result[q], VELOCITIES[q][2], 1)
        fixed[0, x] = kind.astype(F32)
        fixed[1, x] = rate[x]
        return carry

    lax.fori_loop(0, planes, plane, 0)


def side_kernel(c1, fixed, next_nodes, near, far):
    del next_nodes
    planes, rows = c1.shape[1], c1.shape[2]
    inner = lax.axis_index("inner")
    even = lax.rem(inner, 2) == 0

    def pack(out, sign, outside):
        def line(x, carry):
            for slot, (q, depth) in enumerate(face_slots(1, sign)):
                y = rows - 1 - depth if sign > 0 else depth
                out[slot, pl.ds(x, 1)] = c1[q, x, y : y + 1]
            y = rows - 1 if sign > 0 else 0
            for k, slot in enumerate((FLAG_SLOT, RATE_SLOT)):
                out[slot, pl.ds(x, 1)] = fixed[k, x, y : y + 1]
            return carry

        lax.fori_loop(0, planes, line, 0)

        @pl.when(outside)
        def _():
            out[...] = jnp.zeros(out.shape, F32)

    first_row, last_row = inner == 0, inner == lax.axis_size("inner") - 1

    @pl.when(even)
    def _():
        pack(near, 1, last_row)
        pack(far, -1, first_row)

    @pl.when(jnp.logical_not(even))
    def _():
        pack(near, -1, first_row)
        pack(far, 1, last_row)


def gather_both(near, far, both, axis):
    odd = lax.rem(lax.axis_index(axis), 2)
    for slot in range(both.shape[1]):
        both[1 - odd, slot] = near[slot]
        both[odd, slot] = far[slot]


def pack_kernel(c1, fixed, near, far, other, up_or_down, down_or_up, both):
    planes, rows = c1.shape[1], c1.shape[2]
    gather_both(near, far, both, "inner")
    slab = lax.axis_index("slab")
    even = lax.rem(slab, 2) == 0

    def pack(out, sign, outside):
        for slot, (q, depth) in enumerate(face_slots(0, sign)):
            out[slot] = c1[q, planes - 1 - depth if sign > 0 else depth]
        end = planes - 1 if sign > 0 else 0
        out[FLAG_SLOT] = fixed[0, end]
        out[RATE_SLOT] = fixed[1, end]
        for side, sign_y in enumerate((1, -1)):
            picks = corner_rows(sign, sign_y) + [(FLAG_SLOT, 0), (RATE_SLOT, 0)]
            for row, (slot, depth) in enumerate(picks):
                x = planes - 1 - depth if sign > 0 else depth
                at = SLOTS + 3 * side + row // 8
                out[at, row % 8 : row % 8 + 1] = both[side, slot, x : x + 1]
        for part in range(3):
            out[FORCE_SLOT + part] = other[part]

        @pl.when(outside)
        def _():
            out[...] = jnp.zeros(out.shape, F32)

    first_plane, last_plane = slab == 0, slab == lax.axis_size("slab") - 1

    @pl.when(even)
    def _():
        pack(up_or_down, 1, last_plane)
        pack(down_or_up, -1, first_plane)

    @pl.when(jnp.logical_not(even))
    def _():
        pack(up_or_down, -1, first_plane)
        pack(down_or_up, 1, last_plane)


def second_kernel(
    block_source,
    block_target,
    block_node,
    block_count,
    c1,
    fixed,
    near_y,
    far_y,
    near_x,
    far_x,
    internal_own,
    out,
    message,
    both_y,
    both_x,
    extended,
    walls,
    crossing,
    second,
    edges,
    loads,
):
    planes, rows, length = c1.shape[1:]
    half = length // BLK
    slots = block_source.shape[2]
    wide = planes + 4
    slab = lax.axis_index("slab")
    inner = lax.axis_index("inner")
    slab_end = lax.axis_size("slab") - 1
    inner_end = lax.axis_size("inner") - 1
    gather_both(near_y, far_y, both_y, "inner")
    gather_both(near_x, far_x, both_x, "slab")

    for q in range(Q):
        for x in range(planes):
            extended[q, x + 2] = c1[q, x]
        extended[q, 1] = both_x[0, q]
        extended[q, planes + 2] = both_x[1, q]
        if VELOCITIES[q][0] > 0:
            extended[q, 0] = both_x[0, OPPOSITE[q]]
        if VELOCITIES[q][0] < 0:
            extended[q, planes + 3] = both_x[1, OPPOSITE[q]]

    for side, sign in enumerate((1, -1)):
        y = 0 if sign > 0 else rows - 1
        own_row = slice(y, y + 1)
        place = 0
        for slot in range(SLOTS):
            walls[side, slot, 2 : planes + 2] = both_y[side, slot]
        for end, sign_x in enumerate((1, -1)):
            for row, (slot, depth) in enumerate(corner_rows(sign_x, sign)):
                at = (1 - depth) if sign_x > 0 else planes + 2 + depth
                source = SLOTS + 3 * side + row // 8
                walls[side, slot, at : at + 1] = both_x[end, source, row % 8 : row % 8 + 1]
            at = 1 if sign_x > 0 else planes + 2
            for row in (FLAG_SLOT, RATE_SLOT):
                source = SLOTS + 3 * side + row // 8
                walls[side, row, at : at + 1] = both_x[end, source, row % 8 : row % 8 + 1]
        for q in range(Q):
            if VELOCITIES[q][1] != -sign:
                continue
            for x in range(wide):
                crossing[side, place, x : x + 1] = extended[q, x, own_row]
            place += 1

    sub = lax.broadcasted_iota(jnp.int32, (rows, length), 0)
    is_first = sub == 0
    is_last = sub == rows - 1

    def with_edge(block, step_y, edge):
        if step_y > 0:
            return jnp.where(is_first, edge, roll_by(block, 1, 0))
        return jnp.where(is_last, edge, roll_by(block, -1, 0))

    def store_plane(at, rate, kind):
        values = []
        for q in range(Q):
            step_x, step_y, _ = VELOCITIES[q]
            block = extended[q, at + 1 - step_x]
            if step_y != 0:
                edge = walls[0 if step_y > 0 else 1, q, pl.ds(at + 1 - step_x, 1)]
                block = with_edge(block, step_y, edge)
            values.append(block)
        result = collide(values, rate, kind)
        for q in range(Q):
            second[q, at] = roll_by(result[q], VELOCITIES[q][2], 1)

    def inside_plane(x, carry):
        store_plane(x + 1, fixed[1, x], fixed[0, x])
        return carry

    def outside_plane(end, carry):
        store_plane(end * (planes + 1), both_x[end, RATE_SLOT], both_x[end, FLAG_SLOT])
        return carry

    lax.fori_loop(0, planes, inside_plane, 0)
    lax.fori_loop(0, 2, outside_plane, 0)

    @pl.when(slab == 0)
    def _():
        for q in range(Q):
            if VELOCITIES[q][0] > 0:
                second[q, 0] = jnp.zeros((rows, length), F32)

    @pl.when(slab == slab_end)
    def _():
        for q in range(Q):
            if VELOCITIES[q][0] < 0:
                second[q, planes + 1] = jnp.zeros((rows, length), F32)

    across = lax.broadcasted_iota(jnp.int32, (wide, length), 0)
    hidden = ((across <= 1) & (slab == 0)) | ((across >= planes + 2) & (slab == slab_end))
    for side, sign, outside in ((0, 1, inner == 0), (1, -1, inner == inner_end)):
        values = []
        place = 0
        for q in range(Q):
            step_x, step_y, _ = VELOCITIES[q]
            if step_y == 0:
                block = walls[side, q]
            elif step_y == sign:
                block = walls[side, OPPOSITE[q]]
            else:
                block = crossing[side, place]
                place += 1
            values.append(roll_by(block, step_x, 0))
        result = collide(values, walls[side, RATE_SLOT], walls[side, FLAG_SLOT])
        place = 0
        for q in range(Q):
            if VELOCITIES[q][1] == sign:
                kept = jnp.where(hidden | outside, 0.0, result[q])
                edges[side, place] = roll_by(kept, VELOCITIES[q][2], 1)
                place += 1

    def plane_two(x, carry):
        values = []
        places = {1: 0, -1: 0}
        for q in range(Q):
            step_x, step_y, _ = VELOCITIES[q]
            block = second[q, x + 1 - step_x]
            if step_y != 0:
                edge = edges[0 if step_y > 0 else 1, places[step_y], pl.ds(x + 2 - step_x, 1)]
                places[step_y] += 1
                block = with_edge(block, step_y, edge)
            values.append(block)
            out[q, x] = block
        density, flow_x, flow_y, flow_z = moments(values)
        parts = (
            LOAD_SCALE * flow_x,
            LOAD_SCALE * (flow_y + (density - 1.0) / 3.0),
            LOAD_SCALE * flow_z,
        )
        for part in range(3):
            for piece in range(half):
                loads[x * half + piece, part] = parts[part][:, piece * BLK : (piece + 1) * BLK]
        return carry

    lax.fori_loop(0, planes, plane_two, 0)

    node_blocks = internal_own.shape[1]
    live = block_count[0, 0]
    for k in range(slots):
        run = block_source[0, 0, k]
        x = run // (rows * half)
        left = run - x * (rows * half)
        y = left // half
        piece = left - y * half
        for part in range(3):
            message[4 * k + part : 4 * k + part + 1] = loads[x * half + piece, part, pl.ds(y, 1)]
        key = jnp.where(k < live, block_target[0, 0, k] * node_blocks + block_node[0, 0, k], -1)
        message[4 * k + 3 : 4 * k + 4] = jnp.broadcast_to(key, (1, BLK)).astype(F32)
    for part in range(3):
        start = 4 * slots + part * node_blocks
        for piece in range(half):
            at = piece * rows
            message[start + at : start + at + rows] = (
                internal_own[part, at : at + rows]
                + both_x[0, FORCE_SLOT + part, :, piece * BLK : (piece + 1) * BLK]
            )


def element_kernel(
    elements, displacement, next_nodes, shape_inverse, stiffness, low_ids, high_ids, forces, shapes,
    numbers, corners,
):
    node_dev = displacement.shape[1]
    node_blocks = node_dev // BLK
    runs = elements.shape[1] // BLK
    for j in range(runs):
        lanes = slice(j * BLK, (j + 1) * BLK)
        for row in range(3):
            numbers[row, j : j + 1] = elements[row : row + 1, lanes]
            shapes[row, j : j + 1] = shape_inverse[row : row + 1, lanes]
    for row in range(3):
        low_ids[row] = (numbers[row] & (BLK - 1)).astype(F32)
        high_ids[row] = (numbers[row] >> 7).astype(F32)

    def gather(group, carry):
        rows = pl.ds(pl.multiple_of(group * 8, 8), 8)
        low = [numbers[corner, rows] & (BLK - 1) for corner in range(3)]
        high = [numbers[corner, rows] >> 7 for corner in range(3)]
        nodes = [[jnp.zeros((8, BLK), F32)] * 3 for _ in range(3)]
        for block in range(2 * node_blocks):
            source = displacement if block < node_blocks else next_nodes
            start = (block % node_blocks) * BLK
            table = [
                jnp.broadcast_to(source[part : part + 1, start : start + BLK], (8, BLK))
                for part in range(3)
            ]
            for corner in range(3):
                here = high[corner] == block
                for part in range(3):
                    picked = jnp.take_along_axis(
                        table[part], low[corner], axis=1, mode="promise_in_bounds"
                    )
                    nodes[corner][part] = jnp.where(here, picked, nodes[corner][part])
        for corner in range(3):
            for part in range(3):
                corners[corner, part, rows] = nodes[corner][part]
        return carry

    lax.fori_loop(0, runs // 8, gather, 0)

    first, second, third = [[corners[c, p] for p in range(3)] for c in range(3)]
    diag_a = shapes[0]
    skew_b = shapes[1]
    diag_c = shapes[2]
    stiff = stiffness[...]
    edge_one = [second[p] - first[p] for p in range(3)]
    edge_two = [third[p] - first[p] for p in range(3)]
    one = [diag_a * edge_one[p] for p in range(3)]
    two = [skew_b * edge_one[p] + diag_c * edge_two[p] for p in range(3)]
    one[0] = one[0] + 1.0
    two[1] = two[1] + 1.0
    aa = one[0] * one[0] + one[1] * one[1] + one[2] * one[2]
    ab = one[0] * two[0] + one[1] * two[1] + one[2] * two[2]
    bb = two[0] * two[0] + two[1] * two[1] + two[2] * two[2]
    determinant = aa * bb - ab * ab
    scale = 1.0 / determinant
    inverse_aa = bb * scale
    inverse_ab = -ab * scale
    inverse_bb = aa * scale
    pressure = LAME_RATIO * (0.5 * jnp.log(determinant))
    for p in range(3):
        pulled_one = one[p] * inverse_aa + two[p] * inverse_ab
        pulled_two = one[p] * inverse_ab + two[p] * inverse_bb
        stress_one = stiff * (one[p] - pulled_one + pressure * pulled_one)
        stress_two = stiff * (two[p] - pulled_two + pressure * pulled_two)
        force_one = diag_a * stress_one + skew_b * stress_two
        force_two = diag_c * stress_two
        for corner, force in enumerate((-(force_one + force_two), force_one, force_two)):
            rest = force
            for part in range(PIECES):
                piece = rest.astype(jnp.bfloat16).astype(F32)
                rest = rest - piece
                forces[part * 3 + p, corner] = piece


def spread_kernel(low_ids, high_ids, forces, own, other):
    node_blocks = own.shape[1]
    runs = low_ids.shape[1]
    slots = 2 * node_blocks
    kind = jnp.bfloat16
    tile = 16
    slot_ids = lax.broadcasted_iota(jnp.int32, (slots, BLK), 0).astype(F32).astype(kind)
    lane_ids = lax.broadcasted_iota(jnp.int32, (BLK, BLK), 0).astype(F32).astype(kind)
    ones = jnp.ones((BLK, BLK), kind)
    none = jnp.zeros((BLK, BLK), kind)
    blank = jnp.zeros((slots, BLK), kind)

    def tall_row(row, count):
        block = jnp.broadcast_to(row, (tile, BLK)).astype(kind)
        return jnp.concatenate([block] * (count // tile), axis=0)

    total = None
    for corner in range(3):
        left = [[] for _ in range(3 * PIECES)]
        right = []
        for j in range(runs):
            row = slice(j, j + 1)
            here = slot_ids == tall_row(high_ids[corner, row], slots)
            right.append(jnp.where(lane_ids == tall_row(low_ids[corner, row], BLK), ones, none))
            for part in range(3 * PIECES):
                left[part].append(
                    jnp.where(here, tall_row(forces[part, corner, row], slots), blank)
                )
        tall = jnp.concatenate([jnp.concatenate(part, axis=1) for part in left], axis=0)
        wide = jnp.concatenate(right, axis=1)
        product = lax.dot_general(
            tall, wide, (((1,), (1,)), ((), ())), preferred_element_type=F32
        )
        total = product if total is None else total + product
    half = other.shape[2] // BLK
    rows = other.shape[1]
    for p in range(3):
        summed = total[p * slots : (p + 1) * slots]
        for part in range(1, PIECES):
            start = (3 * part + p) * slots
            summed = summed + total[start : start + slots]
        own[p] = summed[:node_blocks]
        for piece in range(half):
            at = node_blocks + piece * rows
            other[p, :, piece * BLK : (piece + 1) * BLK] = summed[at : at + rows]


def store_kernel(values, out_hbm, sem):
    store = pltpu.make_async_copy(values, out_hbm, sem)
    store.start()
    store.wait()


def final_kernel(count, *refs):
    messages = refs[:count]
    residual, motion, keys = refs[count:]
    slots = keys.shape[0]
    node_blocks = residual.shape[1] // BLK
    inner = lax.axis_index("inner")
    mine = messages[0]
    for k in range(slots):
        keys[k : k + 1] = mine[4 * k + 3 : 4 * k + 4]
    wanted = keys[...]
    node_ids = lax.broadcasted_iota(jnp.int32, (node_blocks, BLK), 0)
    own_ids = (node_ids + inner * node_blocks).astype(F32)
    external = [jnp.zeros((node_blocks, BLK), F32)] * 3
    moved = [jnp.zeros((slots, BLK), F32)] * 3
    for message in messages:
        for k in range(slots):
            key = message[4 * k + 3 : 4 * k + 4]
            here = own_ids == key
            same = wanted == key
            for part in range(3):
                row = message[4 * k + part : 4 * k + part + 1]
                external[part] = external[part] + jnp.where(here, row, 0.0)
                moved[part] = moved[part] + jnp.where(same, row, 0.0)
    for distance, message in enumerate(messages):
        sender = lax.rem(inner - distance + count, count)
        for b in range(node_blocks):
            key = jnp.broadcast_to(sender * node_blocks + b, (1, BLK)).astype(F32)
            same = wanted == key
            for part in range(3):
                at = 4 * slots + part * node_blocks + b
                moved[part] = moved[part] - jnp.where(same, message[at : at + 1], 0.0)
    live = wanted >= 0.0
    for part in range(3):
        start = 4 * slots + part * node_blocks
        left = external[part] - mine[start : start + node_blocks]
        for b in range(node_blocks):
            residual[part : part + 1, b * BLK : (b + 1) * BLK] = left[b : b + 1]
        motion[part] = jnp.where(live, COMPLIANCE * moved[part], 0.0)


def call(kernel, outs, operands, spaces, scratch=(), out_spaces=None, micros=1.0):
    spec = lambda space: pl.BlockSpec(memory_space=space)
    out_spaces = out_spaces or (pltpu.VMEM,) * len(outs)
    return pl.pallas_call(
        kernel,
        out_shape=outs,
        in_specs=[spec(space) for space in spaces],
        out_specs=tuple(spec(space) for space in out_spaces),
        scratch_shapes=list(scratch),
        compiler_params=pltpu.CompilerParams(vmem_limit_bytes=VMEM_BYTES),
        cost_estimate=pl.CostEstimate(
            flops=0, bytes_accessed=int(micros * 3.6e6), transcendentals=0
        ),
    )(*operands)


def around(block, axis, step):
    count = lax.axis_size(axis)
    return lax.ppermute(block, axis, [(i, (i + step) % count) for i in range(count)])


def swap(near, far, axis):
    count = lax.axis_size(axis)
    outcome = []
    for block, start in ((near, 0), (far, 1)):
        partner = list(range(count))
        for i in range(start, count - 1, 2):
            partner[i], partner[i + 1] = i + 1, i
        outcome.append(lax.ppermute(block, axis, list(enumerate(partner))))
    return outcome


def shards(
    populations,
    relaxation,
    node_flags,
    displacement,
    elements,
    shape_inverse,
    stiffness,
    block_source,
    block_target,
    block_node,
    block_count,
):
    planes, rows, length = populations.shape[1:]
    half = length // BLK
    node_dev = displacement.shape[1]
    node_blocks = node_dev // BLK
    runs = stiffness.shape[0] // BLK
    slots = block_source.shape[2]
    count = lax.axis_size("inner")
    shape = lambda *dims: jax.ShapeDtypeStruct(dims, F32)
    whole = shape(*populations.shape)
    vmem, hbm, smem = pltpu.VMEM, pltpu.HBM, pltpu.SMEM

    next_nodes = around(displacement, "slab", -1)
    face_y = shape(SLOTS, planes, length)
    pinned = [
        pltpu.with_memory_space_constraint(block, hbm)
        for block in (populations, relaxation, node_flags)
    ]
    c1, fixed = call(
        first_kernel,
        (whole, shape(2, planes, rows, length)),
        pinned,
        (hbm,) * 3,
        scratch=(
            pltpu.VMEM((planes, Q, rows, length), F32),
            pltpu.VMEM((planes, rows, length), F32),
            pltpu.VMEM((planes, rows, length), jnp.int32),
            pltpu.SemaphoreType.DMA((planes + 2,)),
        ),
        micros=1.5,
    )
    near, far = call(
        side_kernel, (face_y, face_y), (c1, fixed, next_nodes), (vmem,) * 3, micros=0.3
    )
    near_y, far_y = swap(near, far, "inner")
    numbers = shape(3, runs, BLK)
    low_ids, high_ids, forces = call(
        element_kernel,
        (numbers, numbers, shape(3 * PIECES, 3, runs, BLK)),
        (elements, displacement, next_nodes, shape_inverse, stiffness.reshape(runs, BLK)),
        (vmem,) * 5,
        scratch=(
            pltpu.VMEM((3, runs, BLK), F32),
            pltpu.VMEM((3, runs, BLK), jnp.int32),
            pltpu.VMEM((3, 3, runs, BLK), F32),
        ),
        micros=2.0,
    )
    own, other = call(
        spread_kernel,
        (shape(3, node_blocks, BLK), shape(3, node_blocks // half, length)),
        (low_ids, high_ids, forces),
        (vmem,) * 3,
        micros=3.0,
    )
    face_x = shape(MESSAGE_SLOTS, rows, length)
    near, far = call(
        pack_kernel,
        (face_x, face_x),
        (c1, fixed, near_y, far_y, other),
        (vmem,) * 5,
        scratch=(pltpu.VMEM((2, SLOTS, planes, length), F32),),
        micros=0.3,
    )
    near_x, far_x = swap(near, far, "slab")
    lines = 4 * slots + 3 * node_blocks
    values, message = call(
        second_kernel,
        (whole, shape(lines, BLK)),
        (
            block_source,
            block_target,
            block_node,
            block_count,
            c1,
            fixed,
            near_y,
            far_y,
            near_x,
            far_x,
            own,
        ),
        (smem,) * 4 + (vmem,) * 7,
        scratch=(
            pltpu.VMEM((2, SLOTS, planes, length), F32),
            pltpu.VMEM((2, MESSAGE_SLOTS, rows, length), F32),
            pltpu.VMEM((Q, planes + 4, rows, length), F32),
            pltpu.VMEM((2, SLOTS, planes + 4, length), F32),
            pltpu.VMEM((2, 5, planes + 4, length), F32),
            pltpu.VMEM((Q, planes + 2, rows, length), F32),
            pltpu.VMEM((2, 5, planes + 4, length), F32),
            pltpu.VMEM((planes * half, 3, rows, BLK), F32),
        ),
        micros=2.5,
    )
    messages = [message] + [around(message, "inner", step) for step in range(1, count)]
    (populations_out,) = call(
        store_kernel,
        (whole,),
        (values,),
        (vmem,),
        out_spaces=(hbm,),
        scratch=(pltpu.SemaphoreType.DMA(()),),
        micros=1.0,
    )
    residual, motion = call(
        functools.partial(final_kernel, count),
        (shape(3, node_dev), shape(3, slots, BLK)),
        messages,
        (vmem,) * count,
        scratch=(pltpu.VMEM((slots, BLK), F32),),
        micros=0.8,
    )
    return populations_out, residual, motion.transpose(1, 0, 2)[None, None]


def solution(mesh):
    return jax.shard_map(
        shards,
        mesh=mesh,
        in_specs=(
            P(None, ("group", "slab"), "inner", None),
            P(("group", "slab"), "inner", None),
            P(("group", "slab"), "inner", None),
            P(None, ("group", "slab", "inner")),
            P(None, ("group", "slab", "inner")),
            P(None, ("group", "slab", "inner")),
            P(("group", "slab", "inner")),
            P(("group", "slab"), "inner", None),
            P(("group", "slab"), "inner", None),
            P(("group", "slab"), "inner", None),
            P(("group", "slab"), "inner"),
        ),
        out_specs=(
            P(None, ("group", "slab"), "inner", None),
            P(None, ("group", "slab", "inner")),
            P(("group", "slab"), "inner", None, None, None),
        ),
        check_vma=False,
    )
```

```python
import functools

import jax
import jax.numpy as jnp
from jax import lax
from jax.experimental import pallas as pl
from jax.experimental.pallas import tpu as pltpu
from jax.sharding import PartitionSpec as P

BLK = 128
VELOCITIES = (
    (0, 0, 0),
    (1, 0, 0),
    (-1, 0, 0),
    (0, 1, 0),
    (0, -1, 0),
    (0, 0, 1),
    (0, 0, -1),
    (1, 1, 0),
    (-1, -1, 0),
    (1, -1, 0),
    (-1, 1, 0),
    (1, 0, 1),
    (-1, 0, -1),
    (1, 0, -1),
    (-1, 0, 1),
    (0, 1, 1),
    (0, -1, -1),
    (0, 1, -1),
    (0, -1, 1),
)
WEIGHTS = (1.0 / 3.0,) + (1.0 / 18.0,) * 6 + (1.0 / 36.0,) * 12
OPPOSITE = (0, 2, 1, 4, 3, 6, 5, 8, 7, 10, 9, 12, 11, 14, 13, 16, 15, 18, 17)
INLET_SPEED = 0.04
LOAD_SCALE = 25.0
COMPLIANCE = 0.5
LAME_RATIO = 2.0
Q = 19
FLAG_SLOT = 19
RATE_SLOT = 20
SLOTS = 21
FORCE_SLOT = 6
CORNER_SLOTS = FORCE_SLOT + 3
PIECES = 2
F32 = jnp.float32
VMEM_BYTES = 48 * 1024 * 1024


def moments(values):
    sums = [values[q] + values[q + 1] for q in range(1, Q, 2)]
    diffs = [values[q] - values[q + 1] for q in range(1, Q, 2)]
    density = values[0]
    for term in sums:
        density = density + term
    flows = []
    for axis in range(3):
        total = None
        for k, q in enumerate(range(1, Q, 2)):
            factor = VELOCITIES[q][axis]
            if factor == 0:
                continue
            if total is None:
                total = diffs[k] if factor > 0 else -diffs[k]
            else:
                total = total + diffs[k] if factor > 0 else total - diffs[k]
        flows.append(total)
    return density, flows[0], flows[1], flows[2]


def collide(values, rate, kind):
    density, flow_x, flow_y, flow_z = moments(values)
    inverse = 1.0 / density
    wall = kind == 1
    inlet = kind == 2
    fluid = kind == 0
    vel = (
        jnp.where(inlet, INLET_SPEED, flow_x * inverse),
        jnp.where(inlet, 0.0, flow_y * inverse),
        jnp.where(inlet, 0.0, flow_z * inverse),
    )
    scale = jnp.where(fluid, density, 1.0)
    rate = jnp.where(fluid, rate, 1.0)
    base = 1.0 - 1.5 * (vel[0] * vel[0] + vel[1] * vel[1] + vel[2] * vel[2])
    weighted = {w: w * scale for w in set(WEIGHTS)}
    out = [None] * Q
    relaxed = values[0] + rate * (weighted[WEIGHTS[0]] * base - values[0])
    out[0] = jnp.where(wall, values[0], relaxed)
    for q in range(1, Q, 2):
        project = None
        for factor, component in zip(VELOCITIES[q], vel):
            if factor == 0:
                continue
            if project is None:
                project = component
            else:
                project = project + component if factor > 0 else project - component
        even = base + 4.5 * (project * project)
        odd = 3.0 * project
        w = weighted[WEIGHTS[q]]
        forward = values[q] + rate * (w * (even + odd) - values[q])
        backward = values[q + 1] + rate * (w * (even - odd) - values[q + 1])
        out[q] = jnp.where(wall, values[q + 1], forward)
        out[q + 1] = jnp.where(wall, values[q], backward)
    return out


def roll_by(block, step, axis):
    if step == 0:
        return block
    return pltpu.roll(block, step % block.shape[axis], axis)


def face_slots(axis, sign):
    picks = []
    for q in range(Q):
        if VELOCITIES[q][axis] * sign >= 0:
            picks.append((q, 0))
        else:
            picks.append((OPPOSITE[q], 1))
    return picks


def mirror(q, axis):
    flipped = tuple(-c if k == axis else c for k, c in enumerate(VELOCITIES[q]))
    return VELOCITIES.index(flipped)


def corner_rows(sign_x, sign_y):
    rows = []
    for q, depth in face_slots(0, sign_x):
        if VELOCITIES[q][1] * sign_y >= 0:
            rows.append((q, depth))
        else:
            rows.append((OPPOSITE[mirror(q, 1)], depth))
    return rows


def first_kernel(
    pops_hbm, rate_hbm, flags_hbm, c1, fixed, near, far, pops, rate, flags, sems
):
    planes = c1.shape[1]
    copies = [
        pltpu.make_async_copy(rate_hbm, rate, sems.at[planes]),
        pltpu.make_async_copy(flags_hbm, flags, sems.at[planes + 1]),
    ]
    loads = [
        pltpu.make_async_copy(pops_hbm.at[:, x], pops.at[x], sems.at[x]) for x in range(planes)
    ]
    for copy in loads[:1] + copies + loads[1:]:
        copy.start()
    for copy in copies:
        copy.wait()

    def plane(x, carry):
        pltpu.make_async_copy(pops_hbm.at[:, x], pops.at[x], sems.at[x]).wait()
        kind = flags[x]
        values = [pops[x, q] for q in range(Q)]
        result = collide(values, rate[x], kind)
        for q in range(Q):
            c1[q, x] = roll_by(result[q], VELOCITIES[q][2], 1)
        fixed[0, x] = kind.astype(F32)
        fixed[1, x] = rate[x]
        return carry

    lax.fori_loop(0, planes, plane, 0)

    def pack(out, sign, outside):
        for slot, (q, depth) in enumerate(face_slots(0, sign)):
            out[slot] = c1[q, planes - 1 - depth if sign > 0 else depth]
        end = planes - 1 if sign > 0 else 0
        out[FLAG_SLOT] = fixed[0, end]
        out[RATE_SLOT] = fixed[1, end]
        clear_outside(out, outside)

    pack_pair(pack, "slab", near, far)


def clear_outside(out, outside):
    @pl.when(outside)
    def _():
        out[...] = jnp.zeros(out.shape, F32)


def pack_pair(pack, axis, near, far):
    at = lax.axis_index(axis)
    even = lax.rem(at, 2) == 0
    first, last = at == 0, at == lax.axis_size(axis) - 1

    @pl.when(even)
    def _():
        pack(near, 1, last)
        pack(far, -1, first)

    @pl.when(jnp.logical_not(even))
    def _():
        pack(near, -1, first)
        pack(far, 1, last)


def side_kernel(c1, fixed, next_nodes, near, far):
    del next_nodes
    planes, rows = c1.shape[1], c1.shape[2]

    def pack(out, sign, outside):
        def line(x, carry):
            for slot, (q, depth) in enumerate(face_slots(1, sign)):
                y = rows - 1 - depth if sign > 0 else depth
                out[slot, pl.ds(x, 1)] = c1[q, x, y : y + 1]
            y = rows - 1 if sign > 0 else 0
            for k, slot in enumerate((FLAG_SLOT, RATE_SLOT)):
                out[slot, pl.ds(x, 1)] = fixed[k, x, y : y + 1]
            return carry

        lax.fori_loop(0, planes, line, 0)
        clear_outside(out, outside)

    pack_pair(pack, "inner", near, far)


def gather_both(near, far, both, axis):
    odd = lax.rem(lax.axis_index(axis), 2)
    for slot in range(both.shape[1]):
        both[1 - odd, slot] = near[slot]
        both[odd, slot] = far[slot]


def corner_kernel(near_y, far_y, other, near, far, both):
    planes = near_y.shape[1]
    gather_both(near_y, far_y, both, "inner")

    def pack(out, sign, outside):
        for side, sign_y in enumerate((1, -1)):
            picks = corner_rows(sign, sign_y) + [(FLAG_SLOT, 0), (RATE_SLOT, 0)]
            for row, (slot, depth) in enumerate(picks):
                x = planes - 1 - depth if sign > 0 else depth
                at = 3 * side + row // 8
                out[at, row % 8 : row % 8 + 1] = both[side, slot, x : x + 1]
        for part in range(3):
            out[FORCE_SLOT + part] = other[part]
        clear_outside(out, outside)

    pack_pair(pack, "slab", near, far)


def with_edge(block, step_y, edge):
    rows = block.shape[0]
    sub = lax.broadcasted_iota(jnp.int32, block.shape, 0)
    if step_y > 0:
        return jnp.where(sub == 0, edge, roll_by(block, 1, 0))
    return jnp.where(sub == rows - 1, edge, roll_by(block, -1, 0))


def store_plane(extended, walls, second, at, rate, kind):
    values = []
    for q in range(Q):
        step_x, step_y, _ = VELOCITIES[q]
        block = extended[q, at + 1 - step_x]
        if step_y != 0:
            edge = walls[0 if step_y > 0 else 1, q, pl.ds(at + 1 - step_x, 1)]
            block = with_edge(block, step_y, edge)
        values.append(block)
    result = collide(values, rate, kind)
    for q in range(Q):
        second[q, at] = roll_by(result[q], VELOCITIES[q][2], 1)


def inside_kernel(
    c1,
    fixed,
    near_y,
    far_y,
    near_x,
    far_x,
    extended,
    walls,
    crossing,
    second,
    ends,
    both_y,
    both_x,
):
    planes, rows, _ = c1.shape[1:]
    wide = planes + 4
    gather_both(near_y, far_y, both_y, "inner")
    gather_both(near_x, far_x, both_x, "slab")
    for q in range(Q):
        for x in range(planes):
            extended[q, x + 2] = c1[q, x]
        extended[q, 1] = both_x[0, q]
        extended[q, planes + 2] = both_x[1, q]
        if VELOCITIES[q][0] > 0:
            extended[q, 0] = both_x[0, OPPOSITE[q]]
        if VELOCITIES[q][0] < 0:
            extended[q, planes + 3] = both_x[1, OPPOSITE[q]]
    for end in range(2):
        ends[end, 0] = both_x[end, FLAG_SLOT]
        ends[end, 1] = both_x[end, RATE_SLOT]

    for side, sign in enumerate((1, -1)):
        y = 0 if sign > 0 else rows - 1
        for slot in range(SLOTS):
            walls[side, slot, 2 : planes + 2] = both_y[side, slot]
        place = 0
        for q in range(Q):
            if VELOCITIES[q][1] != -sign:
                continue
            for x in range(wide):
                crossing[side, place, x : x + 1] = extended[q, x, y : y + 1]
            place += 1

    def inside_plane(x, carry):
        store_plane(extended, walls, second, x + 1, fixed[1, x], fixed[0, x])
        return carry

    lax.fori_loop(1, planes - 1, inside_plane, 0)


def second_kernel(
    block_source_hbm,
    block_target_hbm,
    block_node_hbm,
    block_count,
    near,
    far,
    fixed,
    extended,
    crossing,
    ends,
    internal_own,
    walls_in,
    second_in,
    out,
    message,
    walls,
    second,
    both,
    edges,
    loads,
    block_source,
    block_target,
    block_node,
    sems,
):
    del walls_in, second_in
    copies = [
        pltpu.make_async_copy(block_source_hbm, block_source, sems.at[0]),
        pltpu.make_async_copy(block_target_hbm, block_target, sems.at[1]),
        pltpu.make_async_copy(block_node_hbm, block_node, sems.at[2]),
    ]
    for copy in copies:
        copy.start()
    planes, rows, length = out.shape[1:]
    half = length // BLK
    slots = block_source.shape[2]
    wide = planes + 4
    slab = lax.axis_index("slab")
    inner = lax.axis_index("inner")
    slab_end = lax.axis_size("slab") - 1
    inner_end = lax.axis_size("inner") - 1
    gather_both(near, far, both, "slab")

    for side, sign in enumerate((1, -1)):
        for end, sign_x in enumerate((1, -1)):
            for row, (slot, depth) in enumerate(corner_rows(sign_x, sign)):
                at = (1 - depth) if sign_x > 0 else planes + 2 + depth
                source = 3 * side + row // 8
                walls[side, slot, at : at + 1] = both[end, source, row % 8 : row % 8 + 1]
            at = 1 if sign_x > 0 else planes + 2
            for row in (FLAG_SLOT, RATE_SLOT):
                source = 3 * side + row // 8
                walls[side, row, at : at + 1] = both[end, source, row % 8 : row % 8 + 1]

    def edge_plane(end, carry):
        x = end * (planes - 1)
        store_plane(extended, walls, second, x + 1, fixed[1, x], fixed[0, x])
        return carry

    def outside_plane(end, carry):
        store_plane(extended, walls, second, end * (planes + 1), ends[end, 1], ends[end, 0])
        return carry

    lax.fori_loop(0, 2, edge_plane, 0)
    lax.fori_loop(0, 2, outside_plane, 0)

    @pl.when(slab == 0)
    def _():
        for q in range(Q):
            if VELOCITIES[q][0] > 0:
                second[q, 0] = jnp.zeros((rows, length), F32)

    @pl.when(slab == slab_end)
    def _():
        for q in range(Q):
            if VELOCITIES[q][0] < 0:
                second[q, planes + 1] = jnp.zeros((rows, length), F32)

    across = lax.broadcasted_iota(jnp.int32, (wide, length), 0)
    hidden = ((across <= 1) & (slab == 0)) | ((across >= planes + 2) & (slab == slab_end))
    for side, sign, outside in ((0, 1, inner == 0), (1, -1, inner == inner_end)):
        values = []
        place = 0
        for q in range(Q):
            step_x, step_y, _ = VELOCITIES[q]
            if step_y == 0:
                block = walls[side, q]
            elif step_y == sign:
                block = walls[side, OPPOSITE[q]]
            else:
                block = crossing[side, place]
                place += 1
            values.append(roll_by(block, step_x, 0))
        result = collide(values, walls[side, RATE_SLOT], walls[side, FLAG_SLOT])
        place = 0
        for q in range(Q):
            if VELOCITIES[q][1] == sign:
                kept = jnp.where(hidden | outside, 0.0, result[q])
                edges[side, place] = roll_by(kept, VELOCITIES[q][2], 1)
                place += 1

    def plane_two(x, carry):
        values = []
        places = {1: 0, -1: 0}
        for q in range(Q):
            step_x, step_y, _ = VELOCITIES[q]
            block = second[q, x + 1 - step_x]
            if step_y != 0:
                edge = edges[0 if step_y > 0 else 1, places[step_y], pl.ds(x + 2 - step_x, 1)]
                places[step_y] += 1
                block = with_edge(block, step_y, edge)
            values.append(block)
            out[q, x] = block
        density, flow_x, flow_y, flow_z = moments(values)
        parts = (
            LOAD_SCALE * flow_x,
            LOAD_SCALE * (flow_y + (density - 1.0) / 3.0),
            LOAD_SCALE * flow_z,
        )
        for part in range(3):
            for piece in range(half):
                loads[x * half + piece, part] = parts[part][:, piece * BLK : (piece + 1) * BLK]
        return carry

    lax.fori_loop(0, planes, plane_two, 0)

    for copy in copies:
        copy.wait()
    node_blocks = internal_own.shape[1]
    live = jnp.broadcast_to(block_count[...], (1, BLK))
    for k in range(slots):
        run = block_source[0, 0, k]
        x = run // (rows * half)
        left = run - x * (rows * half)
        y = left // half
        piece = left - y * half
        for part in range(3):
            message[4 * k + part : 4 * k + part + 1] = loads[x * half + piece, part, pl.ds(y, 1)]
        key = block_target[0, 0, k] * node_blocks + block_node[0, 0, k]
        message[4 * k + 3 : 4 * k + 4] = jnp.where(live > k, key, -1).astype(F32)
    for part in range(3):
        start = 4 * slots + part * node_blocks
        for piece in range(half):
            at = piece * rows
            message[start + at : start + at + rows] = (
                internal_own[part, at : at + rows]
                + both[0, FORCE_SLOT + part, :, piece * BLK : (piece + 1) * BLK]
            )


def element_kernel(
    elements, displacement, next_nodes, shape_inverse, stiffness, low_ids, high_ids, forces, shapes,
    numbers, corners,
):
    node_dev = displacement.shape[1]
    node_blocks = node_dev // BLK
    runs = elements.shape[1] // BLK
    for j in range(runs):
        lanes = slice(j * BLK, (j + 1) * BLK)
        for row in range(3):
            numbers[row, j : j + 1] = elements[row : row + 1, lanes]
            shapes[row, j : j + 1] = shape_inverse[row : row + 1, lanes]
    for row in range(3):
        low_ids[row] = (numbers[row] & (BLK - 1)).astype(F32)
        high_ids[row] = (numbers[row] >> 7).astype(F32)

    def gather(group, carry):
        rows = pl.ds(pl.multiple_of(group * 8, 8), 8)
        low = [numbers[corner, rows] & (BLK - 1) for corner in range(3)]
        high = [numbers[corner, rows] >> 7 for corner in range(3)]
        nodes = [[jnp.zeros((8, BLK), F32)] * 3 for _ in range(3)]
        for block in range(2 * node_blocks):
            source = displacement if block < node_blocks else next_nodes
            start = (block % node_blocks) * BLK
            table = [
                jnp.broadcast_to(source[part : part + 1, start : start + BLK], (8, BLK))
                for part in range(3)
            ]
            for corner in range(3):
                here = high[corner] == block
                for part in range(3):
                    picked = jnp.take_along_axis(
                        table[part], low[corner], axis=1, mode="promise_in_bounds"
                    )
                    nodes[corner][part] = jnp.where(here, picked, nodes[corner][part])
        for corner in range(3):
            for part in range(3):
                corners[corner, part, rows] = nodes[corner][part]
        return carry

    lax.fori_loop(0, runs // 8, gather, 0)

    first, second, third = [[corners[c, p] for p in range(3)] for c in range(3)]
    diag_a = shapes[0]
    skew_b = shapes[1]
    diag_c = shapes[2]
    stiff = stiffness[...]
    edge_one = [second[p] - first[p] for p in range(3)]
    edge_two = [third[p] - first[p] for p in range(3)]
    one = [diag_a * edge_one[p] for p in range(3)]
    two = [skew_b * edge_one[p] + diag_c * edge_two[p] for p in range(3)]
    one[0] = one[0] + 1.0
    two[1] = two[1] + 1.0
    aa = one[0] * one[0] + one[1] * one[1] + one[2] * one[2]
    ab = one[0] * two[0] + one[1] * two[1] + one[2] * two[2]
    bb = two[0] * two[0] + two[1] * two[1] + two[2] * two[2]
    determinant = aa * bb - ab * ab
    scale = 1.0 / determinant
    inverse_aa = bb * scale
    inverse_ab = -ab * scale
    inverse_bb = aa * scale
    pressure = LAME_RATIO * (0.5 * jnp.log(determinant))
    for p in range(3):
        pulled_one = one[p] * inverse_aa + two[p] * inverse_ab
        pulled_two = one[p] * inverse_ab + two[p] * inverse_bb
        stress_one = stiff * (one[p] - pulled_one + pressure * pulled_one)
        stress_two = stiff * (two[p] - pulled_two + pressure * pulled_two)
        force_one = diag_a * stress_one + skew_b * stress_two
        force_two = diag_c * stress_two
        for corner, force in enumerate((-(force_one + force_two), force_one, force_two)):
            rest = force
            for part in range(PIECES):
                piece = rest.astype(jnp.bfloat16).astype(F32)
                rest = rest - piece
                forces[part * 3 + p, corner] = piece


def spread_kernel(low_ids, high_ids, forces, own, other):
    node_blocks = own.shape[1]
    runs = low_ids.shape[1]
    slots = 2 * node_blocks
    kind = jnp.bfloat16
    tile = 16
    slot_ids = lax.broadcasted_iota(jnp.int32, (slots, BLK), 0).astype(F32).astype(kind)
    lane_ids = lax.broadcasted_iota(jnp.int32, (BLK, BLK), 0).astype(F32).astype(kind)
    ones = jnp.ones((BLK, BLK), kind)
    none = jnp.zeros((BLK, BLK), kind)
    blank = jnp.zeros((slots, BLK), kind)

    def tall_row(row, count):
        block = jnp.broadcast_to(row, (tile, BLK)).astype(kind)
        return jnp.concatenate([block] * (count // tile), axis=0)

    total = None
    for corner in range(3):
        left = [[] for _ in range(3 * PIECES)]
        right = []
        for j in range(runs):
            row = slice(j, j + 1)
            here = slot_ids == tall_row(high_ids[corner, row], slots)
            right.append(jnp.where(lane_ids == tall_row(low_ids[corner, row], BLK), ones, none))
            for part in range(3 * PIECES):
                left[part].append(
                    jnp.where(here, tall_row(forces[part, corner, row], slots), blank)
                )
        tall = jnp.concatenate([jnp.concatenate(part, axis=1) for part in left], axis=0)
        wide = jnp.concatenate(right, axis=1)
        product = lax.dot_general(
            tall, wide, (((1,), (1,)), ((), ())), preferred_element_type=F32
        )
        total = product if total is None else total + product
    half = other.shape[2] // BLK
    rows = other.shape[1]
    for p in range(3):
        summed = total[p * slots : (p + 1) * slots]
        for part in range(1, PIECES):
            start = (3 * part + p) * slots
            summed = summed + total[start : start + slots]
        own[p] = summed[:node_blocks]
        for piece in range(half):
            at = node_blocks + piece * rows
            other[p, :, piece * BLK : (piece + 1) * BLK] = summed[at : at + rows]


def store_kernel(values, out_hbm, sem):
    store = pltpu.make_async_copy(values, out_hbm, sem)
    store.start()
    store.wait()


def final_kernel(count, *refs):
    messages = refs[:count]
    residual, motion, keys = refs[count:]
    slots = keys.shape[0]
    node_blocks = residual.shape[1] // BLK
    inner = lax.axis_index("inner")
    mine = messages[0]
    for k in range(slots):
        keys[k : k + 1] = mine[4 * k + 3 : 4 * k + 4]
    wanted = keys[...]
    node_ids = lax.broadcasted_iota(jnp.int32, (node_blocks, BLK), 0)
    own_ids = (node_ids + inner * node_blocks).astype(F32)
    external = [jnp.zeros((node_blocks, BLK), F32)] * 3
    moved = [jnp.zeros((slots, BLK), F32)] * 3
    for message in messages:
        for k in range(slots):
            key = message[4 * k + 3 : 4 * k + 4]
            here = own_ids == key
            same = wanted == key
            for part in range(3):
                row = message[4 * k + part : 4 * k + part + 1]
                external[part] = external[part] + jnp.where(here, row, 0.0)
                moved[part] = moved[part] + jnp.where(same, row, 0.0)
    for step, message in enumerate(messages):
        sender = partner_of(inner, step, count)
        for b in range(node_blocks):
            key = jnp.broadcast_to(sender * node_blocks + b, (1, BLK)).astype(F32)
            same = wanted == key
            for part in range(3):
                at = 4 * slots + part * node_blocks + b
                moved[part] = moved[part] - jnp.where(same, message[at : at + 1], 0.0)
    live = wanted >= 0.0
    for part in range(3):
        start = 4 * slots + part * node_blocks
        left = external[part] - mine[start : start + node_blocks]
        for b in range(node_blocks):
            residual[part : part + 1, b * BLK : (b + 1) * BLK] = left[b : b + 1]
        motion[part] = jnp.where(live, COMPLIANCE * moved[part], 0.0)


def call(kernel, outs, operands, spaces, scratch=(), out_spaces=None, micros=1.0, aliases=None):
    spec = lambda space: pl.BlockSpec(memory_space=space)
    out_spaces = out_spaces or (pltpu.VMEM,) * len(outs)
    return pl.pallas_call(
        kernel,
        out_shape=outs,
        in_specs=[spec(space) for space in spaces],
        out_specs=tuple(spec(space) for space in out_spaces),
        scratch_shapes=list(scratch),
        input_output_aliases=aliases or {},
        compiler_params=pltpu.CompilerParams(vmem_limit_bytes=VMEM_BYTES),
        cost_estimate=pl.CostEstimate(
            flops=0, bytes_accessed=int(micros * 3.6e6), transcendentals=0
        ),
    )(*operands)


def partner_of(at, step, count):
    if count & (count - 1) == 0:
        return at ^ step
    return (at + count - step) % count


def exchange(block, axis, step):
    count = lax.axis_size(axis)
    return lax.ppermute(block, axis, [(partner_of(i, step, count), i) for i in range(count)])


def around(block, axis, step):
    count = lax.axis_size(axis)
    return lax.ppermute(block, axis, [(i, (i + step) % count) for i in range(count)])


def swap(near, far, axis):
    count = lax.axis_size(axis)
    outcome = []
    for block, start in ((near, 0), (far, 1)):
        partner = list(range(count))
        for i in range(start, count - 1, 2):
            partner[i], partner[i + 1] = i + 1, i
        outcome.append(lax.ppermute(block, axis, list(enumerate(partner))))
    return outcome


def shards(
    populations,
    relaxation,
    node_flags,
    displacement,
    elements,
    shape_inverse,
    stiffness,
    block_source,
    block_target,
    block_node,
    block_count,
):
    planes, rows, length = populations.shape[1:]
    half = length // BLK
    node_dev = displacement.shape[1]
    node_blocks = node_dev // BLK
    runs = stiffness.shape[0] // BLK
    slots = block_source.shape[2]
    count = lax.axis_size("inner")
    shape = lambda *dims: jax.ShapeDtypeStruct(dims, F32)
    whole = shape(*populations.shape)
    vmem, hbm, smem = pltpu.VMEM, pltpu.HBM, pltpu.SMEM

    next_nodes = around(displacement, "slab", -1)
    face_y = shape(SLOTS, planes, length)
    face_x = shape(SLOTS, rows, length)
    pin = lambda block: pltpu.with_memory_space_constraint(block, hbm)
    c1, fixed, near, far = call(
        first_kernel,
        (whole, shape(2, planes, rows, length), face_x, face_x),
        (pin(populations), pin(relaxation), pin(node_flags)),
        (hbm,) * 3,
        scratch=(
            pltpu.VMEM((planes, Q, rows, length), F32),
            pltpu.VMEM((planes, rows, length), F32),
            pltpu.VMEM((planes, rows, length), jnp.int32),
            pltpu.SemaphoreType.DMA((planes + 2,)),
        ),
        micros=1.5,
    )
    near_x, far_x = swap(near, far, "slab")
    near, far = call(
        side_kernel, (face_y, face_y), (c1, fixed, next_nodes), (vmem,) * 3, micros=0.3
    )
    near_y, far_y = swap(near, far, "inner")
    numbers = shape(3, runs, BLK)
    low_ids, high_ids, forces = call(
        element_kernel,
        (numbers, numbers, shape(3 * PIECES, 3, runs, BLK)),
        (elements, displacement, next_nodes, shape_inverse, stiffness.reshape(runs, BLK)),
        (vmem,) * 5,
        scratch=(
            pltpu.VMEM((3, runs, BLK), F32),
            pltpu.VMEM((3, runs, BLK), jnp.int32),
            pltpu.VMEM((3, 3, runs, BLK), F32),
        ),
        micros=2.0,
    )
    own, other = call(
        spread_kernel,
        (shape(3, node_blocks, BLK), shape(3, node_blocks // half, length)),
        (low_ids, high_ids, forces),
        (vmem,) * 3,
        micros=3.0,
    )
    corner = shape(CORNER_SLOTS, rows, length)
    near, far = call(
        corner_kernel,
        (corner, corner),
        (near_y, far_y, other),
        (vmem,) * 3,
        scratch=(pltpu.VMEM((2, SLOTS, planes, length), F32),),
        micros=0.3,
    )
    near_c, far_c = swap(near, far, "slab")
    wide = planes + 4
    walls_shape = shape(2, SLOTS, wide, length)
    second_shape = shape(Q, planes + 2, rows, length)
    extended, walls, crossing, second, ends = call(
        inside_kernel,
        (
            shape(Q, wide, rows, length),
            walls_shape,
            shape(2, 5, wide, length),
            second_shape,
            shape(2, 2, rows, length),
        ),
        (c1, fixed, near_y, far_y, near_x, far_x),
        (vmem,) * 6,
        scratch=(
            pltpu.VMEM((2, SLOTS, planes, length), F32),
            pltpu.VMEM((2, SLOTS, rows, length), F32),
        ),
        micros=0.8,
    )
    lines = 4 * slots + 3 * node_blocks
    values, message, _, _ = call(
        second_kernel,
        (whole, shape(lines, BLK), walls_shape, second_shape),
        (
            pin(block_source),
            pin(block_target),
            pin(block_node),
            block_count,
            near_c,
            far_c,
            fixed,
            extended,
            crossing,
            ends,
            own,
            walls,
            second,
        ),
        (hbm,) * 3 + (vmem,) * 10,
        aliases={11: 2, 12: 3},
        scratch=(
            pltpu.VMEM((2, CORNER_SLOTS, rows, length), F32),
            pltpu.VMEM((2, 5, wide, length), F32),
            pltpu.VMEM((planes * half, 3, rows, BLK), F32),
            pltpu.SMEM(block_source.shape, jnp.int32),
            pltpu.SMEM(block_target.shape, jnp.int32),
            pltpu.SMEM(block_node.shape, jnp.int32),
            pltpu.SemaphoreType.DMA((3,)),
        ),
        micros=1.5,
    )
    messages = [message] + [exchange(message, "inner", step) for step in range(1, count)]
    (populations_out,) = call(
        store_kernel,
        (whole,),
        (values,),
        (vmem,),
        out_spaces=(hbm,),
        scratch=(pltpu.SemaphoreType.DMA(()),),
        micros=1.0,
    )
    residual, motion = call(
        functools.partial(final_kernel, count),
        (shape(3, node_dev), shape(3, slots, BLK)),
        messages,
        (vmem,) * count,
        scratch=(pltpu.VMEM((slots, BLK), F32),),
        micros=0.8,
    )
    return populations_out, residual, motion.transpose(1, 0, 2)[None, None]


def solution(mesh):
    return jax.shard_map(
        shards,
        mesh=mesh,
        in_specs=(
            P(None, ("group", "slab"), "inner", None),
            P(("group", "slab"), "inner", None),
            P(("group", "slab"), "inner", None),
            P(None, ("group", "slab", "inner")),
            P(None, ("group", "slab", "inner")),
            P(None, ("group", "slab", "inner")),
            P(("group", "slab", "inner")),
            P(("group", "slab"), "inner", None),
            P(("group", "slab"), "inner", None),
            P(("group", "slab"), "inner", None),
            P(("group", "slab"), "inner"),
        ),
        out_specs=(
            P(None, ("group", "slab"), "inner", None),
            P(None, ("group", "slab", "inner")),
            P(("group", "slab"), "inner", None, None, None),
        ),
        check_vma=False,
    )
```

```python
import functools

import jax
import jax.numpy as jnp
from jax import lax
from jax.experimental import pallas as pl
from jax.experimental.pallas import tpu as pltpu
from jax.sharding import PartitionSpec as P

BLK = 128
VELOCITIES = (
    (0, 0, 0),
    (1, 0, 0),
    (-1, 0, 0),
    (0, 1, 0),
    (0, -1, 0),
    (0, 0, 1),
    (0, 0, -1),
    (1, 1, 0),
    (-1, -1, 0),
    (1, -1, 0),
    (-1, 1, 0),
    (1, 0, 1),
    (-1, 0, -1),
    (1, 0, -1),
    (-1, 0, 1),
    (0, 1, 1),
    (0, -1, -1),
    (0, 1, -1),
    (0, -1, 1),
)
WEIGHTS = (1.0 / 3.0,) + (1.0 / 18.0,) * 6 + (1.0 / 36.0,) * 12
OPPOSITE = (0, 2, 1, 4, 3, 6, 5, 8, 7, 10, 9, 12, 11, 14, 13, 16, 15, 18, 17)
INLET_SPEED = 0.04
LOAD_SCALE = 25.0
COMPLIANCE = 0.5
LAME_RATIO = 2.0
Q = 19
FLAG_SLOT = 19
RATE_SLOT = 20
SLOTS = 21
FORCE_SLOT = 6
CORNER_SLOTS = FORCE_SLOT + 3
PIECES = 2
F32 = jnp.float32
VMEM_BYTES = 48 * 1024 * 1024


def moments(values):
    sums = [values[q] + values[q + 1] for q in range(1, Q, 2)]
    diffs = [values[q] - values[q + 1] for q in range(1, Q, 2)]
    density = values[0]
    for term in sums:
        density = density + term
    flows = []
    for axis in range(3):
        total = None
        for k, q in enumerate(range(1, Q, 2)):
            factor = VELOCITIES[q][axis]
            if factor == 0:
                continue
            if total is None:
                total = diffs[k] if factor > 0 else -diffs[k]
            else:
                total = total + diffs[k] if factor > 0 else total - diffs[k]
        flows.append(total)
    return density, flows[0], flows[1], flows[2]


def collide(values, rate, kind):
    density, flow_x, flow_y, flow_z = moments(values)
    inverse = 1.0 / density
    wall = kind == 1
    inlet = kind == 2
    fluid = kind == 0
    vel = (
        jnp.where(inlet, INLET_SPEED, flow_x * inverse),
        jnp.where(inlet, 0.0, flow_y * inverse),
        jnp.where(inlet, 0.0, flow_z * inverse),
    )
    scale = jnp.where(fluid, density, 1.0)
    rate = jnp.where(fluid, rate, 1.0)
    base = 1.0 - 1.5 * (vel[0] * vel[0] + vel[1] * vel[1] + vel[2] * vel[2])
    weighted = {w: w * scale for w in set(WEIGHTS)}
    out = [None] * Q
    relaxed = values[0] + rate * (weighted[WEIGHTS[0]] * base - values[0])
    out[0] = jnp.where(wall, values[0], relaxed)
    for q in range(1, Q, 2):
        project = None
        for factor, component in zip(VELOCITIES[q], vel):
            if factor == 0:
                continue
            if project is None:
                project = component
            else:
                project = project + component if factor > 0 else project - component
        even = base + 4.5 * (project * project)
        odd = 3.0 * project
        w = weighted[WEIGHTS[q]]
        forward = values[q] + rate * (w * (even + odd) - values[q])
        backward = values[q + 1] + rate * (w * (even - odd) - values[q + 1])
        out[q] = jnp.where(wall, values[q + 1], forward)
        out[q + 1] = jnp.where(wall, values[q], backward)
    return out


def roll_by(block, step, axis):
    if step == 0:
        return block
    return pltpu.roll(block, step % block.shape[axis], axis)


def face_slots(axis, sign):
    picks = []
    for q in range(Q):
        if VELOCITIES[q][axis] * sign >= 0:
            picks.append((q, 0))
        else:
            picks.append((OPPOSITE[q], 1))
    return picks


def mirror(q, axis):
    flipped = tuple(-c if k == axis else c for k, c in enumerate(VELOCITIES[q]))
    return VELOCITIES.index(flipped)


def corner_rows(sign_x, sign_y):
    rows = []
    for q, depth in face_slots(0, sign_x):
        if VELOCITIES[q][1] * sign_y >= 0:
            rows.append((q, depth))
        else:
            rows.append((OPPOSITE[mirror(q, 1)], depth))
    return rows


def first_kernel(
    pops_hbm, rate_hbm, flags_hbm, c1, fixed, far, near, pops, rate, flags, sems
):
    planes = c1.shape[1]
    copies = [
        pltpu.make_async_copy(rate_hbm, rate, sems.at[planes]),
        pltpu.make_async_copy(flags_hbm, flags, sems.at[planes + 1]),
    ]
    loads = [
        pltpu.make_async_copy(pops_hbm.at[:, x], pops.at[x], sems.at[x]) for x in range(planes)
    ]
    for copy in loads[:1] + copies + loads[1:]:
        copy.start()
    for copy in copies:
        copy.wait()

    def plane(x, carry):
        pltpu.make_async_copy(pops_hbm.at[:, x], pops.at[x], sems.at[x]).wait()
        kind = flags[x]
        values = [pops[x, q] for q in range(Q)]
        result = collide(values, rate[x], kind)
        for q in range(Q):
            c1[q, x] = roll_by(result[q], VELOCITIES[q][2], 1)
        fixed[0, x] = kind.astype(F32)
        fixed[1, x] = rate[x]
        return carry

    lax.fori_loop(0, planes, plane, 0)

    def pack(out, sign, outside):
        for slot, (q, depth) in enumerate(face_slots(0, sign)):
            out[slot] = c1[q, planes - 1 - depth if sign > 0 else depth]
        end = planes - 1 if sign > 0 else 0
        out[FLAG_SLOT] = fixed[0, end]
        out[RATE_SLOT] = fixed[1, end]
        clear_outside(out, outside)

    pack_pair(pack, "slab", near, far)


def clear_outside(out, outside):
    @pl.when(outside)
    def _():
        out[...] = jnp.zeros(out.shape, F32)


def pack_pair(pack, axis, near, far):
    at = lax.axis_index(axis)
    even = lax.rem(at, 2) == 0
    first, last = at == 0, at == lax.axis_size(axis) - 1

    @pl.when(even)
    def _():
        pack(near, 1, last)
        pack(far, -1, first)

    @pl.when(jnp.logical_not(even))
    def _():
        pack(near, -1, first)
        pack(far, 1, last)


def side_kernel(c1, fixed, next_nodes, far, near):
    del next_nodes
    planes, rows = c1.shape[1], c1.shape[2]

    def pack(out, sign, outside):
        def line(x, carry):
            for slot, (q, depth) in enumerate(face_slots(1, sign)):
                y = rows - 1 - depth if sign > 0 else depth
                out[slot, pl.ds(x, 1)] = c1[q, x, y : y + 1]
            y = rows - 1 if sign > 0 else 0
            for k, slot in enumerate((FLAG_SLOT, RATE_SLOT)):
                out[slot, pl.ds(x, 1)] = fixed[k, x, y : y + 1]
            return carry

        lax.fori_loop(0, planes, line, 0)
        clear_outside(out, outside)

    pack_pair(pack, "inner", near, far)


def gather_both(near, far, both, axis):
    odd = lax.rem(lax.axis_index(axis), 2)
    for slot in range(both.shape[1]):
        both[1 - odd, slot] = near[slot]
        both[odd, slot] = far[slot]


def corner_kernel(far_y, near_y, other, far, near, both):
    planes = near_y.shape[1]
    gather_both(near_y, far_y, both, "inner")

    def pack(out, sign, outside):
        for side, sign_y in enumerate((1, -1)):
            picks = corner_rows(sign, sign_y) + [(FLAG_SLOT, 0), (RATE_SLOT, 0)]
            for row, (slot, depth) in enumerate(picks):
                x = planes - 1 - depth if sign > 0 else depth
                at = 3 * side + row // 8
                out[at, row % 8 : row % 8 + 1] = both[side, slot, x : x + 1]
        for part in range(3):
            out[FORCE_SLOT + part] = other[part]
        clear_outside(out, outside)

    pack_pair(pack, "slab", near, far)


def with_edge(block, step_y, edge):
    rows = block.shape[0]
    sub = lax.broadcasted_iota(jnp.int32, block.shape, 0)
    if step_y > 0:
        return jnp.where(sub == 0, edge, roll_by(block, 1, 0))
    return jnp.where(sub == rows - 1, edge, roll_by(block, -1, 0))


def store_plane(extended, walls, second, at, rate, kind):
    values = []
    for q in range(Q):
        step_x, step_y, _ = VELOCITIES[q]
        block = extended[q, at + 1 - step_x]
        if step_y != 0:
            edge = walls[0 if step_y > 0 else 1, q, pl.ds(at + 1 - step_x, 1)]
            block = with_edge(block, step_y, edge)
        values.append(block)
    result = collide(values, rate, kind)
    for q in range(Q):
        second[q, at] = roll_by(result[q], VELOCITIES[q][2], 1)


def inside_kernel(
    c1,
    fixed,
    far_y,
    near_y,
    far_x,
    near_x,
    extended,
    walls,
    crossing,
    second,
    ends,
    both_y,
    both_x,
):
    planes, rows, _ = c1.shape[1:]
    wide = planes + 4
    gather_both(near_y, far_y, both_y, "inner")
    gather_both(near_x, far_x, both_x, "slab")
    for q in range(Q):
        for x in range(planes):
            extended[q, x + 2] = c1[q, x]
        extended[q, 1] = both_x[0, q]
        extended[q, planes + 2] = both_x[1, q]
        if VELOCITIES[q][0] > 0:
            extended[q, 0] = both_x[0, OPPOSITE[q]]
        if VELOCITIES[q][0] < 0:
            extended[q, planes + 3] = both_x[1, OPPOSITE[q]]
    for end in range(2):
        ends[end, 0] = both_x[end, FLAG_SLOT]
        ends[end, 1] = both_x[end, RATE_SLOT]

    for side, sign in enumerate((1, -1)):
        y = 0 if sign > 0 else rows - 1
        for slot in range(SLOTS):
            walls[side, slot, 2 : planes + 2] = both_y[side, slot]
        place = 0
        for q in range(Q):
            if VELOCITIES[q][1] != -sign:
                continue
            for x in range(wide):
                crossing[side, place, x : x + 1] = extended[q, x, y : y + 1]
            place += 1

    def inside_plane(x, carry):
        store_plane(extended, walls, second, x + 1, fixed[1, x], fixed[0, x])
        return carry

    lax.fori_loop(1, planes - 1, inside_plane, 0)


def second_kernel(
    block_source_hbm,
    block_target_hbm,
    block_node_hbm,
    block_count,
    far,
    near,
    fixed,
    extended,
    crossing,
    ends,
    internal_own,
    walls_in,
    second_in,
    out,
    message,
    walls,
    second,
    both,
    edges,
    loads,
    block_source,
    block_target,
    block_node,
    sems,
):
    del walls_in, second_in
    copies = [
        pltpu.make_async_copy(block_source_hbm, block_source, sems.at[0]),
        pltpu.make_async_copy(block_target_hbm, block_target, sems.at[1]),
        pltpu.make_async_copy(block_node_hbm, block_node, sems.at[2]),
    ]
    for copy in copies:
        copy.start()
    planes, rows, length = out.shape[1:]
    half = length // BLK
    slots = block_source.shape[2]
    wide = planes + 4
    slab = lax.axis_index("slab")
    inner = lax.axis_index("inner")
    slab_end = lax.axis_size("slab") - 1
    inner_end = lax.axis_size("inner") - 1
    gather_both(near, far, both, "slab")

    for side, sign in enumerate((1, -1)):
        for end, sign_x in enumerate((1, -1)):
            for row, (slot, depth) in enumerate(corner_rows(sign_x, sign)):
                at = (1 - depth) if sign_x > 0 else planes + 2 + depth
                source = 3 * side + row // 8
                walls[side, slot, at : at + 1] = both[end, source, row % 8 : row % 8 + 1]
            at = 1 if sign_x > 0 else planes + 2
            for row in (FLAG_SLOT, RATE_SLOT):
                source = 3 * side + row // 8
                walls[side, row, at : at + 1] = both[end, source, row % 8 : row % 8 + 1]

    def edge_plane(end, carry):
        x = end * (planes - 1)
        store_plane(extended, walls, second, x + 1, fixed[1, x], fixed[0, x])
        return carry

    def outside_plane(end, carry):
        store_plane(extended, walls, second, end * (planes + 1), ends[end, 1], ends[end, 0])
        return carry

    lax.fori_loop(0, 2, edge_plane, 0)
    lax.fori_loop(0, 2, outside_plane, 0)

    @pl.when(slab == 0)
    def _():
        for q in range(Q):
            if VELOCITIES[q][0] > 0:
                second[q, 0] = jnp.zeros((rows, length), F32)

    @pl.when(slab == slab_end)
    def _():
        for q in range(Q):
            if VELOCITIES[q][0] < 0:
                second[q, planes + 1] = jnp.zeros((rows, length), F32)

    across = lax.broadcasted_iota(jnp.int32, (wide, length), 0)
    hidden = ((across <= 1) & (slab == 0)) | ((across >= planes + 2) & (slab == slab_end))
    for side, sign, outside in ((0, 1, inner == 0), (1, -1, inner == inner_end)):
        values = []
        place = 0
        for q in range(Q):
            step_x, step_y, _ = VELOCITIES[q]
            if step_y == 0:
                block = walls[side, q]
            elif step_y == sign:
                block = walls[side, OPPOSITE[q]]
            else:
                block = crossing[side, place]
                place += 1
            values.append(roll_by(block, step_x, 0))
        result = collide(values, walls[side, RATE_SLOT], walls[side, FLAG_SLOT])
        place = 0
        for q in range(Q):
            if VELOCITIES[q][1] == sign:
                kept = jnp.where(hidden | outside, 0.0, result[q])
                edges[side, place] = roll_by(kept, VELOCITIES[q][2], 1)
                place += 1

    def plane_two(x, carry):
        values = []
        places = {1: 0, -1: 0}
        for q in range(Q):
            step_x, step_y, _ = VELOCITIES[q]
            block = second[q, x + 1 - step_x]
            if step_y != 0:
                edge = edges[0 if step_y > 0 else 1, places[step_y], pl.ds(x + 2 - step_x, 1)]
                places[step_y] += 1
                block = with_edge(block, step_y, edge)
            values.append(block)
            out[q, x] = block
        density, flow_x, flow_y, flow_z = moments(values)
        parts = (
            LOAD_SCALE * flow_x,
            LOAD_SCALE * (flow_y + (density - 1.0) / 3.0),
            LOAD_SCALE * flow_z,
        )
        for part in range(3):
            for piece in range(half):
                loads[x * half + piece, part] = parts[part][:, piece * BLK : (piece + 1) * BLK]
        return carry

    lax.fori_loop(0, planes, plane_two, 0)

    for copy in copies:
        copy.wait()
    node_blocks = internal_own.shape[1] * half
    live = jnp.broadcast_to(block_count[...], (1, BLK))
    for k in range(slots):
        run = block_source[0, 0, k]
        x = run // (rows * half)
        left = run - x * (rows * half)
        y = left // half
        piece = left - y * half
        for part in range(3):
            message[4 * k + part : 4 * k + part + 1] = loads[x * half + piece, part, pl.ds(y, 1)]
        key = block_target[0, 0, k] * node_blocks + block_node[0, 0, k]
        message[4 * k + 3 : 4 * k + 4] = jnp.where(live > k, key, -1).astype(F32)
    for part in range(3):
        start = 4 * slots + part * node_blocks
        for piece in range(half):
            at = piece * rows
            lanes = slice(piece * BLK, (piece + 1) * BLK)
            message[start + at : start + at + rows] = (
                internal_own[part, :, lanes] + both[0, FORCE_SLOT + part, :, lanes]
            )


def element_kernel(
    elements, displacement, next_nodes, shape_inverse, stiffness, low_ids, high_ids, forces, shapes,
    numbers, corners,
):
    node_dev = displacement.shape[1]
    node_blocks = node_dev // BLK
    runs = elements.shape[1] // BLK
    for j in range(runs):
        lanes = slice(j * BLK, (j + 1) * BLK)
        for row in range(3):
            numbers[row, j : j + 1] = elements[row : row + 1, lanes]
            shapes[row, j : j + 1] = shape_inverse[row : row + 1, lanes]
    for row in range(3):
        low_ids[row] = (numbers[row] & (BLK - 1)).astype(F32)
        high_ids[row] = (numbers[row] >> 7).astype(F32)

    def gather(group, carry):
        rows = pl.ds(pl.multiple_of(group * 8, 8), 8)
        low = [numbers[corner, rows] & (BLK - 1) for corner in range(3)]
        high = [numbers[corner, rows] >> 7 for corner in range(3)]
        nodes = [[jnp.zeros((8, BLK), F32)] * 3 for _ in range(3)]
        for block in range(2 * node_blocks):
            source = displacement if block < node_blocks else next_nodes
            start = (block % node_blocks) * BLK
            table = [
                jnp.broadcast_to(source[part : part + 1, start : start + BLK], (8, BLK))
                for part in range(3)
            ]
            for corner in range(3):
                here = high[corner] == block
                for part in range(3):
                    picked = jnp.take_along_axis(
                        table[part], low[corner], axis=1, mode="promise_in_bounds"
                    )
                    nodes[corner][part] = jnp.where(here, picked, nodes[corner][part])
        for corner in range(3):
            for part in range(3):
                corners[corner, part, rows] = nodes[corner][part]
        return carry

    lax.fori_loop(0, runs // 8, gather, 0)

    first, second, third = [[corners[c, p] for p in range(3)] for c in range(3)]
    diag_a = shapes[0]
    skew_b = shapes[1]
    diag_c = shapes[2]
    stiff = stiffness[...]
    edge_one = [second[p] - first[p] for p in range(3)]
    edge_two = [third[p] - first[p] for p in range(3)]
    one = [diag_a * edge_one[p] for p in range(3)]
    two = [skew_b * edge_one[p] + diag_c * edge_two[p] for p in range(3)]
    one[0] = one[0] + 1.0
    two[1] = two[1] + 1.0
    aa = one[0] * one[0] + one[1] * one[1] + one[2] * one[2]
    ab = one[0] * two[0] + one[1] * two[1] + one[2] * two[2]
    bb = two[0] * two[0] + two[1] * two[1] + two[2] * two[2]
    determinant = aa * bb - ab * ab
    scale = 1.0 / determinant
    inverse_aa = bb * scale
    inverse_ab = -ab * scale
    inverse_bb = aa * scale
    pressure = LAME_RATIO * (0.5 * jnp.log(determinant))
    for p in range(3):
        pulled_one = one[p] * inverse_aa + two[p] * inverse_ab
        pulled_two = one[p] * inverse_ab + two[p] * inverse_bb
        stress_one = stiff * (one[p] - pulled_one + pressure * pulled_one)
        stress_two = stiff * (two[p] - pulled_two + pressure * pulled_two)
        force_one = diag_a * stress_one + skew_b * stress_two
        force_two = diag_c * stress_two
        for corner, force in enumerate((-(force_one + force_two), force_one, force_two)):
            rest = force
            for part in range(PIECES):
                piece = rest.astype(jnp.bfloat16).astype(F32)
                rest = rest - piece
                forces[part * 3 + p, corner] = piece


def spread_kernel(base, low_ids, high_ids, forces, out):
    runs = low_ids.shape[1]
    parts, rows, length = out.shape
    pieces = length // BLK
    slots = pieces * rows
    kind = jnp.bfloat16
    tile = 16
    slot_ids = lax.broadcasted_iota(jnp.int32, (slots, BLK), 0).astype(F32) + base
    slot_ids = slot_ids.astype(kind)
    lane_ids = lax.broadcasted_iota(jnp.int32, (BLK, BLK), 0).astype(F32).astype(kind)
    ones = jnp.ones((BLK, BLK), kind)
    none = jnp.zeros((BLK, BLK), kind)
    blank = jnp.zeros((slots, BLK), kind)

    def tall_row(row, count):
        block = jnp.broadcast_to(row, (tile, BLK)).astype(kind)
        return jnp.concatenate([block] * (count // tile), axis=0)

    total = None
    for corner in range(3):
        left = [[] for _ in range(parts * PIECES)]
        right = []
        for j in range(runs):
            row = slice(j, j + 1)
            here = slot_ids == tall_row(high_ids[corner, row], slots)
            right.append(jnp.where(lane_ids == tall_row(low_ids[corner, row], BLK), ones, none))
            for part in range(parts * PIECES):
                left[part].append(
                    jnp.where(here, tall_row(forces[part, corner, row], slots), blank)
                )
        tall = jnp.concatenate([jnp.concatenate(part, axis=1) for part in left], axis=0)
        wide = jnp.concatenate(right, axis=1)
        product = lax.dot_general(
            tall, wide, (((1,), (1,)), ((), ())), preferred_element_type=F32
        )
        total = product if total is None else total + product
    for p in range(parts):
        summed = total[p * slots : (p + 1) * slots]
        for part in range(1, PIECES):
            start = (parts * part + p) * slots
            summed = summed + total[start : start + slots]
        for piece in range(pieces):
            out[p, :, piece * BLK : (piece + 1) * BLK] = summed[piece * rows : (piece + 1) * rows]


def store_kernel(values, out_hbm, sem):
    store = pltpu.make_async_copy(values, out_hbm, sem)
    store.start()
    store.wait()


def final_kernel(count, *refs):
    messages = refs[:count]
    residual, motion, keys = refs[count:]
    slots = keys.shape[0]
    node_blocks = residual.shape[1] // BLK
    inner = lax.axis_index("inner")
    mine = messages[0]
    for k in range(slots):
        keys[k : k + 1] = mine[4 * k + 3 : 4 * k + 4]
    wanted = keys[...]
    node_ids = lax.broadcasted_iota(jnp.int32, (node_blocks, BLK), 0)
    own_ids = (node_ids + inner * node_blocks).astype(F32)
    external = [jnp.zeros((node_blocks, BLK), F32)] * 3
    moved = [jnp.zeros((slots, BLK), F32)] * 3
    for message in messages:
        for k in range(slots):
            key = message[4 * k + 3 : 4 * k + 4]
            here = own_ids == key
            same = wanted == key
            for part in range(3):
                row = message[4 * k + part : 4 * k + part + 1]
                external[part] = external[part] + jnp.where(here, row, 0.0)
                moved[part] = moved[part] + jnp.where(same, row, 0.0)
    for step, message in enumerate(messages):
        sender = partner_of(inner, step, count)
        for b in range(node_blocks):
            key = jnp.broadcast_to(sender * node_blocks + b, (1, BLK)).astype(F32)
            same = wanted == key
            for part in range(3):
                at = 4 * slots + part * node_blocks + b
                moved[part] = moved[part] - jnp.where(same, message[at : at + 1], 0.0)
    live = wanted >= 0.0
    for part in range(3):
        start = 4 * slots + part * node_blocks
        left = external[part] - mine[start : start + node_blocks]
        for b in range(node_blocks):
            residual[part : part + 1, b * BLK : (b + 1) * BLK] = left[b : b + 1]
        motion[part] = jnp.where(live, COMPLIANCE * moved[part], 0.0)


def call(kernel, outs, operands, spaces, scratch=(), out_spaces=None, micros=1.0, aliases=None):
    spec = lambda space: pl.BlockSpec(memory_space=space)
    out_spaces = out_spaces or (pltpu.VMEM,) * len(outs)
    return pl.pallas_call(
        kernel,
        out_shape=outs,
        in_specs=[spec(space) for space in spaces],
        out_specs=tuple(spec(space) for space in out_spaces),
        scratch_shapes=list(scratch),
        input_output_aliases=aliases or {},
        compiler_params=pltpu.CompilerParams(vmem_limit_bytes=VMEM_BYTES),
        cost_estimate=pl.CostEstimate(
            flops=0, bytes_accessed=int(micros * 3.6e6), transcendentals=0
        ),
    )(*operands)


def partner_of(at, step, count):
    if count & (count - 1) == 0:
        return at ^ step
    return (at + count - step) % count


def exchange(block, axis, step):
    count = lax.axis_size(axis)
    return lax.ppermute(block, axis, [(partner_of(i, step, count), i) for i in range(count)])


def around(block, axis, step):
    count = lax.axis_size(axis)
    return lax.ppermute(block, axis, [(i, (i + step) % count) for i in range(count)])


def swap(near, far, axis):
    count = lax.axis_size(axis)
    outcome = {}
    for block, start in ((far, 1), (near, 0)):
        partner = list(range(count))
        for i in range(start, count - 1, 2):
            partner[i], partner[i + 1] = i + 1, i
        outcome[start] = lax.ppermute(block, axis, list(enumerate(partner)))
    return outcome[0], outcome[1]


def shards(
    populations,
    relaxation,
    node_flags,
    displacement,
    elements,
    shape_inverse,
    stiffness,
    block_source,
    block_target,
    block_node,
    block_count,
):
    planes, rows, length = populations.shape[1:]
    half = length // BLK
    node_dev = displacement.shape[1]
    node_blocks = node_dev // BLK
    runs = stiffness.shape[0] // BLK
    slots = block_source.shape[2]
    count = lax.axis_size("inner")
    shape = lambda *dims: jax.ShapeDtypeStruct(dims, F32)
    whole = shape(*populations.shape)
    vmem, hbm, smem = pltpu.VMEM, pltpu.HBM, pltpu.SMEM

    next_nodes = around(displacement, "slab", -1)
    face_y = shape(SLOTS, planes, length)
    face_x = shape(SLOTS, rows, length)
    pin = lambda block: pltpu.with_memory_space_constraint(block, hbm)
    c1, fixed, far, near = call(
        first_kernel,
        (whole, shape(2, planes, rows, length), face_x, face_x),
        (pin(populations), pin(relaxation), pin(node_flags)),
        (hbm,) * 3,
        scratch=(
            pltpu.VMEM((planes, Q, rows, length), F32),
            pltpu.VMEM((planes, rows, length), F32),
            pltpu.VMEM((planes, rows, length), jnp.int32),
            pltpu.SemaphoreType.DMA((planes + 2,)),
        ),
        micros=1.5,
    )
    near_x, far_x = swap(near, far, "slab")
    far, near = call(
        side_kernel, (face_y, face_y), (c1, fixed, next_nodes), (vmem,) * 3, micros=0.3
    )
    near_y, far_y = swap(near, far, "inner")
    numbers = shape(3, runs, BLK)
    low_ids, high_ids, forces = call(
        element_kernel,
        (numbers, numbers, shape(3 * PIECES, 3, runs, BLK)),
        (elements, displacement, next_nodes, shape_inverse, stiffness.reshape(runs, BLK)),
        (vmem,) * 5,
        scratch=(
            pltpu.VMEM((3, runs, BLK), F32),
            pltpu.VMEM((3, runs, BLK), jnp.int32),
            pltpu.VMEM((3, 3, runs, BLK), F32),
        ),
        micros=2.0,
    )
    nodal = shape(3, node_blocks // half, length)
    (other,) = call(
        functools.partial(spread_kernel, node_blocks),
        (nodal,),
        (low_ids, high_ids, forces),
        (vmem,) * 3,
        micros=0.8,
    )
    corner = shape(CORNER_SLOTS, rows, length)
    far, near = call(
        corner_kernel,
        (corner, corner),
        (far_y, near_y, other),
        (vmem,) * 3,
        scratch=(pltpu.VMEM((2, SLOTS, planes, length), F32),),
        micros=0.3,
    )
    near_c, far_c = swap(near, far, "slab")
    (own,) = call(
        functools.partial(spread_kernel, 0),
        (nodal,),
        (low_ids, high_ids, forces),
        (vmem,) * 3,
        micros=0.8,
    )
    wide = planes + 4
    walls_shape = shape(2, SLOTS, wide, length)
    second_shape = shape(Q, planes + 2, rows, length)
    extended, walls, crossing, second, ends = call(
        inside_kernel,
        (
            shape(Q, wide, rows, length),
            walls_shape,
            shape(2, 5, wide, length),
            second_shape,
            shape(2, 2, rows, length),
        ),
        (c1, fixed, far_y, near_y, far_x, near_x),
        (vmem,) * 6,
        scratch=(
            pltpu.VMEM((2, SLOTS, planes, length), F32),
            pltpu.VMEM((2, SLOTS, rows, length), F32),
        ),
        micros=0.8,
    )
    lines = 4 * slots + 3 * node_blocks
    values, message, _, _ = call(
        second_kernel,
        (whole, shape(lines, BLK), walls_shape, second_shape),
        (
            pin(block_source),
            pin(block_target),
            pin(block_node),
            block_count,
            far_c,
            near_c,
            fixed,
            extended,
            crossing,
            ends,
            own,
            walls,
            second,
        ),
        (hbm,) * 3 + (vmem,) * 10,
        aliases={11: 2, 12: 3},
        scratch=(
            pltpu.VMEM((2, CORNER_SLOTS, rows, length), F32),
            pltpu.VMEM((2, 5, wide, length), F32),
            pltpu.VMEM((planes * half, 3, rows, BLK), F32),
            pltpu.SMEM(block_source.shape, jnp.int32),
            pltpu.SMEM(block_target.shape, jnp.int32),
            pltpu.SMEM(block_node.shape, jnp.int32),
            pltpu.SemaphoreType.DMA((3,)),
        ),
        micros=1.5,
    )
    messages = [message] + [exchange(message, "inner", step) for step in range(1, count)]
    (populations_out,) = call(
        store_kernel,
        (whole,),
        (values,),
        (vmem,),
        out_spaces=(hbm,),
        scratch=(pltpu.SemaphoreType.DMA(()),),
        micros=1.0,
    )
    residual, motion = call(
        functools.partial(final_kernel, count),
        (shape(3, node_dev), shape(3, slots, BLK)),
        messages,
        (vmem,) * count,
        scratch=(pltpu.VMEM((slots, BLK), F32),),
        micros=0.8,
    )
    return populations_out, residual, motion.transpose(1, 0, 2)[None, None]


def solution(mesh):
    return jax.shard_map(
        shards,
        mesh=mesh,
        in_specs=(
            P(None, ("group", "slab"), "inner", None),
            P(("group", "slab"), "inner", None),
            P(("group", "slab"), "inner", None),
            P(None, ("group", "slab", "inner")),
            P(None, ("group", "slab", "inner")),
            P(None, ("group", "slab", "inner")),
            P(("group", "slab", "inner")),
            P(("group", "slab"), "inner", None),
            P(("group", "slab"), "inner", None),
            P(("group", "slab"), "inner", None),
            P(("group", "slab"), "inner"),
        ),
        out_specs=(
            P(None, ("group", "slab"), "inner", None),
            P(None, ("group", "slab", "inner")),
            P(("group", "slab"), "inner", None, None, None),
        ),
        check_vma=False,
    )
```

```python
import functools

import jax
import jax.numpy as jnp
from jax import lax
from jax.experimental import pallas as pl
from jax.experimental.pallas import tpu as pltpu
from jax.sharding import PartitionSpec as P

BLK = 128
VELOCITIES = (
    (0, 0, 0),
    (1, 0, 0),
    (-1, 0, 0),
    (0, 1, 0),
    (0, -1, 0),
    (0, 0, 1),
    (0, 0, -1),
    (1, 1, 0),
    (-1, -1, 0),
    (1, -1, 0),
    (-1, 1, 0),
    (1, 0, 1),
    (-1, 0, -1),
    (1, 0, -1),
    (-1, 0, 1),
    (0, 1, 1),
    (0, -1, -1),
    (0, 1, -1),
    (0, -1, 1),
)
WEIGHTS = (1.0 / 3.0,) + (1.0 / 18.0,) * 6 + (1.0 / 36.0,) * 12
OPPOSITE = (0, 2, 1, 4, 3, 6, 5, 8, 7, 10, 9, 12, 11, 14, 13, 16, 15, 18, 17)
INLET_SPEED = 0.04
LOAD_SCALE = 25.0
COMPLIANCE = 0.5
LAME_RATIO = 2.0
Q = 19
FLAG_SLOT = 19
RATE_SLOT = 20
SLOTS = 21
FORCE_SLOT = 6
CORNER_SLOTS = FORCE_SLOT + 3
PIECES = 2
F32 = jnp.float32
VMEM_BYTES = 48 * 1024 * 1024


def moments(values):
    sums = [values[q] + values[q + 1] for q in range(1, Q, 2)]
    diffs = [values[q] - values[q + 1] for q in range(1, Q, 2)]
    density = values[0]
    for term in sums:
        density = density + term
    flows = []
    for axis in range(3):
        total = None
        for k, q in enumerate(range(1, Q, 2)):
            factor = VELOCITIES[q][axis]
            if factor == 0:
                continue
            if total is None:
                total = diffs[k] if factor > 0 else -diffs[k]
            else:
                total = total + diffs[k] if factor > 0 else total - diffs[k]
        flows.append(total)
    return density, flows[0], flows[1], flows[2]


def collide(values, rate, kind):
    density, flow_x, flow_y, flow_z = moments(values)
    inverse = 1.0 / density
    wall = kind == 1
    inlet = kind == 2
    fluid = kind == 0
    vel = (
        jnp.where(inlet, INLET_SPEED, flow_x * inverse),
        jnp.where(inlet, 0.0, flow_y * inverse),
        jnp.where(inlet, 0.0, flow_z * inverse),
    )
    scale = jnp.where(fluid, density, 1.0)
    rate = jnp.where(fluid, rate, 1.0)
    base = 1.0 - 1.5 * (vel[0] * vel[0] + vel[1] * vel[1] + vel[2] * vel[2])
    weighted = {w: w * scale for w in set(WEIGHTS)}
    out = [None] * Q
    relaxed = values[0] + rate * (weighted[WEIGHTS[0]] * base - values[0])
    out[0] = jnp.where(wall, values[0], relaxed)
    for q in range(1, Q, 2):
        project = None
        for factor, component in zip(VELOCITIES[q], vel):
            if factor == 0:
                continue
            if project is None:
                project = component
            else:
                project = project + component if factor > 0 else project - component
        even = base + 4.5 * (project * project)
        odd = 3.0 * project
        w = weighted[WEIGHTS[q]]
        forward = values[q] + rate * (w * (even + odd) - values[q])
        backward = values[q + 1] + rate * (w * (even - odd) - values[q + 1])
        out[q] = jnp.where(wall, values[q + 1], forward)
        out[q + 1] = jnp.where(wall, values[q], backward)
    return out


def roll_by(block, step, axis):
    if step == 0:
        return block
    return pltpu.roll(block, step % block.shape[axis], axis)


def face_slots(axis, sign):
    picks = []
    for q in range(Q):
        if VELOCITIES[q][axis] * sign >= 0:
            picks.append((q, 0))
        else:
            picks.append((OPPOSITE[q], 1))
    return picks


def mirror(q, axis):
    flipped = tuple(-c if k == axis else c for k, c in enumerate(VELOCITIES[q]))
    return VELOCITIES.index(flipped)


def corner_rows(sign_x, sign_y):
    rows = []
    for q, depth in face_slots(0, sign_x):
        if VELOCITIES[q][1] * sign_y >= 0:
            rows.append((q, depth))
        else:
            rows.append((OPPOSITE[mirror(q, 1)], depth))
    return rows


def first_kernel(
    pops_hbm, rate_hbm, flags_hbm, c1, fixed, far, near, pops, rate, flags, sems
):
    planes = c1.shape[1]
    copies = [
        pltpu.make_async_copy(rate_hbm, rate, sems.at[planes]),
        pltpu.make_async_copy(flags_hbm, flags, sems.at[planes + 1]),
    ]
    loads = [
        pltpu.make_async_copy(pops_hbm.at[:, x], pops.at[x], sems.at[x]) for x in range(planes)
    ]
    for copy in loads[:1] + copies + loads[1:]:
        copy.start()
    for copy in copies:
        copy.wait()

    def plane(x, carry):
        pltpu.make_async_copy(pops_hbm.at[:, x], pops.at[x], sems.at[x]).wait()
        kind = flags[x]
        values = [pops[x, q] for q in range(Q)]
        result = collide(values, rate[x], kind)
        for q in range(Q):
            c1[q, x] = roll_by(result[q], VELOCITIES[q][2], 1)
        fixed[0, x] = kind.astype(F32)
        fixed[1, x] = rate[x]
        return carry

    lax.fori_loop(0, planes, plane, 0)

    def pack(out, sign, outside):
        for slot, (q, depth) in enumerate(face_slots(0, sign)):
            out[slot] = c1[q, planes - 1 - depth if sign > 0 else depth]
        end = planes - 1 if sign > 0 else 0
        out[FLAG_SLOT] = fixed[0, end]
        out[RATE_SLOT] = fixed[1, end]
        clear_outside(out, outside)

    pack_pair(pack, "slab", near, far)


def clear_outside(out, outside):
    @pl.when(outside)
    def _():
        out[...] = jnp.zeros(out.shape, F32)


def pack_pair(pack, axis, near, far):
    at = lax.axis_index(axis)
    even = lax.rem(at, 2) == 0
    first, last = at == 0, at == lax.axis_size(axis) - 1

    @pl.when(even)
    def _():
        pack(near, 1, last)
        pack(far, -1, first)

    @pl.when(jnp.logical_not(even))
    def _():
        pack(near, -1, first)
        pack(far, 1, last)


def side_kernel(c1, fixed, next_nodes, far, near):
    del next_nodes
    planes, rows = c1.shape[1], c1.shape[2]

    def pack(out, sign, outside):
        def line(x, carry):
            for slot, (q, depth) in enumerate(face_slots(1, sign)):
                y = rows - 1 - depth if sign > 0 else depth
                out[slot, pl.ds(x, 1)] = c1[q, x, y : y + 1]
            y = rows - 1 if sign > 0 else 0
            for k, slot in enumerate((FLAG_SLOT, RATE_SLOT)):
                out[slot, pl.ds(x, 1)] = fixed[k, x, y : y + 1]
            return carry

        lax.fori_loop(0, planes, line, 0)
        clear_outside(out, outside)

    pack_pair(pack, "inner", near, far)


def gather_both(near, far, both, axis):
    odd = lax.rem(lax.axis_index(axis), 2)
    for slot in range(both.shape[1]):
        both[1 - odd, slot] = near[slot]
        both[odd, slot] = far[slot]


def corner_kernel(far_y, near_y, other, far, near, both):
    planes = near_y.shape[1]
    gather_both(near_y, far_y, both, "inner")

    def pack(out, sign, outside):
        for side, sign_y in enumerate((1, -1)):
            picks = corner_rows(sign, sign_y) + [(FLAG_SLOT, 0), (RATE_SLOT, 0)]
            for row, (slot, depth) in enumerate(picks):
                x = planes - 1 - depth if sign > 0 else depth
                at = 3 * side + row // 8
                out[at, row % 8 : row % 8 + 1] = both[side, slot, x : x + 1]
        for part in range(3):
            out[FORCE_SLOT + part] = other[part]
        clear_outside(out, outside)

    pack_pair(pack, "slab", near, far)


def with_edge(block, step_y, edge):
    rows = block.shape[0]
    sub = lax.broadcasted_iota(jnp.int32, block.shape, 0)
    if step_y > 0:
        return jnp.where(sub == 0, edge, roll_by(block, 1, 0))
    return jnp.where(sub == rows - 1, edge, roll_by(block, -1, 0))


def store_plane(extended, walls, second, at, rate, kind):
    values = []
    for q in range(Q):
        step_x, step_y, _ = VELOCITIES[q]
        block = extended[q, at + 1 - step_x]
        if step_y != 0:
            edge = walls[0 if step_y > 0 else 1, q, pl.ds(at + 1 - step_x, 1)]
            block = with_edge(block, step_y, edge)
        values.append(block)
    result = collide(values, rate, kind)
    for q in range(Q):
        second[q, at] = roll_by(result[q], VELOCITIES[q][2], 1)


def inside_kernel(
    c1,
    fixed,
    far_y,
    near_y,
    far_x,
    near_x,
    extended,
    walls,
    crossing,
    second,
    ends,
    both_y,
    both_x,
):
    planes, rows, _ = c1.shape[1:]
    wide = planes + 4
    gather_both(near_y, far_y, both_y, "inner")
    gather_both(near_x, far_x, both_x, "slab")
    for q in range(Q):
        for x in range(planes):
            extended[q, x + 2] = c1[q, x]
        extended[q, 1] = both_x[0, q]
        extended[q, planes + 2] = both_x[1, q]
        if VELOCITIES[q][0] > 0:
            extended[q, 0] = both_x[0, OPPOSITE[q]]
        if VELOCITIES[q][0] < 0:
            extended[q, planes + 3] = both_x[1, OPPOSITE[q]]
    for end in range(2):
        ends[end, 0] = both_x[end, FLAG_SLOT]
        ends[end, 1] = both_x[end, RATE_SLOT]

    for side, sign in enumerate((1, -1)):
        y = 0 if sign > 0 else rows - 1
        for slot in range(SLOTS):
            walls[side, slot, 2 : planes + 2] = both_y[side, slot]
        place = 0
        for q in range(Q):
            if VELOCITIES[q][1] != -sign:
                continue
            for x in range(wide):
                crossing[side, place, x : x + 1] = extended[q, x, y : y + 1]
            place += 1

    def inside_plane(x, carry):
        store_plane(extended, walls, second, x + 1, fixed[1, x], fixed[0, x])
        return carry

    lax.fori_loop(1, planes - 1, inside_plane, 0)


def second_kernel(
    block_source_hbm,
    block_target_hbm,
    block_node_hbm,
    block_count,
    far,
    near,
    fixed,
    extended,
    crossing,
    ends,
    internal_own,
    walls_in,
    second_in,
    out,
    message,
    walls,
    second,
    both,
    edges,
    loads,
    block_source,
    block_target,
    block_node,
    sems,
):
    del walls_in, second_in
    copies = [
        pltpu.make_async_copy(block_source_hbm, block_source, sems.at[0]),
        pltpu.make_async_copy(block_target_hbm, block_target, sems.at[1]),
        pltpu.make_async_copy(block_node_hbm, block_node, sems.at[2]),
    ]
    for copy in copies:
        copy.start()
    planes, rows, length = out.shape[1:]
    half = length // BLK
    slots = block_source.shape[2]
    wide = planes + 4
    slab = lax.axis_index("slab")
    inner = lax.axis_index("inner")
    slab_end = lax.axis_size("slab") - 1
    inner_end = lax.axis_size("inner") - 1
    gather_both(near, far, both, "slab")

    for side, sign in enumerate((1, -1)):
        for end, sign_x in enumerate((1, -1)):
            for row, (slot, depth) in enumerate(corner_rows(sign_x, sign)):
                at = (1 - depth) if sign_x > 0 else planes + 2 + depth
                source = 3 * side + row // 8
                walls[side, slot, at : at + 1] = both[end, source, row % 8 : row % 8 + 1]
            at = 1 if sign_x > 0 else planes + 2
            for row in (FLAG_SLOT, RATE_SLOT):
                source = 3 * side + row // 8
                walls[side, row, at : at + 1] = both[end, source, row % 8 : row % 8 + 1]

    def edge_plane(end, carry):
        x = end * (planes - 1)
        store_plane(extended, walls, second, x + 1, fixed[1, x], fixed[0, x])
        return carry

    def outside_plane(end, carry):
        store_plane(extended, walls, second, end * (planes + 1), ends[end, 1], ends[end, 0])
        return carry

    lax.fori_loop(0, 2, edge_plane, 0)
    lax.fori_loop(0, 2, outside_plane, 0)

    @pl.when(slab == 0)
    def _():
        for q in range(Q):
            if VELOCITIES[q][0] > 0:
                second[q, 0] = jnp.zeros((rows, length), F32)

    @pl.when(slab == slab_end)
    def _():
        for q in range(Q):
            if VELOCITIES[q][0] < 0:
                second[q, planes + 1] = jnp.zeros((rows, length), F32)

    across = lax.broadcasted_iota(jnp.int32, (wide, length), 0)
    hidden = ((across <= 1) & (slab == 0)) | ((across >= planes + 2) & (slab == slab_end))
    for side, sign, outside in ((0, 1, inner == 0), (1, -1, inner == inner_end)):
        values = []
        place = 0
        for q in range(Q):
            step_x, step_y, _ = VELOCITIES[q]
            if step_y == 0:
                block = walls[side, q]
            elif step_y == sign:
                block = walls[side, OPPOSITE[q]]
            else:
                block = crossing[side, place]
                place += 1
            values.append(roll_by(block, step_x, 0))
        result = collide(values, walls[side, RATE_SLOT], walls[side, FLAG_SLOT])
        place = 0
        for q in range(Q):
            if VELOCITIES[q][1] == sign:
                kept = jnp.where(hidden | outside, 0.0, result[q])
                edges[side, place] = roll_by(kept, VELOCITIES[q][2], 1)
                place += 1

    def plane_two(x, carry):
        values = []
        places = {1: 0, -1: 0}
        for q in range(Q):
            step_x, step_y, _ = VELOCITIES[q]
            block = second[q, x + 1 - step_x]
            if step_y != 0:
                edge = edges[0 if step_y > 0 else 1, places[step_y], pl.ds(x + 2 - step_x, 1)]
                places[step_y] += 1
                block = with_edge(block, step_y, edge)
            values.append(block)
            out[q, x] = block
        density, flow_x, flow_y, flow_z = moments(values)
        parts = (
            LOAD_SCALE * flow_x,
            LOAD_SCALE * (flow_y + (density - 1.0) / 3.0),
            LOAD_SCALE * flow_z,
        )
        for part in range(3):
            for piece in range(half):
                loads[x * half + piece, part] = parts[part][:, piece * BLK : (piece + 1) * BLK]
        return carry

    lax.fori_loop(0, planes, plane_two, 0)

    for copy in copies:
        copy.wait()
    node_blocks = internal_own.shape[1] * half
    live = jnp.broadcast_to(block_count[...], (1, BLK))
    for k in range(slots):
        run = block_source[0, 0, k]
        x = run // (rows * half)
        left = run - x * (rows * half)
        y = left // half
        piece = left - y * half
        for part in range(3):
            message[4 * k + part : 4 * k + part + 1] = loads[x * half + piece, part, pl.ds(y, 1)]
        key = block_target[0, 0, k] * node_blocks + block_node[0, 0, k]
        message[4 * k + 3 : 4 * k + 4] = jnp.where(live > k, key, -1).astype(F32)
    for part in range(3):
        start = 4 * slots + part * node_blocks
        for piece in range(half):
            at = piece * rows
            lanes = slice(piece * BLK, (piece + 1) * BLK)
            message[start + at : start + at + rows] = (
                internal_own[part, :, lanes] + both[0, FORCE_SLOT + part, :, lanes]
            )


def element_kernel(
    elements, displacement, next_nodes, shape_inverse, stiffness, low_ids, high_ids, forces, shapes,
    numbers, corners,
):
    node_dev = displacement.shape[1]
    node_blocks = node_dev // BLK
    runs = elements.shape[1] // BLK
    for j in range(runs):
        lanes = slice(j * BLK, (j + 1) * BLK)
        for row in range(3):
            numbers[row, j : j + 1] = elements[row : row + 1, lanes]
            shapes[row, j : j + 1] = shape_inverse[row : row + 1, lanes]
    for row in range(3):
        low_ids[row] = (numbers[row] & (BLK - 1)).astype(F32)
        high_ids[row] = (numbers[row] >> 7).astype(F32)

    def gather(group, carry):
        rows = pl.ds(pl.multiple_of(group * 8, 8), 8)
        low = [numbers[corner, rows] & (BLK - 1) for corner in range(3)]
        high = [numbers[corner, rows] >> 7 for corner in range(3)]
        nodes = [[jnp.zeros((8, BLK), F32)] * 3 for _ in range(3)]
        for block in range(2 * node_blocks):
            source = displacement if block < node_blocks else next_nodes
            start = (block % node_blocks) * BLK
            table = [
                jnp.broadcast_to(source[part : part + 1, start : start + BLK], (8, BLK))
                for part in range(3)
            ]
            for corner in range(3):
                here = high[corner] == block
                for part in range(3):
                    picked = jnp.take_along_axis(
                        table[part], low[corner], axis=1, mode="promise_in_bounds"
                    )
                    nodes[corner][part] = jnp.where(here, picked, nodes[corner][part])
        for corner in range(3):
            for part in range(3):
                corners[corner, part, rows] = nodes[corner][part]
        return carry

    lax.fori_loop(0, runs // 8, gather, 0)

    first, second, third = [[corners[c, p] for p in range(3)] for c in range(3)]
    diag_a = shapes[0]
    skew_b = shapes[1]
    diag_c = shapes[2]
    stiff = stiffness[...]
    edge_one = [second[p] - first[p] for p in range(3)]
    edge_two = [third[p] - first[p] for p in range(3)]
    one = [diag_a * edge_one[p] for p in range(3)]
    two = [skew_b * edge_one[p] + diag_c * edge_two[p] for p in range(3)]
    one[0] = one[0] + 1.0
    two[1] = two[1] + 1.0
    aa = one[0] * one[0] + one[1] * one[1] + one[2] * one[2]
    ab = one[0] * two[0] + one[1] * two[1] + one[2] * two[2]
    bb = two[0] * two[0] + two[1] * two[1] + two[2] * two[2]
    determinant = aa * bb - ab * ab
    scale = 1.0 / determinant
    inverse_aa = bb * scale
    inverse_ab = -ab * scale
    inverse_bb = aa * scale
    pressure = LAME_RATIO * (0.5 * jnp.log(determinant))
    for p in range(3):
        pulled_one = one[p] * inverse_aa + two[p] * inverse_ab
        pulled_two = one[p] * inverse_ab + two[p] * inverse_bb
        stress_one = stiff * (one[p] - pulled_one + pressure * pulled_one)
        stress_two = stiff * (two[p] - pulled_two + pressure * pulled_two)
        force_one = diag_a * stress_one + skew_b * stress_two
        force_two = diag_c * stress_two
        for corner, force in enumerate((-(force_one + force_two), force_one, force_two)):
            rest = force
            for part in range(PIECES):
                piece = rest.astype(jnp.bfloat16).astype(F32)
                rest = rest - piece
                forces[part * 3 + p, corner] = piece


def spread_kernel(base, low_ids, high_ids, forces, out):
    runs = low_ids.shape[1]
    parts, rows, length = out.shape
    pieces = length // BLK
    slots = pieces * rows
    kind = jnp.bfloat16
    tile = 16
    slot_ids = lax.broadcasted_iota(jnp.int32, (slots, BLK), 0).astype(F32) + base
    slot_ids = slot_ids.astype(kind)
    lane_ids = lax.broadcasted_iota(jnp.int32, (BLK, BLK), 0).astype(F32).astype(kind)
    ones = jnp.ones((BLK, BLK), kind)
    none = jnp.zeros((BLK, BLK), kind)
    blank = jnp.zeros((slots, BLK), kind)

    def tall_row(row, count):
        block = jnp.broadcast_to(row, (tile, BLK)).astype(kind)
        return jnp.concatenate([block] * (count // tile), axis=0)

    total = None
    for corner in range(3):
        left = [[] for _ in range(parts * PIECES)]
        right = []
        for j in range(runs):
            row = slice(j, j + 1)
            here = slot_ids == tall_row(high_ids[corner, row], slots)
            right.append(jnp.where(lane_ids == tall_row(low_ids[corner, row], BLK), ones, none))
            for part in range(parts * PIECES):
                left[part].append(
                    jnp.where(here, tall_row(forces[part, corner, row], slots), blank)
                )
        tall = jnp.concatenate([jnp.concatenate(part, axis=1) for part in left], axis=0)
        wide = jnp.concatenate(right, axis=1)
        product = lax.dot_general(
            tall, wide, (((1,), (1,)), ((), ())), preferred_element_type=F32
        )
        total = product if total is None else total + product
    for p in range(parts):
        summed = total[p * slots : (p + 1) * slots]
        for part in range(1, PIECES):
            start = (parts * part + p) * slots
            summed = summed + total[start : start + slots]
        for piece in range(pieces):
            out[p, :, piece * BLK : (piece + 1) * BLK] = summed[piece * rows : (piece + 1) * rows]


def store_kernel(values, out_hbm, sem):
    store = pltpu.make_async_copy(values, out_hbm, sem)
    store.start()
    store.wait()


def final_kernel(count, *refs):
    messages = refs[:count]
    residual, motion, keys = refs[count:]
    slots = keys.shape[0]
    node_blocks = residual.shape[1] // BLK
    inner = lax.axis_index("inner")
    mine = messages[0]
    for k in range(slots):
        keys[k : k + 1] = mine[4 * k + 3 : 4 * k + 4]
    wanted = keys[...]
    node_ids = lax.broadcasted_iota(jnp.int32, (node_blocks, BLK), 0)
    own_ids = (node_ids + inner * node_blocks).astype(F32)
    external = [jnp.zeros((node_blocks, BLK), F32)] * 3
    moved = [jnp.zeros((slots, BLK), F32)] * 3
    for message in messages:
        for k in range(slots):
            key = message[4 * k + 3 : 4 * k + 4]
            here = own_ids == key
            same = wanted == key
            for part in range(3):
                row = message[4 * k + part : 4 * k + part + 1]
                external[part] = external[part] + jnp.where(here, row, 0.0)
                moved[part] = moved[part] + jnp.where(same, row, 0.0)
    for step, message in enumerate(messages):
        sender = partner_of(inner, step, count)
        for b in range(node_blocks):
            key = jnp.broadcast_to(sender * node_blocks + b, (1, BLK)).astype(F32)
            same = wanted == key
            for part in range(3):
                at = 4 * slots + part * node_blocks + b
                moved[part] = moved[part] - jnp.where(same, message[at : at + 1], 0.0)
    live = wanted >= 0.0
    for part in range(3):
        start = 4 * slots + part * node_blocks
        left = external[part] - mine[start : start + node_blocks]
        for b in range(node_blocks):
            residual[part : part + 1, b * BLK : (b + 1) * BLK] = left[b : b + 1]
        motion[part] = jnp.where(live, COMPLIANCE * moved[part], 0.0)


def call(kernel, outs, operands, spaces, scratch=(), out_spaces=None, micros=1.0, aliases=None):
    spec = lambda space: pl.BlockSpec(memory_space=space)
    out_spaces = out_spaces or (pltpu.VMEM,) * len(outs)
    return pl.pallas_call(
        kernel,
        out_shape=outs,
        in_specs=[spec(space) for space in spaces],
        out_specs=tuple(spec(space) for space in out_spaces),
        scratch_shapes=list(scratch),
        input_output_aliases=aliases or {},
        compiler_params=pltpu.CompilerParams(vmem_limit_bytes=VMEM_BYTES),
        cost_estimate=pl.CostEstimate(
            flops=0, bytes_accessed=int(micros * 3.6e6), transcendentals=0
        ),
    )(*operands)


def partner_of(at, step, count):
    if count & (count - 1) == 0:
        return at ^ step
    return (at + count - step) % count


def exchange(block, axis, step):
    count = lax.axis_size(axis)
    return lax.ppermute(block, axis, [(partner_of(i, step, count), i) for i in range(count)])


def around(block, axis, step):
    count = lax.axis_size(axis)
    return lax.ppermute(block, axis, [(i, (i + step) % count) for i in range(count)])


def swap(near, far, axis):
    count = lax.axis_size(axis)
    outcome = {}
    for block, start in ((far, 1), (near, 0)):
        partner = list(range(count))
        for i in range(start, start + count - count % 2, 2):
            one, two = i % count, (i + 1) % count
            partner[one], partner[two] = two, one
        outcome[start] = lax.ppermute(block, axis, list(enumerate(partner)))
    return outcome[0], outcome[1]


def shards(
    populations,
    relaxation,
    node_flags,
    displacement,
    elements,
    shape_inverse,
    stiffness,
    block_source,
    block_target,
    block_node,
    block_count,
):
    planes, rows, length = populations.shape[1:]
    half = length // BLK
    node_dev = displacement.shape[1]
    node_blocks = node_dev // BLK
    runs = stiffness.shape[0] // BLK
    slots = block_source.shape[2]
    count = lax.axis_size("inner")
    shape = lambda *dims: jax.ShapeDtypeStruct(dims, F32)
    whole = shape(*populations.shape)
    vmem, hbm, smem = pltpu.VMEM, pltpu.HBM, pltpu.SMEM

    next_nodes = around(displacement, "slab", -1)
    face_y = shape(SLOTS, planes, length)
    face_x = shape(SLOTS, rows, length)
    pin = lambda block: pltpu.with_memory_space_constraint(block, hbm)
    c1, fixed, far, near = call(
        first_kernel,
        (whole, shape(2, planes, rows, length), face_x, face_x),
        (pin(populations), pin(relaxation), pin(node_flags)),
        (hbm,) * 3,
        scratch=(
            pltpu.VMEM((planes, Q, rows, length), F32),
            pltpu.VMEM((planes, rows, length), F32),
            pltpu.VMEM((planes, rows, length), jnp.int32),
            pltpu.SemaphoreType.DMA((planes + 2,)),
        ),
        micros=1.5,
    )
    near_x, far_x = swap(near, far, "slab")
    far, near = call(
        side_kernel, (face_y, face_y), (c1, fixed, next_nodes), (vmem,) * 3, micros=0.3
    )
    near_y, far_y = swap(near, far, "inner")
    numbers = shape(3, runs, BLK)
    low_ids, high_ids, forces = call(
        element_kernel,
        (numbers, numbers, shape(3 * PIECES, 3, runs, BLK)),
        (elements, displacement, next_nodes, shape_inverse, stiffness.reshape(runs, BLK)),
        (vmem,) * 5,
        scratch=(
            pltpu.VMEM((3, runs, BLK), F32),
            pltpu.VMEM((3, runs, BLK), jnp.int32),
            pltpu.VMEM((3, 3, runs, BLK), F32),
        ),
        micros=2.0,
    )
    nodal = shape(3, node_blocks // half, length)
    (other,) = call(
        functools.partial(spread_kernel, node_blocks),
        (nodal,),
        (low_ids, high_ids, forces),
        (vmem,) * 3,
        micros=0.8,
    )
    corner = shape(CORNER_SLOTS, rows, length)
    far, near = call(
        corner_kernel,
        (corner, corner),
        (far_y, near_y, other),
        (vmem,) * 3,
        scratch=(pltpu.VMEM((2, SLOTS, planes, length), F32),),
        micros=0.3,
    )
    near_c, far_c = swap(near, far, "slab")
    (own,) = call(
        functools.partial(spread_kernel, 0),
        (nodal,),
        (low_ids, high_ids, forces),
        (vmem,) * 3,
        micros=0.8,
    )
    wide = planes + 4
    walls_shape = shape(2, SLOTS, wide, length)
    second_shape = shape(Q, planes + 2, rows, length)
    extended, walls, crossing, second, ends = call(
        inside_kernel,
        (
            shape(Q, wide, rows, length),
            walls_shape,
            shape(2, 5, wide, length),
            second_shape,
            shape(2, 2, rows, length),
        ),
        (c1, fixed, far_y, near_y, far_x, near_x),
        (vmem,) * 6,
        scratch=(
            pltpu.VMEM((2, SLOTS, planes, length), F32),
            pltpu.VMEM((2, SLOTS, rows, length), F32),
        ),
        micros=0.8,
    )
    lines = 4 * slots + 3 * node_blocks
    values, message, _, _ = call(
        second_kernel,
        (whole, shape(lines, BLK), walls_shape, second_shape),
        (
            pin(block_source),
            pin(block_target),
            pin(block_node),
            block_count,
            far_c,
            near_c,
            fixed,
            extended,
            crossing,
            ends,
            own,
            walls,
            second,
        ),
        (hbm,) * 3 + (vmem,) * 10,
        aliases={11: 2, 12: 3},
        scratch=(
            pltpu.VMEM((2, CORNER_SLOTS, rows, length), F32),
            pltpu.VMEM((2, 5, wide, length), F32),
            pltpu.VMEM((planes * half, 3, rows, BLK), F32),
            pltpu.SMEM(block_source.shape, jnp.int32),
            pltpu.SMEM(block_target.shape, jnp.int32),
            pltpu.SMEM(block_node.shape, jnp.int32),
            pltpu.SemaphoreType.DMA((3,)),
        ),
        micros=1.5,
    )
    messages = [message] + [exchange(message, "inner", step) for step in range(1, count)]
    (populations_out,) = call(
        store_kernel,
        (whole,),
        (values,),
        (vmem,),
        out_spaces=(hbm,),
        scratch=(pltpu.SemaphoreType.DMA(()),),
        micros=1.0,
    )
    residual, motion = call(
        functools.partial(final_kernel, count),
        (shape(3, node_dev), shape(3, slots, BLK)),
        messages,
        (vmem,) * count,
        scratch=(pltpu.VMEM((slots, BLK), F32),),
        micros=0.8,
    )
    return populations_out, residual, motion.transpose(1, 0, 2)[None, None]


def solution(mesh):
    return jax.shard_map(
        shards,
        mesh=mesh,
        in_specs=(
            P(None, ("group", "slab"), "inner", None),
            P(("group", "slab"), "inner", None),
            P(("group", "slab"), "inner", None),
            P(None, ("group", "slab", "inner")),
            P(None, ("group", "slab", "inner")),
            P(None, ("group", "slab", "inner")),
            P(("group", "slab", "inner")),
            P(("group", "slab"), "inner", None),
            P(("group", "slab"), "inner", None),
            P(("group", "slab"), "inner", None),
            P(("group", "slab"), "inner"),
        ),
        out_specs=(
            P(None, ("group", "slab"), "inner", None),
            P(None, ("group", "slab", "inner")),
            P(("group", "slab"), "inner", None, None, None),
        ),
        check_vma=False,
    )
```

```python
import functools

import jax
import jax.numpy as jnp
from jax import lax
from jax.experimental import pallas as pl
from jax.experimental.pallas import tpu as pltpu
from jax.sharding import PartitionSpec as P

BLK = 128
VELOCITIES = (
    (0, 0, 0),
    (1, 0, 0),
    (-1, 0, 0),
    (0, 1, 0),
    (0, -1, 0),
    (0, 0, 1),
    (0, 0, -1),
    (1, 1, 0),
    (-1, -1, 0),
    (1, -1, 0),
    (-1, 1, 0),
    (1, 0, 1),
    (-1, 0, -1),
    (1, 0, -1),
    (-1, 0, 1),
    (0, 1, 1),
    (0, -1, -1),
    (0, 1, -1),
    (0, -1, 1),
)
WEIGHTS = (1.0 / 3.0,) + (1.0 / 18.0,) * 6 + (1.0 / 36.0,) * 12
OPPOSITE = (0, 2, 1, 4, 3, 6, 5, 8, 7, 10, 9, 12, 11, 14, 13, 16, 15, 18, 17)
INLET_SPEED = 0.04
LOAD_SCALE = 25.0
COMPLIANCE = 0.5
LAME_RATIO = 2.0
Q = 19
FLAG_SLOT = 19
RATE_SLOT = 20
SLOTS = 21
FORCE_SLOT = 6
CORNER_SLOTS = FORCE_SLOT + 3
PIECES = 2
F32 = jnp.float32
VMEM_BYTES = 48 * 1024 * 1024


def moments(values):
    sums = [values[q] + values[q + 1] for q in range(1, Q, 2)]
    diffs = [values[q] - values[q + 1] for q in range(1, Q, 2)]
    density = values[0]
    for term in sums:
        density = density + term
    flows = []
    for axis in range(3):
        total = None
        for k, q in enumerate(range(1, Q, 2)):
            factor = VELOCITIES[q][axis]
            if factor == 0:
                continue
            if total is None:
                total = diffs[k] if factor > 0 else -diffs[k]
            else:
                total = total + diffs[k] if factor > 0 else total - diffs[k]
        flows.append(total)
    return density, flows[0], flows[1], flows[2]


def collide(values, rate, kind):
    density, flow_x, flow_y, flow_z = moments(values)
    inverse = 1.0 / density
    wall = kind == 1
    inlet = kind == 2
    fluid = kind == 0
    vel = (
        jnp.where(inlet, INLET_SPEED, flow_x * inverse),
        jnp.where(inlet, 0.0, flow_y * inverse),
        jnp.where(inlet, 0.0, flow_z * inverse),
    )
    scale = jnp.where(fluid, density, 1.0)
    rate = jnp.where(fluid, rate, 1.0)
    base = 1.0 - 1.5 * (vel[0] * vel[0] + vel[1] * vel[1] + vel[2] * vel[2])
    weighted = {w: w * scale for w in set(WEIGHTS)}
    out = [None] * Q
    relaxed = values[0] + rate * (weighted[WEIGHTS[0]] * base - values[0])
    out[0] = jnp.where(wall, values[0], relaxed)
    for q in range(1, Q, 2):
        project = None
        for factor, component in zip(VELOCITIES[q], vel):
            if factor == 0:
                continue
            if project is None:
                project = component
            else:
                project = project + component if factor > 0 else project - component
        even = base + 4.5 * (project * project)
        odd = 3.0 * project
        w = weighted[WEIGHTS[q]]
        forward = values[q] + rate * (w * (even + odd) - values[q])
        backward = values[q + 1] + rate * (w * (even - odd) - values[q + 1])
        out[q] = jnp.where(wall, values[q + 1], forward)
        out[q + 1] = jnp.where(wall, values[q], backward)
    return out


def roll_by(block, step, axis):
    if step == 0:
        return block
    return pltpu.roll(block, step % block.shape[axis], axis)


def face_slots(axis, sign):
    picks = []
    for q in range(Q):
        if VELOCITIES[q][axis] * sign >= 0:
            picks.append((q, 0))
        else:
            picks.append((OPPOSITE[q], 1))
    return picks


def mirror(q, axis):
    flipped = tuple(-c if k == axis else c for k, c in enumerate(VELOCITIES[q]))
    return VELOCITIES.index(flipped)


def corner_rows(sign_x, sign_y):
    rows = []
    for q, depth in face_slots(0, sign_x):
        if VELOCITIES[q][1] * sign_y >= 0:
            rows.append((q, depth))
        else:
            rows.append((OPPOSITE[mirror(q, 1)], depth))
    return rows


def first_kernel(
    pops_hbm, rate_hbm, flags_hbm, c1, fixed, far, near, pops, rate, flags, sems
):
    planes = c1.shape[1]
    copies = [
        pltpu.make_async_copy(rate_hbm, rate, sems.at[planes]),
        pltpu.make_async_copy(flags_hbm, flags, sems.at[planes + 1]),
    ]
    loads = [
        pltpu.make_async_copy(pops_hbm.at[:, x], pops.at[x], sems.at[x]) for x in range(planes)
    ]
    for copy in loads[:1] + copies + loads[1:]:
        copy.start()
    for copy in copies:
        copy.wait()

    def plane(x, carry):
        pltpu.make_async_copy(pops_hbm.at[:, x], pops.at[x], sems.at[x]).wait()
        kind = flags[x]
        values = [pops[x, q] for q in range(Q)]
        result = collide(values, rate[x], kind)
        for q in range(Q):
            c1[q, x] = roll_by(result[q], VELOCITIES[q][2], 1)
        fixed[0, x] = kind.astype(F32)
        fixed[1, x] = rate[x]
        return carry

    lax.fori_loop(0, planes, plane, 0)

    def pack(out, sign, outside):
        for slot, (q, depth) in enumerate(face_slots(0, sign)):
            out[slot] = c1[q, planes - 1 - depth if sign > 0 else depth]
        end = planes - 1 if sign > 0 else 0
        out[FLAG_SLOT] = fixed[0, end]
        out[RATE_SLOT] = fixed[1, end]
        clear_outside(out, outside)

    pack_pair(pack, "slab", near, far)


def clear_outside(out, outside):
    @pl.when(outside)
    def _():
        out[...] = jnp.zeros(out.shape, F32)


def pack_pair(pack, axis, near, far):
    at = lax.axis_index(axis)
    even = lax.rem(at, 2) == 0
    first, last = at == 0, at == lax.axis_size(axis) - 1

    @pl.when(even)
    def _():
        pack(near, 1, last)
        pack(far, -1, first)

    @pl.when(jnp.logical_not(even))
    def _():
        pack(near, -1, first)
        pack(far, 1, last)


def side_kernel(c1, fixed, next_nodes, far, near):
    del next_nodes
    planes, rows = c1.shape[1], c1.shape[2]

    def pack(out, sign, outside):
        def line(x, carry):
            for slot, (q, depth) in enumerate(face_slots(1, sign)):
                y = rows - 1 - depth if sign > 0 else depth
                out[slot, pl.ds(x, 1)] = c1[q, x, y : y + 1]
            y = rows - 1 if sign > 0 else 0
            for k, slot in enumerate((FLAG_SLOT, RATE_SLOT)):
                out[slot, pl.ds(x, 1)] = fixed[k, x, y : y + 1]
            return carry

        lax.fori_loop(0, planes, line, 0)
        clear_outside(out, outside)

    pack_pair(pack, "inner", near, far)


def gather_both(near, far, both, axis):
    odd = lax.rem(lax.axis_index(axis), 2)
    for slot in range(both.shape[1]):
        both[1 - odd, slot] = near[slot]
        both[odd, slot] = far[slot]


def corner_kernel(far_y, near_y, other, far, near, both):
    planes = near_y.shape[1]
    gather_both(near_y, far_y, both, "inner")

    def pack(out, sign, outside):
        for side, sign_y in enumerate((1, -1)):
            picks = corner_rows(sign, sign_y) + [(FLAG_SLOT, 0), (RATE_SLOT, 0)]
            for row, (slot, depth) in enumerate(picks):
                x = planes - 1 - depth if sign > 0 else depth
                at = 3 * side + row // 8
                out[at, row % 8 : row % 8 + 1] = both[side, slot, x : x + 1]
        for part in range(3):
            out[FORCE_SLOT + part] = other[part]
        clear_outside(out, outside)

    pack_pair(pack, "slab", near, far)


def with_edge(block, step_y, edge):
    rows = block.shape[0]
    sub = lax.broadcasted_iota(jnp.int32, block.shape, 0)
    if step_y > 0:
        return jnp.where(sub == 0, edge, roll_by(block, 1, 0))
    return jnp.where(sub == rows - 1, edge, roll_by(block, -1, 0))


def store_plane(extended, walls, second, at, rate, kind):
    values = []
    for q in range(Q):
        step_x, step_y, _ = VELOCITIES[q]
        block = extended[q, at + 1 - step_x]
        if step_y != 0:
            edge = walls[0 if step_y > 0 else 1, q, pl.ds(at + 1 - step_x, 1)]
            block = with_edge(block, step_y, edge)
        values.append(block)
    result = collide(values, rate, kind)
    for q in range(Q):
        second[q, at] = roll_by(result[q], VELOCITIES[q][2], 1)


def inside_kernel(
    c1,
    fixed,
    far_y,
    near_y,
    far_x,
    near_x,
    extended,
    walls,
    crossing,
    second,
    ends,
    both_y,
    both_x,
):
    planes, rows, _ = c1.shape[1:]
    wide = planes + 4
    gather_both(near_y, far_y, both_y, "inner")
    gather_both(near_x, far_x, both_x, "slab")
    for q in range(Q):
        for x in range(planes):
            extended[q, x + 2] = c1[q, x]
        extended[q, 1] = both_x[0, q]
        extended[q, planes + 2] = both_x[1, q]
        if VELOCITIES[q][0] > 0:
            extended[q, 0] = both_x[0, OPPOSITE[q]]
        if VELOCITIES[q][0] < 0:
            extended[q, planes + 3] = both_x[1, OPPOSITE[q]]
    for end in range(2):
        ends[end, 0] = both_x[end, FLAG_SLOT]
        ends[end, 1] = both_x[end, RATE_SLOT]

    for side, sign in enumerate((1, -1)):
        y = 0 if sign > 0 else rows - 1
        for slot in range(SLOTS):
            walls[side, slot, 2 : planes + 2] = both_y[side, slot]
        place = 0
        for q in range(Q):
            if VELOCITIES[q][1] != -sign:
                continue
            for x in range(wide):
                crossing[side, place, x : x + 1] = extended[q, x, y : y + 1]
            place += 1

    def inside_plane(x, carry):
        store_plane(extended, walls, second, x + 1, fixed[1, x], fixed[0, x])
        return carry

    lax.fori_loop(1, planes - 1, inside_plane, 0)


def second_kernel(
    block_source_hbm,
    block_target_hbm,
    block_node_hbm,
    block_count,
    far,
    near,
    fixed,
    extended,
    crossing,
    ends,
    internal_own,
    walls_in,
    second_in,
    out,
    message,
    walls,
    second,
    both,
    edges,
    loads,
    block_source,
    block_target,
    block_node,
    sems,
):
    del walls_in, second_in
    copies = [
        pltpu.make_async_copy(block_source_hbm, block_source, sems.at[0]),
        pltpu.make_async_copy(block_target_hbm, block_target, sems.at[1]),
        pltpu.make_async_copy(block_node_hbm, block_node, sems.at[2]),
    ]
    for copy in copies:
        copy.start()
    planes, rows, length = out.shape[1:]
    half = length // BLK
    slots = block_source.shape[2]
    wide = planes + 4
    slab = lax.axis_index("slab")
    inner = lax.axis_index("inner")
    slab_end = lax.axis_size("slab") - 1
    inner_end = lax.axis_size("inner") - 1
    gather_both(near, far, both, "slab")

    for side, sign in enumerate((1, -1)):
        for end, sign_x in enumerate((1, -1)):
            for row, (slot, depth) in enumerate(corner_rows(sign_x, sign)):
                at = (1 - depth) if sign_x > 0 else planes + 2 + depth
                source = 3 * side + row // 8
                walls[side, slot, at : at + 1] = both[end, source, row % 8 : row % 8 + 1]
            at = 1 if sign_x > 0 else planes + 2
            for row in (FLAG_SLOT, RATE_SLOT):
                source = 3 * side + row // 8
                walls[side, row, at : at + 1] = both[end, source, row % 8 : row % 8 + 1]

    def edge_plane(end, carry):
        x = end * (planes - 1)
        store_plane(extended, walls, second, x + 1, fixed[1, x], fixed[0, x])
        return carry

    def outside_plane(end, carry):
        store_plane(extended, walls, second, end * (planes + 1), ends[end, 1], ends[end, 0])
        return carry

    lax.fori_loop(0, 2, edge_plane, 0)
    lax.fori_loop(0, 2, outside_plane, 0)

    @pl.when(slab == 0)
    def _():
        for q in range(Q):
            if VELOCITIES[q][0] > 0:
                second[q, 0] = jnp.zeros((rows, length), F32)

    @pl.when(slab == slab_end)
    def _():
        for q in range(Q):
            if VELOCITIES[q][0] < 0:
                second[q, planes + 1] = jnp.zeros((rows, length), F32)

    across = lax.broadcasted_iota(jnp.int32, (wide, length), 0)
    hidden = ((across <= 1) & (slab == 0)) | ((across >= planes + 2) & (slab == slab_end))
    for side, sign, outside in ((0, 1, inner == 0), (1, -1, inner == inner_end)):
        values = []
        place = 0
        for q in range(Q):
            step_x, step_y, _ = VELOCITIES[q]
            if step_y == 0:
                block = walls[side, q]
            elif step_y == sign:
                block = walls[side, OPPOSITE[q]]
            else:
                block = crossing[side, place]
                place += 1
            values.append(roll_by(block, step_x, 0))
        result = collide(values, walls[side, RATE_SLOT], walls[side, FLAG_SLOT])
        place = 0
        for q in range(Q):
            if VELOCITIES[q][1] == sign:
                kept = jnp.where(hidden | outside, 0.0, result[q])
                edges[side, place] = roll_by(kept, VELOCITIES[q][2], 1)
                place += 1

    def plane_two(x, carry):
        values = []
        places = {1: 0, -1: 0}
        for q in range(Q):
            step_x, step_y, _ = VELOCITIES[q]
            block = second[q, x + 1 - step_x]
            if step_y != 0:
                edge = edges[0 if step_y > 0 else 1, places[step_y], pl.ds(x + 2 - step_x, 1)]
                places[step_y] += 1
                block = with_edge(block, step_y, edge)
            values.append(block)
            out[q, x] = block
        density, flow_x, flow_y, flow_z = moments(values)
        parts = (
            LOAD_SCALE * flow_x,
            LOAD_SCALE * (flow_y + (density - 1.0) / 3.0),
            LOAD_SCALE * flow_z,
        )
        for part in range(3):
            for piece in range(half):
                loads[x * half + piece, part] = parts[part][:, piece * BLK : (piece + 1) * BLK]
        return carry

    lax.fori_loop(0, planes, plane_two, 0)

    for copy in copies:
        copy.wait()
    node_blocks = internal_own.shape[1] * half
    live = jnp.broadcast_to(block_count[...], (1, BLK))
    for k in range(slots):
        run = block_source[0, 0, k]
        x = run // (rows * half)
        left = run - x * (rows * half)
        y = left // half
        piece = left - y * half
        for part in range(3):
            message[4 * k + part : 4 * k + part + 1] = loads[x * half + piece, part, pl.ds(y, 1)]
        key = block_target[0, 0, k] * node_blocks + block_node[0, 0, k]
        message[4 * k + 3 : 4 * k + 4] = jnp.where(live > k, key, -1).astype(F32)
    for part in range(3):
        start = 4 * slots + part * node_blocks
        for piece in range(half):
            at = piece * rows
            lanes = slice(piece * BLK, (piece + 1) * BLK)
            message[start + at : start + at + rows] = (
                internal_own[part, :, lanes] + both[0, FORCE_SLOT + part, :, lanes]
            )


def element_kernel(
    elements, displacement, next_nodes, shape_inverse, stiffness, low_ids, high_ids, forces, shapes,
    numbers, corners,
):
    node_dev = displacement.shape[1]
    node_blocks = node_dev // BLK
    runs = elements.shape[1] // BLK
    for j in range(runs):
        lanes = slice(j * BLK, (j + 1) * BLK)
        for row in range(3):
            numbers[row, j : j + 1] = elements[row : row + 1, lanes]
            shapes[row, j : j + 1] = shape_inverse[row : row + 1, lanes]
    for row in range(3):
        low_ids[row] = (numbers[row] & (BLK - 1)).astype(F32)
        high_ids[row] = (numbers[row] >> 7).astype(F32)

    def gather(group, carry):
        rows = pl.ds(pl.multiple_of(group * 8, 8), 8)
        low = [numbers[corner, rows] & (BLK - 1) for corner in range(3)]
        high = [numbers[corner, rows] >> 7 for corner in range(3)]
        for corner in range(3):
            nodes = [jnp.zeros((8, BLK), F32)] * 3
            for block in range(2 * node_blocks):
                source = displacement if block < node_blocks else next_nodes
                start = (block % node_blocks) * BLK
                here = high[corner] == block
                for part in range(3):
                    row = source[part : part + 1, start : start + BLK]
                    picked = jnp.take_along_axis(
                        jnp.broadcast_to(row, (8, BLK)),
                        low[corner],
                        axis=1,
                        mode="promise_in_bounds",
                    )
                    nodes[part] = jnp.where(here, picked, nodes[part])
            for part in range(3):
                corners[corner, part, rows] = nodes[part]
        return carry

    lax.fori_loop(0, runs // 8, gather, 0)

    first, second, third = [[corners[c, p] for p in range(3)] for c in range(3)]
    diag_a = shapes[0]
    skew_b = shapes[1]
    diag_c = shapes[2]
    stiff = stiffness[...]
    edge_one = [second[p] - first[p] for p in range(3)]
    edge_two = [third[p] - first[p] for p in range(3)]
    one = [diag_a * edge_one[p] for p in range(3)]
    two = [skew_b * edge_one[p] + diag_c * edge_two[p] for p in range(3)]
    one[0] = one[0] + 1.0
    two[1] = two[1] + 1.0
    aa = one[0] * one[0] + one[1] * one[1] + one[2] * one[2]
    ab = one[0] * two[0] + one[1] * two[1] + one[2] * two[2]
    bb = two[0] * two[0] + two[1] * two[1] + two[2] * two[2]
    determinant = aa * bb - ab * ab
    scale = 1.0 / determinant
    inverse_aa = bb * scale
    inverse_ab = -ab * scale
    inverse_bb = aa * scale
    pressure = LAME_RATIO * (0.5 * jnp.log(determinant))
    for p in range(3):
        pulled_one = one[p] * inverse_aa + two[p] * inverse_ab
        pulled_two = one[p] * inverse_ab + two[p] * inverse_bb
        stress_one = stiff * (one[p] - pulled_one + pressure * pulled_one)
        stress_two = stiff * (two[p] - pulled_two + pressure * pulled_two)
        force_one = diag_a * stress_one + skew_b * stress_two
        force_two = diag_c * stress_two
        for corner, force in enumerate((-(force_one + force_two), force_one, force_two)):
            rest = force
            for part in range(PIECES):
                piece = rest.astype(jnp.bfloat16).astype(F32)
                rest = rest - piece
                forces[part * 3 + p, corner] = piece


def spread_kernel(base, low_ids, high_ids, forces, out):
    runs = low_ids.shape[1]
    parts, rows, length = out.shape
    pieces = length // BLK
    slots = pieces * rows
    kind = jnp.bfloat16
    tile = 16
    slot_ids = lax.broadcasted_iota(jnp.int32, (slots, BLK), 0).astype(F32) + base
    slot_ids = slot_ids.astype(kind)
    lane_ids = lax.broadcasted_iota(jnp.int32, (BLK, BLK), 0).astype(F32).astype(kind)
    ones = jnp.ones((BLK, BLK), kind)
    none = jnp.zeros((BLK, BLK), kind)
    blank = jnp.zeros((slots, BLK), kind)

    def tall_row(row, count):
        block = jnp.broadcast_to(row, (tile, BLK)).astype(kind)
        return jnp.concatenate([block] * (count // tile), axis=0)

    total = None
    for corner in range(3):
        left = [[] for _ in range(parts * PIECES)]
        right = []
        for j in range(runs):
            row = slice(j, j + 1)
            here = slot_ids == tall_row(high_ids[corner, row], slots)
            right.append(jnp.where(lane_ids == tall_row(low_ids[corner, row], BLK), ones, none))
            for part in range(parts * PIECES):
                left[part].append(
                    jnp.where(here, tall_row(forces[part, corner, row], slots), blank)
                )
        tall = jnp.concatenate([jnp.concatenate(part, axis=1) for part in left], axis=0)
        wide = jnp.concatenate(right, axis=1)
        product = lax.dot_general(
            tall, wide, (((1,), (1,)), ((), ())), preferred_element_type=F32
        )
        total = product if total is None else total + product
    for p in range(parts):
        summed = total[p * slots : (p + 1) * slots]
        for part in range(1, PIECES):
            start = (parts * part + p) * slots
            summed = summed + total[start : start + slots]
        for piece in range(pieces):
            out[p, :, piece * BLK : (piece + 1) * BLK] = summed[piece * rows : (piece + 1) * rows]


def store_kernel(values, out_hbm, sem):
    store = pltpu.make_async_copy(values, out_hbm, sem)
    store.start()
    store.wait()


def final_kernel(count, *refs):
    messages = refs[:count]
    residual, motion, keys = refs[count:]
    slots = keys.shape[0]
    node_blocks = residual.shape[1] // BLK
    inner = lax.axis_index("inner")
    mine = messages[0]
    for k in range(slots):
        keys[k : k + 1] = mine[4 * k + 3 : 4 * k + 4]
    wanted = keys[...]
    node_ids = lax.broadcasted_iota(jnp.int32, (node_blocks, BLK), 0)
    own_ids = (node_ids + inner * node_blocks).astype(F32)
    external = [jnp.zeros((node_blocks, BLK), F32)] * 3
    moved = [jnp.zeros((slots, BLK), F32)] * 3
    for message in messages:
        for k in range(slots):
            key = message[4 * k + 3 : 4 * k + 4]
            here = own_ids == key
            same = wanted == key
            for part in range(3):
                row = message[4 * k + part : 4 * k + part + 1]
                external[part] = external[part] + jnp.where(here, row, 0.0)
                moved[part] = moved[part] + jnp.where(same, row, 0.0)
    for step, message in enumerate(messages):
        sender = partner_of(inner, step, count)
        for b in range(node_blocks):
            key = jnp.broadcast_to(sender * node_blocks + b, (1, BLK)).astype(F32)
            same = wanted == key
            for part in range(3):
                at = 4 * slots + part * node_blocks + b
                moved[part] = moved[part] - jnp.where(same, message[at : at + 1], 0.0)
    live = wanted >= 0.0
    for part in range(3):
        start = 4 * slots + part * node_blocks
        left = external[part] - mine[start : start + node_blocks]
        for b in range(node_blocks):
            residual[part : part + 1, b * BLK : (b + 1) * BLK] = left[b : b + 1]
        motion[part] = jnp.where(live, COMPLIANCE * moved[part], 0.0)


def call(kernel, outs, operands, spaces, scratch=(), out_spaces=None, micros=1.0, aliases=None):
    spec = lambda space: pl.BlockSpec(memory_space=space)
    out_spaces = out_spaces or (pltpu.VMEM,) * len(outs)
    return pl.pallas_call(
        kernel,
        out_shape=outs,
        in_specs=[spec(space) for space in spaces],
        out_specs=tuple(spec(space) for space in out_spaces),
        scratch_shapes=list(scratch),
        input_output_aliases=aliases or {},
        compiler_params=pltpu.CompilerParams(vmem_limit_bytes=VMEM_BYTES),
        cost_estimate=pl.CostEstimate(
            flops=0, bytes_accessed=int(micros * 3.6e6), transcendentals=0
        ),
    )(*operands)


def partner_of(at, step, count):
    if count & (count - 1) == 0:
        return at ^ step
    return (at + count - step) % count


def exchange(block, axis, step):
    count = lax.axis_size(axis)
    return lax.ppermute(block, axis, [(partner_of(i, step, count), i) for i in range(count)])


def around(block, axis, step):
    count = lax.axis_size(axis)
    return lax.ppermute(block, axis, [(i, (i + step) % count) for i in range(count)])


def swap(near, far, axis, beside):
    count, others = lax.axis_size(axis), lax.axis_size(beside)
    routes = []
    for start in (0, 1):
        route = []
        for other in range(others):
            for i in range(count):
                j = i + 1 if i % 2 == start else i - 1
                to = other
                if not 0 <= j < count:
                    j = i
                    to = other ^ 1 if others % 2 == 0 else other
                route.append((other * count + i, to * count + j))
        routes.append(route)
    axes = (beside, axis)
    return lax.ppermute(near, axes, routes[0]), lax.ppermute(far, axes, routes[1])


def shards(
    populations,
    relaxation,
    node_flags,
    displacement,
    elements,
    shape_inverse,
    stiffness,
    block_source,
    block_target,
    block_node,
    block_count,
):
    planes, rows, length = populations.shape[1:]
    half = length // BLK
    node_dev = displacement.shape[1]
    node_blocks = node_dev // BLK
    runs = stiffness.shape[0] // BLK
    slots = block_source.shape[2]
    count = lax.axis_size("inner")
    shape = lambda *dims: jax.ShapeDtypeStruct(dims, F32)
    whole = shape(*populations.shape)
    vmem, hbm, smem = pltpu.VMEM, pltpu.HBM, pltpu.SMEM

    next_nodes = around(displacement, "slab", -1)
    face_y = shape(SLOTS, planes, length)
    face_x = shape(SLOTS, rows, length)
    pin = lambda block: pltpu.with_memory_space_constraint(block, hbm)
    c1, fixed, far, near = call(
        first_kernel,
        (whole, shape(2, planes, rows, length), face_x, face_x),
        (pin(populations), pin(relaxation), pin(node_flags)),
        (hbm,) * 3,
        scratch=(
            pltpu.VMEM((planes, Q, rows, length), F32),
            pltpu.VMEM((planes, rows, length), F32),
            pltpu.VMEM((planes, rows, length), jnp.int32),
            pltpu.SemaphoreType.DMA((planes + 2,)),
        ),
        micros=1.5,
    )
    near_x, far_x = swap(near, far, "slab", "group")
    far, near = call(
        side_kernel, (face_y, face_y), (c1, fixed, next_nodes), (vmem,) * 3, micros=0.3
    )
    near_y, far_y = swap(near, far, "inner", "slab")
    numbers = shape(3, runs, BLK)
    low_ids, high_ids, forces = call(
        element_kernel,
        (numbers, numbers, shape(3 * PIECES, 3, runs, BLK)),
        (elements, displacement, next_nodes, shape_inverse, stiffness.reshape(runs, BLK)),
        (vmem,) * 5,
        scratch=(
            pltpu.VMEM((3, runs, BLK), F32),
            pltpu.VMEM((3, runs, BLK), jnp.int32),
            pltpu.VMEM((3, 3, runs, BLK), F32),
        ),
        micros=2.0,
    )
    nodal = shape(3, node_blocks // half, length)
    (other,) = call(
        functools.partial(spread_kernel, node_blocks),
        (nodal,),
        (low_ids, high_ids, forces),
        (vmem,) * 3,
        micros=0.8,
    )
    corner = shape(CORNER_SLOTS, rows, length)
    far, near = call(
        corner_kernel,
        (corner, corner),
        (far_y, near_y, other),
        (vmem,) * 3,
        scratch=(pltpu.VMEM((2, SLOTS, planes, length), F32),),
        micros=0.3,
    )
    near_c, far_c = swap(near, far, "slab", "group")
    (own,) = call(
        functools.partial(spread_kernel, 0),
        (nodal,),
        (low_ids, high_ids, forces),
        (vmem,) * 3,
        micros=0.8,
    )
    wide = planes + 4
    walls_shape = shape(2, SLOTS, wide, length)
    second_shape = shape(Q, planes + 2, rows, length)
    extended, walls, crossing, second, ends = call(
        inside_kernel,
        (
            shape(Q, wide, rows, length),
            walls_shape,
            shape(2, 5, wide, length),
            second_shape,
            shape(2, 2, rows, length),
        ),
        (c1, fixed, far_y, near_y, far_x, near_x),
        (vmem,) * 6,
        scratch=(
            pltpu.VMEM((2, SLOTS, planes, length), F32),
            pltpu.VMEM((2, SLOTS, rows, length), F32),
        ),
        micros=0.8,
    )
    lines = 4 * slots + 3 * node_blocks
    values, message, _, _ = call(
        second_kernel,
        (whole, shape(lines, BLK), walls_shape, second_shape),
        (
            pin(block_source),
            pin(block_target),
            pin(block_node),
            block_count,
            far_c,
            near_c,
            fixed,
            extended,
            crossing,
            ends,
            own,
            walls,
            second,
        ),
        (hbm,) * 3 + (vmem,) * 10,
        aliases={11: 2, 12: 3},
        scratch=(
            pltpu.VMEM((2, CORNER_SLOTS, rows, length), F32),
            pltpu.VMEM((2, 5, wide, length), F32),
            pltpu.VMEM((planes * half, 3, rows, BLK), F32),
            pltpu.SMEM(block_source.shape, jnp.int32),
            pltpu.SMEM(block_target.shape, jnp.int32),
            pltpu.SMEM(block_node.shape, jnp.int32),
            pltpu.SemaphoreType.DMA((3,)),
        ),
        micros=1.5,
    )
    messages = [message] + [exchange(message, "inner", step) for step in range(1, count)]
    (populations_out,) = call(
        store_kernel,
        (whole,),
        (values,),
        (vmem,),
        out_spaces=(hbm,),
        scratch=(pltpu.SemaphoreType.DMA(()),),
        micros=1.0,
    )
    residual, motion = call(
        functools.partial(final_kernel, count),
        (shape(3, node_dev), shape(3, slots, BLK)),
        messages,
        (vmem,) * count,
        scratch=(pltpu.VMEM((slots, BLK), F32),),
        micros=0.8,
    )
    return populations_out, residual, motion.transpose(1, 0, 2)[None, None]


def solution(mesh):
    return jax.shard_map(
        shards,
        mesh=mesh,
        in_specs=(
            P(None, ("group", "slab"), "inner", None),
            P(("group", "slab"), "inner", None),
            P(("group", "slab"), "inner", None),
            P(None, ("group", "slab", "inner")),
            P(None, ("group", "slab", "inner")),
            P(None, ("group", "slab", "inner")),
            P(("group", "slab", "inner")),
            P(("group", "slab"), "inner", None),
            P(("group", "slab"), "inner", None),
            P(("group", "slab"), "inner", None),
            P(("group", "slab"), "inner"),
        ),
        out_specs=(
            P(None, ("group", "slab"), "inner", None),
            P(None, ("group", "slab", "inner")),
            P(("group", "slab"), "inner", None, None, None),
        ),
        check_vma=False,
    )
```

```python
import functools

import jax
import jax.numpy as jnp
from jax import lax
from jax.experimental import pallas as pl
from jax.experimental.pallas import tpu as pltpu
from jax.sharding import PartitionSpec as P

BLK = 128
VELOCITIES = (
    (0, 0, 0),
    (1, 0, 0),
    (-1, 0, 0),
    (0, 1, 0),
    (0, -1, 0),
    (0, 0, 1),
    (0, 0, -1),
    (1, 1, 0),
    (-1, -1, 0),
    (1, -1, 0),
    (-1, 1, 0),
    (1, 0, 1),
    (-1, 0, -1),
    (1, 0, -1),
    (-1, 0, 1),
    (0, 1, 1),
    (0, -1, -1),
    (0, 1, -1),
    (0, -1, 1),
)
WEIGHTS = (1.0 / 3.0,) + (1.0 / 18.0,) * 6 + (1.0 / 36.0,) * 12
OPPOSITE = (0, 2, 1, 4, 3, 6, 5, 8, 7, 10, 9, 12, 11, 14, 13, 16, 15, 18, 17)
INLET_SPEED = 0.04
LOAD_SCALE = 25.0
COMPLIANCE = 0.5
LAME_RATIO = 2.0
Q = 19
FLAG_SLOT = 19
RATE_SLOT = 20
SLOTS = 21
FORCE_SLOT = 6
CORNER_SLOTS = FORCE_SLOT + 3
PIECES = 2
CAP = 3
F32 = jnp.float32
VMEM_BYTES = 48 * 1024 * 1024


def moments(values):
    sums = [values[q] + values[q + 1] for q in range(1, Q, 2)]
    diffs = [values[q] - values[q + 1] for q in range(1, Q, 2)]
    density = values[0]
    for term in sums:
        density = density + term
    flows = []
    for axis in range(3):
        total = None
        for k, q in enumerate(range(1, Q, 2)):
            factor = VELOCITIES[q][axis]
            if factor == 0:
                continue
            if total is None:
                total = diffs[k] if factor > 0 else -diffs[k]
            else:
                total = total + diffs[k] if factor > 0 else total - diffs[k]
        flows.append(total)
    return density, flows[0], flows[1], flows[2]


def collide(values, rate, kind):
    density, flow_x, flow_y, flow_z = moments(values)
    inverse = 1.0 / density
    wall = kind == 1
    inlet = kind == 2
    fluid = kind == 0
    vel = (
        jnp.where(inlet, INLET_SPEED, flow_x * inverse),
        jnp.where(inlet, 0.0, flow_y * inverse),
        jnp.where(inlet, 0.0, flow_z * inverse),
    )
    scale = jnp.where(fluid, density, 1.0)
    rate = jnp.where(fluid, rate, 1.0)
    base = 1.0 - 1.5 * (vel[0] * vel[0] + vel[1] * vel[1] + vel[2] * vel[2])
    weighted = {w: w * scale for w in set(WEIGHTS)}
    out = [None] * Q
    relaxed = values[0] + rate * (weighted[WEIGHTS[0]] * base - values[0])
    out[0] = jnp.where(wall, values[0], relaxed)
    for q in range(1, Q, 2):
        project = None
        for factor, component in zip(VELOCITIES[q], vel):
            if factor == 0:
                continue
            if project is None:
                project = component
            else:
                project = project + component if factor > 0 else project - component
        even = base + 4.5 * (project * project)
        odd = 3.0 * project
        w = weighted[WEIGHTS[q]]
        forward = values[q] + rate * (w * (even + odd) - values[q])
        backward = values[q + 1] + rate * (w * (even - odd) - values[q + 1])
        out[q] = jnp.where(wall, values[q + 1], forward)
        out[q + 1] = jnp.where(wall, values[q], backward)
    return out


def roll_by(block, step, axis):
    if step == 0:
        return block
    return pltpu.roll(block, step % block.shape[axis], axis)


def face_slots(axis, sign):
    picks = []
    for q in range(Q):
        if VELOCITIES[q][axis] * sign >= 0:
            picks.append((q, 0))
        else:
            picks.append((OPPOSITE[q], 1))
    return picks


def mirror(q, axis):
    flipped = tuple(-c if k == axis else c for k, c in enumerate(VELOCITIES[q]))
    return VELOCITIES.index(flipped)


def corner_rows(sign_x, sign_y):
    rows = []
    for q, depth in face_slots(0, sign_x):
        if VELOCITIES[q][1] * sign_y >= 0:
            rows.append((q, depth))
        else:
            rows.append((OPPOSITE[mirror(q, 1)], depth))
    return rows


def first_kernel(
    pops_hbm, rate_hbm, flags_hbm, c1, fixed, far, near, pops, rate, flags, sems
):
    planes = c1.shape[1]
    copies = [
        pltpu.make_async_copy(rate_hbm, rate, sems.at[planes]),
        pltpu.make_async_copy(flags_hbm, flags, sems.at[planes + 1]),
    ]
    loads = [
        pltpu.make_async_copy(pops_hbm.at[:, x], pops.at[x], sems.at[x]) for x in range(planes)
    ]
    for copy in loads[:1] + copies + loads[1:]:
        copy.start()
    for copy in copies:
        copy.wait()

    def plane(x, carry):
        pltpu.make_async_copy(pops_hbm.at[:, x], pops.at[x], sems.at[x]).wait()
        kind = flags[x]
        values = [pops[x, q] for q in range(Q)]
        result = collide(values, rate[x], kind)
        for q in range(Q):
            c1[q, x] = roll_by(result[q], VELOCITIES[q][2], 1)
        fixed[0, x] = kind.astype(F32)
        fixed[1, x] = rate[x]
        return carry

    lax.fori_loop(0, planes, plane, 0)

    def pack(out, sign, outside):
        for slot, (q, depth) in enumerate(face_slots(0, sign)):
            out[slot] = c1[q, planes - 1 - depth if sign > 0 else depth]
        end = planes - 1 if sign > 0 else 0
        out[FLAG_SLOT] = fixed[0, end]
        out[RATE_SLOT] = fixed[1, end]
        clear_outside(out, outside)

    pack_pair(pack, "slab", near, far)


def clear_outside(out, outside):
    @pl.when(outside)
    def _():
        out[...] = jnp.zeros(out.shape, F32)


def pack_pair(pack, axis, near, far):
    at = lax.axis_index(axis)
    even = lax.rem(at, 2) == 0
    first, last = at == 0, at == lax.axis_size(axis) - 1

    @pl.when(even)
    def _():
        pack(near, 1, last)
        pack(far, -1, first)

    @pl.when(jnp.logical_not(even))
    def _():
        pack(near, -1, first)
        pack(far, 1, last)


def side_kernel(c1, fixed, next_nodes, far, near):
    del next_nodes
    planes, rows = c1.shape[1], c1.shape[2]

    def pack(out, sign, outside):
        def line(x, carry):
            for slot, (q, depth) in enumerate(face_slots(1, sign)):
                y = rows - 1 - depth if sign > 0 else depth
                out[slot, pl.ds(x, 1)] = c1[q, x, y : y + 1]
            y = rows - 1 if sign > 0 else 0
            for k, slot in enumerate((FLAG_SLOT, RATE_SLOT)):
                out[slot, pl.ds(x, 1)] = fixed[k, x, y : y + 1]
            return carry

        lax.fori_loop(0, planes, line, 0)
        clear_outside(out, outside)

    pack_pair(pack, "inner", near, far)


def gather_both(near, far, both, axis):
    odd = lax.rem(lax.axis_index(axis), 2)
    for slot in range(both.shape[1]):
        both[1 - odd, slot] = near[slot]
        both[odd, slot] = far[slot]


def corner_kernel(far_y, near_y, other, far, near, both):
    planes = near_y.shape[1]
    gather_both(near_y, far_y, both, "inner")

    def pack(out, sign, outside):
        for side, sign_y in enumerate((1, -1)):
            picks = corner_rows(sign, sign_y) + [(FLAG_SLOT, 0), (RATE_SLOT, 0)]
            for row, (slot, depth) in enumerate(picks):
                x = planes - 1 - depth if sign > 0 else depth
                at = 3 * side + row // 8
                out[at, row % 8 : row % 8 + 1] = both[side, slot, x : x + 1]
        for part in range(3):
            out[FORCE_SLOT + part] = other[part]
        clear_outside(out, outside)

    pack_pair(pack, "slab", near, far)


def with_edge(block, step_y, edge):
    rows = block.shape[0]
    sub = lax.broadcasted_iota(jnp.int32, block.shape, 0)
    if step_y > 0:
        return jnp.where(sub == 0, edge, roll_by(block, 1, 0))
    return jnp.where(sub == rows - 1, edge, roll_by(block, -1, 0))


def store_plane(extended, walls, second, at, rate, kind):
    values = []
    for q in range(Q):
        step_x, step_y, _ = VELOCITIES[q]
        block = extended[q, at + 1 - step_x]
        if step_y != 0:
            edge = walls[0 if step_y > 0 else 1, q, pl.ds(at + 1 - step_x, 1)]
            block = with_edge(block, step_y, edge)
        values.append(block)
    result = collide(values, rate, kind)
    for q in range(Q):
        second[q, at] = roll_by(result[q], VELOCITIES[q][2], 1)


def inside_kernel(
    c1,
    fixed,
    far_y,
    near_y,
    far_x,
    near_x,
    extended,
    walls,
    crossing,
    second,
    ends,
    both_y,
    both_x,
):
    planes, rows, _ = c1.shape[1:]
    wide = planes + 4
    gather_both(near_y, far_y, both_y, "inner")
    gather_both(near_x, far_x, both_x, "slab")
    for q in range(Q):
        for x in range(planes):
            extended[q, x + 2] = c1[q, x]
        extended[q, 1] = both_x[0, q]
        extended[q, planes + 2] = both_x[1, q]
        if VELOCITIES[q][0] > 0:
            extended[q, 0] = both_x[0, OPPOSITE[q]]
        if VELOCITIES[q][0] < 0:
            extended[q, planes + 3] = both_x[1, OPPOSITE[q]]
    for end in range(2):
        ends[end, 0] = both_x[end, FLAG_SLOT]
        ends[end, 1] = both_x[end, RATE_SLOT]

    for side, sign in enumerate((1, -1)):
        y = 0 if sign > 0 else rows - 1
        for slot in range(SLOTS):
            walls[side, slot, 2 : planes + 2] = both_y[side, slot]
        place = 0
        for q in range(Q):
            if VELOCITIES[q][1] != -sign:
                continue
            for x in range(wide):
                crossing[side, place, x : x + 1] = extended[q, x, y : y + 1]
            place += 1

    def inside_plane(x, carry):
        store_plane(extended, walls, second, x + 1, fixed[1, x], fixed[0, x])
        return carry

    lax.fori_loop(1, planes - 1, inside_plane, 0)


def targets_of(keys, dest, node_blocks):
    found = []
    before = jnp.zeros((1, BLK), F32)
    low = (dest * node_blocks).astype(F32)
    for k in range(keys.shape[0]):
        key = keys[k : k + 1]
        named = (key >= low) & (key < low + node_blocks)
        found.append((key, named, before))
        before = before + jnp.where(named, 1.0, 0.0)
    return found


def second_kernel(count, *refs):
    block_source_hbm, keys = refs[0], refs[1 : 1 + count]
    far, near, fixed, extended, crossing, ends, internal_own = refs[1 + count : 8 + count]
    out = refs[10 + count]
    messages = refs[11 + count : 11 + 2 * count]
    walls, second = refs[11 + 2 * count : 13 + 2 * count]
    both, edges, loads, internal, block_source, sem = refs[13 + 2 * count :]
    copy = pltpu.make_async_copy(block_source_hbm, block_source, sem)
    copy.start()
    planes, rows, length = out.shape[1:]
    half = length // BLK
    slots = block_source.shape[2]
    wide = planes + 4
    slab = lax.axis_index("slab")
    inner = lax.axis_index("inner")
    slab_end = lax.axis_size("slab") - 1
    inner_end = lax.axis_size("inner") - 1
    gather_both(near, far, both, "slab")

    for side, sign in enumerate((1, -1)):
        for end, sign_x in enumerate((1, -1)):
            for row, (slot, depth) in enumerate(corner_rows(sign_x, sign)):
                at = (1 - depth) if sign_x > 0 else planes + 2 + depth
                source = 3 * side + row // 8
                walls[side, slot, at : at + 1] = both[end, source, row % 8 : row % 8 + 1]
            at = 1 if sign_x > 0 else planes + 2
            for row in (FLAG_SLOT, RATE_SLOT):
                source = 3 * side + row // 8
                walls[side, row, at : at + 1] = both[end, source, row % 8 : row % 8 + 1]

    def edge_plane(end, carry):
        x = end * (planes - 1)
        store_plane(extended, walls, second, x + 1, fixed[1, x], fixed[0, x])
        return carry

    def outside_plane(end, carry):
        store_plane(extended, walls, second, end * (planes + 1), ends[end, 1], ends[end, 0])
        return carry

    lax.fori_loop(0, 2, edge_plane, 0)
    lax.fori_loop(0, 2, outside_plane, 0)

    @pl.when(slab == 0)
    def _():
        for q in range(Q):
            if VELOCITIES[q][0] > 0:
                second[q, 0] = jnp.zeros((rows, length), F32)

    @pl.when(slab == slab_end)
    def _():
        for q in range(Q):
            if VELOCITIES[q][0] < 0:
                second[q, planes + 1] = jnp.zeros((rows, length), F32)

    across = lax.broadcasted_iota(jnp.int32, (wide, length), 0)
    hidden = ((across <= 1) & (slab == 0)) | ((across >= planes + 2) & (slab == slab_end))
    for side, sign, outside in ((0, 1, inner == 0), (1, -1, inner == inner_end)):
        values = []
        place = 0
        for q in range(Q):
            step_x, step_y, _ = VELOCITIES[q]
            if step_y == 0:
                block = walls[side, q]
            elif step_y == sign:
                block = walls[side, OPPOSITE[q]]
            else:
                block = crossing[side, place]
                place += 1
            values.append(roll_by(block, step_x, 0))
        result = collide(values, walls[side, RATE_SLOT], walls[side, FLAG_SLOT])
        place = 0
        for q in range(Q):
            if VELOCITIES[q][1] == sign:
                kept = jnp.where(hidden | outside, 0.0, result[q])
                edges[side, place] = roll_by(kept, VELOCITIES[q][2], 1)
                place += 1

    def plane_two(x, carry):
        values = []
        places = {1: 0, -1: 0}
        for q in range(Q):
            step_x, step_y, _ = VELOCITIES[q]
            block = second[q, x + 1 - step_x]
            if step_y != 0:
                edge = edges[0 if step_y > 0 else 1, places[step_y], pl.ds(x + 2 - step_x, 1)]
                places[step_y] += 1
                block = with_edge(block, step_y, edge)
            values.append(block)
            out[q, x] = block
        density, flow_x, flow_y, flow_z = moments(values)
        parts = (
            LOAD_SCALE * flow_x,
            LOAD_SCALE * (flow_y + (density - 1.0) / 3.0),
            LOAD_SCALE * flow_z,
        )
        for part in range(3):
            for piece in range(half):
                loads[x * half + piece, part] = parts[part][:, piece * BLK : (piece + 1) * BLK]
        return carry

    lax.fori_loop(0, planes, plane_two, 0)

    node_blocks = internal_own.shape[1] * half
    for part in range(3):
        for piece in range(half):
            at = piece * rows
            lanes = slice(piece * BLK, (piece + 1) * BLK)
            internal[part, at : at + rows] = (
                internal_own[part, :, lanes] + both[0, FORCE_SLOT + part, :, lanes]
            )
    copy.wait()
    blocks = []
    for k in range(slots):
        run = block_source[0, 0, k]
        x = run // (rows * half)
        left = run - x * (rows * half)
        y = left // half
        piece = left - y * half
        blocks.append([loads[x * half + piece, part, pl.ds(y, 1)] for part in range(3)])
    slot_ids = lax.broadcasted_iota(jnp.int32, (8, BLK), 0).astype(F32)
    for step in range(count):
        message = messages[-step]
        dest = partner_of(inner, step, count)
        wanted = keys[step][...]
        moved = [jnp.zeros((slots, BLK), F32)] * 3
        chosen = [jnp.zeros((8, BLK), F32)] * 3
        for k, (key, named, before) in enumerate(targets_of(keys[0], dest, node_blocks)):
            same = (wanted == key) & (key >= 0.0)
            here = named & (slot_ids == before)
            for part in range(3):
                moved[part] = moved[part] + jnp.where(same, blocks[k][part], 0.0)
                chosen[part] = chosen[part] + jnp.where(here, blocks[k][part], 0.0)
        for b in range(node_blocks):
            same = wanted == (inner * node_blocks + b).astype(F32)
            for part in range(3):
                moved[part] = moved[part] - jnp.where(same, internal[part, b : b + 1], 0.0)
        for part in range(3):
            message[part * slots : (part + 1) * slots] = moved[part]
            at = 3 * slots + part * CAP
            message[at : at + CAP] = chosen[part][:CAP]
        if step == 0:
            for part in range(3):
                at = 3 * slots + 3 * CAP + part * node_blocks
                message[at : at + node_blocks] = internal[part]


def element_kernel(
    elements,
    displacement,
    next_nodes,
    shape_inverse,
    stiffness,
    low_ids,
    high_ids,
    forces,
    shapes,
    numbers,
    corners,
):
    node_dev = displacement.shape[1]
    node_blocks = node_dev // BLK
    runs = elements.shape[1] // BLK
    for j in range(runs):
        lanes = slice(j * BLK, (j + 1) * BLK)
        for row in range(3):
            numbers[row, j : j + 1] = elements[row : row + 1, lanes]
            shapes[row, j : j + 1] = shape_inverse[row : row + 1, lanes]
    for row in range(3):
        low_ids[row] = (numbers[row] & (BLK - 1)).astype(F32)
        high_ids[row] = (numbers[row] >> 7).astype(F32)

    def gather(group, carry):
        rows = pl.ds(pl.multiple_of(group * 8, 8), 8)
        low = [numbers[corner, rows] & (BLK - 1) for corner in range(3)]
        high = [numbers[corner, rows] >> 7 for corner in range(3)]
        for corner in range(3):
            nodes = [jnp.zeros((8, BLK), F32)] * 3
            for block in range(2 * node_blocks):
                source = displacement if block < node_blocks else next_nodes
                start = (block % node_blocks) * BLK
                here = high[corner] == block
                for part in range(3):
                    row = source[part : part + 1, start : start + BLK]
                    picked = jnp.take_along_axis(
                        jnp.broadcast_to(row, (8, BLK)),
                        low[corner],
                        axis=1,
                        mode="promise_in_bounds",
                    )
                    nodes[part] = jnp.where(here, picked, nodes[part])
            for part in range(3):
                corners[corner, part, rows] = nodes[part]
        return carry

    lax.fori_loop(0, runs // 8, gather, 0)

    first, second, third = [[corners[c, p] for p in range(3)] for c in range(3)]
    diag_a = shapes[0]
    skew_b = shapes[1]
    diag_c = shapes[2]
    stiff = stiffness[...]
    edge_one = [second[p] - first[p] for p in range(3)]
    edge_two = [third[p] - first[p] for p in range(3)]
    one = [diag_a * edge_one[p] for p in range(3)]
    two = [skew_b * edge_one[p] + diag_c * edge_two[p] for p in range(3)]
    one[0] = one[0] + 1.0
    two[1] = two[1] + 1.0
    aa = one[0] * one[0] + one[1] * one[1] + one[2] * one[2]
    ab = one[0] * two[0] + one[1] * two[1] + one[2] * two[2]
    bb = two[0] * two[0] + two[1] * two[1] + two[2] * two[2]
    determinant = aa * bb - ab * ab
    scale = 1.0 / determinant
    inverse_aa = bb * scale
    inverse_ab = -ab * scale
    inverse_bb = aa * scale
    pressure = LAME_RATIO * (0.5 * jnp.log(determinant))
    for p in range(3):
        pulled_one = one[p] * inverse_aa + two[p] * inverse_ab
        pulled_two = one[p] * inverse_ab + two[p] * inverse_bb
        stress_one = stiff * (one[p] - pulled_one + pressure * pulled_one)
        stress_two = stiff * (two[p] - pulled_two + pressure * pulled_two)
        force_one = diag_a * stress_one + skew_b * stress_two
        force_two = diag_c * stress_two
        for corner, force in enumerate((-(force_one + force_two), force_one, force_two)):
            rest = force
            for part in range(PIECES):
                piece = rest.astype(jnp.bfloat16).astype(F32)
                rest = rest - piece
                forces[part * 3 + p, corner] = piece


def key_kernel(node_blocks, block_target, block_node, block_count, face, keys):
    del face
    live = block_count[0, 0]
    for k in range(keys.shape[0]):
        key = jnp.where(k < live, block_target[0, 0, k] * node_blocks + block_node[0, 0, k], -1)
        keys[k : k + 1] = jnp.broadcast_to(key, (1, BLK)).astype(F32)


def spread_kernel(base, low_ids, high_ids, forces, out):
    runs = low_ids.shape[1]
    parts, rows, length = out.shape
    pieces = length // BLK
    slots = pieces * rows
    kind = jnp.bfloat16
    tile = 16
    slot_ids = lax.broadcasted_iota(jnp.int32, (slots, BLK), 0).astype(F32) + base
    slot_ids = slot_ids.astype(kind)
    lane_ids = lax.broadcasted_iota(jnp.int32, (BLK, BLK), 0).astype(F32).astype(kind)
    ones = jnp.ones((BLK, BLK), kind)
    none = jnp.zeros((BLK, BLK), kind)
    blank = jnp.zeros((slots, BLK), kind)

    def tall_row(row, count):
        block = jnp.broadcast_to(row, (tile, BLK)).astype(kind)
        return jnp.concatenate([block] * (count // tile), axis=0)

    total = None
    for corner in range(3):
        left = [[] for _ in range(parts * PIECES)]
        right = []
        for j in range(runs):
            row = slice(j, j + 1)
            here = slot_ids == tall_row(high_ids[corner, row], slots)
            right.append(jnp.where(lane_ids == tall_row(low_ids[corner, row], BLK), ones, none))
            for part in range(parts * PIECES):
                left[part].append(
                    jnp.where(here, tall_row(forces[part, corner, row], slots), blank)
                )
        tall = jnp.concatenate([jnp.concatenate(part, axis=1) for part in left], axis=0)
        wide = jnp.concatenate(right, axis=1)
        product = lax.dot_general(
            tall, wide, (((1,), (1,)), ((), ())), preferred_element_type=F32
        )
        total = product if total is None else total + product
    for p in range(parts):
        summed = total[p * slots : (p + 1) * slots]
        for part in range(1, PIECES):
            start = (parts * part + p) * slots
            summed = summed + total[start : start + slots]
        for piece in range(pieces):
            out[p, :, piece * BLK : (piece + 1) * BLK] = summed[piece * rows : (piece + 1) * rows]


def store_kernel(values, out_hbm, sem):
    store = pltpu.make_async_copy(values, out_hbm, sem)
    store.start()
    store.wait()


def final_kernel(count, *refs):
    messages, keys = refs[:count], refs[count : 2 * count]
    residual, motion = refs[2 * count :]
    slots = keys[0].shape[0]
    node_blocks = residual.shape[1] // BLK
    inner = lax.axis_index("inner")
    node_ids = lax.broadcasted_iota(jnp.int32, (node_blocks, BLK), 0)
    own_ids = (node_ids + inner * node_blocks).astype(F32)
    slot_ids = lax.broadcasted_iota(jnp.int32, (8, BLK), 0).astype(F32)
    start = 3 * slots + 3 * CAP
    total = [-messages[0][start + p * node_blocks : start + (p + 1) * node_blocks] for p in range(3)]
    moved = [jnp.zeros((slots, BLK), F32)] * 3
    for message, sender in zip(messages, keys):
        nodes = jnp.full((8, BLK), -1.0, F32)
        for key, named, before in targets_of(sender, inner, node_blocks):
            nodes = jnp.where(named & (slot_ids == before), key, nodes)
        for place in range(CAP):
            here = own_ids == nodes[place : place + 1]
            for part in range(3):
                at = 3 * slots + part * CAP + place
                total[part] = total[part] + jnp.where(here, message[at : at + 1], 0.0)
        for part in range(3):
            moved[part] = moved[part] + message[part * slots : (part + 1) * slots]
    for part in range(3):
        for b in range(node_blocks):
            residual[part : part + 1, b * BLK : (b + 1) * BLK] = total[part][b : b + 1]
        motion[part] = COMPLIANCE * moved[part]


def call(kernel, outs, operands, spaces, scratch=(), out_spaces=None, micros=1.0, aliases=None):
    spec = lambda space: pl.BlockSpec(memory_space=space)
    out_spaces = out_spaces or (pltpu.VMEM,) * len(outs)
    return pl.pallas_call(
        kernel,
        out_shape=outs,
        in_specs=[spec(space) for space in spaces],
        out_specs=tuple(spec(space) for space in out_spaces),
        scratch_shapes=list(scratch),
        input_output_aliases=aliases or {},
        compiler_params=pltpu.CompilerParams(vmem_limit_bytes=VMEM_BYTES),
        cost_estimate=pl.CostEstimate(
            flops=0, bytes_accessed=int(micros * 3.6e6), transcendentals=0
        ),
    )(*operands)


def partner_of(at, step, count):
    if count & (count - 1) == 0:
        return at ^ step
    return (at + step) % count


def reply(step, count):
    return step if count & (count - 1) == 0 else count - step


def exchange(block, axis, step):
    count = lax.axis_size(axis)
    return lax.ppermute(block, axis, [(i, partner_of(i, step, count)) for i in range(count)])


def around(block, axis, step):
    count = lax.axis_size(axis)
    return lax.ppermute(block, axis, [(i, (i + step) % count) for i in range(count)])


def swap(near, far, axis, beside):
    count, others = lax.axis_size(axis), lax.axis_size(beside)
    routes = []
    for start in (0, 1):
        route = []
        for other in range(others):
            for i in range(count):
                j = i + 1 if i % 2 == start else i - 1
                to = other
                if not 0 <= j < count:
                    j = i
                    to = other ^ 1 if others % 2 == 0 else other
                route.append((other * count + i, to * count + j))
        routes.append(route)
    axes = (beside, axis)
    return lax.ppermute(near, axes, routes[0]), lax.ppermute(far, axes, routes[1])


def shards(
    populations,
    relaxation,
    node_flags,
    displacement,
    elements,
    shape_inverse,
    stiffness,
    block_source,
    block_target,
    block_node,
    block_count,
):
    planes, rows, length = populations.shape[1:]
    half = length // BLK
    node_dev = displacement.shape[1]
    node_blocks = node_dev // BLK
    runs = stiffness.shape[0] // BLK
    slots = block_source.shape[2]
    count = lax.axis_size("inner")
    shape = lambda *dims: jax.ShapeDtypeStruct(dims, F32)
    whole = shape(*populations.shape)
    vmem, hbm, smem = pltpu.VMEM, pltpu.HBM, pltpu.SMEM

    next_nodes = around(displacement, "slab", -1)
    face_y = shape(SLOTS, planes, length)
    face_x = shape(SLOTS, rows, length)
    pin = lambda block: pltpu.with_memory_space_constraint(block, hbm)
    c1, fixed, far, near = call(
        first_kernel,
        (whole, shape(2, planes, rows, length), face_x, face_x),
        (pin(populations), pin(relaxation), pin(node_flags)),
        (hbm,) * 3,
        scratch=(
            pltpu.VMEM((planes, Q, rows, length), F32),
            pltpu.VMEM((planes, rows, length), F32),
            pltpu.VMEM((planes, rows, length), jnp.int32),
            pltpu.SemaphoreType.DMA((planes + 2,)),
        ),
        micros=1.5,
    )
    near_x, far_x = swap(near, far, "slab", "group")
    far, near = call(
        side_kernel, (face_y, face_y), (c1, fixed, next_nodes), (vmem,) * 3, micros=0.3
    )
    near_y, far_y = swap(near, far, "inner", "slab")
    numbers = shape(3, runs, BLK)
    low_ids, high_ids, forces = call(
        element_kernel,
        (numbers, numbers, shape(3 * PIECES, 3, runs, BLK)),
        (elements, displacement, next_nodes, shape_inverse, stiffness.reshape(runs, BLK)),
        (vmem,) * 5,
        scratch=(
            pltpu.VMEM((3, runs, BLK), F32),
            pltpu.VMEM((3, runs, BLK), jnp.int32),
            pltpu.VMEM((3, 3, runs, BLK), F32),
        ),
        micros=2.0,
    )
    nodal = shape(3, node_blocks // half, length)
    (other,) = call(
        functools.partial(spread_kernel, node_blocks),
        (nodal,),
        (low_ids, high_ids, forces),
        (vmem,) * 3,
        micros=0.8,
    )
    corner = shape(CORNER_SLOTS, rows, length)
    far, near = call(
        corner_kernel,
        (corner, corner),
        (far_y, near_y, other),
        (vmem,) * 3,
        scratch=(pltpu.VMEM((2, SLOTS, planes, length), F32),),
        micros=0.3,
    )
    near_c, far_c = swap(near, far, "slab", "group")
    (own,) = call(
        functools.partial(spread_kernel, 0),
        (nodal,),
        (low_ids, high_ids, forces),
        (vmem,) * 3,
        micros=0.8,
    )
    wide = planes + 4
    walls_shape = shape(2, SLOTS, wide, length)
    second_shape = shape(Q, planes + 2, rows, length)
    extended, walls, crossing, second, ends = call(
        inside_kernel,
        (
            shape(Q, wide, rows, length),
            walls_shape,
            shape(2, 5, wide, length),
            second_shape,
            shape(2, 2, rows, length),
        ),
        (c1, fixed, far_y, near_y, far_x, near_x),
        (vmem,) * 6,
        scratch=(
            pltpu.VMEM((2, SLOTS, planes, length), F32),
            pltpu.VMEM((2, SLOTS, rows, length), F32),
        ),
        micros=0.8,
    )
    (own_keys,) = call(
        functools.partial(key_kernel, node_blocks),
        (shape(slots, BLK),),
        (block_target, block_node, block_count, near),
        (smem,) * 3 + (vmem,),
        micros=0.1,
    )
    keys = [own_keys] + [exchange(own_keys, "inner", step) for step in range(1, count)]
    towards = [keys[0]] + [keys[reply(step, count)] for step in range(1, count)]
    lines = -(-(3 * slots + 3 * CAP) // 8) * 8
    outs = call(
        functools.partial(second_kernel, count),
        (
            whole,
            shape(lines + 3 * node_blocks, BLK),
            *([shape(lines, BLK)] * (count - 1)),
            walls_shape,
            second_shape,
        ),
        (
            pin(block_source),
            *towards,
            far_c,
            near_c,
            fixed,
            extended,
            crossing,
            ends,
            own,
            walls,
            second,
        ),
        (hbm,) + (vmem,) * (9 + count),
        aliases={8 + count: 1 + count, 9 + count: 2 + count},
        scratch=(
            pltpu.VMEM((2, CORNER_SLOTS, rows, length), F32),
            pltpu.VMEM((2, 5, wide, length), F32),
            pltpu.VMEM((planes * half, 3, rows, BLK), F32),
            pltpu.VMEM((3, node_blocks, BLK), F32),
            pltpu.SMEM(block_source.shape, jnp.int32),
            pltpu.SemaphoreType.DMA(()),
        ),
        micros=1.5,
    )
    values = outs[0]
    messages = [outs[1]]
    messages += [exchange(outs[1 + count - step], "inner", step) for step in range(1, count)]
    (populations_out,) = call(
        store_kernel,
        (whole,),
        (values,),
        (vmem,),
        out_spaces=(hbm,),
        scratch=(pltpu.SemaphoreType.DMA(()),),
        micros=1.0,
    )
    residual, motion = call(
        functools.partial(final_kernel, count),
        (shape(3, node_dev), shape(3, slots, BLK)),
        (*messages, *keys),
        (vmem,) * (2 * count),
        micros=0.8,
    )
    return populations_out, residual, motion.transpose(1, 0, 2)[None, None]


def solution(mesh):
    return jax.shard_map(
        shards,
        mesh=mesh,
        in_specs=(
            P(None, ("group", "slab"), "inner", None),
            P(("group", "slab"), "inner", None),
            P(("group", "slab"), "inner", None),
            P(None, ("group", "slab", "inner")),
            P(None, ("group", "slab", "inner")),
            P(None, ("group", "slab", "inner")),
            P(("group", "slab", "inner")),
            P(("group", "slab"), "inner", None),
            P(("group", "slab"), "inner", None),
            P(("group", "slab"), "inner", None),
            P(("group", "slab"), "inner"),
        ),
        out_specs=(
            P(None, ("group", "slab"), "inner", None),
            P(None, ("group", "slab", "inner")),
            P(("group", "slab"), "inner", None, None, None),
        ),
        check_vma=False,
    )
```

```python
import functools

import jax
import jax.numpy as jnp
from jax import lax
from jax.experimental import pallas as pl
from jax.experimental.pallas import tpu as pltpu
from jax.sharding import PartitionSpec as P

BLK = 128
VELOCITIES = (
    (0, 0, 0),
    (1, 0, 0),
    (-1, 0, 0),
    (0, 1, 0),
    (0, -1, 0),
    (0, 0, 1),
    (0, 0, -1),
    (1, 1, 0),
    (-1, -1, 0),
    (1, -1, 0),
    (-1, 1, 0),
    (1, 0, 1),
    (-1, 0, -1),
    (1, 0, -1),
    (-1, 0, 1),
    (0, 1, 1),
    (0, -1, -1),
    (0, 1, -1),
    (0, -1, 1),
)
WEIGHTS = (1.0 / 3.0,) + (1.0 / 18.0,) * 6 + (1.0 / 36.0,) * 12
OPPOSITE = (0, 2, 1, 4, 3, 6, 5, 8, 7, 10, 9, 12, 11, 14, 13, 16, 15, 18, 17)
INLET_SPEED = 0.04
LOAD_SCALE = 25.0
COMPLIANCE = 0.5
LAME_RATIO = 2.0
Q = 19
FLAG_SLOT = 19
RATE_SLOT = 20
SLOTS = 21
FORCE_SLOT = 6
CORNER_SLOTS = FORCE_SLOT + 3
PIECES = 2
F32 = jnp.float32
VMEM_BYTES = 48 * 1024 * 1024


def moments(values):
    sums = [values[q] + values[q + 1] for q in range(1, Q, 2)]
    diffs = [values[q] - values[q + 1] for q in range(1, Q, 2)]
    density = values[0]
    for term in sums:
        density = density + term
    flows = []
    for axis in range(3):
        total = None
        for k, q in enumerate(range(1, Q, 2)):
            factor = VELOCITIES[q][axis]
            if factor == 0:
                continue
            if total is None:
                total = diffs[k] if factor > 0 else -diffs[k]
            else:
                total = total + diffs[k] if factor > 0 else total - diffs[k]
        flows.append(total)
    return density, flows[0], flows[1], flows[2]


def collide(values, rate, kind):
    density, flow_x, flow_y, flow_z = moments(values)
    inverse = 1.0 / density
    wall = kind == 1
    inlet = kind == 2
    fluid = kind == 0
    vel = (
        jnp.where(inlet, INLET_SPEED, flow_x * inverse),
        jnp.where(inlet, 0.0, flow_y * inverse),
        jnp.where(inlet, 0.0, flow_z * inverse),
    )
    scale = jnp.where(fluid, density, 1.0)
    rate = jnp.where(fluid, rate, 1.0)
    base = 1.0 - 1.5 * (vel[0] * vel[0] + vel[1] * vel[1] + vel[2] * vel[2])
    weighted = {w: w * scale for w in set(WEIGHTS)}
    out = [None] * Q
    relaxed = values[0] + rate * (weighted[WEIGHTS[0]] * base - values[0])
    out[0] = jnp.where(wall, values[0], relaxed)
    for q in range(1, Q, 2):
        project = None
        for factor, component in zip(VELOCITIES[q], vel):
            if factor == 0:
                continue
            if project is None:
                project = component
            else:
                project = project + component if factor > 0 else project - component
        even = base + 4.5 * (project * project)
        odd = 3.0 * project
        w = weighted[WEIGHTS[q]]
        forward = values[q] + rate * (w * (even + odd) - values[q])
        backward = values[q + 1] + rate * (w * (even - odd) - values[q + 1])
        out[q] = jnp.where(wall, values[q + 1], forward)
        out[q + 1] = jnp.where(wall, values[q], backward)
    return out


def roll_by(block, step, axis):
    if step == 0:
        return block
    return pltpu.roll(block, step % block.shape[axis], axis)


def face_slots(axis, sign):
    picks = []
    for q in range(Q):
        if VELOCITIES[q][axis] * sign >= 0:
            picks.append((q, 0))
        else:
            picks.append((OPPOSITE[q], 1))
    return picks


def mirror(q, axis):
    flipped = tuple(-c if k == axis else c for k, c in enumerate(VELOCITIES[q]))
    return VELOCITIES.index(flipped)


def corner_rows(sign_x, sign_y):
    rows = []
    for q, depth in face_slots(0, sign_x):
        if VELOCITIES[q][1] * sign_y >= 0:
            rows.append((q, depth))
        else:
            rows.append((OPPOSITE[mirror(q, 1)], depth))
    return rows


def first_kernel(
    pops_hbm, rate_hbm, flags_hbm, c1, fixed, far, near, pops, rate, flags, sems
):
    planes = c1.shape[1]
    copies = [
        pltpu.make_async_copy(rate_hbm, rate, sems.at[planes]),
        pltpu.make_async_copy(flags_hbm, flags, sems.at[planes + 1]),
    ]
    loads = [
        pltpu.make_async_copy(pops_hbm.at[:, x], pops.at[x], sems.at[x]) for x in range(planes)
    ]
    for copy in loads[:1] + copies + loads[1:]:
        copy.start()
    for copy in copies:
        copy.wait()

    def plane(x, carry):
        pltpu.make_async_copy(pops_hbm.at[:, x], pops.at[x], sems.at[x]).wait()
        kind = flags[x]
        values = [pops[x, q] for q in range(Q)]
        result = collide(values, rate[x], kind)
        for q in range(Q):
            c1[q, x] = roll_by(result[q], VELOCITIES[q][2], 1)
        fixed[0, x] = kind.astype(F32)
        fixed[1, x] = rate[x]
        return carry

    lax.fori_loop(0, planes, plane, 0)

    def pack(out, sign, outside):
        for slot, (q, depth) in enumerate(face_slots(0, sign)):
            out[slot] = c1[q, planes - 1 - depth if sign > 0 else depth]
        end = planes - 1 if sign > 0 else 0
        out[FLAG_SLOT] = fixed[0, end]
        out[RATE_SLOT] = fixed[1, end]
        clear_outside(out, outside)

    pack_pair(pack, "slab", near, far)


def clear_outside(out, outside):
    @pl.when(outside)
    def _():
        out[...] = jnp.zeros(out.shape, F32)


def pack_pair(pack, axis, near, far):
    at = lax.axis_index(axis)
    even = lax.rem(at, 2) == 0
    first, last = at == 0, at == lax.axis_size(axis) - 1

    @pl.when(even)
    def _():
        pack(near, 1, last)
        pack(far, -1, first)

    @pl.when(jnp.logical_not(even))
    def _():
        pack(near, -1, first)
        pack(far, 1, last)


def side_kernel(c1, fixed, next_nodes, far, near):
    del next_nodes
    planes, rows = c1.shape[1], c1.shape[2]

    def pack(out, sign, outside):
        def line(x, carry):
            for slot, (q, depth) in enumerate(face_slots(1, sign)):
                y = rows - 1 - depth if sign > 0 else depth
                out[slot, pl.ds(x, 1)] = c1[q, x, y : y + 1]
            y = rows - 1 if sign > 0 else 0
            for k, slot in enumerate((FLAG_SLOT, RATE_SLOT)):
                out[slot, pl.ds(x, 1)] = fixed[k, x, y : y + 1]
            return carry

        lax.fori_loop(0, planes, line, 0)
        clear_outside(out, outside)

    pack_pair(pack, "inner", near, far)


def gather_both(near, far, both, axis):
    odd = lax.rem(lax.axis_index(axis), 2)
    for slot in range(both.shape[1]):
        both[1 - odd, slot] = near[slot]
        both[odd, slot] = far[slot]


def corner_kernel(far_y, near_y, other, far, near, both):
    planes = near_y.shape[1]
    gather_both(near_y, far_y, both, "inner")

    def pack(out, sign, outside):
        for side, sign_y in enumerate((1, -1)):
            picks = corner_rows(sign, sign_y) + [(FLAG_SLOT, 0), (RATE_SLOT, 0)]
            for row, (slot, depth) in enumerate(picks):
                x = planes - 1 - depth if sign > 0 else depth
                at = 3 * side + row // 8
                out[at, row % 8 : row % 8 + 1] = both[side, slot, x : x + 1]
        for part in range(3):
            out[FORCE_SLOT + part] = other[part]
        clear_outside(out, outside)

    pack_pair(pack, "slab", near, far)


def with_edge(block, step_y, edge):
    rows = block.shape[0]
    sub = lax.broadcasted_iota(jnp.int32, block.shape, 0)
    if step_y > 0:
        return jnp.where(sub == 0, edge, roll_by(block, 1, 0))
    return jnp.where(sub == rows - 1, edge, roll_by(block, -1, 0))


def store_plane(extended, walls, second, at, rate, kind):
    values = []
    for q in range(Q):
        step_x, step_y, _ = VELOCITIES[q]
        block = extended[q, at + 1 - step_x]
        if step_y != 0:
            edge = walls[0 if step_y > 0 else 1, q, pl.ds(at + 1 - step_x, 1)]
            block = with_edge(block, step_y, edge)
        values.append(block)
    result = collide(values, rate, kind)
    for q in range(Q):
        second[q, at] = roll_by(result[q], VELOCITIES[q][2], 1)


def inside_kernel(
    c1,
    fixed,
    far_y,
    near_y,
    far_x,
    near_x,
    extended,
    walls,
    crossing,
    second,
    ends,
    both_y,
    both_x,
):
    planes, rows, _ = c1.shape[1:]
    wide = planes + 4
    gather_both(near_y, far_y, both_y, "inner")
    gather_both(near_x, far_x, both_x, "slab")
    for q in range(Q):
        for x in range(planes):
            extended[q, x + 2] = c1[q, x]
        extended[q, 1] = both_x[0, q]
        extended[q, planes + 2] = both_x[1, q]
        if VELOCITIES[q][0] > 0:
            extended[q, 0] = both_x[0, OPPOSITE[q]]
        if VELOCITIES[q][0] < 0:
            extended[q, planes + 3] = both_x[1, OPPOSITE[q]]
    for end in range(2):
        ends[end, 0] = both_x[end, FLAG_SLOT]
        ends[end, 1] = both_x[end, RATE_SLOT]

    for side, sign in enumerate((1, -1)):
        y = 0 if sign > 0 else rows - 1
        for slot in range(SLOTS):
            walls[side, slot, 2 : planes + 2] = both_y[side, slot]
        place = 0
        for q in range(Q):
            if VELOCITIES[q][1] != -sign:
                continue
            for x in range(wide):
                crossing[side, place, x : x + 1] = extended[q, x, y : y + 1]
            place += 1

    def inside_plane(x, carry):
        store_plane(extended, walls, second, x + 1, fixed[1, x], fixed[0, x])
        return carry

    lax.fori_loop(1, planes - 1, inside_plane, 0)


def second_kernel(
    block_source_hbm,
    block_target_hbm,
    block_node_hbm,
    block_count,
    far,
    near,
    fixed,
    extended,
    crossing,
    ends,
    internal_own,
    walls_in,
    second_in,
    out,
    message_all,
    walls,
    second,
    both,
    edges,
    loads,
    block_source,
    block_target,
    block_node,
    sems,
):
    del walls_in, second_in
    message = message_all.at[0]
    copies = [
        pltpu.make_async_copy(block_source_hbm, block_source, sems.at[0]),
        pltpu.make_async_copy(block_target_hbm, block_target, sems.at[1]),
        pltpu.make_async_copy(block_node_hbm, block_node, sems.at[2]),
    ]
    for copy in copies:
        copy.start()
    planes, rows, length = out.shape[1:]
    half = length // BLK
    slots = block_source.shape[2]
    wide = planes + 4
    slab = lax.axis_index("slab")
    inner = lax.axis_index("inner")
    slab_end = lax.axis_size("slab") - 1
    inner_end = lax.axis_size("inner") - 1
    gather_both(near, far, both, "slab")

    for side, sign in enumerate((1, -1)):
        for end, sign_x in enumerate((1, -1)):
            for row, (slot, depth) in enumerate(corner_rows(sign_x, sign)):
                at = (1 - depth) if sign_x > 0 else planes + 2 + depth
                source = 3 * side + row // 8
                walls[side, slot, at : at + 1] = both[end, source, row % 8 : row % 8 + 1]
            at = 1 if sign_x > 0 else planes + 2
            for row in (FLAG_SLOT, RATE_SLOT):
                source = 3 * side + row // 8
                walls[side, row, at : at + 1] = both[end, source, row % 8 : row % 8 + 1]

    def edge_plane(end, carry):
        x = end * (planes - 1)
        store_plane(extended, walls, second, x + 1, fixed[1, x], fixed[0, x])
        return carry

    def outside_plane(end, carry):
        store_plane(extended, walls, second, end * (planes + 1), ends[end, 1], ends[end, 0])
        return carry

    lax.fori_loop(0, 2, edge_plane, 0)
    lax.fori_loop(0, 2, outside_plane, 0)

    @pl.when(slab == 0)
    def _():
        for q in range(Q):
            if VELOCITIES[q][0] > 0:
                second[q, 0] = jnp.zeros((rows, length), F32)

    @pl.when(slab == slab_end)
    def _():
        for q in range(Q):
            if VELOCITIES[q][0] < 0:
                second[q, planes + 1] = jnp.zeros((rows, length), F32)

    across = lax.broadcasted_iota(jnp.int32, (wide, length), 0)
    hidden = ((across <= 1) & (slab == 0)) | ((across >= planes + 2) & (slab == slab_end))
    for side, sign, outside in ((0, 1, inner == 0), (1, -1, inner == inner_end)):
        values = []
        place = 0
        for q in range(Q):
            step_x, step_y, _ = VELOCITIES[q]
            if step_y == 0:
                block = walls[side, q]
            elif step_y == sign:
                block = walls[side, OPPOSITE[q]]
            else:
                block = crossing[side, place]
                place += 1
            values.append(roll_by(block, step_x, 0))
        result = collide(values, walls[side, RATE_SLOT], walls[side, FLAG_SLOT])
        place = 0
        for q in range(Q):
            if VELOCITIES[q][1] == sign:
                kept = jnp.where(hidden | outside, 0.0, result[q])
                edges[side, place] = roll_by(kept, VELOCITIES[q][2], 1)
                place += 1

    def plane_two(x, carry):
        values = []
        places = {1: 0, -1: 0}
        for q in range(Q):
            step_x, step_y, _ = VELOCITIES[q]
            block = second[q, x + 1 - step_x]
            if step_y != 0:
                edge = edges[0 if step_y > 0 else 1, places[step_y], pl.ds(x + 2 - step_x, 1)]
                places[step_y] += 1
                block = with_edge(block, step_y, edge)
            values.append(block)
            out[q, x] = block
        density, flow_x, flow_y, flow_z = moments(values)
        parts = (
            LOAD_SCALE * flow_x,
            LOAD_SCALE * (flow_y + (density - 1.0) / 3.0),
            LOAD_SCALE * flow_z,
        )
        for part in range(3):
            for piece in range(half):
                loads[x * half + piece, part] = parts[part][:, piece * BLK : (piece + 1) * BLK]
        return carry

    lax.fori_loop(0, planes, plane_two, 0)

    for copy in copies:
        copy.wait()
    node_blocks = internal_own.shape[1] * half
    live = jnp.broadcast_to(block_count[...], (1, BLK))
    for k in range(slots):
        run = block_source[0, 0, k]
        x = run // (rows * half)
        left = run - x * (rows * half)
        y = left // half
        piece = left - y * half
        for part in range(3):
            message[4 * k + part : 4 * k + part + 1] = loads[x * half + piece, part, pl.ds(y, 1)]
        key = block_target[0, 0, k] * node_blocks + block_node[0, 0, k]
        message[4 * k + 3 : 4 * k + 4] = jnp.where(live > k, key, -1).astype(F32)
    for part in range(3):
        start = 4 * slots + part * node_blocks
        for piece in range(half):
            at = piece * rows
            lanes = slice(piece * BLK, (piece + 1) * BLK)
            message[start + at : start + at + rows] = (
                internal_own[part, :, lanes] + both[0, FORCE_SLOT + part, :, lanes]
            )
    for other in range(1, message_all.shape[0]):
        message_all[other] = message[...]


def element_kernel(
    elements, displacement, next_nodes, shape_inverse, stiffness, low_ids, high_ids, forces, shapes,
    numbers, corners,
):
    node_dev = displacement.shape[1]
    node_blocks = node_dev // BLK
    runs = elements.shape[1] // BLK
    for j in range(runs):
        lanes = slice(j * BLK, (j + 1) * BLK)
        for row in range(3):
            numbers[row, j : j + 1] = elements[row : row + 1, lanes]
            shapes[row, j : j + 1] = shape_inverse[row : row + 1, lanes]
    for row in range(3):
        low_ids[row] = (numbers[row] & (BLK - 1)).astype(F32)
        high_ids[row] = (numbers[row] >> 7).astype(F32)

    def gather(group, carry):
        rows = pl.ds(pl.multiple_of(group * 8, 8), 8)
        low = [numbers[corner, rows] & (BLK - 1) for corner in range(3)]
        high = [numbers[corner, rows] >> 7 for corner in range(3)]
        for corner in range(3):
            nodes = [jnp.zeros((8, BLK), F32)] * 3
            for block in range(2 * node_blocks):
                source = displacement if block < node_blocks else next_nodes
                start = (block % node_blocks) * BLK
                here = high[corner] == block
                for part in range(3):
                    row = source[part : part + 1, start : start + BLK]
                    picked = jnp.take_along_axis(
                        jnp.broadcast_to(row, (8, BLK)),
                        low[corner],
                        axis=1,
                        mode="promise_in_bounds",
                    )
                    nodes[part] = jnp.where(here, picked, nodes[part])
            for part in range(3):
                corners[corner, part, rows] = nodes[part]
        return carry

    lax.fori_loop(0, runs // 8, gather, 0)

    first, second, third = [[corners[c, p] for p in range(3)] for c in range(3)]
    diag_a = shapes[0]
    skew_b = shapes[1]
    diag_c = shapes[2]
    stiff = stiffness[...]
    edge_one = [second[p] - first[p] for p in range(3)]
    edge_two = [third[p] - first[p] for p in range(3)]
    one = [diag_a * edge_one[p] for p in range(3)]
    two = [skew_b * edge_one[p] + diag_c * edge_two[p] for p in range(3)]
    one[0] = one[0] + 1.0
    two[1] = two[1] + 1.0
    aa = one[0] * one[0] + one[1] * one[1] + one[2] * one[2]
    ab = one[0] * two[0] + one[1] * two[1] + one[2] * two[2]
    bb = two[0] * two[0] + two[1] * two[1] + two[2] * two[2]
    determinant = aa * bb - ab * ab
    scale = 1.0 / determinant
    inverse_aa = bb * scale
    inverse_ab = -ab * scale
    inverse_bb = aa * scale
    pressure = LAME_RATIO * (0.5 * jnp.log(determinant))
    for p in range(3):
        pulled_one = one[p] * inverse_aa + two[p] * inverse_ab
        pulled_two = one[p] * inverse_ab + two[p] * inverse_bb
        stress_one = stiff * (one[p] - pulled_one + pressure * pulled_one)
        stress_two = stiff * (two[p] - pulled_two + pressure * pulled_two)
        force_one = diag_a * stress_one + skew_b * stress_two
        force_two = diag_c * stress_two
        for corner, force in enumerate((-(force_one + force_two), force_one, force_two)):
            rest = force
            for part in range(PIECES):
                piece = rest.astype(jnp.bfloat16).astype(F32)
                rest = rest - piece
                forces[part * 3 + p, corner] = piece


def spread_kernel(base, low_ids, high_ids, forces, out):
    runs = low_ids.shape[1]
    parts, rows, length = out.shape
    pieces = length // BLK
    slots = pieces * rows
    kind = jnp.bfloat16
    tile = 16
    slot_ids = lax.broadcasted_iota(jnp.int32, (slots, BLK), 0).astype(F32) + base
    slot_ids = slot_ids.astype(kind)
    lane_ids = lax.broadcasted_iota(jnp.int32, (BLK, BLK), 0).astype(F32).astype(kind)
    ones = jnp.ones((BLK, BLK), kind)
    none = jnp.zeros((BLK, BLK), kind)
    blank = jnp.zeros((slots, BLK), kind)

    def tall_row(row, count):
        block = jnp.broadcast_to(row, (tile, BLK)).astype(kind)
        return jnp.concatenate([block] * (count // tile), axis=0)

    total = None
    for corner in range(3):
        left = [[] for _ in range(parts * PIECES)]
        right = []
        for j in range(runs):
            row = slice(j, j + 1)
            here = slot_ids == tall_row(high_ids[corner, row], slots)
            right.append(jnp.where(lane_ids == tall_row(low_ids[corner, row], BLK), ones, none))
            for part in range(parts * PIECES):
                left[part].append(
                    jnp.where(here, tall_row(forces[part, corner, row], slots), blank)
                )
        tall = jnp.concatenate([jnp.concatenate(part, axis=1) for part in left], axis=0)
        wide = jnp.concatenate(right, axis=1)
        product = lax.dot_general(
            tall, wide, (((1,), (1,)), ((), ())), preferred_element_type=F32
        )
        total = product if total is None else total + product
    for p in range(parts):
        summed = total[p * slots : (p + 1) * slots]
        for part in range(1, PIECES):
            start = (parts * part + p) * slots
            summed = summed + total[start : start + slots]
        for piece in range(pieces):
            out[p, :, piece * BLK : (piece + 1) * BLK] = summed[piece * rows : (piece + 1) * rows]


def store_kernel(values, out_hbm, sem):
    store = pltpu.make_async_copy(values, out_hbm, sem)
    store.start()
    store.wait()


def final_kernel(arrived, residual, motion, keys):
    slots = keys.shape[0]
    node_blocks = residual.shape[1] // BLK
    inner = lax.axis_index("inner")
    messages = [arrived.at[i] for i in range(arrived.shape[0])]
    mine = arrived.at[inner]
    for k in range(slots):
        keys[k : k + 1] = mine[4 * k + 3 : 4 * k + 4]
    wanted = keys[...]
    node_ids = lax.broadcasted_iota(jnp.int32, (node_blocks, BLK), 0)
    own_ids = (node_ids + inner * node_blocks).astype(F32)
    external = [jnp.zeros((node_blocks, BLK), F32)] * 3
    moved = [jnp.zeros((slots, BLK), F32)] * 3
    for message in messages:
        for k in range(slots):
            key = message[4 * k + 3 : 4 * k + 4]
            here = own_ids == key
            same = wanted == key
            for part in range(3):
                row = message[4 * k + part : 4 * k + part + 1]
                external[part] = external[part] + jnp.where(here, row, 0.0)
                moved[part] = moved[part] + jnp.where(same, row, 0.0)
    for sender, message in enumerate(messages):
        for b in range(node_blocks):
            same = wanted == float(sender * node_blocks + b)
            for part in range(3):
                at = 4 * slots + part * node_blocks + b
                moved[part] = moved[part] - jnp.where(same, message[at : at + 1], 0.0)
    live = wanted >= 0.0
    for part in range(3):
        start = 4 * slots + part * node_blocks
        left = external[part] - mine[start : start + node_blocks]
        for b in range(node_blocks):
            residual[part : part + 1, b * BLK : (b + 1) * BLK] = left[b : b + 1]
        motion[part] = jnp.where(live, COMPLIANCE * moved[part], 0.0)


def call(kernel, outs, operands, spaces, scratch=(), out_spaces=None, micros=1.0, aliases=None):
    spec = lambda space: pl.BlockSpec(memory_space=space)
    out_spaces = out_spaces or (pltpu.VMEM,) * len(outs)
    return pl.pallas_call(
        kernel,
        out_shape=outs,
        in_specs=[spec(space) for space in spaces],
        out_specs=tuple(spec(space) for space in out_spaces),
        scratch_shapes=list(scratch),
        input_output_aliases=aliases or {},
        compiler_params=pltpu.CompilerParams(vmem_limit_bytes=VMEM_BYTES),
        cost_estimate=pl.CostEstimate(
            flops=0, bytes_accessed=int(micros * 3.6e6), transcendentals=0
        ),
    )(*operands)


def around(block, axis, step):
    count = lax.axis_size(axis)
    return lax.ppermute(block, axis, [(i, (i + step) % count) for i in range(count)])


def swap(near, far, axis, beside):
    count, others = lax.axis_size(axis), lax.axis_size(beside)
    routes = []
    for start in (0, 1):
        route = []
        for other in range(others):
            for i in range(count):
                j = i + 1 if i % 2 == start else i - 1
                to = other
                if not 0 <= j < count:
                    j = i
                    to = other ^ 1 if others % 2 == 0 else other
                route.append((other * count + i, to * count + j))
        routes.append(route)
    axes = (beside, axis)
    return lax.ppermute(near, axes, routes[0]), lax.ppermute(far, axes, routes[1])


def shards(
    populations,
    relaxation,
    node_flags,
    displacement,
    elements,
    shape_inverse,
    stiffness,
    block_source,
    block_target,
    block_node,
    block_count,
):
    planes, rows, length = populations.shape[1:]
    half = length // BLK
    node_dev = displacement.shape[1]
    node_blocks = node_dev // BLK
    runs = stiffness.shape[0] // BLK
    slots = block_source.shape[2]
    count = lax.axis_size("inner")
    shape = lambda *dims: jax.ShapeDtypeStruct(dims, F32)
    whole = shape(*populations.shape)
    vmem, hbm, smem = pltpu.VMEM, pltpu.HBM, pltpu.SMEM

    next_nodes = around(displacement, "slab", -1)
    face_y = shape(SLOTS, planes, length)
    face_x = shape(SLOTS, rows, length)
    pin = lambda block: pltpu.with_memory_space_constraint(block, hbm)
    c1, fixed, far, near = call(
        first_kernel,
        (whole, shape(2, planes, rows, length), face_x, face_x),
        (pin(populations), pin(relaxation), pin(node_flags)),
        (hbm,) * 3,
        scratch=(
            pltpu.VMEM((planes, Q, rows, length), F32),
            pltpu.VMEM((planes, rows, length), F32),
            pltpu.VMEM((planes, rows, length), jnp.int32),
            pltpu.SemaphoreType.DMA((planes + 2,)),
        ),
        micros=1.5,
    )
    near_x, far_x = swap(near, far, "slab", "group")
    far, near = call(
        side_kernel, (face_y, face_y), (c1, fixed, next_nodes), (vmem,) * 3, micros=0.3
    )
    near_y, far_y = swap(near, far, "inner", "slab")
    numbers = shape(3, runs, BLK)
    low_ids, high_ids, forces = call(
        element_kernel,
        (numbers, numbers, shape(3 * PIECES, 3, runs, BLK)),
        (elements, displacement, next_nodes, shape_inverse, stiffness.reshape(runs, BLK)),
        (vmem,) * 5,
        scratch=(
            pltpu.VMEM((3, runs, BLK), F32),
            pltpu.VMEM((3, runs, BLK), jnp.int32),
            pltpu.VMEM((3, 3, runs, BLK), F32),
        ),
        micros=2.0,
    )
    nodal = shape(3, node_blocks // half, length)
    (other,) = call(
        functools.partial(spread_kernel, node_blocks),
        (nodal,),
        (low_ids, high_ids, forces),
        (vmem,) * 3,
        micros=0.8,
    )
    corner = shape(CORNER_SLOTS, rows, length)
    far, near = call(
        corner_kernel,
        (corner, corner),
        (far_y, near_y, other),
        (vmem,) * 3,
        scratch=(pltpu.VMEM((2, SLOTS, planes, length), F32),),
        micros=0.3,
    )
    near_c, far_c = swap(near, far, "slab", "group")
    (own,) = call(
        functools.partial(spread_kernel, 0),
        (nodal,),
        (low_ids, high_ids, forces),
        (vmem,) * 3,
        micros=0.8,
    )
    wide = planes + 4
    walls_shape = shape(2, SLOTS, wide, length)
    second_shape = shape(Q, planes + 2, rows, length)
    extended, walls, crossing, second, ends = call(
        inside_kernel,
        (
            shape(Q, wide, rows, length),
            walls_shape,
            shape(2, 5, wide, length),
            second_shape,
            shape(2, 2, rows, length),
        ),
        (c1, fixed, far_y, near_y, far_x, near_x),
        (vmem,) * 6,
        scratch=(
            pltpu.VMEM((2, SLOTS, planes, length), F32),
            pltpu.VMEM((2, SLOTS, rows, length), F32),
        ),
        micros=0.8,
    )
    lines = 4 * slots + 3 * node_blocks
    values, message, _, _ = call(
        second_kernel,
        (whole, shape(count, lines, BLK), walls_shape, second_shape),
        (
            pin(block_source),
            pin(block_target),
            pin(block_node),
            block_count,
            far_c,
            near_c,
            fixed,
            extended,
            crossing,
            ends,
            own,
            walls,
            second,
        ),
        (hbm,) * 3 + (vmem,) * 10,
        aliases={11: 2, 12: 3},
        scratch=(
            pltpu.VMEM((2, CORNER_SLOTS, rows, length), F32),
            pltpu.VMEM((2, 5, wide, length), F32),
            pltpu.VMEM((planes * half, 3, rows, BLK), F32),
            pltpu.SMEM(block_source.shape, jnp.int32),
            pltpu.SMEM(block_target.shape, jnp.int32),
            pltpu.SMEM(block_node.shape, jnp.int32),
            pltpu.SemaphoreType.DMA((3,)),
        ),
        micros=1.5,
    )
    messages = lax.all_to_all(message, "inner", split_axis=0, concat_axis=0, tiled=False)
    (populations_out,) = call(
        store_kernel,
        (whole,),
        (values,),
        (vmem,),
        out_spaces=(hbm,),
        scratch=(pltpu.SemaphoreType.DMA(()),),
        micros=1.0,
    )
    residual, motion = call(
        final_kernel,
        (shape(3, node_dev), shape(3, slots, BLK)),
        (messages,),
        (vmem,),
        scratch=(pltpu.VMEM((slots, BLK), F32),),
        micros=0.8,
    )
    return populations_out, residual, motion.transpose(1, 0, 2)[None, None]


def solution(mesh):
    return jax.shard_map(
        shards,
        mesh=mesh,
        in_specs=(
            P(None, ("group", "slab"), "inner", None),
            P(("group", "slab"), "inner", None),
            P(("group", "slab"), "inner", None),
            P(None, ("group", "slab", "inner")),
            P(None, ("group", "slab", "inner")),
            P(None, ("group", "slab", "inner")),
            P(("group", "slab", "inner")),
            P(("group", "slab"), "inner", None),
            P(("group", "slab"), "inner", None),
            P(("group", "slab"), "inner", None),
            P(("group", "slab"), "inner"),
        ),
        out_specs=(
            P(None, ("group", "slab"), "inner", None),
            P(None, ("group", "slab", "inner")),
            P(("group", "slab"), "inner", None, None, None),
        ),
        check_vma=False,
    )
```

```python
import functools

import jax
import jax.numpy as jnp
from jax import lax
from jax.experimental import pallas as pl
from jax.experimental.pallas import tpu as pltpu
from jax.sharding import PartitionSpec as P

BLK = 128
VELOCITIES = (
    (0, 0, 0),
    (1, 0, 0),
    (-1, 0, 0),
    (0, 1, 0),
    (0, -1, 0),
    (0, 0, 1),
    (0, 0, -1),
    (1, 1, 0),
    (-1, -1, 0),
    (1, -1, 0),
    (-1, 1, 0),
    (1, 0, 1),
    (-1, 0, -1),
    (1, 0, -1),
    (-1, 0, 1),
    (0, 1, 1),
    (0, -1, -1),
    (0, 1, -1),
    (0, -1, 1),
)
WEIGHTS = (1.0 / 3.0,) + (1.0 / 18.0,) * 6 + (1.0 / 36.0,) * 12
OPPOSITE = (0, 2, 1, 4, 3, 6, 5, 8, 7, 10, 9, 12, 11, 14, 13, 16, 15, 18, 17)
INLET_SPEED = 0.04
LOAD_SCALE = 25.0
COMPLIANCE = 0.5
LAME_RATIO = 2.0
Q = 19
FLAG_SLOT = 19
RATE_SLOT = 20
SLOTS = 21
SIDE_SLOTS = 24
FORCE_SLOT = 6
CORNER_SLOTS = FORCE_SLOT + 3
PIECES = 2
F32 = jnp.float32
VMEM_BYTES = 48 * 1024 * 1024


def moments(values):
    sums = [values[q] + values[q + 1] for q in range(1, Q, 2)]
    diffs = [values[q] - values[q + 1] for q in range(1, Q, 2)]
    density = values[0]
    for term in sums:
        density = density + term
    flows = []
    for axis in range(3):
        total = None
        for k, q in enumerate(range(1, Q, 2)):
            factor = VELOCITIES[q][axis]
            if factor == 0:
                continue
            if total is None:
                total = diffs[k] if factor > 0 else -diffs[k]
            else:
                total = total + diffs[k] if factor > 0 else total - diffs[k]
        flows.append(total)
    return density, flows[0], flows[1], flows[2]


def collide(values, rate, kind):
    density, flow_x, flow_y, flow_z = moments(values)
    inverse = 1.0 / density
    wall = kind == 1
    inlet = kind == 2
    fluid = kind == 0
    vel = (
        jnp.where(inlet, INLET_SPEED, flow_x * inverse),
        jnp.where(inlet, 0.0, flow_y * inverse),
        jnp.where(inlet, 0.0, flow_z * inverse),
    )
    scale = jnp.where(fluid, density, 1.0)
    rate = jnp.where(fluid, rate, 1.0)
    base = 1.0 - 1.5 * (vel[0] * vel[0] + vel[1] * vel[1] + vel[2] * vel[2])
    weighted = {w: w * scale for w in set(WEIGHTS)}
    out = [None] * Q
    relaxed = values[0] + rate * (weighted[WEIGHTS[0]] * base - values[0])
    out[0] = jnp.where(wall, values[0], relaxed)
    for q in range(1, Q, 2):
        project = None
        for factor, component in zip(VELOCITIES[q], vel):
            if factor == 0:
                continue
            if project is None:
                project = component
            else:
                project = project + component if factor > 0 else project - component
        even = base + 4.5 * (project * project)
        odd = 3.0 * project
        w = weighted[WEIGHTS[q]]
        forward = values[q] + rate * (w * (even + odd) - values[q])
        backward = values[q + 1] + rate * (w * (even - odd) - values[q + 1])
        out[q] = jnp.where(wall, values[q + 1], forward)
        out[q + 1] = jnp.where(wall, values[q], backward)
    return out


def roll_by(block, step, axis):
    if step == 0:
        return block
    return pltpu.roll(block, step % block.shape[axis], axis)


def face_slots(axis, sign):
    picks = []
    for q in range(Q):
        if VELOCITIES[q][axis] * sign >= 0:
            picks.append((q, 0))
        else:
            picks.append((OPPOSITE[q], 1))
    return picks


def mirror(q, axis):
    flipped = tuple(-c if k == axis else c for k, c in enumerate(VELOCITIES[q]))
    return VELOCITIES.index(flipped)


def corner_rows(sign_x, sign_y):
    rows = []
    for q, depth in face_slots(0, sign_x):
        if VELOCITIES[q][1] * sign_y >= 0:
            rows.append((q, depth))
        else:
            rows.append((OPPOSITE[mirror(q, 1)], depth))
    return rows


def first_kernel(
    pops_hbm, rate_hbm, flags_hbm, c1, fixed, far, near, pops, rate, flags, sems
):
    planes, rows = c1.shape[1], c1.shape[2]
    copies = [
        pltpu.make_async_copy(rate_hbm, rate, sems.at[planes]),
        pltpu.make_async_copy(flags_hbm, flags, sems.at[planes + 1]),
    ]
    loads = [
        pltpu.make_async_copy(pops_hbm.at[:, x], pops.at[x], sems.at[x]) for x in range(planes)
    ]
    for copy in loads[:1] + copies + loads[1:]:
        copy.start()
    for copy in copies:
        copy.wait()

    def plane(x, carry):
        pltpu.make_async_copy(pops_hbm.at[:, x], pops.at[x], sems.at[x]).wait()
        kind = flags[x]
        values = [pops[x, q] for q in range(Q)]
        result = collide(values, rate[x], kind)
        for q in range(Q):
            c1[q, x] = roll_by(result[q], VELOCITIES[q][2], 1)
        fixed[0, x] = kind.astype(F32)
        fixed[1, x] = rate[x]
        return carry

    lax.fori_loop(0, planes, plane, 0)

    def pack(out, sign, outside):
        def line(x, carry):
            for slot, (q, depth) in enumerate(face_slots(1, sign)):
                y = rows - 1 - depth if sign > 0 else depth
                out[slot, pl.ds(x, 1)] = c1[q, x, y : y + 1]
            y = rows - 1 if sign > 0 else 0
            for k, slot in enumerate((FLAG_SLOT, RATE_SLOT)):
                out[slot, pl.ds(x, 1)] = fixed[k, x, y : y + 1]
            return carry

        lax.fori_loop(0, planes, line, 0)
        for slot in range(SLOTS, SIDE_SLOTS):
            out[slot] = jnp.zeros(out.shape[1:], F32)
        clear_outside(out, outside)

    pack_pair(pack, "inner", near, far)


def clear_outside(out, outside):
    @pl.when(outside)
    def _():
        out[...] = jnp.zeros(out.shape, F32)


def pack_pair(pack, axis, near, far):
    at = lax.axis_index(axis)
    even = lax.rem(at, 2) == 0
    first, last = at == 0, at == lax.axis_size(axis) - 1

    @pl.when(even)
    def _():
        pack(near, 1, last)
        pack(far, -1, first)

    @pl.when(jnp.logical_not(even))
    def _():
        pack(near, -1, first)
        pack(far, 1, last)


def slab_face_kernel(c1, fixed, numbers, far, near):
    del numbers
    planes = c1.shape[1]

    def pack(out, sign, outside):
        for slot, (q, depth) in enumerate(face_slots(0, sign)):
            out[slot] = c1[q, planes - 1 - depth if sign > 0 else depth]
        end = planes - 1 if sign > 0 else 0
        out[FLAG_SLOT] = fixed[0, end]
        out[RATE_SLOT] = fixed[1, end]
        clear_outside(out, outside)

    pack_pair(pack, "slab", near, far)


def gather_both(near, far, both, axis):
    odd = lax.rem(lax.axis_index(axis), 2)
    for slot in range(both.shape[1]):
        both[1 - odd, slot] = near[slot]
        both[odd, slot] = far[slot]


def corner_kernel(far_y, near_y, other, far, near, both):
    planes = near_y.shape[1]
    gather_both(near_y, far_y, both, "inner")

    def pack(out, sign, outside):
        for side, sign_y in enumerate((1, -1)):
            picks = corner_rows(sign, sign_y) + [(FLAG_SLOT, 0), (RATE_SLOT, 0)]
            for row, (slot, depth) in enumerate(picks):
                x = planes - 1 - depth if sign > 0 else depth
                at = 3 * side + row // 8
                out[at, row % 8 : row % 8 + 1] = both[side, slot, x : x + 1]
        for part in range(3):
            out[FORCE_SLOT + part] = other[part]
        clear_outside(out, outside)

    pack_pair(pack, "slab", near, far)


def with_edge(block, step_y, edge):
    rows = block.shape[0]
    sub = lax.broadcasted_iota(jnp.int32, block.shape, 0)
    if step_y > 0:
        return jnp.where(sub == 0, edge, roll_by(block, 1, 0))
    return jnp.where(sub == rows - 1, edge, roll_by(block, -1, 0))


def store_plane(extended, walls, second, at, rate, kind):
    values = []
    for q in range(Q):
        step_x, step_y, _ = VELOCITIES[q]
        block = extended[q, at + 1 - step_x]
        if step_y != 0:
            edge = walls[0 if step_y > 0 else 1, q, pl.ds(at + 1 - step_x, 1)]
            block = with_edge(block, step_y, edge)
        values.append(block)
    result = collide(values, rate, kind)
    for q in range(Q):
        second[q, at] = roll_by(result[q], VELOCITIES[q][2], 1)


def inside_kernel(
    c1,
    fixed,
    far_y,
    near_y,
    far_x,
    near_x,
    extended,
    walls,
    crossing,
    second,
    ends,
    both_y,
    both_x,
):
    planes, rows, _ = c1.shape[1:]
    wide = planes + 4
    gather_both(near_y, far_y, both_y, "inner")
    gather_both(near_x, far_x, both_x, "slab")
    for q in range(Q):
        for x in range(planes):
            extended[q, x + 2] = c1[q, x]
        extended[q, 1] = both_x[0, q]
        extended[q, planes + 2] = both_x[1, q]
        if VELOCITIES[q][0] > 0:
            extended[q, 0] = both_x[0, OPPOSITE[q]]
        if VELOCITIES[q][0] < 0:
            extended[q, planes + 3] = both_x[1, OPPOSITE[q]]
    for end in range(2):
        ends[end, 0] = both_x[end, FLAG_SLOT]
        ends[end, 1] = both_x[end, RATE_SLOT]

    for side, sign in enumerate((1, -1)):
        y = 0 if sign > 0 else rows - 1
        for slot in range(SLOTS):
            walls[side, slot, 2 : planes + 2] = both_y[side, slot]
        place = 0
        for q in range(Q):
            if VELOCITIES[q][1] != -sign:
                continue
            for x in range(wide):
                crossing[side, place, x : x + 1] = extended[q, x, y : y + 1]
            place += 1

    def inside_plane(x, carry):
        store_plane(extended, walls, second, x + 1, fixed[1, x], fixed[0, x])
        return carry

    lax.fori_loop(1, planes - 1, inside_plane, 0)


def second_kernel(
    block_source_hbm,
    block_target_hbm,
    block_node_hbm,
    block_count,
    far,
    near,
    fixed,
    extended,
    crossing,
    ends,
    internal_own,
    walls_in,
    second_in,
    out,
    message,
    walls,
    second,
    both,
    edges,
    loads,
    block_source,
    block_target,
    block_node,
    sems,
):
    del walls_in, second_in
    copies = [
        pltpu.make_async_copy(block_source_hbm, block_source, sems.at[0]),
        pltpu.make_async_copy(block_target_hbm, block_target, sems.at[1]),
        pltpu.make_async_copy(block_node_hbm, block_node, sems.at[2]),
    ]
    for copy in copies:
        copy.start()
    planes, rows, length = out.shape[1:]
    half = length // BLK
    slots = block_source.shape[2]
    wide = planes + 4
    slab = lax.axis_index("slab")
    inner = lax.axis_index("inner")
    slab_end = lax.axis_size("slab") - 1
    inner_end = lax.axis_size("inner") - 1
    gather_both(near, far, both, "slab")

    for side, sign in enumerate((1, -1)):
        for end, sign_x in enumerate((1, -1)):
            for row, (slot, depth) in enumerate(corner_rows(sign_x, sign)):
                at = (1 - depth) if sign_x > 0 else planes + 2 + depth
                source = 3 * side + row // 8
                walls[side, slot, at : at + 1] = both[end, source, row % 8 : row % 8 + 1]
            at = 1 if sign_x > 0 else planes + 2
            for row in (FLAG_SLOT, RATE_SLOT):
                source = 3 * side + row // 8
                walls[side, row, at : at + 1] = both[end, source, row % 8 : row % 8 + 1]

    def edge_plane(end, carry):
        x = end * (planes - 1)
        store_plane(extended, walls, second, x + 1, fixed[1, x], fixed[0, x])
        return carry

    def outside_plane(end, carry):
        store_plane(extended, walls, second, end * (planes + 1), ends[end, 1], ends[end, 0])
        return carry

    lax.fori_loop(0, 2, edge_plane, 0)
    lax.fori_loop(0, 2, outside_plane, 0)

    @pl.when(slab == 0)
    def _():
        for q in range(Q):
            if VELOCITIES[q][0] > 0:
                second[q, 0] = jnp.zeros((rows, length), F32)

    @pl.when(slab == slab_end)
    def _():
        for q in range(Q):
            if VELOCITIES[q][0] < 0:
                second[q, planes + 1] = jnp.zeros((rows, length), F32)

    across = lax.broadcasted_iota(jnp.int32, (wide, length), 0)
    hidden = ((across <= 1) & (slab == 0)) | ((across >= planes + 2) & (slab == slab_end))
    for side, sign, outside in ((0, 1, inner == 0), (1, -1, inner == inner_end)):
        values = []
        place = 0
        for q in range(Q):
            step_x, step_y, _ = VELOCITIES[q]
            if step_y == 0:
                block = walls[side, q]
            elif step_y == sign:
                block = walls[side, OPPOSITE[q]]
            else:
                block = crossing[side, place]
                place += 1
            values.append(roll_by(block, step_x, 0))
        result = collide(values, walls[side, RATE_SLOT], walls[side, FLAG_SLOT])
        place = 0
        for q in range(Q):
            if VELOCITIES[q][1] == sign:
                kept = jnp.where(hidden | outside, 0.0, result[q])
                edges[side, place] = roll_by(kept, VELOCITIES[q][2], 1)
                place += 1

    def plane_two(x, carry):
        values = []
        places = {1: 0, -1: 0}
        for q in range(Q):
            step_x, step_y, _ = VELOCITIES[q]
            block = second[q, x + 1 - step_x]
            if step_y != 0:
                edge = edges[0 if step_y > 0 else 1, places[step_y], pl.ds(x + 2 - step_x, 1)]
                places[step_y] += 1
                block = with_edge(block, step_y, edge)
            values.append(block)
            out[q, x] = block
        density, flow_x, flow_y, flow_z = moments(values)
        parts = (
            LOAD_SCALE * flow_x,
            LOAD_SCALE * (flow_y + (density - 1.0) / 3.0),
            LOAD_SCALE * flow_z,
        )
        for part in range(3):
            for piece in range(half):
                loads[x * half + piece, part] = parts[part][:, piece * BLK : (piece + 1) * BLK]
        return carry

    lax.fori_loop(0, planes, plane_two, 0)

    for copy in copies:
        copy.wait()
    node_blocks = internal_own.shape[1] * half
    live = jnp.broadcast_to(block_count[...], (1, BLK))
    for k in range(slots):
        run = block_source[0, 0, k]
        x = run // (rows * half)
        left = run - x * (rows * half)
        y = left // half
        piece = left - y * half
        for part in range(3):
            message[4 * k + part : 4 * k + part + 1] = loads[x * half + piece, part, pl.ds(y, 1)]
        key = block_target[0, 0, k] * node_blocks + block_node[0, 0, k]
        message[4 * k + 3 : 4 * k + 4] = jnp.where(live > k, key, -1).astype(F32)
    for part in range(3):
        start = 4 * slots + part * node_blocks
        for piece in range(half):
            at = piece * rows
            lanes = slice(piece * BLK, (piece + 1) * BLK)
            message[start + at : start + at + rows] = (
                internal_own[part, :, lanes] + both[0, FORCE_SLOT + part, :, lanes]
            )


def element_kernel(
    elements, displacement, next_nodes, shape_inverse, stiffness, low_ids, high_ids, forces, shapes,
    numbers, corners,
):
    node_dev = displacement.shape[1]
    node_blocks = node_dev // BLK
    runs = elements.shape[1] // BLK
    for j in range(runs):
        lanes = slice(j * BLK, (j + 1) * BLK)
        for row in range(3):
            numbers[row, j : j + 1] = elements[row : row + 1, lanes]
            shapes[row, j : j + 1] = shape_inverse[row : row + 1, lanes]
    for row in range(3):
        low_ids[row] = (numbers[row] & (BLK - 1)).astype(F32)
        high_ids[row] = (numbers[row] >> 7).astype(F32)

    def gather(group, carry):
        rows = pl.ds(pl.multiple_of(group * 8, 8), 8)
        low = [numbers[corner, rows] & (BLK - 1) for corner in range(3)]
        high = [numbers[corner, rows] >> 7 for corner in range(3)]
        for corner in range(3):
            nodes = [jnp.zeros((8, BLK), F32)] * 3
            for block in range(2 * node_blocks):
                source = displacement if block < node_blocks else next_nodes
                start = (block % node_blocks) * BLK
                here = high[corner] == block
                for part in range(3):
                    row = source[part : part + 1, start : start + BLK]
                    picked = jnp.take_along_axis(
                        jnp.broadcast_to(row, (8, BLK)),
                        low[corner],
                        axis=1,
                        mode="promise_in_bounds",
                    )
                    nodes[part] = jnp.where(here, picked, nodes[part])
            for part in range(3):
                corners[corner, part, rows] = nodes[part]
        return carry

    lax.fori_loop(0, runs // 8, gather, 0)

    first, second, third = [[corners[c, p] for p in range(3)] for c in range(3)]
    diag_a = shapes[0]
    skew_b = shapes[1]
    diag_c = shapes[2]
    stiff = stiffness[...]
    edge_one = [second[p] - first[p] for p in range(3)]
    edge_two = [third[p] - first[p] for p in range(3)]
    one = [diag_a * edge_one[p] for p in range(3)]
    two = [skew_b * edge_one[p] + diag_c * edge_two[p] for p in range(3)]
    one[0] = one[0] + 1.0
    two[1] = two[1] + 1.0
    aa = one[0] * one[0] + one[1] * one[1] + one[2] * one[2]
    ab = one[0] * two[0] + one[1] * two[1] + one[2] * two[2]
    bb = two[0] * two[0] + two[1] * two[1] + two[2] * two[2]
    determinant = aa * bb - ab * ab
    scale = 1.0 / determinant
    inverse_aa = bb * scale
    inverse_ab = -ab * scale
    inverse_bb = aa * scale
    pressure = LAME_RATIO * (0.5 * jnp.log(determinant))
    for p in range(3):
        pulled_one = one[p] * inverse_aa + two[p] * inverse_ab
        pulled_two = one[p] * inverse_ab + two[p] * inverse_bb
        stress_one = stiff * (one[p] - pulled_one + pressure * pulled_one)
        stress_two = stiff * (two[p] - pulled_two + pressure * pulled_two)
        force_one = diag_a * stress_one + skew_b * stress_two
        force_two = diag_c * stress_two
        for corner, force in enumerate((-(force_one + force_two), force_one, force_two)):
            rest = force
            for part in range(PIECES):
                piece = rest.astype(jnp.bfloat16).astype(F32)
                rest = rest - piece
                forces[part * 3 + p, corner] = piece


def spread_kernel(base, low_ids, high_ids, forces, out):
    runs = low_ids.shape[1]
    parts, rows, length = out.shape
    pieces = length // BLK
    slots = pieces * rows
    kind = jnp.bfloat16
    tile = 16
    slot_ids = lax.broadcasted_iota(jnp.int32, (slots, BLK), 0).astype(F32) + base
    slot_ids = slot_ids.astype(kind)
    lane_ids = lax.broadcasted_iota(jnp.int32, (BLK, BLK), 0).astype(F32).astype(kind)
    ones = jnp.ones((BLK, BLK), kind)
    none = jnp.zeros((BLK, BLK), kind)
    blank = jnp.zeros((slots, BLK), kind)

    def tall_row(row, count):
        block = jnp.broadcast_to(row, (tile, BLK)).astype(kind)
        return jnp.concatenate([block] * (count // tile), axis=0)

    total = None
    for corner in range(3):
        left = [[] for _ in range(parts * PIECES)]
        right = []
        for j in range(runs):
            row = slice(j, j + 1)
            here = slot_ids == tall_row(high_ids[corner, row], slots)
            right.append(jnp.where(lane_ids == tall_row(low_ids[corner, row], BLK), ones, none))
            for part in range(parts * PIECES):
                left[part].append(
                    jnp.where(here, tall_row(forces[part, corner, row], slots), blank)
                )
        tall = jnp.concatenate([jnp.concatenate(part, axis=1) for part in left], axis=0)
        wide = jnp.concatenate(right, axis=1)
        product = lax.dot_general(
            tall, wide, (((1,), (1,)), ((), ())), preferred_element_type=F32
        )
        total = product if total is None else total + product
    for p in range(parts):
        summed = total[p * slots : (p + 1) * slots]
        for part in range(1, PIECES):
            start = (parts * part + p) * slots
            summed = summed + total[start : start + slots]
        for piece in range(pieces):
            out[p, :, piece * BLK : (piece + 1) * BLK] = summed[piece * rows : (piece + 1) * rows]


def store_kernel(values, out_hbm, sem):
    store = pltpu.make_async_copy(values, out_hbm, sem)
    store.start()
    store.wait()


def final_kernel(count, *refs):
    messages = refs[:count]
    residual, motion, keys = refs[count:]
    slots = keys.shape[0]
    node_blocks = residual.shape[1] // BLK
    inner = lax.axis_index("inner")
    mine = messages[0]
    for k in range(slots):
        keys[k : k + 1] = mine[4 * k + 3 : 4 * k + 4]
    wanted = keys[...]
    node_ids = lax.broadcasted_iota(jnp.int32, (node_blocks, BLK), 0)
    own_ids = (node_ids + inner * node_blocks).astype(F32)
    external = [jnp.zeros((node_blocks, BLK), F32)] * 3
    moved = [jnp.zeros((slots, BLK), F32)] * 3
    for message in messages:
        for k in range(slots):
            key = message[4 * k + 3 : 4 * k + 4]
            here = own_ids == key
            same = wanted == key
            for part in range(3):
                row = message[4 * k + part : 4 * k + part + 1]
                external[part] = external[part] + jnp.where(here, row, 0.0)
                moved[part] = moved[part] + jnp.where(same, row, 0.0)
    for step, message in enumerate(messages):
        sender = partner_of(inner, step, count)
        for b in range(node_blocks):
            key = jnp.broadcast_to(sender * node_blocks + b, (1, BLK)).astype(F32)
            same = wanted == key
            for part in range(3):
                at = 4 * slots + part * node_blocks + b
                moved[part] = moved[part] - jnp.where(same, message[at : at + 1], 0.0)
    live = wanted >= 0.0
    for part in range(3):
        start = 4 * slots + part * node_blocks
        left = external[part] - mine[start : start + node_blocks]
        for b in range(node_blocks):
            residual[part : part + 1, b * BLK : (b + 1) * BLK] = left[b : b + 1]
        motion[part] = jnp.where(live, COMPLIANCE * moved[part], 0.0)


def call(kernel, outs, operands, spaces, scratch=(), out_spaces=None, micros=1.0, aliases=None):
    spec = lambda space: pl.BlockSpec(memory_space=space)
    out_spaces = out_spaces or (pltpu.VMEM,) * len(outs)
    return pl.pallas_call(
        kernel,
        out_shape=outs,
        in_specs=[spec(space) for space in spaces],
        out_specs=tuple(spec(space) for space in out_spaces),
        scratch_shapes=list(scratch),
        input_output_aliases=aliases or {},
        compiler_params=pltpu.CompilerParams(vmem_limit_bytes=VMEM_BYTES),
        cost_estimate=pl.CostEstimate(
            flops=0, bytes_accessed=int(micros * 3.6e6), transcendentals=0
        ),
    )(*operands)


def partner_of(at, step, count):
    if count & (count - 1) == 0:
        return at ^ step
    return (at + count - step) % count


def exchange(block, axis, step):
    count = lax.axis_size(axis)
    return lax.ppermute(block, axis, [(partner_of(i, step, count), i) for i in range(count)])


def around(block, axis, step):
    count = lax.axis_size(axis)
    return lax.ppermute(block, axis, [(i, (i + step) % count) for i in range(count)])


def swap(near, far, axis, beside):
    count, others = lax.axis_size(axis), lax.axis_size(beside)
    routes = []
    for start in (0, 1):
        route = []
        for other in range(others):
            for i in range(count):
                j = i + 1 if i % 2 == start else i - 1
                to = other
                if not 0 <= j < count:
                    j = i
                    to = other ^ 1 if others % 2 == 0 else other
                route.append((other * count + i, to * count + j))
        routes.append(route)
    axes = (beside, axis)
    return lax.ppermute(near, axes, routes[0]), lax.ppermute(far, axes, routes[1])


def shards(
    populations,
    relaxation,
    node_flags,
    displacement,
    elements,
    shape_inverse,
    stiffness,
    block_source,
    block_target,
    block_node,
    block_count,
):
    planes, rows, length = populations.shape[1:]
    half = length // BLK
    node_dev = displacement.shape[1]
    node_blocks = node_dev // BLK
    runs = stiffness.shape[0] // BLK
    slots = block_source.shape[2]
    count = lax.axis_size("inner")
    shape = lambda *dims: jax.ShapeDtypeStruct(dims, F32)
    whole = shape(*populations.shape)
    vmem, hbm, smem = pltpu.VMEM, pltpu.HBM, pltpu.SMEM

    next_nodes = around(displacement, "slab", -1)
    face_y = shape(SIDE_SLOTS, planes, length)
    face_x = shape(SLOTS, rows, length)
    pin = lambda block: pltpu.with_memory_space_constraint(block, hbm)
    c1, fixed, far, near = call(
        first_kernel,
        (whole, shape(2, planes, rows, length), face_y, face_y),
        (pin(populations), pin(relaxation), pin(node_flags)),
        (hbm,) * 3,
        scratch=(
            pltpu.VMEM((planes, Q, rows, length), F32),
            pltpu.VMEM((planes, rows, length), F32),
            pltpu.VMEM((planes, rows, length), jnp.int32),
            pltpu.SemaphoreType.DMA((planes + 2,)),
        ),
        micros=1.5,
    )
    near_y, far_y = swap(near, far, "inner", "slab")
    numbers = shape(3, runs, BLK)
    low_ids, high_ids, forces = call(
        element_kernel,
        (numbers, numbers, shape(3 * PIECES, 3, runs, BLK)),
        (elements, displacement, next_nodes, shape_inverse, stiffness.reshape(runs, BLK)),
        (vmem,) * 5,
        scratch=(
            pltpu.VMEM((3, runs, BLK), F32),
            pltpu.VMEM((3, runs, BLK), jnp.int32),
            pltpu.VMEM((3, 3, runs, BLK), F32),
        ),
        micros=0.001,
    )
    far, near = call(
        slab_face_kernel, (face_x, face_x), (c1, fixed, low_ids), (vmem,) * 3, micros=0.001
    )
    near_x, far_x = swap(near, far, "slab", "group")
    nodal = shape(3, node_blocks // half, length)
    (other,) = call(
        functools.partial(spread_kernel, node_blocks),
        (nodal,),
        (low_ids, high_ids, forces),
        (vmem,) * 3,
        micros=0.001,
    )
    corner = shape(CORNER_SLOTS, rows, length)
    far, near = call(
        corner_kernel,
        (corner, corner),
        (far_y, near_y, other),
        (vmem,) * 3,
        scratch=(pltpu.VMEM((2, SLOTS, planes, length), F32),),
        micros=0.3,
    )
    near_c, far_c = swap(near, far, "slab", "group")
    (own,) = call(
        functools.partial(spread_kernel, 0),
        (nodal,),
        (low_ids, high_ids, forces),
        (vmem,) * 3,
        micros=0.8,
    )
    wide = planes + 4
    walls_shape = shape(2, SLOTS, wide, length)
    second_shape = shape(Q, planes + 2, rows, length)
    extended, walls, crossing, second, ends = call(
        inside_kernel,
        (
            shape(Q, wide, rows, length),
            walls_shape,
            shape(2, 5, wide, length),
            second_shape,
            shape(2, 2, rows, length),
        ),
        (c1, fixed, far_y, near_y, far_x, near_x),
        (vmem,) * 6,
        scratch=(
            pltpu.VMEM((2, SLOTS, planes, length), F32),
            pltpu.VMEM((2, SLOTS, rows, length), F32),
        ),
        micros=0.8,
    )
    lines = 4 * slots + 3 * node_blocks
    values, message, _, _ = call(
        second_kernel,
        (whole, shape(lines, BLK), walls_shape, second_shape),
        (
            pin(block_source),
            pin(block_target),
            pin(block_node),
            block_count,
            far_c,
            near_c,
            fixed,
            extended,
            crossing,
            ends,
            own,
            walls,
            second,
        ),
        (hbm,) * 3 + (vmem,) * 10,
        aliases={11: 2, 12: 3},
        scratch=(
            pltpu.VMEM((2, CORNER_SLOTS, rows, length), F32),
            pltpu.VMEM((2, 5, wide, length), F32),
            pltpu.VMEM((planes * half, 3, rows, BLK), F32),
            pltpu.SMEM(block_source.shape, jnp.int32),
            pltpu.SMEM(block_target.shape, jnp.int32),
            pltpu.SMEM(block_node.shape, jnp.int32),
            pltpu.SemaphoreType.DMA((3,)),
        ),
        micros=1.5,
    )
    messages = [message] + [exchange(message, "inner", step) for step in range(1, count)]
    (populations_out,) = call(
        store_kernel,
        (whole,),
        (values,),
        (vmem,),
        out_spaces=(hbm,),
        scratch=(pltpu.SemaphoreType.DMA(()),),
        micros=1.0,
    )
    residual, motion = call(
        functools.partial(final_kernel, count),
        (shape(3, node_dev), shape(3, slots, BLK)),
        messages,
        (vmem,) * count,
        scratch=(pltpu.VMEM((slots, BLK), F32),),
        micros=0.8,
    )
    return populations_out, residual, motion.transpose(1, 0, 2)[None, None]


def solution(mesh):
    return jax.shard_map(
        shards,
        mesh=mesh,
        in_specs=(
            P(None, ("group", "slab"), "inner", None),
            P(("group", "slab"), "inner", None),
            P(("group", "slab"), "inner", None),
            P(None, ("group", "slab", "inner")),
            P(None, ("group", "slab", "inner")),
            P(None, ("group", "slab", "inner")),
            P(("group", "slab", "inner")),
            P(("group", "slab"), "inner", None),
            P(("group", "slab"), "inner", None),
            P(("group", "slab"), "inner", None),
            P(("group", "slab"), "inner"),
        ),
        out_specs=(
            P(None, ("group", "slab"), "inner", None),
            P(None, ("group", "slab", "inner")),
            P(("group", "slab"), "inner", None, None, None),
        ),
        check_vma=False,
    )
```

```python
import functools

import jax
import jax.numpy as jnp
from jax import lax
from jax.experimental import pallas as pl
from jax.experimental.pallas import tpu as pltpu
from jax.sharding import PartitionSpec as P

BLK = 128
VELOCITIES = (
    (0, 0, 0),
    (1, 0, 0),
    (-1, 0, 0),
    (0, 1, 0),
    (0, -1, 0),
    (0, 0, 1),
    (0, 0, -1),
    (1, 1, 0),
    (-1, -1, 0),
    (1, -1, 0),
    (-1, 1, 0),
    (1, 0, 1),
    (-1, 0, -1),
    (1, 0, -1),
    (-1, 0, 1),
    (0, 1, 1),
    (0, -1, -1),
    (0, 1, -1),
    (0, -1, 1),
)
WEIGHTS = (1.0 / 3.0,) + (1.0 / 18.0,) * 6 + (1.0 / 36.0,) * 12
OPPOSITE = (0, 2, 1, 4, 3, 6, 5, 8, 7, 10, 9, 12, 11, 14, 13, 16, 15, 18, 17)
INLET_SPEED = 0.04
LOAD_SCALE = 25.0
COMPLIANCE = 0.5
LAME_RATIO = 2.0
Q = 19
FLAG_SLOT = 19
RATE_SLOT = 20
SLOTS = 21
SIDE_SLOTS = 24
FORCE_SLOT = 6
CORNER_SLOTS = FORCE_SLOT + 3
PIECES = 2
F32 = jnp.float32
VMEM_BYTES = 48 * 1024 * 1024


def moments(values):
    sums = [values[q] + values[q + 1] for q in range(1, Q, 2)]
    diffs = [values[q] - values[q + 1] for q in range(1, Q, 2)]
    density = values[0]
    for term in sums:
        density = density + term
    flows = []
    for axis in range(3):
        total = None
        for k, q in enumerate(range(1, Q, 2)):
            factor = VELOCITIES[q][axis]
            if factor == 0:
                continue
            if total is None:
                total = diffs[k] if factor > 0 else -diffs[k]
            else:
                total = total + diffs[k] if factor > 0 else total - diffs[k]
        flows.append(total)
    return density, flows[0], flows[1], flows[2]


def collide(values, rate, kind):
    density, flow_x, flow_y, flow_z = moments(values)
    inverse = 1.0 / density
    wall = kind == 1
    inlet = kind == 2
    fluid = kind == 0
    vel = (
        jnp.where(inlet, INLET_SPEED, flow_x * inverse),
        jnp.where(inlet, 0.0, flow_y * inverse),
        jnp.where(inlet, 0.0, flow_z * inverse),
    )
    scale = jnp.where(fluid, density, 1.0)
    rate = jnp.where(fluid, rate, 1.0)
    base = 1.0 - 1.5 * (vel[0] * vel[0] + vel[1] * vel[1] + vel[2] * vel[2])
    weighted = {w: w * scale for w in set(WEIGHTS)}
    out = [None] * Q
    relaxed = values[0] + rate * (weighted[WEIGHTS[0]] * base - values[0])
    out[0] = jnp.where(wall, values[0], relaxed)
    for q in range(1, Q, 2):
        project = None
        for factor, component in zip(VELOCITIES[q], vel):
            if factor == 0:
                continue
            if project is None:
                project = component
            else:
                project = project + component if factor > 0 else project - component
        even = base + 4.5 * (project * project)
        odd = 3.0 * project
        w = weighted[WEIGHTS[q]]
        forward = values[q] + rate * (w * (even + odd) - values[q])
        backward = values[q + 1] + rate * (w * (even - odd) - values[q + 1])
        out[q] = jnp.where(wall, values[q + 1], forward)
        out[q + 1] = jnp.where(wall, values[q], backward)
    return out


def roll_by(block, step, axis):
    if step == 0:
        return block
    return pltpu.roll(block, step % block.shape[axis], axis)


def face_slots(axis, sign):
    picks = []
    for q in range(Q):
        if VELOCITIES[q][axis] * sign >= 0:
            picks.append((q, 0))
        else:
            picks.append((OPPOSITE[q], 1))
    return picks


def mirror(q, axis):
    flipped = tuple(-c if k == axis else c for k, c in enumerate(VELOCITIES[q]))
    return VELOCITIES.index(flipped)


def corner_rows(sign_x, sign_y):
    rows = []
    for q, depth in face_slots(0, sign_x):
        if VELOCITIES[q][1] * sign_y >= 0:
            rows.append((q, depth))
        else:
            rows.append((OPPOSITE[mirror(q, 1)], depth))
    return rows


def first_kernel(
    pops_hbm,
    rate_hbm,
    flags_hbm,
    displacement_hbm,
    elements_hbm,
    shape_hbm,
    stiffness_hbm,
    c1,
    fixed,
    far,
    near,
    displacement,
    elements,
    shape_inverse,
    stiffness,
    pops,
    rate,
    flags,
    sems,
):
    planes, rows = c1.shape[1], c1.shape[2]
    copies = [
        pltpu.make_async_copy(rate_hbm, rate, sems.at[planes]),
        pltpu.make_async_copy(flags_hbm, flags, sems.at[planes + 1]),
    ]
    loads = [
        pltpu.make_async_copy(pops_hbm.at[:, x], pops.at[x], sems.at[x]) for x in range(planes)
    ]
    shell = [
        pltpu.make_async_copy(source, target, sems.at[planes + 2 + k])
        for k, (source, target) in enumerate(
            (
                (displacement_hbm, displacement),
                (elements_hbm, elements),
                (shape_hbm, shape_inverse),
                (stiffness_hbm, stiffness),
            )
        )
    ]
    for copy in loads[:1] + copies + loads[1:] + shell:
        copy.start()
    for copy in copies:
        copy.wait()

    def plane(x, carry):
        pltpu.make_async_copy(pops_hbm.at[:, x], pops.at[x], sems.at[x]).wait()
        kind = flags[x]
        values = [pops[x, q] for q in range(Q)]
        result = collide(values, rate[x], kind)
        for q in range(Q):
            c1[q, x] = roll_by(result[q], VELOCITIES[q][2], 1)
        fixed[0, x] = kind.astype(F32)
        fixed[1, x] = rate[x]
        return carry

    lax.fori_loop(0, planes, plane, 0)

    def pack(out, sign, outside):
        def line(x, carry):
            for slot, (q, depth) in enumerate(face_slots(1, sign)):
                y = rows - 1 - depth if sign > 0 else depth
                out[slot, pl.ds(x, 1)] = c1[q, x, y : y + 1]
            y = rows - 1 if sign > 0 else 0
            for k, slot in enumerate((FLAG_SLOT, RATE_SLOT)):
                out[slot, pl.ds(x, 1)] = fixed[k, x, y : y + 1]
            return carry

        lax.fori_loop(0, planes, line, 0)
        for slot in range(SLOTS, SIDE_SLOTS):
            out[slot] = jnp.zeros(out.shape[1:], F32)
        clear_outside(out, outside)

    pack_pair(pack, "inner", near, far)
    for copy in shell:
        copy.wait()


def clear_outside(out, outside):
    @pl.when(outside)
    def _():
        out[...] = jnp.zeros(out.shape, F32)


def pack_pair(pack, axis, near, far):
    at = lax.axis_index(axis)
    even = lax.rem(at, 2) == 0
    first, last = at == 0, at == lax.axis_size(axis) - 1

    @pl.when(even)
    def _():
        pack(near, 1, last)
        pack(far, -1, first)

    @pl.when(jnp.logical_not(even))
    def _():
        pack(near, -1, first)
        pack(far, 1, last)


def slab_face_kernel(c1, fixed, numbers, far, near):
    del numbers
    planes = c1.shape[1]

    def pack(out, sign, outside):
        for slot, (q, depth) in enumerate(face_slots(0, sign)):
            out[slot] = c1[q, planes - 1 - depth if sign > 0 else depth]
        end = planes - 1 if sign > 0 else 0
        out[FLAG_SLOT] = fixed[0, end]
        out[RATE_SLOT] = fixed[1, end]
        clear_outside(out, outside)

    pack_pair(pack, "slab", near, far)


def gather_both(near, far, both, axis):
    odd = lax.rem(lax.axis_index(axis), 2)
    for slot in range(both.shape[1]):
        both[1 - odd, slot] = near[slot]
        both[odd, slot] = far[slot]


def corner_kernel(far_y, near_y, other, far, near, both):
    planes = near_y.shape[1]
    gather_both(near_y, far_y, both, "inner")

    def pack(out, sign, outside):
        for side, sign_y in enumerate((1, -1)):
            picks = corner_rows(sign, sign_y) + [(FLAG_SLOT, 0), (RATE_SLOT, 0)]
            for row, (slot, depth) in enumerate(picks):
                x = planes - 1 - depth if sign > 0 else depth
                at = 3 * side + row // 8
                out[at, row % 8 : row % 8 + 1] = both[side, slot, x : x + 1]
        for part in range(3):
            out[FORCE_SLOT + part] = other[part]
        clear_outside(out, outside)

    pack_pair(pack, "slab", near, far)


def with_edge(block, step_y, edge):
    rows = block.shape[0]
    sub = lax.broadcasted_iota(jnp.int32, block.shape, 0)
    if step_y > 0:
        return jnp.where(sub == 0, edge, roll_by(block, 1, 0))
    return jnp.where(sub == rows - 1, edge, roll_by(block, -1, 0))


def store_plane(extended, walls, second, at, rate, kind):
    values = []
    for q in range(Q):
        step_x, step_y, _ = VELOCITIES[q]
        block = extended[q, at + 1 - step_x]
        if step_y != 0:
            edge = walls[0 if step_y > 0 else 1, q, pl.ds(at + 1 - step_x, 1)]
            block = with_edge(block, step_y, edge)
        values.append(block)
    result = collide(values, rate, kind)
    for q in range(Q):
        second[q, at] = roll_by(result[q], VELOCITIES[q][2], 1)


def inside_kernel(
    c1,
    fixed,
    far_y,
    near_y,
    far_x,
    near_x,
    extended,
    walls,
    crossing,
    second,
    ends,
    both_y,
    both_x,
):
    planes, rows, _ = c1.shape[1:]
    wide = planes + 4
    gather_both(near_y, far_y, both_y, "inner")
    gather_both(near_x, far_x, both_x, "slab")
    for q in range(Q):
        for x in range(planes):
            extended[q, x + 2] = c1[q, x]
        extended[q, 1] = both_x[0, q]
        extended[q, planes + 2] = both_x[1, q]
        if VELOCITIES[q][0] > 0:
            extended[q, 0] = both_x[0, OPPOSITE[q]]
        if VELOCITIES[q][0] < 0:
            extended[q, planes + 3] = both_x[1, OPPOSITE[q]]
    for end in range(2):
        ends[end, 0] = both_x[end, FLAG_SLOT]
        ends[end, 1] = both_x[end, RATE_SLOT]

    for side, sign in enumerate((1, -1)):
        y = 0 if sign > 0 else rows - 1
        for slot in range(SLOTS):
            walls[side, slot, 2 : planes + 2] = both_y[side, slot]
        place = 0
        for q in range(Q):
            if VELOCITIES[q][1] != -sign:
                continue
            for x in range(wide):
                crossing[side, place, x : x + 1] = extended[q, x, y : y + 1]
            place += 1

    def inside_plane(x, carry):
        store_plane(extended, walls, second, x + 1, fixed[1, x], fixed[0, x])
        return carry

    lax.fori_loop(1, planes - 1, inside_plane, 0)


def second_kernel(
    block_source_hbm,
    block_target_hbm,
    block_node_hbm,
    block_count,
    far,
    near,
    fixed,
    extended,
    crossing,
    ends,
    internal_own,
    walls_in,
    second_in,
    out,
    message,
    walls,
    second,
    both,
    edges,
    loads,
    block_source,
    block_target,
    block_node,
    sems,
):
    del walls_in, second_in
    copies = [
        pltpu.make_async_copy(block_source_hbm, block_source, sems.at[0]),
        pltpu.make_async_copy(block_target_hbm, block_target, sems.at[1]),
        pltpu.make_async_copy(block_node_hbm, block_node, sems.at[2]),
    ]
    for copy in copies:
        copy.start()
    planes, rows, length = out.shape[1:]
    half = length // BLK
    slots = block_source.shape[2]
    wide = planes + 4
    slab = lax.axis_index("slab")
    inner = lax.axis_index("inner")
    slab_end = lax.axis_size("slab") - 1
    inner_end = lax.axis_size("inner") - 1
    gather_both(near, far, both, "slab")

    for side, sign in enumerate((1, -1)):
        for end, sign_x in enumerate((1, -1)):
            for row, (slot, depth) in enumerate(corner_rows(sign_x, sign)):
                at = (1 - depth) if sign_x > 0 else planes + 2 + depth
                source = 3 * side + row // 8
                walls[side, slot, at : at + 1] = both[end, source, row % 8 : row % 8 + 1]
            at = 1 if sign_x > 0 else planes + 2
            for row in (FLAG_SLOT, RATE_SLOT):
                source = 3 * side + row // 8
                walls[side, row, at : at + 1] = both[end, source, row % 8 : row % 8 + 1]

    def edge_planes(end, carry):
        x = end * (planes - 1)
        store_plane(extended, walls, second, x + 1, fixed[1, x], fixed[0, x])
        store_plane(extended, walls, second, end * (planes + 1), ends[end, 1], ends[end, 0])
        return carry

    lax.fori_loop(0, 2, edge_planes, 0)

    @pl.when(slab == 0)
    def _():
        for q in range(Q):
            if VELOCITIES[q][0] > 0:
                second[q, 0] = jnp.zeros((rows, length), F32)

    @pl.when(slab == slab_end)
    def _():
        for q in range(Q):
            if VELOCITIES[q][0] < 0:
                second[q, planes + 1] = jnp.zeros((rows, length), F32)

    across = lax.broadcasted_iota(jnp.int32, (wide, length), 0)
    hidden = ((across <= 1) & (slab == 0)) | ((across >= planes + 2) & (slab == slab_end))
    for side, sign, outside in ((0, 1, inner == 0), (1, -1, inner == inner_end)):
        values = []
        place = 0
        for q in range(Q):
            step_x, step_y, _ = VELOCITIES[q]
            if step_y == 0:
                block = walls[side, q]
            elif step_y == sign:
                block = walls[side, OPPOSITE[q]]
            else:
                block = crossing[side, place]
                place += 1
            values.append(roll_by(block, step_x, 0))
        result = collide(values, walls[side, RATE_SLOT], walls[side, FLAG_SLOT])
        place = 0
        for q in range(Q):
            if VELOCITIES[q][1] == sign:
                kept = jnp.where(hidden | outside, 0.0, result[q])
                edges[side, place] = roll_by(kept, VELOCITIES[q][2], 1)
                place += 1

    def plane_two(x, carry):
        values = []
        places = {1: 0, -1: 0}
        for q in range(Q):
            step_x, step_y, _ = VELOCITIES[q]
            block = second[q, x + 1 - step_x]
            if step_y != 0:
                edge = edges[0 if step_y > 0 else 1, places[step_y], pl.ds(x + 2 - step_x, 1)]
                places[step_y] += 1
                block = with_edge(block, step_y, edge)
            values.append(block)
            out[q, x] = block
        density, flow_x, flow_y, flow_z = moments(values)
        parts = (
            LOAD_SCALE * flow_x,
            LOAD_SCALE * (flow_y + (density - 1.0) / 3.0),
            LOAD_SCALE * flow_z,
        )
        for part in range(3):
            for piece in range(half):
                loads[x * half + piece, part] = parts[part][:, piece * BLK : (piece + 1) * BLK]
        return carry

    lax.fori_loop(0, planes, plane_two, 0)

    for copy in copies:
        copy.wait()
    node_blocks = internal_own.shape[1] * half
    live = jnp.broadcast_to(block_count[...], (1, BLK))
    for k in range(slots):
        run = block_source[0, 0, k]
        x = run // (rows * half)
        left = run - x * (rows * half)
        y = left // half
        piece = left - y * half
        for part in range(3):
            message[4 * k + part : 4 * k + part + 1] = loads[x * half + piece, part, pl.ds(y, 1)]
        key = block_target[0, 0, k] * node_blocks + block_node[0, 0, k]
        message[4 * k + 3 : 4 * k + 4] = jnp.where(live > k, key, -1).astype(F32)
    for part in range(3):
        start = 4 * slots + part * node_blocks
        for piece in range(half):
            at = piece * rows
            lanes = slice(piece * BLK, (piece + 1) * BLK)
            message[start + at : start + at + rows] = (
                internal_own[part, :, lanes] + both[0, FORCE_SLOT + part, :, lanes]
            )


def element_kernel(
    elements, displacement, next_nodes, shape_inverse, stiffness, low_ids, high_ids, forces, shapes,
    numbers, corners,
):
    node_dev = displacement.shape[1]
    node_blocks = node_dev // BLK
    runs = elements.shape[1] // BLK
    for j in range(runs):
        lanes = slice(j * BLK, (j + 1) * BLK)
        for row in range(3):
            numbers[row, j : j + 1] = elements[row : row + 1, lanes]
            shapes[row, j : j + 1] = shape_inverse[row : row + 1, lanes]
    for row in range(3):
        low_ids[row] = (numbers[row] & (BLK - 1)).astype(F32)
        high_ids[row] = (numbers[row] >> 7).astype(F32)

    def gather(group, carry):
        rows = pl.ds(pl.multiple_of(group * 8, 8), 8)
        low = [numbers[corner, rows] & (BLK - 1) for corner in range(3)]
        high = [numbers[corner, rows] >> 7 for corner in range(3)]
        for corner in range(3):
            nodes = [jnp.zeros((8, BLK), F32)] * 3
            for block in range(2 * node_blocks):
                source = displacement if block < node_blocks else next_nodes
                start = (block % node_blocks) * BLK
                here = high[corner] == block
                for part in range(3):
                    row = source[part : part + 1, start : start + BLK]
                    picked = jnp.take_along_axis(
                        jnp.broadcast_to(row, (8, BLK)),
                        low[corner],
                        axis=1,
                        mode="promise_in_bounds",
                    )
                    nodes[part] = jnp.where(here, picked, nodes[part])
            for part in range(3):
                corners[corner, part, rows] = nodes[part]
        return carry

    lax.fori_loop(0, runs // 8, gather, 0)

    first, second, third = [[corners[c, p] for p in range(3)] for c in range(3)]
    diag_a = shapes[0]
    skew_b = shapes[1]
    diag_c = shapes[2]
    stiff = stiffness[...]
    edge_one = [second[p] - first[p] for p in range(3)]
    edge_two = [third[p] - first[p] for p in range(3)]
    one = [diag_a * edge_one[p] for p in range(3)]
    two = [skew_b * edge_one[p] + diag_c * edge_two[p] for p in range(3)]
    one[0] = one[0] + 1.0
    two[1] = two[1] + 1.0
    aa = one[0] * one[0] + one[1] * one[1] + one[2] * one[2]
    ab = one[0] * two[0] + one[1] * two[1] + one[2] * two[2]
    bb = two[0] * two[0] + two[1] * two[1] + two[2] * two[2]
    determinant = aa * bb - ab * ab
    scale = 1.0 / determinant
    inverse_aa = bb * scale
    inverse_ab = -ab * scale
    inverse_bb = aa * scale
    pressure = LAME_RATIO * (0.5 * jnp.log(determinant))
    for p in range(3):
        pulled_one = one[p] * inverse_aa + two[p] * inverse_ab
        pulled_two = one[p] * inverse_ab + two[p] * inverse_bb
        stress_one = stiff * (one[p] - pulled_one + pressure * pulled_one)
        stress_two = stiff * (two[p] - pulled_two + pressure * pulled_two)
        force_one = diag_a * stress_one + skew_b * stress_two
        force_two = diag_c * stress_two
        for corner, force in enumerate((-(force_one + force_two), force_one, force_two)):
            rest = force
            for part in range(PIECES):
                piece = rest.astype(jnp.bfloat16).astype(F32)
                rest = rest - piece
                forces[part * 3 + p, corner] = piece


def spread_kernel(base, low_ids, high_ids, forces, out):
    runs = low_ids.shape[1]
    parts, rows, length = out.shape
    pieces = length // BLK
    slots = pieces * rows
    kind = jnp.bfloat16
    tile = 16
    slot_ids = lax.broadcasted_iota(jnp.int32, (slots, BLK), 0).astype(F32) + base
    slot_ids = slot_ids.astype(kind)
    lane_ids = lax.broadcasted_iota(jnp.int32, (BLK, BLK), 0).astype(F32).astype(kind)
    ones = jnp.ones((BLK, BLK), kind)
    none = jnp.zeros((BLK, BLK), kind)
    blank = jnp.zeros((slots, BLK), kind)

    def tall_row(row, count):
        block = jnp.broadcast_to(row, (tile, BLK)).astype(kind)
        return jnp.concatenate([block] * (count // tile), axis=0)

    total = None
    for corner in range(3):
        left = [[] for _ in range(parts * PIECES)]
        right = []
        for j in range(runs):
            row = slice(j, j + 1)
            here = slot_ids == tall_row(high_ids[corner, row], slots)
            right.append(jnp.where(lane_ids == tall_row(low_ids[corner, row], BLK), ones, none))
            for part in range(parts * PIECES):
                left[part].append(
                    jnp.where(here, tall_row(forces[part, corner, row], slots), blank)
                )
        tall = jnp.concatenate([jnp.concatenate(part, axis=1) for part in left], axis=0)
        wide = jnp.concatenate(right, axis=1)
        product = lax.dot_general(
            tall, wide, (((1,), (1,)), ((), ())), preferred_element_type=F32
        )
        total = product if total is None else total + product
    for p in range(parts):
        summed = total[p * slots : (p + 1) * slots]
        for part in range(1, PIECES):
            start = (parts * part + p) * slots
            summed = summed + total[start : start + slots]
        for piece in range(pieces):
            out[p, :, piece * BLK : (piece + 1) * BLK] = summed[piece * rows : (piece + 1) * rows]


def store_kernel(values, out_hbm, sem):
    store = pltpu.make_async_copy(values, out_hbm, sem)
    store.start()
    store.wait()


def final_kernel(count, *refs):
    messages = refs[:count]
    residual, motion, keys = refs[count:]
    slots = keys.shape[0]
    node_blocks = residual.shape[1] // BLK
    inner = lax.axis_index("inner")
    mine = messages[0]
    for k in range(slots):
        keys[k : k + 1] = mine[4 * k + 3 : 4 * k + 4]
    wanted = keys[...]
    node_ids = lax.broadcasted_iota(jnp.int32, (node_blocks, BLK), 0)
    own_ids = (node_ids + inner * node_blocks).astype(F32)
    external = [jnp.zeros((node_blocks, BLK), F32)] * 3
    moved = [jnp.zeros((slots, BLK), F32)] * 3
    for message in messages:
        for k in range(slots):
            key = message[4 * k + 3 : 4 * k + 4]
            here = own_ids == key
            same = wanted == key
            for part in range(3):
                row = message[4 * k + part : 4 * k + part + 1]
                external[part] = external[part] + jnp.where(here, row, 0.0)
                moved[part] = moved[part] + jnp.where(same, row, 0.0)
    for step, message in enumerate(messages):
        sender = partner_of(inner, step, count)
        for b in range(node_blocks):
            key = jnp.broadcast_to(sender * node_blocks + b, (1, BLK)).astype(F32)
            same = wanted == key
            for part in range(3):
                at = 4 * slots + part * node_blocks + b
                moved[part] = moved[part] - jnp.where(same, message[at : at + 1], 0.0)
    live = wanted >= 0.0
    for part in range(3):
        start = 4 * slots + part * node_blocks
        left = external[part] - mine[start : start + node_blocks]
        for b in range(node_blocks):
            residual[part : part + 1, b * BLK : (b + 1) * BLK] = left[b : b + 1]
        motion[part] = jnp.where(live, COMPLIANCE * moved[part], 0.0)


def call(kernel, outs, operands, spaces, scratch=(), out_spaces=None, micros=1.0, aliases=None):
    spec = lambda space: pl.BlockSpec(memory_space=space)
    out_spaces = out_spaces or (pltpu.VMEM,) * len(outs)
    return pl.pallas_call(
        kernel,
        out_shape=outs,
        in_specs=[spec(space) for space in spaces],
        out_specs=tuple(spec(space) for space in out_spaces),
        scratch_shapes=list(scratch),
        input_output_aliases=aliases or {},
        compiler_params=pltpu.CompilerParams(vmem_limit_bytes=VMEM_BYTES),
        cost_estimate=pl.CostEstimate(
            flops=0, bytes_accessed=int(micros * 3.6e6), transcendentals=0
        ),
    )(*operands)


def partner_of(at, step, count):
    if count & (count - 1) == 0:
        return at ^ step
    return (at + count - step) % count


def exchange(block, axis, step):
    count = lax.axis_size(axis)
    return lax.ppermute(block, axis, [(partner_of(i, step, count), i) for i in range(count)])


def around(block, axis, step):
    count = lax.axis_size(axis)
    return lax.ppermute(block, axis, [(i, (i + step) % count) for i in range(count)])


def swap(near, far, axis, beside):
    count, others = lax.axis_size(axis), lax.axis_size(beside)
    routes = []
    for start in (0, 1):
        route = []
        for other in range(others):
            for i in range(count):
                j = i + 1 if i % 2 == start else i - 1
                to = other
                if not 0 <= j < count:
                    j = i
                    to = other ^ 1 if others % 2 == 0 else other
                route.append((other * count + i, to * count + j))
        routes.append(route)
    axes = (beside, axis)
    return lax.ppermute(near, axes, routes[0]), lax.ppermute(far, axes, routes[1])


def shards(
    populations,
    relaxation,
    node_flags,
    displacement,
    elements,
    shape_inverse,
    stiffness,
    block_source,
    block_target,
    block_node,
    block_count,
):
    planes, rows, length = populations.shape[1:]
    half = length // BLK
    node_dev = displacement.shape[1]
    node_blocks = node_dev // BLK
    runs = stiffness.shape[0] // BLK
    slots = block_source.shape[2]
    count = lax.axis_size("inner")
    shape = lambda *dims: jax.ShapeDtypeStruct(dims, F32)
    whole = shape(*populations.shape)
    vmem, hbm, smem = pltpu.VMEM, pltpu.HBM, pltpu.SMEM

    next_nodes = around(displacement, "slab", -1)
    face_y = shape(SIDE_SLOTS, planes, length)
    face_x = shape(SLOTS, rows, length)
    pin = lambda block: pltpu.with_memory_space_constraint(block, hbm)
    whole_like = lambda block: jax.ShapeDtypeStruct(block.shape, block.dtype)
    shell = (displacement, elements, shape_inverse, stiffness.reshape(runs, BLK))
    c1, fixed, far, near, own_nodes, corners, inverses, stiff = call(
        first_kernel,
        (
            whole,
            shape(2, planes, rows, length),
            face_y,
            face_y,
            *(whole_like(block) for block in shell),
        ),
        tuple(pin(block) for block in (populations, relaxation, node_flags, *shell)),
        (hbm,) * 7,
        scratch=(
            pltpu.VMEM((planes, Q, rows, length), F32),
            pltpu.VMEM((planes, rows, length), F32),
            pltpu.VMEM((planes, rows, length), jnp.int32),
            pltpu.SemaphoreType.DMA((planes + 6,)),
        ),
        micros=1.5,
    )
    near_y, far_y = swap(near, far, "inner", "slab")
    numbers = shape(3, runs, BLK)
    low_ids, high_ids, forces = call(
        element_kernel,
        (numbers, numbers, shape(3 * PIECES, 3, runs, BLK)),
        (corners, own_nodes, next_nodes, inverses, stiff),
        (vmem,) * 5,
        scratch=(
            pltpu.VMEM((3, runs, BLK), F32),
            pltpu.VMEM((3, runs, BLK), jnp.int32),
            pltpu.VMEM((3, 3, runs, BLK), F32),
        ),
        micros=0.001,
    )
    far, near = call(
        slab_face_kernel, (face_x, face_x), (c1, fixed, low_ids), (vmem,) * 3, micros=0.001
    )
    near_x, far_x = swap(near, far, "slab", "group")
    nodal = shape(3, node_blocks // half, length)
    (other,) = call(
        functools.partial(spread_kernel, node_blocks),
        (nodal,),
        (low_ids, high_ids, forces),
        (vmem,) * 3,
        micros=0.001,
    )
    corner = shape(CORNER_SLOTS, rows, length)
    far, near = call(
        corner_kernel,
        (corner, corner),
        (far_y, near_y, other),
        (vmem,) * 3,
        scratch=(pltpu.VMEM((2, SLOTS, planes, length), F32),),
        micros=0.3,
    )
    near_c, far_c = swap(near, far, "slab", "group")
    (own,) = call(
        functools.partial(spread_kernel, 0),
        (nodal,),
        (low_ids, high_ids, forces),
        (vmem,) * 3,
        micros=0.8,
    )
    wide = planes + 4
    walls_shape = shape(2, SLOTS, wide, length)
    second_shape = shape(Q, planes + 2, rows, length)
    extended, walls, crossing, second, ends = call(
        inside_kernel,
        (
            shape(Q, wide, rows, length),
            walls_shape,
            shape(2, 5, wide, length),
            second_shape,
            shape(2, 2, rows, length),
        ),
        (c1, fixed, far_y, near_y, far_x, near_x),
        (vmem,) * 6,
        scratch=(
            pltpu.VMEM((2, SLOTS, planes, length), F32),
            pltpu.VMEM((2, SLOTS, rows, length), F32),
        ),
        micros=0.8,
    )
    lines = 4 * slots + 3 * node_blocks
    values, message, _, _ = call(
        second_kernel,
        (whole, shape(lines, BLK), walls_shape, second_shape),
        (
            pin(block_source),
            pin(block_target),
            pin(block_node),
            block_count,
            far_c,
            near_c,
            fixed,
            extended,
            crossing,
            ends,
            own,
            walls,
            second,
        ),
        (hbm,) * 3 + (vmem,) * 10,
        aliases={11: 2, 12: 3},
        scratch=(
            pltpu.VMEM((2, CORNER_SLOTS, rows, length), F32),
            pltpu.VMEM((2, 5, wide, length), F32),
            pltpu.VMEM((planes * half, 3, rows, BLK), F32),
            pltpu.SMEM(block_source.shape, jnp.int32),
            pltpu.SMEM(block_target.shape, jnp.int32),
            pltpu.SMEM(block_node.shape, jnp.int32),
            pltpu.SemaphoreType.DMA((3,)),
        ),
        micros=1.5,
    )
    messages = [message] + [exchange(message, "inner", step) for step in range(1, count)]
    (populations_out,) = call(
        store_kernel,
        (whole,),
        (values,),
        (vmem,),
        out_spaces=(hbm,),
        scratch=(pltpu.SemaphoreType.DMA(()),),
        micros=1.0,
    )
    residual, motion = call(
        functools.partial(final_kernel, count),
        (shape(3, node_dev), shape(3, slots, BLK)),
        messages,
        (vmem,) * count,
        scratch=(pltpu.VMEM((slots, BLK), F32),),
        micros=0.8,
    )
    return populations_out, residual, motion.transpose(1, 0, 2)[None, None]


def solution(mesh):
    return jax.shard_map(
        shards,
        mesh=mesh,
        in_specs=(
            P(None, ("group", "slab"), "inner", None),
            P(("group", "slab"), "inner", None),
            P(("group", "slab"), "inner", None),
            P(None, ("group", "slab", "inner")),
            P(None, ("group", "slab", "inner")),
            P(None, ("group", "slab", "inner")),
            P(("group", "slab", "inner")),
            P(("group", "slab"), "inner", None),
            P(("group", "slab"), "inner", None),
            P(("group", "slab"), "inner", None),
            P(("group", "slab"), "inner"),
        ),
        out_specs=(
            P(None, ("group", "slab"), "inner", None),
            P(None, ("group", "slab", "inner")),
            P(("group", "slab"), "inner", None, None, None),
        ),
        check_vma=False,
    )
```

```python
import functools

import jax
import jax.numpy as jnp
from jax import lax
from jax.experimental import pallas as pl
from jax.experimental.pallas import tpu as pltpu
from jax.sharding import PartitionSpec as P

BLK = 128
VELOCITIES = (
    (0, 0, 0),
    (1, 0, 0),
    (-1, 0, 0),
    (0, 1, 0),
    (0, -1, 0),
    (0, 0, 1),
    (0, 0, -1),
    (1, 1, 0),
    (-1, -1, 0),
    (1, -1, 0),
    (-1, 1, 0),
    (1, 0, 1),
    (-1, 0, -1),
    (1, 0, -1),
    (-1, 0, 1),
    (0, 1, 1),
    (0, -1, -1),
    (0, 1, -1),
    (0, -1, 1),
)
WEIGHTS = (1.0 / 3.0,) + (1.0 / 18.0,) * 6 + (1.0 / 36.0,) * 12
OPPOSITE = (0, 2, 1, 4, 3, 6, 5, 8, 7, 10, 9, 12, 11, 14, 13, 16, 15, 18, 17)
INLET_SPEED = 0.04
LOAD_SCALE = 25.0
COMPLIANCE = 0.5
LAME_RATIO = 2.0
Q = 19
FLAG_SLOT = 19
RATE_SLOT = 20
SLOTS = 21
SIDE_SLOTS = 24
FORCE_SLOT = 6
CORNER_SLOTS = FORCE_SLOT + 3
PIECES = 2
STEP = 4
F32 = jnp.float32
VMEM_BYTES = 48 * 1024 * 1024


def moments(values):
    sums = [values[q] + values[q + 1] for q in range(1, Q, 2)]
    diffs = [values[q] - values[q + 1] for q in range(1, Q, 2)]
    density = values[0]
    for term in sums:
        density = density + term
    flows = []
    for axis in range(3):
        total = None
        for k, q in enumerate(range(1, Q, 2)):
            factor = VELOCITIES[q][axis]
            if factor == 0:
                continue
            if total is None:
                total = diffs[k] if factor > 0 else -diffs[k]
            else:
                total = total + diffs[k] if factor > 0 else total - diffs[k]
        flows.append(total)
    return density, flows[0], flows[1], flows[2]


def collide(values, rate, kind):
    density, flow_x, flow_y, flow_z = moments(values)
    inverse = 1.0 / density
    wall = kind == 1
    inlet = kind == 2
    fluid = kind == 0
    vel = (
        jnp.where(inlet, INLET_SPEED, flow_x * inverse),
        jnp.where(inlet, 0.0, flow_y * inverse),
        jnp.where(inlet, 0.0, flow_z * inverse),
    )
    scale = jnp.where(fluid, density, 1.0)
    rate = jnp.where(fluid, rate, 1.0)
    base = 1.0 - 1.5 * (vel[0] * vel[0] + vel[1] * vel[1] + vel[2] * vel[2])
    weighted = {w: w * scale for w in set(WEIGHTS)}
    out = [None] * Q
    relaxed = values[0] + rate * (weighted[WEIGHTS[0]] * base - values[0])
    out[0] = jnp.where(wall, values[0], relaxed)
    for q in range(1, Q, 2):
        project = None
        for factor, component in zip(VELOCITIES[q], vel):
            if factor == 0:
                continue
            if project is None:
                project = component
            else:
                project = project + component if factor > 0 else project - component
        even = base + 4.5 * (project * project)
        odd = 3.0 * project
        w = weighted[WEIGHTS[q]]
        forward = values[q] + rate * (w * (even + odd) - values[q])
        backward = values[q + 1] + rate * (w * (even - odd) - values[q + 1])
        out[q] = jnp.where(wall, values[q + 1], forward)
        out[q + 1] = jnp.where(wall, values[q], backward)
    return out


def roll_by(block, step, axis):
    if step == 0:
        return block
    return pltpu.roll(block, step % block.shape[axis], axis)


def face_slots(axis, sign):
    picks = []
    for q in range(Q):
        if VELOCITIES[q][axis] * sign >= 0:
            picks.append((q, 0))
        else:
            picks.append((OPPOSITE[q], 1))
    return picks


def mirror(q, axis):
    flipped = tuple(-c if k == axis else c for k, c in enumerate(VELOCITIES[q]))
    return VELOCITIES.index(flipped)


def corner_rows(sign_x, sign_y):
    rows = []
    for q, depth in face_slots(0, sign_x):
        if VELOCITIES[q][1] * sign_y >= 0:
            rows.append((q, depth))
        else:
            rows.append((OPPOSITE[mirror(q, 1)], depth))
    return rows


def first_kernel(
    pops_hbm,
    rate_hbm,
    flags_hbm,
    displacement_hbm,
    elements_hbm,
    shape_hbm,
    stiffness_hbm,
    c1,
    fixed,
    far,
    near,
    displacement,
    elements,
    shape_inverse,
    stiffness,
    pops,
    rate,
    flags,
    sems,
):
    planes, rows = c1.shape[1], c1.shape[2]
    copies = [
        pltpu.make_async_copy(rate_hbm, rate, sems.at[planes]),
        pltpu.make_async_copy(flags_hbm, flags, sems.at[planes + 1]),
    ]
    loads = [
        pltpu.make_async_copy(pops_hbm.at[:, x], pops.at[x], sems.at[x]) for x in range(planes)
    ]
    shell = [
        pltpu.make_async_copy(source, target, sems.at[planes + 2 + k])
        for k, (source, target) in enumerate(
            (
                (displacement_hbm, displacement),
                (elements_hbm, elements),
                (shape_hbm, shape_inverse),
                (stiffness_hbm, stiffness),
            )
        )
    ]
    for copy in loads[:1] + copies + loads[1:] + shell:
        copy.start()
    for copy in copies:
        copy.wait()

    def plane(x, carry):
        pltpu.make_async_copy(pops_hbm.at[:, x], pops.at[x], sems.at[x]).wait()
        kind = flags[x]
        values = [pops[x, q] for q in range(Q)]
        result = collide(values, rate[x], kind)
        for q in range(Q):
            c1[q, x] = roll_by(result[q], VELOCITIES[q][2], 1)
        fixed[0, x] = kind.astype(F32)
        fixed[1, x] = rate[x]
        return carry

    lax.fori_loop(0, planes, plane, 0)

    def pack(out, sign, outside):
        def line(x, carry):
            for slot, (q, depth) in enumerate(face_slots(1, sign)):
                y = rows - 1 - depth if sign > 0 else depth
                out[slot, pl.ds(x, 1)] = c1[q, x, y : y + 1]
            y = rows - 1 if sign > 0 else 0
            for k, slot in enumerate((FLAG_SLOT, RATE_SLOT)):
                out[slot, pl.ds(x, 1)] = fixed[k, x, y : y + 1]
            return carry

        lax.fori_loop(0, planes, line, 0)
        for slot in range(SLOTS, SIDE_SLOTS):
            out[slot] = jnp.zeros(out.shape[1:], F32)
        clear_outside(out, outside)

    pack_pair(pack, "inner", near, far)
    for copy in shell:
        copy.wait()


def clear_outside(out, outside):
    @pl.when(outside)
    def _():
        out[...] = jnp.zeros(out.shape, F32)


def pack_pair(pack, axis, near, far):
    at = lax.axis_index(axis)
    even = lax.rem(at, 2) == 0
    first, last = at == 0, at == lax.axis_size(axis) - 1

    @pl.when(even)
    def _():
        pack(near, 1, last)
        pack(far, -1, first)

    @pl.when(jnp.logical_not(even))
    def _():
        pack(near, -1, first)
        pack(far, 1, last)


def slab_face_kernel(c1, fixed, numbers, far, near):
    del numbers
    planes = c1.shape[1]

    def pack(out, sign, outside):
        for slot, (q, depth) in enumerate(face_slots(0, sign)):
            out[slot] = c1[q, planes - 1 - depth if sign > 0 else depth]
        end = planes - 1 if sign > 0 else 0
        out[FLAG_SLOT] = fixed[0, end]
        out[RATE_SLOT] = fixed[1, end]
        clear_outside(out, outside)

    pack_pair(pack, "slab", near, far)


def gather_both(near, far, both, axis):
    odd = lax.rem(lax.axis_index(axis), 2)
    for slot in range(both.shape[1]):
        both[1 - odd, slot] = near[slot]
        both[odd, slot] = far[slot]


def corner_kernel(far_y, near_y, other, far, near, both):
    planes = near_y.shape[1]
    gather_both(near_y, far_y, both, "inner")

    def pack(out, sign, outside):
        for side, sign_y in enumerate((1, -1)):
            picks = corner_rows(sign, sign_y) + [(FLAG_SLOT, 0), (RATE_SLOT, 0)]
            for row, (slot, depth) in enumerate(picks):
                x = planes - 1 - depth if sign > 0 else depth
                at = 3 * side + row // 8
                out[at, row % 8 : row % 8 + 1] = both[side, slot, x : x + 1]
        for part in range(3):
            out[FORCE_SLOT + part] = other[part]
        clear_outside(out, outside)

    pack_pair(pack, "slab", near, far)


def with_edge(block, step_y, edge):
    rows = block.shape[0]
    sub = lax.broadcasted_iota(jnp.int32, block.shape, 0)
    if step_y > 0:
        return jnp.where(sub == 0, edge, roll_by(block, 1, 0))
    return jnp.where(sub == rows - 1, edge, roll_by(block, -1, 0))


def store_plane(extended, walls, second, at, rate, kind):
    values = []
    for q in range(Q):
        step_x, step_y, _ = VELOCITIES[q]
        block = extended[q, at + 1 - step_x]
        if step_y != 0:
            edge = walls[0 if step_y > 0 else 1, q, pl.ds(at + 1 - step_x, 1)]
            block = with_edge(block, step_y, edge)
        values.append(block)
    result = collide(values, rate, kind)
    for q in range(Q):
        second[q, at] = roll_by(result[q], VELOCITIES[q][2], 1)


def inside_kernel(
    c1,
    fixed,
    far_y,
    near_y,
    far_x,
    near_x,
    extended,
    walls,
    crossing,
    second,
    ends,
    both_y,
    both_x,
):
    planes, rows, _ = c1.shape[1:]
    wide = planes + 4
    gather_both(near_y, far_y, both_y, "inner")
    gather_both(near_x, far_x, both_x, "slab")
    for q in range(Q):
        for x in range(planes):
            extended[q, x + 2] = c1[q, x]
        extended[q, 1] = both_x[0, q]
        extended[q, planes + 2] = both_x[1, q]
        if VELOCITIES[q][0] > 0:
            extended[q, 0] = both_x[0, OPPOSITE[q]]
        if VELOCITIES[q][0] < 0:
            extended[q, planes + 3] = both_x[1, OPPOSITE[q]]
    for end in range(2):
        ends[end, 0] = both_x[end, FLAG_SLOT]
        ends[end, 1] = both_x[end, RATE_SLOT]

    for side, sign in enumerate((1, -1)):
        y = 0 if sign > 0 else rows - 1
        for slot in range(SLOTS):
            walls[side, slot, 2 : planes + 2] = both_y[side, slot]
        place = 0
        for q in range(Q):
            if VELOCITIES[q][1] != -sign:
                continue
            for x in range(wide):
                crossing[side, place, x : x + 1] = extended[q, x, y : y + 1]
            place += 1

    def inside_plane(x, carry):
        store_plane(extended, walls, second, x + 1, fixed[1, x], fixed[0, x])
        return carry

    lax.fori_loop(1, planes - 1, inside_plane, 0)


def second_kernel(
    block_source_hbm,
    block_target_hbm,
    block_node_hbm,
    block_count,
    far,
    near,
    fixed,
    extended,
    crossing,
    ends,
    internal_own,
    walls_in,
    second_in,
    out,
    message,
    walls,
    second,
    both,
    edges,
    loads,
    block_source,
    block_target,
    block_node,
    sems,
):
    del walls_in, second_in
    copies = [
        pltpu.make_async_copy(block_source_hbm, block_source, sems.at[0]),
        pltpu.make_async_copy(block_target_hbm, block_target, sems.at[1]),
        pltpu.make_async_copy(block_node_hbm, block_node, sems.at[2]),
    ]
    for copy in copies:
        copy.start()
    planes, rows, length = out.shape[1:]
    half = length // BLK
    slots = block_source.shape[2]
    wide = planes + 4
    slab = lax.axis_index("slab")
    inner = lax.axis_index("inner")
    slab_end = lax.axis_size("slab") - 1
    inner_end = lax.axis_size("inner") - 1
    gather_both(near, far, both, "slab")

    for side, sign in enumerate((1, -1)):
        for end, sign_x in enumerate((1, -1)):
            for row, (slot, depth) in enumerate(corner_rows(sign_x, sign)):
                at = (1 - depth) if sign_x > 0 else planes + 2 + depth
                source = 3 * side + row // 8
                walls[side, slot, at : at + 1] = both[end, source, row % 8 : row % 8 + 1]
            at = 1 if sign_x > 0 else planes + 2
            for row in (FLAG_SLOT, RATE_SLOT):
                source = 3 * side + row // 8
                walls[side, row, at : at + 1] = both[end, source, row % 8 : row % 8 + 1]

    def edge_planes(end, carry):
        x = end * (planes - 1)
        store_plane(extended, walls, second, x + 1, fixed[1, x], fixed[0, x])
        store_plane(extended, walls, second, end * (planes + 1), ends[end, 1], ends[end, 0])
        return carry

    lax.fori_loop(0, 2, edge_planes, 0)

    @pl.when(slab == 0)
    def _():
        for q in range(Q):
            if VELOCITIES[q][0] > 0:
                second[q, 0] = jnp.zeros((rows, length), F32)

    @pl.when(slab == slab_end)
    def _():
        for q in range(Q):
            if VELOCITIES[q][0] < 0:
                second[q, planes + 1] = jnp.zeros((rows, length), F32)

    across = lax.broadcasted_iota(jnp.int32, (wide, length), 0)
    hidden = ((across <= 1) & (slab == 0)) | ((across >= planes + 2) & (slab == slab_end))
    for side, sign, outside in ((0, 1, inner == 0), (1, -1, inner == inner_end)):
        values = []
        place = 0
        for q in range(Q):
            step_x, step_y, _ = VELOCITIES[q]
            if step_y == 0:
                block = walls[side, q]
            elif step_y == sign:
                block = walls[side, OPPOSITE[q]]
            else:
                block = crossing[side, place]
                place += 1
            values.append(roll_by(block, step_x, 0))
        result = collide(values, walls[side, RATE_SLOT], walls[side, FLAG_SLOT])
        place = 0
        for q in range(Q):
            if VELOCITIES[q][1] == sign:
                kept = jnp.where(hidden | outside, 0.0, result[q])
                edges[side, place] = roll_by(kept, VELOCITIES[q][2], 1)
                place += 1

    def plane_two(x, carry):
        values = []
        places = {1: 0, -1: 0}
        for q in range(Q):
            step_x, step_y, _ = VELOCITIES[q]
            block = second[q, x + 1 - step_x]
            if step_y != 0:
                edge = edges[0 if step_y > 0 else 1, places[step_y], pl.ds(x + 2 - step_x, 1)]
                places[step_y] += 1
                block = with_edge(block, step_y, edge)
            values.append(block)
            out[q, x] = block
        density, flow_x, flow_y, flow_z = moments(values)
        parts = (
            LOAD_SCALE * flow_x,
            LOAD_SCALE * (flow_y + (density - 1.0) / 3.0),
            LOAD_SCALE * flow_z,
        )
        for part in range(3):
            for piece in range(half):
                loads[x * half + piece, part] = parts[part][:, piece * BLK : (piece + 1) * BLK]
        return carry

    lax.fori_loop(0, planes, plane_two, 0)

    for copy in copies:
        copy.wait()
    node_blocks = internal_own.shape[1] * half
    live = jnp.broadcast_to(block_count[...], (1, BLK))
    lanes_of = lax.broadcasted_iota(jnp.int32, (1, BLK), 1) // (BLK // slots)
    all_keys = jnp.full((1, BLK), -1, jnp.int32)
    for k in range(slots):
        run = block_source[0, 0, k]
        x = run // (rows * half)
        left = run - x * (rows * half)
        y = left // half
        piece = left - y * half
        for part in range(3):
            message[3 * k + part] = loads[x * half + piece, part, pl.ds(y, 1)]
        key = block_target[0, 0, k] * node_blocks + block_node[0, 0, k]
        all_keys = jnp.where((lanes_of == k) & (live > k), key, all_keys)
    message[3 * slots] = all_keys.astype(F32)
    for part in range(3):
        start = 3 * slots + 1 + part * node_blocks
        for piece in range(half):
            at = piece * rows
            lanes = slice(piece * BLK, (piece + 1) * BLK)
            message[start + at : start + at + rows, 0] = (
                internal_own[part, :, lanes] + both[0, FORCE_SLOT + part, :, lanes]
            )


def element_kernel(
    elements, displacement, next_nodes, shape_inverse, stiffness, low_ids, high_ids, forces, shapes,
    numbers, corners,
):
    node_dev = displacement.shape[1]
    node_blocks = node_dev // BLK
    runs = elements.shape[1] // BLK
    for j in range(runs):
        lanes = slice(j * BLK, (j + 1) * BLK)
        for row in range(3):
            numbers[row, j : j + 1] = elements[row : row + 1, lanes]
            shapes[row, j : j + 1] = shape_inverse[row : row + 1, lanes]
    for row in range(3):
        low_ids[row] = (numbers[row] & (BLK - 1)).astype(F32)
        high_ids[row] = (numbers[row] >> 7).astype(F32)

    def gather(group, carry):
        rows = pl.ds(pl.multiple_of(group * 8, 8), 8)
        low = [numbers[corner, rows] & (BLK - 1) for corner in range(3)]
        high = [numbers[corner, rows] >> 7 for corner in range(3)]
        for corner in range(3):
            nodes = [jnp.zeros((8, BLK), F32)] * 3
            for block in range(2 * node_blocks):
                source = displacement if block < node_blocks else next_nodes
                start = (block % node_blocks) * BLK
                here = high[corner] == block
                for part in range(3):
                    row = source[part : part + 1, start : start + BLK]
                    picked = jnp.take_along_axis(
                        jnp.broadcast_to(row, (8, BLK)),
                        low[corner],
                        axis=1,
                        mode="promise_in_bounds",
                    )
                    nodes[part] = jnp.where(here, picked, nodes[part])
            for part in range(3):
                corners[corner, part, rows] = nodes[part]
        return carry

    lax.fori_loop(0, runs // 8, gather, 0)

    first, second, third = [[corners[c, p] for p in range(3)] for c in range(3)]
    diag_a = shapes[0]
    skew_b = shapes[1]
    diag_c = shapes[2]
    stiff = stiffness[...]
    edge_one = [second[p] - first[p] for p in range(3)]
    edge_two = [third[p] - first[p] for p in range(3)]
    one = [diag_a * edge_one[p] for p in range(3)]
    two = [skew_b * edge_one[p] + diag_c * edge_two[p] for p in range(3)]
    one[0] = one[0] + 1.0
    two[1] = two[1] + 1.0
    aa = one[0] * one[0] + one[1] * one[1] + one[2] * one[2]
    ab = one[0] * two[0] + one[1] * two[1] + one[2] * two[2]
    bb = two[0] * two[0] + two[1] * two[1] + two[2] * two[2]
    determinant = aa * bb - ab * ab
    scale = 1.0 / determinant
    inverse_aa = bb * scale
    inverse_ab = -ab * scale
    inverse_bb = aa * scale
    pressure = LAME_RATIO * (0.5 * jnp.log(determinant))
    for p in range(3):
        pulled_one = one[p] * inverse_aa + two[p] * inverse_ab
        pulled_two = one[p] * inverse_ab + two[p] * inverse_bb
        stress_one = stiff * (one[p] - pulled_one + pressure * pulled_one)
        stress_two = stiff * (two[p] - pulled_two + pressure * pulled_two)
        force_one = diag_a * stress_one + skew_b * stress_two
        force_two = diag_c * stress_two
        for corner, force in enumerate((-(force_one + force_two), force_one, force_two)):
            rest = force
            for part in range(PIECES):
                piece = rest.astype(jnp.bfloat16).astype(F32)
                rest = rest - piece
                forces[part * 3 + p, corner] = piece


def spread_kernel(base, low_ids, high_ids, forces, out):
    runs = low_ids.shape[1]
    parts, rows, length = out.shape
    pieces = length // BLK
    slots = pieces * rows
    kind = jnp.bfloat16
    tile = 16
    slot_ids = lax.broadcasted_iota(jnp.int32, (slots, BLK), 0).astype(F32) + base
    slot_ids = slot_ids.astype(kind)
    lane_ids = lax.broadcasted_iota(jnp.int32, (BLK, BLK), 0).astype(F32).astype(kind)
    ones = jnp.ones((BLK, BLK), kind)
    none = jnp.zeros((BLK, BLK), kind)
    blank = jnp.zeros((slots, BLK), kind)

    def tall_row(row, count):
        block = jnp.broadcast_to(row, (tile, BLK)).astype(kind)
        return jnp.concatenate([block] * (count // tile), axis=0)

    total = None
    for corner in range(3):
        for first in range(0, runs, STEP):
            left = [[] for _ in range(parts * PIECES)]
            right = []
            for j in range(first, min(first + STEP, runs)):
                row = slice(j, j + 1)
                here = slot_ids == tall_row(high_ids[corner, row], slots)
                there = lane_ids == tall_row(low_ids[corner, row], BLK)
                right.append(jnp.where(there, ones, none))
                for part in range(parts * PIECES):
                    left[part].append(
                        jnp.where(here, tall_row(forces[part, corner, row], slots), blank)
                    )
            tall = jnp.concatenate([jnp.concatenate(part, axis=1) for part in left], axis=0)
            wide = jnp.concatenate(right, axis=1)
            product = lax.dot_general(
                tall, wide, (((1,), (1,)), ((), ())), preferred_element_type=F32
            )
            total = product if total is None else total + product
    for p in range(parts):
        summed = total[p * slots : (p + 1) * slots]
        for part in range(1, PIECES):
            start = (parts * part + p) * slots
            summed = summed + total[start : start + slots]
        for piece in range(pieces):
            out[p, :, piece * BLK : (piece + 1) * BLK] = summed[piece * rows : (piece + 1) * rows]


def store_kernel(values, out_hbm, sem):
    store = pltpu.make_async_copy(values, out_hbm, sem)
    store.start()
    store.wait()


def final_kernel(count, *refs):
    messages = refs[:count]
    residual, motion, keys = refs[count:]
    slots = keys.shape[0]
    node_blocks = residual.shape[1] // BLK
    inner = lax.axis_index("inner")
    width = BLK // slots

    def key_of(message, k):
        return jnp.broadcast_to(message[3 * slots][:, k * width : k * width + 1], (1, BLK))

    mine = messages[0]
    for k in range(slots):
        keys[k : k + 1] = key_of(mine, k)
    wanted = keys[...]
    node_ids = lax.broadcasted_iota(jnp.int32, (node_blocks, BLK), 0)
    own_ids = (node_ids + inner * node_blocks).astype(F32)
    external = [jnp.zeros((node_blocks, BLK), F32)] * 3
    moved = [jnp.zeros((slots, BLK), F32)] * 3
    for message in messages:
        for k in range(slots):
            key = key_of(message, k)
            here = own_ids == key
            same = wanted == key
            for part in range(3):
                row = message[3 * k + part]
                external[part] = external[part] + jnp.where(here, row, 0.0)
                moved[part] = moved[part] + jnp.where(same, row, 0.0)
    for step, message in enumerate(messages):
        sender = partner_of(inner, step, count)
        for b in range(node_blocks):
            key = jnp.broadcast_to(sender * node_blocks + b, (1, BLK)).astype(F32)
            same = wanted == key
            for part in range(3):
                at = 3 * slots + 1 + part * node_blocks + b
                moved[part] = moved[part] - jnp.where(same, message[at], 0.0)
    live = wanted >= 0.0
    for part in range(3):
        start = 3 * slots + 1 + part * node_blocks
        left = external[part] - mine[start : start + node_blocks, 0]
        for b in range(node_blocks):
            residual[part : part + 1, b * BLK : (b + 1) * BLK] = left[b : b + 1]
        motion[part] = jnp.where(live, COMPLIANCE * moved[part], 0.0)


def call(kernel, outs, operands, spaces, scratch=(), out_spaces=None, micros=1.0, aliases=None):
    spec = lambda space: pl.BlockSpec(memory_space=space)
    out_spaces = out_spaces or (pltpu.VMEM,) * len(outs)
    return pl.pallas_call(
        kernel,
        out_shape=outs,
        in_specs=[spec(space) for space in spaces],
        out_specs=tuple(spec(space) for space in out_spaces),
        scratch_shapes=list(scratch),
        input_output_aliases=aliases or {},
        compiler_params=pltpu.CompilerParams(vmem_limit_bytes=VMEM_BYTES),
        cost_estimate=pl.CostEstimate(
            flops=0, bytes_accessed=int(micros * 3.6e6), transcendentals=0
        ),
    )(*operands)


def partner_of(at, step, count):
    if count & (count - 1) == 0:
        return at ^ step
    return (at + count - step) % count


def exchange(block, axis, step):
    count = lax.axis_size(axis)
    return lax.ppermute(block, axis, [(partner_of(i, step, count), i) for i in range(count)])


def around(block, axis, step):
    count = lax.axis_size(axis)
    return lax.ppermute(block, axis, [(i, (i + step) % count) for i in range(count)])


def swap(near, far, axis, beside):
    count, others = lax.axis_size(axis), lax.axis_size(beside)
    routes = []
    for start in (0, 1):
        route = []
        for other in range(others):
            for i in range(count):
                j = i + 1 if i % 2 == start else i - 1
                to = other
                if not 0 <= j < count:
                    j = i
                    to = other ^ 1 if others % 2 == 0 else other
                route.append((other * count + i, to * count + j))
        routes.append(route)
    axes = (beside, axis)
    return lax.ppermute(near, axes, routes[0]), lax.ppermute(far, axes, routes[1])


def shards(
    populations,
    relaxation,
    node_flags,
    displacement,
    elements,
    shape_inverse,
    stiffness,
    block_source,
    block_target,
    block_node,
    block_count,
):
    planes, rows, length = populations.shape[1:]
    half = length // BLK
    node_dev = displacement.shape[1]
    node_blocks = node_dev // BLK
    runs = stiffness.shape[0] // BLK
    slots = block_source.shape[2]
    count = lax.axis_size("inner")
    shape = lambda *dims: jax.ShapeDtypeStruct(dims, F32)
    whole = shape(*populations.shape)
    vmem, hbm, smem = pltpu.VMEM, pltpu.HBM, pltpu.SMEM

    next_nodes = around(displacement, "slab", -1)
    face_y = shape(SIDE_SLOTS, planes, length)
    face_x = shape(SLOTS, rows, length)
    pin = lambda block: pltpu.with_memory_space_constraint(block, hbm)
    whole_like = lambda block: jax.ShapeDtypeStruct(block.shape, block.dtype)
    shell = (displacement, elements, shape_inverse, stiffness.reshape(runs, BLK))
    c1, fixed, far, near, own_nodes, corners, inverses, stiff = call(
        first_kernel,
        (
            whole,
            shape(2, planes, rows, length),
            face_y,
            face_y,
            *(whole_like(block) for block in shell),
        ),
        tuple(pin(block) for block in (populations, relaxation, node_flags, *shell)),
        (hbm,) * 7,
        scratch=(
            pltpu.VMEM((planes, Q, rows, length), F32),
            pltpu.VMEM((planes, rows, length), F32),
            pltpu.VMEM((planes, rows, length), jnp.int32),
            pltpu.SemaphoreType.DMA((planes + 6,)),
        ),
        micros=1.5,
    )
    near_y, far_y = swap(near, far, "inner", "slab")
    numbers = shape(3, runs, BLK)
    low_ids, high_ids, forces = call(
        element_kernel,
        (numbers, numbers, shape(3 * PIECES, 3, runs, BLK)),
        (corners, own_nodes, next_nodes, inverses, stiff),
        (vmem,) * 5,
        scratch=(
            pltpu.VMEM((3, runs, BLK), F32),
            pltpu.VMEM((3, runs, BLK), jnp.int32),
            pltpu.VMEM((3, 3, runs, BLK), F32),
        ),
        micros=0.001,
    )
    far, near = call(
        slab_face_kernel, (face_x, face_x), (c1, fixed, low_ids), (vmem,) * 3, micros=0.001
    )
    near_x, far_x = swap(near, far, "slab", "group")
    nodal = shape(3, node_blocks // half, length)
    (other,) = call(
        functools.partial(spread_kernel, node_blocks),
        (nodal,),
        (low_ids, high_ids, forces),
        (vmem,) * 3,
        micros=0.001,
    )
    corner = shape(CORNER_SLOTS, rows, length)
    far, near = call(
        corner_kernel,
        (corner, corner),
        (far_y, near_y, other),
        (vmem,) * 3,
        scratch=(pltpu.VMEM((2, SLOTS, planes, length), F32),),
        micros=0.3,
    )
    near_c, far_c = swap(near, far, "slab", "group")
    (own,) = call(
        functools.partial(spread_kernel, 0),
        (nodal,),
        (low_ids, high_ids, forces),
        (vmem,) * 3,
        micros=0.8,
    )
    wide = planes + 4
    walls_shape = shape(2, SLOTS, wide, length)
    second_shape = shape(Q, planes + 2, rows, length)
    extended, walls, crossing, second, ends = call(
        inside_kernel,
        (
            shape(Q, wide, rows, length),
            walls_shape,
            shape(2, 5, wide, length),
            second_shape,
            shape(2, 2, rows, length),
        ),
        (c1, fixed, far_y, near_y, far_x, near_x),
        (vmem,) * 6,
        scratch=(
            pltpu.VMEM((2, SLOTS, planes, length), F32),
            pltpu.VMEM((2, SLOTS, rows, length), F32),
        ),
        micros=0.8,
    )
    lines = 3 * slots + 1 + 3 * node_blocks
    values, message, _, _ = call(
        second_kernel,
        (whole, shape(lines, 1, BLK), walls_shape, second_shape),
        (
            pin(block_source),
            pin(block_target),
            pin(block_node),
            block_count,
            far_c,
            near_c,
            fixed,
            extended,
            crossing,
            ends,
            own,
            walls,
            second,
        ),
        (hbm,) * 3 + (vmem,) * 10,
        aliases={11: 2, 12: 3},
        scratch=(
            pltpu.VMEM((2, CORNER_SLOTS, rows, length), F32),
            pltpu.VMEM((2, 5, wide, length), F32),
            pltpu.VMEM((planes * half, 3, rows, BLK), F32),
            pltpu.SMEM(block_source.shape, jnp.int32),
            pltpu.SMEM(block_target.shape, jnp.int32),
            pltpu.SMEM(block_node.shape, jnp.int32),
            pltpu.SemaphoreType.DMA((3,)),
        ),
        micros=1.5,
    )
    messages = [message] + [exchange(message, "inner", step) for step in range(1, count)]
    (populations_out,) = call(
        store_kernel,
        (whole,),
        (values,),
        (vmem,),
        out_spaces=(hbm,),
        scratch=(pltpu.SemaphoreType.DMA(()),),
        micros=1.0,
    )
    residual, motion = call(
        functools.partial(final_kernel, count),
        (shape(3, node_dev), shape(3, slots, BLK)),
        messages,
        (vmem,) * count,
        scratch=(pltpu.VMEM((slots, BLK), F32),),
        micros=0.8,
    )
    return populations_out, residual, motion.transpose(1, 0, 2)[None, None]


def solution(mesh):
    return jax.shard_map(
        shards,
        mesh=mesh,
        in_specs=(
            P(None, ("group", "slab"), "inner", None),
            P(("group", "slab"), "inner", None),
            P(("group", "slab"), "inner", None),
            P(None, ("group", "slab", "inner")),
            P(None, ("group", "slab", "inner")),
            P(None, ("group", "slab", "inner")),
            P(("group", "slab", "inner")),
            P(("group", "slab"), "inner", None),
            P(("group", "slab"), "inner", None),
            P(("group", "slab"), "inner", None),
            P(("group", "slab"), "inner"),
        ),
        out_specs=(
            P(None, ("group", "slab"), "inner", None),
            P(None, ("group", "slab", "inner")),
            P(("group", "slab"), "inner", None, None, None),
        ),
        check_vma=False,
    )
```

```python
import functools

import jax
import jax.numpy as jnp
from jax import lax
from jax.experimental import pallas as pl
from jax.experimental.pallas import tpu as pltpu
from jax.sharding import PartitionSpec as P

BLK = 128
VELOCITIES = (
    (0, 0, 0),
    (1, 0, 0),
    (-1, 0, 0),
    (0, 1, 0),
    (0, -1, 0),
    (0, 0, 1),
    (0, 0, -1),
    (1, 1, 0),
    (-1, -1, 0),
    (1, -1, 0),
    (-1, 1, 0),
    (1, 0, 1),
    (-1, 0, -1),
    (1, 0, -1),
    (-1, 0, 1),
    (0, 1, 1),
    (0, -1, -1),
    (0, 1, -1),
    (0, -1, 1),
)
WEIGHTS = (1.0 / 3.0,) + (1.0 / 18.0,) * 6 + (1.0 / 36.0,) * 12
OPPOSITE = (0, 2, 1, 4, 3, 6, 5, 8, 7, 10, 9, 12, 11, 14, 13, 16, 15, 18, 17)
INLET_SPEED = 0.04
LOAD_SCALE = 25.0
COMPLIANCE = 0.5
LAME_RATIO = 2.0
Q = 19
FLAG_SLOT = 19
RATE_SLOT = 20
SLOTS = 21
SIDE_SLOTS = 24
FORCE_SLOT = 6
CORNER_SLOTS = FORCE_SLOT + 3
PIECES = 2
STEP = 4
F32 = jnp.float32
VMEM_BYTES = 48 * 1024 * 1024


def moments(values):
    sums = [values[q] + values[q + 1] for q in range(1, Q, 2)]
    diffs = [values[q] - values[q + 1] for q in range(1, Q, 2)]
    density = values[0]
    for term in sums:
        density = density + term
    flows = []
    for axis in range(3):
        total = None
        for k, q in enumerate(range(1, Q, 2)):
            factor = VELOCITIES[q][axis]
            if factor == 0:
                continue
            if total is None:
                total = diffs[k] if factor > 0 else -diffs[k]
            else:
                total = total + diffs[k] if factor > 0 else total - diffs[k]
        flows.append(total)
    return density, flows[0], flows[1], flows[2]


def collide(values, rate, kind):
    density, flow_x, flow_y, flow_z = moments(values)
    inverse = 1.0 / density
    wall = kind == 1
    inlet = kind == 2
    fluid = kind == 0
    vel = (
        jnp.where(inlet, INLET_SPEED, flow_x * inverse),
        jnp.where(inlet, 0.0, flow_y * inverse),
        jnp.where(inlet, 0.0, flow_z * inverse),
    )
    scale = jnp.where(fluid, density, 1.0)
    rate = jnp.where(fluid, rate, 1.0)
    base = 1.0 - 1.5 * (vel[0] * vel[0] + vel[1] * vel[1] + vel[2] * vel[2])
    weighted = {w: w * scale for w in set(WEIGHTS)}
    out = [None] * Q
    relaxed = values[0] + rate * (weighted[WEIGHTS[0]] * base - values[0])
    out[0] = jnp.where(wall, values[0], relaxed)
    for q in range(1, Q, 2):
        project = None
        for factor, component in zip(VELOCITIES[q], vel):
            if factor == 0:
                continue
            if project is None:
                project = component
            else:
                project = project + component if factor > 0 else project - component
        even = base + 4.5 * (project * project)
        odd = 3.0 * project
        w = weighted[WEIGHTS[q]]
        forward = values[q] + rate * (w * (even + odd) - values[q])
        backward = values[q + 1] + rate * (w * (even - odd) - values[q + 1])
        out[q] = jnp.where(wall, values[q + 1], forward)
        out[q + 1] = jnp.where(wall, values[q], backward)
    return out


def roll_by(block, step, axis):
    if step == 0:
        return block
    return pltpu.roll(block, step % block.shape[axis], axis)


def face_slots(axis, sign):
    picks = []
    for q in range(Q):
        if VELOCITIES[q][axis] * sign >= 0:
            picks.append((q, 0))
        else:
            picks.append((OPPOSITE[q], 1))
    return picks


def mirror(q, axis):
    flipped = tuple(-c if k == axis else c for k, c in enumerate(VELOCITIES[q]))
    return VELOCITIES.index(flipped)


def corner_rows(sign_x, sign_y):
    rows = []
    for q, depth in face_slots(0, sign_x):
        if VELOCITIES[q][1] * sign_y >= 0:
            rows.append((q, depth))
        else:
            rows.append((OPPOSITE[mirror(q, 1)], depth))
    return rows


def first_kernel(
    pops_hbm,
    rate_hbm,
    flags_hbm,
    displacement_hbm,
    elements_hbm,
    shape_hbm,
    stiffness_hbm,
    c1,
    fixed,
    near,
    far,
    displacement,
    elements,
    shape_inverse,
    stiffness,
    pops,
    rate,
    flags,
    sems,
):
    planes, rows = c1.shape[1], c1.shape[2]
    copies = [
        pltpu.make_async_copy(rate_hbm, rate, sems.at[planes]),
        pltpu.make_async_copy(flags_hbm, flags, sems.at[planes + 1]),
    ]
    loads = [
        pltpu.make_async_copy(pops_hbm.at[:, x], pops.at[x], sems.at[x]) for x in range(planes)
    ]
    shell = [
        pltpu.make_async_copy(source, target, sems.at[planes + 2 + k])
        for k, (source, target) in enumerate(
            (
                (displacement_hbm, displacement),
                (elements_hbm, elements),
                (shape_hbm, shape_inverse),
                (stiffness_hbm, stiffness),
            )
        )
    ]
    for copy in loads[:1] + copies + loads[1:] + shell:
        copy.start()
    for copy in copies:
        copy.wait()

    def plane(x, carry):
        pltpu.make_async_copy(pops_hbm.at[:, x], pops.at[x], sems.at[x]).wait()
        kind = flags[x]
        values = [pops[x, q] for q in range(Q)]
        result = collide(values, rate[x], kind)
        for q in range(Q):
            c1[q, x] = roll_by(result[q], VELOCITIES[q][2], 1)
        fixed[0, x] = kind.astype(F32)
        fixed[1, x] = rate[x]
        return carry

    lax.fori_loop(0, planes, plane, 0)

    def pack(out, sign, outside):
        def line(x, carry):
            for slot, (q, depth) in enumerate(face_slots(1, sign)):
                y = rows - 1 - depth if sign > 0 else depth
                out[slot, pl.ds(x, 1)] = c1[q, x, y : y + 1]
            y = rows - 1 if sign > 0 else 0
            for k, slot in enumerate((FLAG_SLOT, RATE_SLOT)):
                out[slot, pl.ds(x, 1)] = fixed[k, x, y : y + 1]
            return carry

        lax.fori_loop(0, planes, line, 0)
        for slot in range(SLOTS, SIDE_SLOTS):
            out[slot] = jnp.zeros(out.shape[1:], F32)
        clear_outside(out, outside)

    pack_pair(pack, "inner", near, far)
    for copy in shell:
        copy.wait()


def clear_outside(out, outside):
    @pl.when(outside)
    def _():
        out[...] = jnp.zeros(out.shape, F32)


def pack_pair(pack, axis, near, far):
    at = lax.axis_index(axis)
    even = lax.rem(at, 2) == 0
    first, last = at == 0, at == lax.axis_size(axis) - 1

    @pl.when(even)
    def _():
        pack(near, 1, last)
        pack(far, -1, first)

    @pl.when(jnp.logical_not(even))
    def _():
        pack(near, -1, first)
        pack(far, 1, last)


def slab_face_kernel(c1, fixed, numbers, near, far):
    del numbers
    planes = c1.shape[1]

    def pack(out, sign, outside):
        for slot, (q, depth) in enumerate(face_slots(0, sign)):
            out[slot] = c1[q, planes - 1 - depth if sign > 0 else depth]
        end = planes - 1 if sign > 0 else 0
        out[FLAG_SLOT] = fixed[0, end]
        out[RATE_SLOT] = fixed[1, end]
        clear_outside(out, outside)

    pack_pair(pack, "slab", near, far)


def gather_both(near, far, both, axis):
    odd = lax.rem(lax.axis_index(axis), 2)
    for slot in range(both.shape[1]):
        both[1 - odd, slot] = near[slot]
        both[odd, slot] = far[slot]


def corner_kernel(near_y, far_y, other, near, far, both):
    planes = near_y.shape[1]
    gather_both(near_y, far_y, both, "inner")

    def pack(out, sign, outside):
        for side, sign_y in enumerate((1, -1)):
            picks = corner_rows(sign, sign_y) + [(FLAG_SLOT, 0), (RATE_SLOT, 0)]
            for row, (slot, depth) in enumerate(picks):
                x = planes - 1 - depth if sign > 0 else depth
                at = 3 * side + row // 8
                out[at, row % 8 : row % 8 + 1] = both[side, slot, x : x + 1]
        for part in range(3):
            out[FORCE_SLOT + part] = other[part]
        clear_outside(out, outside)

    pack_pair(pack, "slab", near, far)


def with_edge(block, step_y, edge):
    rows = block.shape[0]
    sub = lax.broadcasted_iota(jnp.int32, block.shape, 0)
    if step_y > 0:
        return jnp.where(sub == 0, edge, roll_by(block, 1, 0))
    return jnp.where(sub == rows - 1, edge, roll_by(block, -1, 0))


def store_plane(extended, walls, second, at, rate, kind):
    values = []
    for q in range(Q):
        step_x, step_y, _ = VELOCITIES[q]
        block = extended[q, at + 1 - step_x]
        if step_y != 0:
            edge = walls[0 if step_y > 0 else 1, q, pl.ds(at + 1 - step_x, 1)]
            block = with_edge(block, step_y, edge)
        values.append(block)
    result = collide(values, rate, kind)
    for q in range(Q):
        second[q, at] = roll_by(result[q], VELOCITIES[q][2], 1)


def inside_kernel(
    c1,
    fixed,
    near_y,
    far_y,
    near_x,
    far_x,
    extended,
    walls,
    crossing,
    second,
    ends,
    both_y,
    both_x,
):
    planes, rows, _ = c1.shape[1:]
    wide = planes + 4
    gather_both(near_y, far_y, both_y, "inner")
    gather_both(near_x, far_x, both_x, "slab")
    for q in range(Q):
        for x in range(planes):
            extended[q, x + 2] = c1[q, x]
        extended[q, 1] = both_x[0, q]
        extended[q, planes + 2] = both_x[1, q]
        if VELOCITIES[q][0] > 0:
            extended[q, 0] = both_x[0, OPPOSITE[q]]
        if VELOCITIES[q][0] < 0:
            extended[q, planes + 3] = both_x[1, OPPOSITE[q]]
    for end in range(2):
        ends[end, 0] = both_x[end, FLAG_SLOT]
        ends[end, 1] = both_x[end, RATE_SLOT]

    for side, sign in enumerate((1, -1)):
        y = 0 if sign > 0 else rows - 1
        for slot in range(SLOTS):
            walls[side, slot, 2 : planes + 2] = both_y[side, slot]
        place = 0
        for q in range(Q):
            if VELOCITIES[q][1] != -sign:
                continue
            for x in range(wide):
                crossing[side, place, x : x + 1] = extended[q, x, y : y + 1]
            place += 1

    def inside_plane(x, carry):
        store_plane(extended, walls, second, x + 1, fixed[1, x], fixed[0, x])
        return carry

    lax.fori_loop(1, planes - 1, inside_plane, 0)


def second_kernel(
    block_source_hbm,
    block_target_hbm,
    block_node_hbm,
    block_count,
    near,
    far,
    fixed,
    extended,
    crossing,
    ends,
    internal_own,
    walls_in,
    second_in,
    out,
    message,
    walls,
    second,
    both,
    edges,
    loads,
    block_source,
    block_target,
    block_node,
    sems,
):
    del walls_in, second_in
    copies = [
        pltpu.make_async_copy(block_source_hbm, block_source, sems.at[0]),
        pltpu.make_async_copy(block_target_hbm, block_target, sems.at[1]),
        pltpu.make_async_copy(block_node_hbm, block_node, sems.at[2]),
    ]
    for copy in copies:
        copy.start()
    planes, rows, length = out.shape[1:]
    half = length // BLK
    slots = block_source.shape[2]
    wide = planes + 4
    slab = lax.axis_index("slab")
    inner = lax.axis_index("inner")
    slab_end = lax.axis_size("slab") - 1
    inner_end = lax.axis_size("inner") - 1
    gather_both(near, far, both, "slab")

    for side, sign in enumerate((1, -1)):
        for end, sign_x in enumerate((1, -1)):
            for row, (slot, depth) in enumerate(corner_rows(sign_x, sign)):
                at = (1 - depth) if sign_x > 0 else planes + 2 + depth
                source = 3 * side + row // 8
                walls[side, slot, at : at + 1] = both[end, source, row % 8 : row % 8 + 1]
            at = 1 if sign_x > 0 else planes + 2
            for row in (FLAG_SLOT, RATE_SLOT):
                source = 3 * side + row // 8
                walls[side, row, at : at + 1] = both[end, source, row % 8 : row % 8 + 1]

    def edge_planes(end, carry):
        x = end * (planes - 1)
        store_plane(extended, walls, second, x + 1, fixed[1, x], fixed[0, x])
        store_plane(extended, walls, second, end * (planes + 1), ends[end, 1], ends[end, 0])
        return carry

    lax.fori_loop(0, 2, edge_planes, 0)

    @pl.when(slab == 0)
    def _():
        for q in range(Q):
            if VELOCITIES[q][0] > 0:
                second[q, 0] = jnp.zeros((rows, length), F32)

    @pl.when(slab == slab_end)
    def _():
        for q in range(Q):
            if VELOCITIES[q][0] < 0:
                second[q, planes + 1] = jnp.zeros((rows, length), F32)

    across = lax.broadcasted_iota(jnp.int32, (wide, length), 0)
    hidden = ((across <= 1) & (slab == 0)) | ((across >= planes + 2) & (slab == slab_end))
    for side, sign, outside in ((0, 1, inner == 0), (1, -1, inner == inner_end)):
        values = []
        place = 0
        for q in range(Q):
            step_x, step_y, _ = VELOCITIES[q]
            if step_y == 0:
                block = walls[side, q]
            elif step_y == sign:
                block = walls[side, OPPOSITE[q]]
            else:
                block = crossing[side, place]
                place += 1
            values.append(roll_by(block, step_x, 0))
        result = collide(values, walls[side, RATE_SLOT], walls[side, FLAG_SLOT])
        place = 0
        for q in range(Q):
            if VELOCITIES[q][1] == sign:
                kept = jnp.where(hidden | outside, 0.0, result[q])
                edges[side, place] = roll_by(kept, VELOCITIES[q][2], 1)
                place += 1

    def plane_two(x, carry):
        values = []
        places = {1: 0, -1: 0}
        for q in range(Q):
            step_x, step_y, _ = VELOCITIES[q]
            block = second[q, x + 1 - step_x]
            if step_y != 0:
                edge = edges[0 if step_y > 0 else 1, places[step_y], pl.ds(x + 2 - step_x, 1)]
                places[step_y] += 1
                block = with_edge(block, step_y, edge)
            values.append(block)
            out[q, x] = block
        density, flow_x, flow_y, flow_z = moments(values)
        parts = (
            LOAD_SCALE * flow_x,
            LOAD_SCALE * (flow_y + (density - 1.0) / 3.0),
            LOAD_SCALE * flow_z,
        )
        for part in range(3):
            for piece in range(half):
                loads[x * half + piece, part] = parts[part][:, piece * BLK : (piece + 1) * BLK]
        return carry

    lax.fori_loop(0, planes, plane_two, 0)

    for copy in copies:
        copy.wait()
    node_blocks = internal_own.shape[1] * half
    live = jnp.broadcast_to(block_count[...], (1, BLK))
    lanes_of = lax.broadcasted_iota(jnp.int32, (1, BLK), 1) // (BLK // slots)
    all_keys = jnp.full((1, BLK), -1, jnp.int32)
    for k in range(slots):
        run = block_source[0, 0, k]
        x = run // (rows * half)
        left = run - x * (rows * half)
        y = left // half
        piece = left - y * half
        for part in range(3):
            message[3 * k + part] = loads[x * half + piece, part, pl.ds(y, 1)]
        key = block_target[0, 0, k] * node_blocks + block_node[0, 0, k]
        all_keys = jnp.where((lanes_of == k) & (live > k), key, all_keys)
    message[3 * slots] = all_keys.astype(F32)
    for part in range(3):
        start = 3 * slots + 1 + part * node_blocks
        for piece in range(half):
            at = piece * rows
            lanes = slice(piece * BLK, (piece + 1) * BLK)
            message[start + at : start + at + rows, 0] = (
                internal_own[part, :, lanes] + both[0, FORCE_SLOT + part, :, lanes]
            )


def element_kernel(
    elements, displacement, next_nodes, shape_inverse, stiffness, low_ids, high_ids, forces, shapes,
    numbers, corners,
):
    node_dev = displacement.shape[1]
    node_blocks = node_dev // BLK
    runs = elements.shape[1] // BLK
    for j in range(runs):
        lanes = slice(j * BLK, (j + 1) * BLK)
        for row in range(3):
            numbers[row, j : j + 1] = elements[row : row + 1, lanes]
            shapes[row, j : j + 1] = shape_inverse[row : row + 1, lanes]
    for row in range(3):
        low_ids[row] = (numbers[row] & (BLK - 1)).astype(F32)
        high_ids[row] = (numbers[row] >> 7).astype(F32)

    def gather(group, carry):
        rows = pl.ds(pl.multiple_of(group * 8, 8), 8)
        low = [numbers[corner, rows] & (BLK - 1) for corner in range(3)]
        high = [numbers[corner, rows] >> 7 for corner in range(3)]
        for corner in range(3):
            nodes = [jnp.zeros((8, BLK), F32)] * 3
            for block in range(2 * node_blocks):
                source = displacement if block < node_blocks else next_nodes
                start = (block % node_blocks) * BLK
                here = high[corner] == block
                for part in range(3):
                    row = source[part : part + 1, start : start + BLK]
                    picked = jnp.take_along_axis(
                        jnp.broadcast_to(row, (8, BLK)),
                        low[corner],
                        axis=1,
                        mode="promise_in_bounds",
                    )
                    nodes[part] = jnp.where(here, picked, nodes[part])
            for part in range(3):
                corners[corner, part, rows] = nodes[part]
        return carry

    lax.fori_loop(0, runs // 8, gather, 0)

    first, second, third = [[corners[c, p] for p in range(3)] for c in range(3)]
    diag_a = shapes[0]
    skew_b = shapes[1]
    diag_c = shapes[2]
    stiff = stiffness[...]
    edge_one = [second[p] - first[p] for p in range(3)]
    edge_two = [third[p] - first[p] for p in range(3)]
    one = [diag_a * edge_one[p] for p in range(3)]
    two = [skew_b * edge_one[p] + diag_c * edge_two[p] for p in range(3)]
    one[0] = one[0] + 1.0
    two[1] = two[1] + 1.0
    aa = one[0] * one[0] + one[1] * one[1] + one[2] * one[2]
    ab = one[0] * two[0] + one[1] * two[1] + one[2] * two[2]
    bb = two[0] * two[0] + two[1] * two[1] + two[2] * two[2]
    determinant = aa * bb - ab * ab
    scale = 1.0 / determinant
    inverse_aa = bb * scale
    inverse_ab = -ab * scale
    inverse_bb = aa * scale
    pressure = LAME_RATIO * (0.5 * jnp.log(determinant))
    for p in range(3):
        pulled_one = one[p] * inverse_aa + two[p] * inverse_ab
        pulled_two = one[p] * inverse_ab + two[p] * inverse_bb
        stress_one = stiff * (one[p] - pulled_one + pressure * pulled_one)
        stress_two = stiff * (two[p] - pulled_two + pressure * pulled_two)
        force_one = diag_a * stress_one + skew_b * stress_two
        force_two = diag_c * stress_two
        for corner, force in enumerate((-(force_one + force_two), force_one, force_two)):
            rest = force
            for part in range(PIECES):
                piece = rest.astype(jnp.bfloat16).astype(F32)
                rest = rest - piece
                forces[part * 3 + p, corner] = piece


def spread_kernel(base, low_ids, high_ids, forces, out):
    runs = low_ids.shape[1]
    parts, rows, length = out.shape
    pieces = length // BLK
    slots = pieces * rows
    kind = jnp.bfloat16
    tile = 16
    slot_ids = lax.broadcasted_iota(jnp.int32, (slots, BLK), 0).astype(F32) + base
    slot_ids = slot_ids.astype(kind)
    lane_ids = lax.broadcasted_iota(jnp.int32, (BLK, BLK), 0).astype(F32).astype(kind)
    ones = jnp.ones((BLK, BLK), kind)
    none = jnp.zeros((BLK, BLK), kind)
    blank = jnp.zeros((slots, BLK), kind)

    def tall_row(row, count):
        block = jnp.broadcast_to(row, (tile, BLK)).astype(kind)
        return jnp.concatenate([block] * (count // tile), axis=0)

    total = None
    for corner in range(3):
        for first in range(0, runs, STEP):
            left = [[] for _ in range(parts * PIECES)]
            right = []
            for j in range(first, min(first + STEP, runs)):
                row = slice(j, j + 1)
                here = slot_ids == tall_row(high_ids[corner, row], slots)
                there = lane_ids == tall_row(low_ids[corner, row], BLK)
                right.append(jnp.where(there, ones, none))
                for part in range(parts * PIECES):
                    left[part].append(
                        jnp.where(here, tall_row(forces[part, corner, row], slots), blank)
                    )
            tall = jnp.concatenate([jnp.concatenate(part, axis=1) for part in left], axis=0)
            wide = jnp.concatenate(right, axis=1)
            product = lax.dot_general(
                tall, wide, (((1,), (1,)), ((), ())), preferred_element_type=F32
            )
            total = product if total is None else total + product
    for p in range(parts):
        summed = total[p * slots : (p + 1) * slots]
        for part in range(1, PIECES):
            start = (parts * part + p) * slots
            summed = summed + total[start : start + slots]
        for piece in range(pieces):
            out[p, :, piece * BLK : (piece + 1) * BLK] = summed[piece * rows : (piece + 1) * rows]


def store_kernel(values, out_hbm, sem):
    store = pltpu.make_async_copy(values, out_hbm, sem)
    store.start()
    store.wait()


def final_kernel(count, *refs):
    messages = refs[:count]
    residual_hbm, motion_hbm, residual, motion, keys, sems = refs[count:]
    slots = keys.shape[0]
    node_blocks = residual.shape[1] // BLK
    inner = lax.axis_index("inner")
    width = BLK // slots
    found = [
        [
            jnp.broadcast_to(message[3 * slots][:, k * width : k * width + 1], (1, BLK))
            for k in range(slots)
        ]
        for message in messages
    ]
    node_ids = lax.broadcasted_iota(jnp.int32, (node_blocks, BLK), 0)
    own_ids = (node_ids + inner * node_blocks).astype(F32)
    start = 3 * slots + 1
    left = [-messages[0][start + p * node_blocks : start + (p + 1) * node_blocks, 0] for p in range(3)]
    for message, all_keys in zip(messages, found):
        for k, key in enumerate(all_keys):
            here = own_ids == key
            for part in range(3):
                left[part] = left[part] + jnp.where(here, message[3 * k + part], 0.0)
    for part in range(3):
        for b in range(node_blocks):
            residual[part : part + 1, b * BLK : (b + 1) * BLK] = left[part][b : b + 1]
    store_residual = pltpu.make_async_copy(residual, residual_hbm, sems.at[0])
    store_residual.start()

    for k in range(slots):
        keys[k : k + 1] = found[0][k]
    wanted = keys[...]
    moved = [jnp.zeros((slots, BLK), F32)] * 3
    for message, all_keys in zip(messages, found):
        for k, key in enumerate(all_keys):
            same = wanted == key
            for part in range(3):
                moved[part] = moved[part] + jnp.where(same, message[3 * k + part], 0.0)
    for step, message in enumerate(messages):
        sender = partner_of(inner, step, count)
        for b in range(node_blocks):
            same = wanted == (sender * node_blocks + b).astype(F32)
            for part in range(3):
                row = message[start + part * node_blocks + b]
                moved[part] = moved[part] - jnp.where(same, row, 0.0)
    live = wanted >= 0.0
    for part in range(3):
        motion[part] = jnp.where(live, COMPLIANCE * moved[part], 0.0)
    store_motion = pltpu.make_async_copy(motion, motion_hbm, sems.at[1])
    store_motion.start()
    store_residual.wait()
    store_motion.wait()


def call(kernel, outs, operands, spaces, scratch=(), out_spaces=None, micros=1.0, aliases=None):
    spec = lambda space: pl.BlockSpec(memory_space=space)
    out_spaces = out_spaces or (pltpu.VMEM,) * len(outs)
    return pl.pallas_call(
        kernel,
        out_shape=outs,
        in_specs=[spec(space) for space in spaces],
        out_specs=tuple(spec(space) for space in out_spaces),
        scratch_shapes=list(scratch),
        input_output_aliases=aliases or {},
        compiler_params=pltpu.CompilerParams(vmem_limit_bytes=VMEM_BYTES),
        cost_estimate=pl.CostEstimate(
            flops=0, bytes_accessed=int(micros * 3.6e6), transcendentals=0
        ),
    )(*operands)


def partner_of(at, step, count):
    if count & (count - 1) == 0:
        return at ^ step
    return (at + count - step) % count


def exchange(block, axis, step):
    count = lax.axis_size(axis)
    return lax.ppermute(block, axis, [(partner_of(i, step, count), i) for i in range(count)])


def around(block, axis, step):
    count = lax.axis_size(axis)
    return lax.ppermute(block, axis, [(i, (i + step) % count) for i in range(count)])


def swap(near, far, axis, beside):
    count, others = lax.axis_size(axis), lax.axis_size(beside)
    routes = []
    for start in (0, 1):
        route = []
        for other in range(others):
            for i in range(count):
                j = i + 1 if i % 2 == start else i - 1
                to = other
                if not 0 <= j < count:
                    j = i
                    to = other ^ 1 if others % 2 == 0 else other
                route.append((other * count + i, to * count + j))
        routes.append(route)
    axes = (beside, axis)
    return lax.ppermute(near, axes, routes[0]), lax.ppermute(far, axes, routes[1])


def shards(
    populations,
    relaxation,
    node_flags,
    displacement,
    elements,
    shape_inverse,
    stiffness,
    block_source,
    block_target,
    block_node,
    block_count,
):
    planes, rows, length = populations.shape[1:]
    half = length // BLK
    node_dev = displacement.shape[1]
    node_blocks = node_dev // BLK
    runs = stiffness.shape[0] // BLK
    slots = block_source.shape[2]
    count = lax.axis_size("inner")
    shape = lambda *dims: jax.ShapeDtypeStruct(dims, F32)
    whole = shape(*populations.shape)
    vmem, hbm, smem = pltpu.VMEM, pltpu.HBM, pltpu.SMEM

    next_nodes = around(displacement, "slab", -1)
    face_y = shape(SIDE_SLOTS, planes, length)
    face_x = shape(SLOTS, rows, length)
    pin = lambda block: pltpu.with_memory_space_constraint(block, hbm)
    whole_like = lambda block: jax.ShapeDtypeStruct(block.shape, block.dtype)
    shell = (displacement, elements, shape_inverse, stiffness.reshape(runs, BLK))
    c1, fixed, near, far, own_nodes, corners, inverses, stiff = call(
        first_kernel,
        (
            whole,
            shape(2, planes, rows, length),
            face_y,
            face_y,
            *(whole_like(block) for block in shell),
        ),
        tuple(pin(block) for block in (populations, relaxation, node_flags, *shell)),
        (hbm,) * 7,
        scratch=(
            pltpu.VMEM((planes, Q, rows, length), F32),
            pltpu.VMEM((planes, rows, length), F32),
            pltpu.VMEM((planes, rows, length), jnp.int32),
            pltpu.SemaphoreType.DMA((planes + 6,)),
        ),
        micros=1.5,
    )
    near_y, far_y = swap(near, far, "inner", "slab")
    numbers = shape(3, runs, BLK)
    low_ids, high_ids, forces = call(
        element_kernel,
        (numbers, numbers, shape(3 * PIECES, 3, runs, BLK)),
        (corners, own_nodes, next_nodes, inverses, stiff),
        (vmem,) * 5,
        scratch=(
            pltpu.VMEM((3, runs, BLK), F32),
            pltpu.VMEM((3, runs, BLK), jnp.int32),
            pltpu.VMEM((3, 3, runs, BLK), F32),
        ),
        micros=0.001,
    )
    near, far = call(
        slab_face_kernel, (face_x, face_x), (c1, fixed, low_ids), (vmem,) * 3, micros=0.001
    )
    near_x, far_x = swap(near, far, "slab", "group")
    nodal = shape(3, node_blocks // half, length)
    (other,) = call(
        functools.partial(spread_kernel, node_blocks),
        (nodal,),
        (low_ids, high_ids, forces),
        (vmem,) * 3,
        micros=0.001,
    )
    corner = shape(CORNER_SLOTS, rows, length)
    near, far = call(
        corner_kernel,
        (corner, corner),
        (near_y, far_y, other),
        (vmem,) * 3,
        scratch=(pltpu.VMEM((2, SLOTS, planes, length), F32),),
        micros=0.3,
    )
    near_c, far_c = swap(near, far, "slab", "group")
    (own,) = call(
        functools.partial(spread_kernel, 0),
        (nodal,),
        (low_ids, high_ids, forces),
        (vmem,) * 3,
        micros=0.8,
    )
    wide = planes + 4
    walls_shape = shape(2, SLOTS, wide, length)
    second_shape = shape(Q, planes + 2, rows, length)
    extended, walls, crossing, second, ends = call(
        inside_kernel,
        (
            shape(Q, wide, rows, length),
            walls_shape,
            shape(2, 5, wide, length),
            second_shape,
            shape(2, 2, rows, length),
        ),
        (c1, fixed, near_y, far_y, near_x, far_x),
        (vmem,) * 6,
        scratch=(
            pltpu.VMEM((2, SLOTS, planes, length), F32),
            pltpu.VMEM((2, SLOTS, rows, length), F32),
        ),
        micros=0.8,
    )
    lines = 3 * slots + 1 + 3 * node_blocks
    values, message, _, _ = call(
        second_kernel,
        (whole, shape(lines, 1, BLK), walls_shape, second_shape),
        (
            pin(block_source),
            pin(block_target),
            pin(block_node),
            block_count,
            near_c,
            far_c,
            fixed,
            extended,
            crossing,
            ends,
            own,
            walls,
            second,
        ),
        (hbm,) * 3 + (vmem,) * 10,
        aliases={11: 2, 12: 3},
        scratch=(
            pltpu.VMEM((2, CORNER_SLOTS, rows, length), F32),
            pltpu.VMEM((2, 5, wide, length), F32),
            pltpu.VMEM((planes * half, 3, rows, BLK), F32),
            pltpu.SMEM(block_source.shape, jnp.int32),
            pltpu.SMEM(block_target.shape, jnp.int32),
            pltpu.SMEM(block_node.shape, jnp.int32),
            pltpu.SemaphoreType.DMA((3,)),
        ),
        micros=1.5,
    )
    messages = [message] + [exchange(message, "inner", step) for step in range(1, count)]
    (populations_out,) = call(
        store_kernel,
        (whole,),
        (values,),
        (vmem,),
        out_spaces=(hbm,),
        scratch=(pltpu.SemaphoreType.DMA(()),),
        micros=1.0,
    )
    residual, motion = call(
        functools.partial(final_kernel, count),
        (shape(3, node_dev), shape(3, slots, BLK)),
        messages,
        (vmem,) * count,
        out_spaces=(hbm, hbm),
        scratch=(
            pltpu.VMEM((3, node_dev), F32),
            pltpu.VMEM((3, slots, BLK), F32),
            pltpu.VMEM((slots, BLK), F32),
            pltpu.SemaphoreType.DMA((2,)),
        ),
        micros=0.8,
    )
    return populations_out, residual, motion.transpose(1, 0, 2)[None, None]


def solution(mesh):
    return jax.shard_map(
        shards,
        mesh=mesh,
        in_specs=(
            P(None, ("group", "slab"), "inner", None),
            P(("group", "slab"), "inner", None),
            P(("group", "slab"), "inner", None),
            P(None, ("group", "slab", "inner")),
            P(None, ("group", "slab", "inner")),
            P(None, ("group", "slab", "inner")),
            P(("group", "slab", "inner")),
            P(("group", "slab"), "inner", None),
            P(("group", "slab"), "inner", None),
            P(("group", "slab"), "inner", None),
            P(("group", "slab"), "inner"),
        ),
        out_specs=(
            P(None, ("group", "slab"), "inner", None),
            P(None, ("group", "slab", "inner")),
            P(("group", "slab"), "inner", None, None, None),
        ),
        check_vma=False,
    )
```

```python
import functools

import jax
import jax.numpy as jnp
from jax import lax
from jax.experimental import pallas as pl
from jax.experimental.pallas import tpu as pltpu
from jax.sharding import PartitionSpec as P

BLK = 128
VELOCITIES = (
    (0, 0, 0),
    (1, 0, 0),
    (-1, 0, 0),
    (0, 1, 0),
    (0, -1, 0),
    (0, 0, 1),
    (0, 0, -1),
    (1, 1, 0),
    (-1, -1, 0),
    (1, -1, 0),
    (-1, 1, 0),
    (1, 0, 1),
    (-1, 0, -1),
    (1, 0, -1),
    (-1, 0, 1),
    (0, 1, 1),
    (0, -1, -1),
    (0, 1, -1),
    (0, -1, 1),
)
WEIGHTS = (1.0 / 3.0,) + (1.0 / 18.0,) * 6 + (1.0 / 36.0,) * 12
OPPOSITE = (0, 2, 1, 4, 3, 6, 5, 8, 7, 10, 9, 12, 11, 14, 13, 16, 15, 18, 17)
INLET_SPEED = 0.04
LOAD_SCALE = 25.0
COMPLIANCE = 0.5
LAME_RATIO = 2.0
Q = 19
FLAG_SLOT = 19
RATE_SLOT = 20
SLOTS = 21
PADDED_SLOTS = 24
FORCE_SLOT = 6
CORNER_SLOTS = FORCE_SLOT + 3
PIECES = 2
CAP = 3
STEP = 4
F32 = jnp.float32
VMEM_BYTES = 48 * 1024 * 1024


def moments(values):
    sums = [values[q] + values[q + 1] for q in range(1, Q, 2)]
    diffs = [values[q] - values[q + 1] for q in range(1, Q, 2)]
    density = values[0]
    for term in sums:
        density = density + term
    flows = []
    for axis in range(3):
        total = None
        for k, q in enumerate(range(1, Q, 2)):
            factor = VELOCITIES[q][axis]
            if factor == 0:
                continue
            if total is None:
                total = diffs[k] if factor > 0 else -diffs[k]
            else:
                total = total + diffs[k] if factor > 0 else total - diffs[k]
        flows.append(total)
    return density, flows[0], flows[1], flows[2]


def collide(values, rate, kind):
    density, flow_x, flow_y, flow_z = moments(values)
    inverse = 1.0 / density
    wall = kind == 1
    inlet = kind == 2
    fluid = kind == 0
    vel = (
        jnp.where(inlet, INLET_SPEED, flow_x * inverse),
        jnp.where(inlet, 0.0, flow_y * inverse),
        jnp.where(inlet, 0.0, flow_z * inverse),
    )
    scale = jnp.where(fluid, density, 1.0)
    rate = jnp.where(fluid, rate, 1.0)
    base = 1.0 - 1.5 * (vel[0] * vel[0] + vel[1] * vel[1] + vel[2] * vel[2])
    weighted = {w: w * scale for w in set(WEIGHTS)}
    out = [None] * Q
    relaxed = values[0] + rate * (weighted[WEIGHTS[0]] * base - values[0])
    out[0] = jnp.where(wall, values[0], relaxed)
    for q in range(1, Q, 2):
        project = None
        for factor, component in zip(VELOCITIES[q], vel):
            if factor == 0:
                continue
            if project is None:
                project = component
            else:
                project = project + component if factor > 0 else project - component
        even = base + 4.5 * (project * project)
        odd = 3.0 * project
        w = weighted[WEIGHTS[q]]
        forward = values[q] + rate * (w * (even + odd) - values[q])
        backward = values[q + 1] + rate * (w * (even - odd) - values[q + 1])
        out[q] = jnp.where(wall, values[q + 1], forward)
        out[q + 1] = jnp.where(wall, values[q], backward)
    return out


def roll_by(block, step, axis):
    if step == 0:
        return block
    return pltpu.roll(block, step % block.shape[axis], axis)


def face_slots(axis, sign):
    picks = []
    for q in range(Q):
        if VELOCITIES[q][axis] * sign >= 0:
            picks.append((q, 0))
        else:
            picks.append((OPPOSITE[q], 1))
    return picks


def mirror(q, axis):
    flipped = tuple(-c if k == axis else c for k, c in enumerate(VELOCITIES[q]))
    return VELOCITIES.index(flipped)


def corner_rows(sign_x, sign_y):
    rows = []
    for q, depth in face_slots(0, sign_x):
        if VELOCITIES[q][1] * sign_y >= 0:
            rows.append((q, depth))
        else:
            rows.append((OPPOSITE[mirror(q, 1)], depth))
    return rows


def first_kernel(
    pops_hbm,
    rate_hbm,
    flags_hbm,
    displacement_hbm,
    elements_hbm,
    shape_hbm,
    stiffness_hbm,
    block_target_hbm,
    block_node_hbm,
    c1,
    fixed,
    far,
    near,
    displacement,
    elements,
    shape_inverse,
    stiffness,
    keys,
    pops,
    rate,
    flags,
    block_target,
    block_node,
    sems,
):
    planes, rows = c1.shape[1], c1.shape[2]
    copies = [
        pltpu.make_async_copy(rate_hbm, rate, sems.at[planes]),
        pltpu.make_async_copy(flags_hbm, flags, sems.at[planes + 1]),
    ]
    loads = [
        pltpu.make_async_copy(pops_hbm.at[:, x], pops.at[x], sems.at[x]) for x in range(planes)
    ]
    shell = [
        pltpu.make_async_copy(source, target, sems.at[planes + 2 + k])
        for k, (source, target) in enumerate(
            (
                (displacement_hbm, displacement),
                (elements_hbm, elements),
                (shape_hbm, shape_inverse),
                (stiffness_hbm, stiffness),
                (block_target_hbm, block_target),
                (block_node_hbm, block_node),
            )
        )
    ]
    for copy in loads[:1] + copies + loads[1:] + shell:
        copy.start()
    for copy in copies:
        copy.wait()

    def plane(x, carry):
        pltpu.make_async_copy(pops_hbm.at[:, x], pops.at[x], sems.at[x]).wait()
        kind = flags[x]
        values = [pops[x, q] for q in range(Q)]
        result = collide(values, rate[x], kind)
        for q in range(Q):
            c1[q, x] = roll_by(result[q], VELOCITIES[q][2], 1)
        fixed[0, x] = kind.astype(F32)
        fixed[1, x] = rate[x]
        return carry

    lax.fori_loop(0, planes, plane, 0)

    def pack(out, sign, outside):
        def line(x, carry):
            for slot, (q, depth) in enumerate(face_slots(1, sign)):
                y = rows - 1 - depth if sign > 0 else depth
                out[slot, pl.ds(x, 1)] = c1[q, x, y : y + 1]
            y = rows - 1 if sign > 0 else 0
            for k, slot in enumerate((FLAG_SLOT, RATE_SLOT)):
                out[slot, pl.ds(x, 1)] = fixed[k, x, y : y + 1]
            return carry

        lax.fori_loop(0, planes, line, 0)
        for slot in range(SLOTS, out.shape[0]):
            out[slot] = jnp.zeros(out.shape[1:], F32)
        clear_outside(out, outside)

    pack_pair(pack, "inner", near, far)
    for copy in shell:
        copy.wait()
    node_blocks = displacement.shape[1] // BLK
    for k in range(keys.shape[0]):
        key = block_target[0, 0, k] * node_blocks + block_node[0, 0, k]
        line = jnp.broadcast_to(key, (1, BLK)).astype(F32)
        keys[k : k + 1] = line
        slot, row, lanes = key_place(near, k)
        near[slot, row, lanes] = line


def key_place(face, k):
    planes, pieces = face.shape[1], face.shape[2] // BLK
    row, piece = divmod(k, pieces)
    slot, row = divmod(row, planes)
    return SLOTS + slot, slice(row, row + 1), slice(piece * BLK, (piece + 1) * BLK)


def clear_outside(out, outside):
    @pl.when(outside)
    def _():
        out[...] = jnp.zeros(out.shape, F32)


def pack_pair(pack, axis, near, far):
    at = lax.axis_index(axis)
    even = lax.rem(at, 2) == 0
    first, last = at == 0, at == lax.axis_size(axis) - 1

    @pl.when(even)
    def _():
        pack(near, 1, last)
        pack(far, -1, first)

    @pl.when(jnp.logical_not(even))
    def _():
        pack(near, -1, first)
        pack(far, 1, last)


def slab_face_kernel(c1, fixed, numbers, far, near):
    del numbers
    planes = c1.shape[1]

    def pack(out, sign, outside):
        for slot, (q, depth) in enumerate(face_slots(0, sign)):
            out[slot] = c1[q, planes - 1 - depth if sign > 0 else depth]
        end = planes - 1 if sign > 0 else 0
        out[FLAG_SLOT] = fixed[0, end]
        out[RATE_SLOT] = fixed[1, end]
        clear_outside(out, outside)

    pack_pair(pack, "slab", near, far)


def gather_both(near, far, both, axis):
    odd = lax.rem(lax.axis_index(axis), 2)
    for slot in range(both.shape[1]):
        both[1 - odd, slot] = near[slot]
        both[odd, slot] = far[slot]


def corner_kernel(far_y, near_y, other, keys, far, near, known, both):
    planes = near_y.shape[1]
    gather_both(near_y, far_y, both, "inner")

    def pack(out, sign, outside):
        for side, sign_y in enumerate((1, -1)):
            picks = corner_rows(sign, sign_y) + [(FLAG_SLOT, 0), (RATE_SLOT, 0)]
            for row, (slot, depth) in enumerate(picks):
                x = planes - 1 - depth if sign > 0 else depth
                at = 3 * side + row // 8
                out[at, row % 8 : row % 8 + 1] = both[side, slot, x : x + 1]
        for part in range(3):
            out[FORCE_SLOT + part] = other[part]
        clear_outside(out, outside)

    pack_pair(pack, "slab", near, far)
    slots = keys.shape[0]
    known[:slots] = keys[...]
    for k in range(slots):
        slot, row, lanes = key_place(near_y, k)
        known[slots + k : slots + k + 1] = near_y[slot, row, lanes]


def with_edge(block, step_y, edge):
    rows = block.shape[0]
    sub = lax.broadcasted_iota(jnp.int32, block.shape, 0)
    if step_y > 0:
        return jnp.where(sub == 0, edge, roll_by(block, 1, 0))
    return jnp.where(sub == rows - 1, edge, roll_by(block, -1, 0))


def store_plane(extended, walls, second, at, rate, kind):
    values = []
    for q in range(Q):
        step_x, step_y, _ = VELOCITIES[q]
        block = extended[q, at + 1 - step_x]
        if step_y != 0:
            edge = walls[0 if step_y > 0 else 1, q, pl.ds(at + 1 - step_x, 1)]
            block = with_edge(block, step_y, edge)
        values.append(block)
    result = collide(values, rate, kind)
    for q in range(Q):
        second[q, at] = roll_by(result[q], VELOCITIES[q][2], 1)


def inside_kernel(
    c1,
    fixed,
    far_y,
    near_y,
    far_x,
    near_x,
    extended,
    walls,
    crossing,
    second,
    ends,
    both_y,
    both_x,
):
    planes, rows, _ = c1.shape[1:]
    wide = planes + 4
    gather_both(near_y, far_y, both_y, "inner")
    gather_both(near_x, far_x, both_x, "slab")
    for q in range(Q):
        for x in range(planes):
            extended[q, x + 2] = c1[q, x]
        extended[q, 1] = both_x[0, q]
        extended[q, planes + 2] = both_x[1, q]
        if VELOCITIES[q][0] > 0:
            extended[q, 0] = both_x[0, OPPOSITE[q]]
        if VELOCITIES[q][0] < 0:
            extended[q, planes + 3] = both_x[1, OPPOSITE[q]]
    for end in range(2):
        ends[end, 0] = both_x[end, FLAG_SLOT]
        ends[end, 1] = both_x[end, RATE_SLOT]

    for side, sign in enumerate((1, -1)):
        y = 0 if sign > 0 else rows - 1
        for slot in range(SLOTS):
            walls[side, slot, 2 : planes + 2] = both_y[side, slot]
        place = 0
        for q in range(Q):
            if VELOCITIES[q][1] != -sign:
                continue
            for x in range(wide):
                crossing[side, place, x : x + 1] = extended[q, x, y : y + 1]
            place += 1

    def inside_plane(x, carry):
        store_plane(extended, walls, second, x + 1, fixed[1, x], fixed[0, x])
        return carry

    lax.fori_loop(1, planes - 1, inside_plane, 0)


def second_kernel(count, tables, *refs):
    block_source_hbm, block_count = refs[:2]
    known = refs[2 : 2 + tables]
    far, near, fixed, extended, crossing, ends, internal_own = refs[2 + tables : 9 + tables]
    rest = refs[11 + tables :]
    out, mine = rest[:2]
    messages = rest[2 : 1 + count]
    walls, second = rest[1 + count : 3 + count]
    both, edges, loads, internal, block_source, sem = rest[3 + count :]
    copy = pltpu.make_async_copy(block_source_hbm, block_source, sem)
    copy.start()
    planes, rows, length = out.shape[1:]
    half = length // BLK
    slots = block_source.shape[2]
    wide = planes + 4
    slab = lax.axis_index("slab")
    inner = lax.axis_index("inner")
    slab_end = lax.axis_size("slab") - 1
    inner_end = lax.axis_size("inner") - 1
    gather_both(near, far, both, "slab")

    for side, sign in enumerate((1, -1)):
        for end, sign_x in enumerate((1, -1)):
            for row, (slot, depth) in enumerate(corner_rows(sign_x, sign)):
                at = (1 - depth) if sign_x > 0 else planes + 2 + depth
                source = 3 * side + row // 8
                walls[side, slot, at : at + 1] = both[end, source, row % 8 : row % 8 + 1]
            at = 1 if sign_x > 0 else planes + 2
            for row in (FLAG_SLOT, RATE_SLOT):
                source = 3 * side + row // 8
                walls[side, row, at : at + 1] = both[end, source, row % 8 : row % 8 + 1]

    def edge_planes(end, carry):
        x = end * (planes - 1)
        store_plane(extended, walls, second, x + 1, fixed[1, x], fixed[0, x])
        store_plane(extended, walls, second, end * (planes + 1), ends[end, 1], ends[end, 0])
        return carry

    lax.fori_loop(0, 2, edge_planes, 0)

    @pl.when(slab == 0)
    def _():
        for q in range(Q):
            if VELOCITIES[q][0] > 0:
                second[q, 0] = jnp.zeros((rows, length), F32)

    @pl.when(slab == slab_end)
    def _():
        for q in range(Q):
            if VELOCITIES[q][0] < 0:
                second[q, planes + 1] = jnp.zeros((rows, length), F32)

    across = lax.broadcasted_iota(jnp.int32, (wide, length), 0)
    hidden = ((across <= 1) & (slab == 0)) | ((across >= planes + 2) & (slab == slab_end))
    for side, sign, outside in ((0, 1, inner == 0), (1, -1, inner == inner_end)):
        values = []
        place = 0
        for q in range(Q):
            step_x, step_y, _ = VELOCITIES[q]
            if step_y == 0:
                block = walls[side, q]
            elif step_y == sign:
                block = walls[side, OPPOSITE[q]]
            else:
                block = crossing[side, place]
                place += 1
            values.append(roll_by(block, step_x, 0))
        result = collide(values, walls[side, RATE_SLOT], walls[side, FLAG_SLOT])
        place = 0
        for q in range(Q):
            if VELOCITIES[q][1] == sign:
                kept = jnp.where(hidden | outside, 0.0, result[q])
                edges[side, place] = roll_by(kept, VELOCITIES[q][2], 1)
                place += 1

    def plane_two(x, carry):
        values = []
        places = {1: 0, -1: 0}
        for q in range(Q):
            step_x, step_y, _ = VELOCITIES[q]
            block = second[q, x + 1 - step_x]
            if step_y != 0:
                edge = edges[0 if step_y > 0 else 1, places[step_y], pl.ds(x + 2 - step_x, 1)]
                places[step_y] += 1
                block = with_edge(block, step_y, edge)
            values.append(block)
            out[q, x] = block
        density, flow_x, flow_y, flow_z = moments(values)
        parts = (
            LOAD_SCALE * flow_x,
            LOAD_SCALE * (flow_y + (density - 1.0) / 3.0),
            LOAD_SCALE * flow_z,
        )
        for part in range(3):
            for piece in range(half):
                loads[x * half + piece, part] = parts[part][:, piece * BLK : (piece + 1) * BLK]
        return carry

    lax.fori_loop(0, planes, plane_two, 0)

    node_blocks = internal_own.shape[1] * half
    for part in range(3):
        for piece in range(half):
            at = piece * rows
            lanes = slice(piece * BLK, (piece + 1) * BLK)
            internal[part, at : at + rows] = (
                internal_own[part, :, lanes] + both[0, FORCE_SLOT + part, :, lanes]
            )
    copy.wait()
    live = jnp.broadcast_to(block_count[...], (1, BLK))
    blocks, keys = [], []
    for k in range(slots):
        run = block_source[0, 0, k]
        x = run // (rows * half)
        left = run - x * (rows * half)
        y = left // half
        piece = left - y * half
        blocks.append([loads[x * half + piece, part, pl.ds(y, 1)] for part in range(3)])
        keys.append(jnp.where(live > k, known[0][k : k + 1], -1.0))

    def summed(wanted):
        moved = [jnp.zeros((slots, BLK), F32)] * 3
        for k in range(slots):
            same = wanted == keys[k]
            for part in range(3):
                moved[part] = moved[part] + jnp.where(same, blocks[k][part], 0.0)
        for b in range(node_blocks):
            same = wanted == (inner * node_blocks + b).astype(F32)
            for part in range(3):
                moved[part] = moved[part] - jnp.where(same, internal[part, b : b + 1], 0.0)
        return moved

    node_ids = lax.broadcasted_iota(jnp.int32, (node_blocks, BLK), 0)
    own_ids = (node_ids + inner * node_blocks).astype(F32)
    moved = summed(known[0][:slots])
    for part in range(3):
        total = -internal[part]
        for k in range(slots):
            total = total + jnp.where(own_ids == keys[k], blocks[k][part], 0.0)
        mine[part * node_blocks : (part + 1) * node_blocks] = total
        start = 3 * node_blocks + part * slots
        mine[start : start + slots] = moved[part]
    for k in range(slots):
        start = 3 * (node_blocks + slots) + k
        mine[start : start + 1] = keys[k]

    table = []
    for ref in known:
        table += [ref[k * slots : (k + 1) * slots] for k in range(ref.shape[0] // slots)]
    place_ids = lax.broadcasted_iota(jnp.int32, (8, BLK), 0).astype(F32)
    for step, message in enumerate(messages, 1):
        dest = partner_of(inner, step, count)
        moved = summed(table[step])
        low = (dest * node_blocks).astype(F32)
        before = jnp.zeros((1, BLK), F32)
        chosen = [jnp.zeros((8, BLK), F32)] * 3
        nodes = jnp.full((8, BLK), -1.0, F32)
        for k in range(slots):
            named = (keys[k] >= low) & (keys[k] < low + node_blocks)
            here = named & (place_ids == before)
            for part in range(3):
                chosen[part] = jnp.where(here, blocks[k][part], chosen[part])
            nodes = jnp.where(here, keys[k], nodes)
            before = before + jnp.where(named, 1.0, 0.0)
        for part in range(3):
            message[part * slots : (part + 1) * slots, 0] = moved[part]
            at = 3 * slots + part * CAP
            message[at : at + CAP, 0] = chosen[part][:CAP]
        at = 3 * slots + 3 * CAP
        message[at : at + CAP, 0] = nodes[:CAP]


def element_kernel(
    elements, displacement, next_nodes, shape_inverse, stiffness, low_ids, high_ids, forces, shapes,
    numbers, corners,
):
    node_dev = displacement.shape[1]
    node_blocks = node_dev // BLK
    runs = elements.shape[1] // BLK
    for j in range(runs):
        lanes = slice(j * BLK, (j + 1) * BLK)
        for row in range(3):
            numbers[row, j : j + 1] = elements[row : row + 1, lanes]
            shapes[row, j : j + 1] = shape_inverse[row : row + 1, lanes]
    for row in range(3):
        low_ids[row] = (numbers[row] & (BLK - 1)).astype(F32)
        high_ids[row] = (numbers[row] >> 7).astype(F32)

    def gather(group, carry):
        rows = pl.ds(pl.multiple_of(group * 8, 8), 8)
        low = [numbers[corner, rows] & (BLK - 1) for corner in range(3)]
        high = [numbers[corner, rows] >> 7 for corner in range(3)]
        for corner in range(3):
            nodes = [jnp.zeros((8, BLK), F32)] * 3
            for block in range(2 * node_blocks):
                source = displacement if block < node_blocks else next_nodes
                start = (block % node_blocks) * BLK
                here = high[corner] == block
                for part in range(3):
                    row = source[part : part + 1, start : start + BLK]
                    picked = jnp.take_along_axis(
                        jnp.broadcast_to(row, (8, BLK)),
                        low[corner],
                        axis=1,
                        mode="promise_in_bounds",
                    )
                    nodes[part] = jnp.where(here, picked, nodes[part])
            for part in range(3):
                corners[corner, part, rows] = nodes[part]
        return carry

    lax.fori_loop(0, runs // 8, gather, 0)

    first, second, third = [[corners[c, p] for p in range(3)] for c in range(3)]
    diag_a = shapes[0]
    skew_b = shapes[1]
    diag_c = shapes[2]
    stiff = stiffness[...]
    edge_one = [second[p] - first[p] for p in range(3)]
    edge_two = [third[p] - first[p] for p in range(3)]
    one = [diag_a * edge_one[p] for p in range(3)]
    two = [skew_b * edge_one[p] + diag_c * edge_two[p] for p in range(3)]
    one[0] = one[0] + 1.0
    two[1] = two[1] + 1.0
    aa = one[0] * one[0] + one[1] * one[1] + one[2] * one[2]
    ab = one[0] * two[0] + one[1] * two[1] + one[2] * two[2]
    bb = two[0] * two[0] + two[1] * two[1] + two[2] * two[2]
    determinant = aa * bb - ab * ab
    scale = 1.0 / determinant
    inverse_aa = bb * scale
    inverse_ab = -ab * scale
    inverse_bb = aa * scale
    pressure = LAME_RATIO * (0.5 * jnp.log(determinant))
    for p in range(3):
        pulled_one = one[p] * inverse_aa + two[p] * inverse_ab
        pulled_two = one[p] * inverse_ab + two[p] * inverse_bb
        stress_one = stiff * (one[p] - pulled_one + pressure * pulled_one)
        stress_two = stiff * (two[p] - pulled_two + pressure * pulled_two)
        force_one = diag_a * stress_one + skew_b * stress_two
        force_two = diag_c * stress_two
        for corner, force in enumerate((-(force_one + force_two), force_one, force_two)):
            rest = force
            for part in range(PIECES):
                piece = rest.astype(jnp.bfloat16).astype(F32)
                rest = rest - piece
                forces[part * 3 + p, corner] = piece


def spread_kernel(base, low_ids, high_ids, forces, out):
    runs = low_ids.shape[1]
    parts, rows, length = out.shape
    pieces = length // BLK
    slots = pieces * rows
    kind = jnp.bfloat16
    tile = 16
    slot_ids = lax.broadcasted_iota(jnp.int32, (slots, BLK), 0).astype(F32) + base
    slot_ids = slot_ids.astype(kind)
    lane_ids = lax.broadcasted_iota(jnp.int32, (BLK, BLK), 0).astype(F32).astype(kind)
    ones = jnp.ones((BLK, BLK), kind)
    none = jnp.zeros((BLK, BLK), kind)
    blank = jnp.zeros((slots, BLK), kind)

    def tall_row(row, count):
        block = jnp.broadcast_to(row, (tile, BLK)).astype(kind)
        return jnp.concatenate([block] * (count // tile), axis=0)

    total = None
    for corner in range(3):
        for first in range(0, runs, STEP):
            left = [[] for _ in range(parts * PIECES)]
            right = []
            for j in range(first, min(first + STEP, runs)):
                row = slice(j, j + 1)
                here = slot_ids == tall_row(high_ids[corner, row], slots)
                there = lane_ids == tall_row(low_ids[corner, row], BLK)
                right.append(jnp.where(there, ones, none))
                for part in range(parts * PIECES):
                    left[part].append(
                        jnp.where(here, tall_row(forces[part, corner, row], slots), blank)
                    )
            tall = jnp.concatenate([jnp.concatenate(part, axis=1) for part in left], axis=0)
            wide = jnp.concatenate(right, axis=1)
            product = lax.dot_general(
                tall, wide, (((1,), (1,)), ((), ())), preferred_element_type=F32
            )
            total = product if total is None else total + product
    for p in range(parts):
        summed = total[p * slots : (p + 1) * slots]
        for part in range(1, PIECES):
            start = (parts * part + p) * slots
            summed = summed + total[start : start + slots]
        for piece in range(pieces):
            out[p, :, piece * BLK : (piece + 1) * BLK] = summed[piece * rows : (piece + 1) * rows]


def store_kernel(values, out_hbm, sem):
    store = pltpu.make_async_copy(values, out_hbm, sem)
    store.start()
    store.wait()


def final_kernel(mine, *refs):
    messages, (residual, motion) = refs[:-2], refs[-2:]
    slots = motion.shape[1]
    node_blocks = residual.shape[1] // BLK
    inner = lax.axis_index("inner")
    node_ids = lax.broadcasted_iota(jnp.int32, (node_blocks, BLK), 0)
    own_ids = (node_ids + inner * node_blocks).astype(F32)
    total = [mine[p * node_blocks : (p + 1) * node_blocks] for p in range(3)]
    start = 3 * node_blocks
    moved = [mine[start + p * slots : start + (p + 1) * slots] for p in range(3)]
    live = mine[start + 3 * slots : start + 4 * slots] >= 0.0
    for message in messages:
        for place in range(CAP):
            here = own_ids == message[3 * slots + 3 * CAP + place]
            for part in range(3):
                row = message[3 * slots + part * CAP + place]
                total[part] = total[part] + jnp.where(here, row, 0.0)
        for part in range(3):
            moved[part] = moved[part] + message[part * slots : (part + 1) * slots, 0]
    for part in range(3):
        for b in range(node_blocks):
            residual[part : part + 1, b * BLK : (b + 1) * BLK] = total[part][b : b + 1]
        motion[part] = jnp.where(live, COMPLIANCE * moved[part], 0.0)


def call(kernel, outs, operands, spaces, scratch=(), out_spaces=None, micros=1.0, aliases=None):
    spec = lambda space: pl.BlockSpec(memory_space=space)
    out_spaces = out_spaces or (pltpu.VMEM,) * len(outs)
    return pl.pallas_call(
        kernel,
        out_shape=outs,
        in_specs=[spec(space) for space in spaces],
        out_specs=tuple(spec(space) for space in out_spaces),
        scratch_shapes=list(scratch),
        input_output_aliases=aliases or {},
        compiler_params=pltpu.CompilerParams(vmem_limit_bytes=VMEM_BYTES),
        cost_estimate=pl.CostEstimate(
            flops=0, bytes_accessed=int(micros * 3.6e6), transcendentals=0
        ),
    )(*operands)


def in_pairs(count):
    return count > 1 and count & (count - 1) == 0


def partner_of(at, step, count):
    return at ^ step if in_pairs(count) else (at + step) % count


def exchange(block, axis, step):
    count = lax.axis_size(axis)
    return lax.ppermute(block, axis, [(i, partner_of(i, step, count)) for i in range(count)])


def all_keys(own, known, axis):
    count = lax.axis_size(axis)
    if not in_pairs(count):
        return [own] + [exchange(own, axis, count - step) for step in range(1, count)]
    tables = [known]
    reach = 2
    while reach < count:
        joined = tables[0] if len(tables) == 1 else jnp.concatenate(tables, axis=0)
        tables.append(exchange(joined, axis, reach))
        reach *= 2
    return tables


def around(block, axis, step):
    count = lax.axis_size(axis)
    return lax.ppermute(block, axis, [(i, (i + step) % count) for i in range(count)])


def swap(near, far, axis, beside):
    count, others = lax.axis_size(axis), lax.axis_size(beside)
    routes = []
    for start in (0, 1):
        route = []
        for other in range(others):
            for i in range(count):
                j = i + 1 if i % 2 == start else i - 1
                to = other
                if not 0 <= j < count:
                    j = i
                    to = other ^ 1 if others % 2 == 0 else other
                route.append((other * count + i, to * count + j))
        routes.append(route)
    axes = (beside, axis)
    return lax.ppermute(near, axes, routes[0]), lax.ppermute(far, axes, routes[1])


def shards(
    populations,
    relaxation,
    node_flags,
    displacement,
    elements,
    shape_inverse,
    stiffness,
    block_source,
    block_target,
    block_node,
    block_count,
):
    planes, rows, length = populations.shape[1:]
    half = length // BLK
    node_dev = displacement.shape[1]
    node_blocks = node_dev // BLK
    runs = stiffness.shape[0] // BLK
    slots = block_source.shape[2]
    count = lax.axis_size("inner")
    shape = lambda *dims: jax.ShapeDtypeStruct(dims, F32)
    whole = shape(*populations.shape)
    vmem, hbm, smem = pltpu.VMEM, pltpu.HBM, pltpu.SMEM

    next_nodes = around(displacement, "slab", -1)
    room = -(-slots // (planes * half))
    face_y = shape(max(SLOTS + room, PADDED_SLOTS), planes, length)
    face_x = shape(SLOTS, rows, length)
    pin = lambda block: pltpu.with_memory_space_constraint(block, hbm)
    whole_like = lambda block: jax.ShapeDtypeStruct(block.shape, block.dtype)
    shell = (displacement, elements, shape_inverse, stiffness.reshape(runs, BLK))
    c1, fixed, far, near, own_nodes, corners, inverses, stiff, own_keys = call(
        first_kernel,
        (
            whole,
            shape(2, planes, rows, length),
            face_y,
            face_y,
            *(whole_like(block) for block in shell),
            shape(slots, BLK),
        ),
        tuple(
            pin(block)
            for block in (populations, relaxation, node_flags, *shell, block_target, block_node)
        ),
        (hbm,) * 9,
        scratch=(
            pltpu.VMEM((planes, Q, rows, length), F32),
            pltpu.VMEM((planes, rows, length), F32),
            pltpu.VMEM((planes, rows, length), jnp.int32),
            pltpu.SMEM(block_target.shape, jnp.int32),
            pltpu.SMEM(block_node.shape, jnp.int32),
            pltpu.SemaphoreType.DMA((planes + 8,)),
        ),
        micros=1.5,
    )
    near_y, far_y = swap(near, far, "inner", "slab")
    numbers = shape(3, runs, BLK)
    low_ids, high_ids, forces = call(
        element_kernel,
        (numbers, numbers, shape(3 * PIECES, 3, runs, BLK)),
        (corners, own_nodes, next_nodes, inverses, stiff),
        (vmem,) * 5,
        scratch=(
            pltpu.VMEM((3, runs, BLK), F32),
            pltpu.VMEM((3, runs, BLK), jnp.int32),
            pltpu.VMEM((3, 3, runs, BLK), F32),
        ),
        micros=0.001,
    )
    far, near = call(
        slab_face_kernel, (face_x, face_x), (c1, fixed, low_ids), (vmem,) * 3, micros=0.001
    )
    near_x, far_x = swap(near, far, "slab", "group")
    nodal = shape(3, node_blocks // half, length)
    (other,) = call(
        functools.partial(spread_kernel, node_blocks),
        (nodal,),
        (low_ids, high_ids, forces),
        (vmem,) * 3,
        micros=0.001,
    )
    corner = shape(CORNER_SLOTS, rows, length)
    far, near, known = call(
        corner_kernel,
        (corner, corner, shape(2 * slots, BLK)),
        (far_y, near_y, other, own_keys),
        (vmem,) * 4,
        scratch=(pltpu.VMEM((2, SLOTS, planes, length), F32),),
        micros=0.3,
    )
    near_c, far_c = swap(near, far, "slab", "group")
    (own,) = call(
        functools.partial(spread_kernel, 0),
        (nodal,),
        (low_ids, high_ids, forces),
        (vmem,) * 3,
        micros=0.8,
    )
    wide = planes + 4
    walls_shape = shape(2, SLOTS, wide, length)
    second_shape = shape(Q, planes + 2, rows, length)
    extended, walls, crossing, second, ends = call(
        inside_kernel,
        (
            shape(Q, wide, rows, length),
            walls_shape,
            shape(2, 5, wide, length),
            second_shape,
            shape(2, 2, rows, length),
        ),
        (c1, fixed, far_y, near_y, far_x, near_x),
        (vmem,) * 6,
        scratch=(
            pltpu.VMEM((2, SLOTS, planes, length), F32),
            pltpu.VMEM((2, SLOTS, rows, length), F32),
        ),
        micros=0.8,
    )
    tables = all_keys(own_keys, known, "inner")
    first = 2 + len(tables)
    line = shape(3 * slots + 4 * CAP, 1, BLK)
    outs = call(
        functools.partial(second_kernel, count, len(tables)),
        (
            whole,
            shape(3 * node_blocks + 4 * slots, BLK),
            *([line] * (count - 1)),
            walls_shape,
            second_shape,
        ),
        (
            pin(block_source),
            block_count,
            *tables,
            far_c,
            near_c,
            fixed,
            extended,
            crossing,
            ends,
            own,
            walls,
            second,
        ),
        (hbm,) + (vmem,) * (first + 8),
        aliases={first + 7: 1 + count, first + 8: 2 + count},
        scratch=(
            pltpu.VMEM((2, CORNER_SLOTS, rows, length), F32),
            pltpu.VMEM((2, 5, wide, length), F32),
            pltpu.VMEM((planes * half, 3, rows, BLK), F32),
            pltpu.VMEM((3, node_blocks, BLK), F32),
            pltpu.SMEM(block_source.shape, jnp.int32),
            pltpu.SemaphoreType.DMA(()),
        ),
        micros=1.5,
    )
    values, mine = outs[:2]
    arrived = [exchange(outs[1 + step], "inner", step) for step in range(count - 1, 0, -1)]
    (populations_out,) = call(
        store_kernel,
        (whole,),
        (values,),
        (vmem,),
        out_spaces=(hbm,),
        scratch=(pltpu.SemaphoreType.DMA(()),),
        micros=1.0,
    )
    residual, motion = call(
        final_kernel,
        (shape(3, node_dev), shape(3, slots, BLK)),
        (mine, *arrived),
        (vmem,) * count,
        micros=0.8,
    )
    return populations_out, residual, motion.transpose(1, 0, 2)[None, None]


def solution(mesh):
    return jax.shard_map(
        shards,
        mesh=mesh,
        in_specs=(
            P(None, ("group", "slab"), "inner", None),
            P(("group", "slab"), "inner", None),
            P(("group", "slab"), "inner", None),
            P(None, ("group", "slab", "inner")),
            P(None, ("group", "slab", "inner")),
            P(None, ("group", "slab", "inner")),
            P(("group", "slab", "inner")),
            P(("group", "slab"), "inner", None),
            P(("group", "slab"), "inner", None),
            P(("group", "slab"), "inner", None),
            P(("group", "slab"), "inner"),
        ),
        out_specs=(
            P(None, ("group", "slab"), "inner", None),
            P(None, ("group", "slab", "inner")),
            P(("group", "slab"), "inner", None, None, None),
        ),
        check_vma=False,
    )
```

```python
import functools

import jax
import jax.numpy as jnp
from jax import lax
from jax.experimental import pallas as pl
from jax.experimental.pallas import tpu as pltpu
from jax.sharding import PartitionSpec as P

BLK = 128
VELOCITIES = (
    (0, 0, 0),
    (1, 0, 0),
    (-1, 0, 0),
    (0, 1, 0),
    (0, -1, 0),
    (0, 0, 1),
    (0, 0, -1),
    (1, 1, 0),
    (-1, -1, 0),
    (1, -1, 0),
    (-1, 1, 0),
    (1, 0, 1),
    (-1, 0, -1),
    (1, 0, -1),
    (-1, 0, 1),
    (0, 1, 1),
    (0, -1, -1),
    (0, 1, -1),
    (0, -1, 1),
)
WEIGHTS = (1.0 / 3.0,) + (1.0 / 18.0,) * 6 + (1.0 / 36.0,) * 12
OPPOSITE = (0, 2, 1, 4, 3, 6, 5, 8, 7, 10, 9, 12, 11, 14, 13, 16, 15, 18, 17)
INLET_SPEED = 0.04
LOAD_SCALE = 25.0
COMPLIANCE = 0.5
LAME_RATIO = 2.0
Q = 19
FLAG_SLOT = 19
RATE_SLOT = 20
SLOTS = 21
PADDED_SLOTS = 24
FORCE_SLOT = 6
CORNER_SLOTS = FORCE_SLOT + 3
PIECES = 2
CAP = 3
STEP = 4
F32 = jnp.float32
VMEM_BYTES = 48 * 1024 * 1024


def moments(values):
    sums = [values[q] + values[q + 1] for q in range(1, Q, 2)]
    diffs = [values[q] - values[q + 1] for q in range(1, Q, 2)]
    density = values[0]
    for term in sums:
        density = density + term
    flows = []
    for axis in range(3):
        total = None
        for k, q in enumerate(range(1, Q, 2)):
            factor = VELOCITIES[q][axis]
            if factor == 0:
                continue
            if total is None:
                total = diffs[k] if factor > 0 else -diffs[k]
            else:
                total = total + diffs[k] if factor > 0 else total - diffs[k]
        flows.append(total)
    return density, flows[0], flows[1], flows[2]


def collide(values, rate, kind):
    density, flow_x, flow_y, flow_z = moments(values)
    inverse = 1.0 / density
    wall = kind == 1
    inlet = kind == 2
    fluid = kind == 0
    vel = (
        jnp.where(inlet, INLET_SPEED, flow_x * inverse),
        jnp.where(inlet, 0.0, flow_y * inverse),
        jnp.where(inlet, 0.0, flow_z * inverse),
    )
    scale = jnp.where(fluid, density, 1.0)
    rate = jnp.where(fluid, rate, 1.0)
    base = 1.0 - 1.5 * (vel[0] * vel[0] + vel[1] * vel[1] + vel[2] * vel[2])
    weighted = {w: w * scale for w in set(WEIGHTS)}
    out = [None] * Q
    relaxed = values[0] + rate * (weighted[WEIGHTS[0]] * base - values[0])
    out[0] = jnp.where(wall, values[0], relaxed)
    for q in range(1, Q, 2):
        project = None
        for factor, component in zip(VELOCITIES[q], vel):
            if factor == 0:
                continue
            if project is None:
                project = component
            else:
                project = project + component if factor > 0 else project - component
        even = base + 4.5 * (project * project)
        odd = 3.0 * project
        w = weighted[WEIGHTS[q]]
        forward = values[q] + rate * (w * (even + odd) - values[q])
        backward = values[q + 1] + rate * (w * (even - odd) - values[q + 1])
        out[q] = jnp.where(wall, values[q + 1], forward)
        out[q + 1] = jnp.where(wall, values[q], backward)
    return out


def roll_by(block, step, axis):
    if step == 0:
        return block
    return pltpu.roll(block, step % block.shape[axis], axis)


def face_slots(axis, sign):
    picks = []
    for q in range(Q):
        if VELOCITIES[q][axis] * sign >= 0:
            picks.append((q, 0))
        else:
            picks.append((OPPOSITE[q], 1))
    return picks


def mirror(q, axis):
    flipped = tuple(-c if k == axis else c for k, c in enumerate(VELOCITIES[q]))
    return VELOCITIES.index(flipped)


def corner_rows(sign_x, sign_y):
    rows = []
    for q, depth in face_slots(0, sign_x):
        if VELOCITIES[q][1] * sign_y >= 0:
            rows.append((q, depth))
        else:
            rows.append((OPPOSITE[mirror(q, 1)], depth))
    return rows


def first_kernel(
    pops_hbm,
    rate_hbm,
    flags_hbm,
    displacement_hbm,
    elements_hbm,
    shape_hbm,
    stiffness_hbm,
    block_target_hbm,
    block_node_hbm,
    c1,
    fixed,
    far,
    near,
    displacement,
    elements,
    shape_inverse,
    stiffness,
    keys,
    pops,
    rate,
    flags,
    block_target,
    block_node,
    sems,
):
    planes, rows = c1.shape[1], c1.shape[2]
    copies = [
        pltpu.make_async_copy(rate_hbm, rate, sems.at[planes]),
        pltpu.make_async_copy(flags_hbm, flags, sems.at[planes + 1]),
    ]
    loads = [
        pltpu.make_async_copy(pops_hbm.at[:, x], pops.at[x], sems.at[x]) for x in range(planes)
    ]
    shell = [
        pltpu.make_async_copy(source, target, sems.at[planes + 2 + k])
        for k, (source, target) in enumerate(
            (
                (displacement_hbm, displacement),
                (elements_hbm, elements),
                (shape_hbm, shape_inverse),
                (stiffness_hbm, stiffness),
                (block_target_hbm, block_target),
                (block_node_hbm, block_node),
            )
        )
    ]
    for copy in loads[:1] + copies + loads[1:] + shell:
        copy.start()
    for copy in copies:
        copy.wait()

    def plane(x, carry):
        pltpu.make_async_copy(pops_hbm.at[:, x], pops.at[x], sems.at[x]).wait()
        kind = flags[x]
        values = [pops[x, q] for q in range(Q)]
        result = collide(values, rate[x], kind)
        for q in range(Q):
            c1[q, x] = roll_by(result[q], VELOCITIES[q][2], 1)
        fixed[0, x] = kind.astype(F32)
        fixed[1, x] = rate[x]
        return carry

    lax.fori_loop(0, planes, plane, 0)

    def pack(out, sign, outside):
        def line(x, carry):
            for slot, (q, depth) in enumerate(face_slots(1, sign)):
                y = rows - 1 - depth if sign > 0 else depth
                out[slot, pl.ds(x, 1)] = c1[q, x, y : y + 1]
            y = rows - 1 if sign > 0 else 0
            for k, slot in enumerate((FLAG_SLOT, RATE_SLOT)):
                out[slot, pl.ds(x, 1)] = fixed[k, x, y : y + 1]
            return carry

        lax.fori_loop(0, planes, line, 0)
        for slot in range(SLOTS, out.shape[0]):
            out[slot] = jnp.zeros(out.shape[1:], F32)
        clear_outside(out, outside)

    pack_pair(pack, "inner", near, far)
    for copy in shell:
        copy.wait()
    node_blocks = displacement.shape[1] // BLK
    for k in range(keys.shape[0]):
        key = block_target[0, 0, k] * node_blocks + block_node[0, 0, k]
        line = jnp.broadcast_to(key, (1, BLK)).astype(F32)
        keys[k : k + 1] = line
        slot, row, lanes = key_place(near, k)
        near[slot, row, lanes] = line


def key_place(face, k):
    planes, pieces = face.shape[1], face.shape[2] // BLK
    row, piece = divmod(k, pieces)
    slot, row = divmod(row, planes)
    return SLOTS + slot, slice(row, row + 1), slice(piece * BLK, (piece + 1) * BLK)


def clear_outside(out, outside):
    @pl.when(outside)
    def _():
        out[...] = jnp.zeros(out.shape, F32)


def pack_pair(pack, axis, near, far):
    at = lax.axis_index(axis)
    even = lax.rem(at, 2) == 0
    first, last = at == 0, at == lax.axis_size(axis) - 1

    @pl.when(even)
    def _():
        pack(near, 1, last)
        pack(far, -1, first)

    @pl.when(jnp.logical_not(even))
    def _():
        pack(near, -1, first)
        pack(far, 1, last)


def slab_face_kernel(c1, fixed, numbers, far, near):
    del numbers
    planes = c1.shape[1]

    def pack(out, sign, outside):
        for slot, (q, depth) in enumerate(face_slots(0, sign)):
            out[slot] = c1[q, planes - 1 - depth if sign > 0 else depth]
        end = planes - 1 if sign > 0 else 0
        out[FLAG_SLOT] = fixed[0, end]
        out[RATE_SLOT] = fixed[1, end]
        clear_outside(out, outside)

    pack_pair(pack, "slab", near, far)


def gather_both(near, far, both, axis):
    odd = lax.rem(lax.axis_index(axis), 2)
    for slot in range(both.shape[1]):
        both[1 - odd, slot] = near[slot]
        both[odd, slot] = far[slot]


def corner_kernel(far_y, near_y, other, keys, far, near, known, both):
    planes = near_y.shape[1]
    gather_both(near_y, far_y, both, "inner")

    def pack(out, sign, outside):
        for side, sign_y in enumerate((1, -1)):
            picks = corner_rows(sign, sign_y) + [(FLAG_SLOT, 0), (RATE_SLOT, 0)]
            for row, (slot, depth) in enumerate(picks):
                x = planes - 1 - depth if sign > 0 else depth
                at = 3 * side + row // 8
                out[at, row % 8 : row % 8 + 1] = both[side, slot, x : x + 1]
        for part in range(3):
            out[FORCE_SLOT + part] = other[part]
        clear_outside(out, outside)

    pack_pair(pack, "slab", near, far)
    slots = keys.shape[0]
    known[:slots] = keys[...]
    for k in range(slots):
        slot, row, lanes = key_place(near_y, k)
        known[slots + k : slots + k + 1] = near_y[slot, row, lanes]


def with_edge(block, step_y, edge):
    rows = block.shape[0]
    sub = lax.broadcasted_iota(jnp.int32, block.shape, 0)
    if step_y > 0:
        return jnp.where(sub == 0, edge, roll_by(block, 1, 0))
    return jnp.where(sub == rows - 1, edge, roll_by(block, -1, 0))


def store_plane(extended, walls, second, at, rate, kind):
    values = []
    for q in range(Q):
        step_x, step_y, _ = VELOCITIES[q]
        block = extended[q, at + 1 - step_x]
        if step_y != 0:
            edge = walls[0 if step_y > 0 else 1, q, pl.ds(at + 1 - step_x, 1)]
            block = with_edge(block, step_y, edge)
        values.append(block)
    result = collide(values, rate, kind)
    for q in range(Q):
        second[q, at] = roll_by(result[q], VELOCITIES[q][2], 1)


def inside_kernel(
    c1,
    fixed,
    far_y,
    near_y,
    far_x,
    near_x,
    extended,
    walls,
    crossing,
    second,
    ends,
    both_y,
    both_x,
):
    planes, rows, _ = c1.shape[1:]
    wide = planes + 4
    gather_both(near_y, far_y, both_y, "inner")
    gather_both(near_x, far_x, both_x, "slab")
    for q in range(Q):
        for x in range(planes):
            extended[q, x + 2] = c1[q, x]
        extended[q, 1] = both_x[0, q]
        extended[q, planes + 2] = both_x[1, q]
        if VELOCITIES[q][0] > 0:
            extended[q, 0] = both_x[0, OPPOSITE[q]]
        if VELOCITIES[q][0] < 0:
            extended[q, planes + 3] = both_x[1, OPPOSITE[q]]
    for end in range(2):
        ends[end, 0] = both_x[end, FLAG_SLOT]
        ends[end, 1] = both_x[end, RATE_SLOT]

    for side, sign in enumerate((1, -1)):
        y = 0 if sign > 0 else rows - 1
        for slot in range(SLOTS):
            walls[side, slot, 2 : planes + 2] = both_y[side, slot]
        place = 0
        for q in range(Q):
            if VELOCITIES[q][1] != -sign:
                continue
            for x in range(wide):
                crossing[side, place, x : x + 1] = extended[q, x, y : y + 1]
            place += 1

    def inside_plane(x, carry):
        store_plane(extended, walls, second, x + 1, fixed[1, x], fixed[0, x])
        return carry

    lax.fori_loop(1, planes - 1, inside_plane, 0)


def second_kernel(count, tables, *refs):
    block_source_hbm, block_count = refs[:2]
    known = refs[2 : 2 + tables]
    far, near, fixed, extended, crossing, ends, internal_own = refs[2 + tables : 9 + tables]
    rest = refs[11 + tables :]
    out, mine = rest[:2]
    messages = rest[2 : 1 + count]
    walls, second = rest[1 + count : 3 + count]
    both, edges, loads, internal, block_source, sem = rest[3 + count :]
    copy = pltpu.make_async_copy(block_source_hbm, block_source, sem)
    copy.start()
    planes, rows, length = out.shape[1:]
    half = length // BLK
    slots = block_source.shape[2]
    wide = planes + 4
    slab = lax.axis_index("slab")
    inner = lax.axis_index("inner")
    slab_end = lax.axis_size("slab") - 1
    inner_end = lax.axis_size("inner") - 1
    gather_both(near, far, both, "slab")

    for side, sign in enumerate((1, -1)):
        for end, sign_x in enumerate((1, -1)):
            for row, (slot, depth) in enumerate(corner_rows(sign_x, sign)):
                at = (1 - depth) if sign_x > 0 else planes + 2 + depth
                source = 3 * side + row // 8
                walls[side, slot, at : at + 1] = both[end, source, row % 8 : row % 8 + 1]
            at = 1 if sign_x > 0 else planes + 2
            for row in (FLAG_SLOT, RATE_SLOT):
                source = 3 * side + row // 8
                walls[side, row, at : at + 1] = both[end, source, row % 8 : row % 8 + 1]

    def edge_planes(end, carry):
        x = end * (planes - 1)
        store_plane(extended, walls, second, x + 1, fixed[1, x], fixed[0, x])
        store_plane(extended, walls, second, end * (planes + 1), ends[end, 1], ends[end, 0])
        return carry

    lax.fori_loop(0, 2, edge_planes, 0)

    @pl.when(slab == 0)
    def _():
        for q in range(Q):
            if VELOCITIES[q][0] > 0:
                second[q, 0] = jnp.zeros((rows, length), F32)

    @pl.when(slab == slab_end)
    def _():
        for q in range(Q):
            if VELOCITIES[q][0] < 0:
                second[q, planes + 1] = jnp.zeros((rows, length), F32)

    across = lax.broadcasted_iota(jnp.int32, (wide, length), 0)
    hidden = ((across <= 1) & (slab == 0)) | ((across >= planes + 2) & (slab == slab_end))
    for side, sign, outside in ((0, 1, inner == 0), (1, -1, inner == inner_end)):
        values = []
        place = 0
        for q in range(Q):
            step_x, step_y, _ = VELOCITIES[q]
            if step_y == 0:
                block = walls[side, q]
            elif step_y == sign:
                block = walls[side, OPPOSITE[q]]
            else:
                block = crossing[side, place]
                place += 1
            values.append(roll_by(block, step_x, 0))
        result = collide(values, walls[side, RATE_SLOT], walls[side, FLAG_SLOT])
        place = 0
        for q in range(Q):
            if VELOCITIES[q][1] == sign:
                kept = jnp.where(hidden | outside, 0.0, result[q])
                edges[side, place] = roll_by(kept, VELOCITIES[q][2], 1)
                place += 1

    def plane_two(x, carry):
        values = []
        places = {1: 0, -1: 0}
        for q in range(Q):
            step_x, step_y, _ = VELOCITIES[q]
            block = second[q, x + 1 - step_x]
            if step_y != 0:
                edge = edges[0 if step_y > 0 else 1, places[step_y], pl.ds(x + 2 - step_x, 1)]
                places[step_y] += 1
                block = with_edge(block, step_y, edge)
            values.append(block)
            out[q, x] = block
        density, flow_x, flow_y, flow_z = moments(values)
        parts = (
            LOAD_SCALE * flow_x,
            LOAD_SCALE * (flow_y + (density - 1.0) / 3.0),
            LOAD_SCALE * flow_z,
        )
        for part in range(3):
            for piece in range(half):
                loads[x * half + piece, part] = parts[part][:, piece * BLK : (piece + 1) * BLK]
        return carry

    lax.fori_loop(0, planes, plane_two, 0)

    node_blocks = internal_own.shape[1] * half
    for part in range(3):
        for piece in range(half):
            at = piece * rows
            lanes = slice(piece * BLK, (piece + 1) * BLK)
            internal[part, at : at + rows] = (
                internal_own[part, :, lanes] + both[0, FORCE_SLOT + part, :, lanes]
            )
    copy.wait()
    live = jnp.broadcast_to(block_count[...], (1, BLK))
    blocks, keys = [], []
    for k in range(slots):
        run = block_source[0, 0, k]
        x = run // (rows * half)
        left = run - x * (rows * half)
        y = left // half
        piece = left - y * half
        blocks.append([loads[x * half + piece, part, pl.ds(y, 1)] for part in range(3)])
        keys.append(jnp.where(live > k, known[0][k : k + 1], -1.0))

    def summed(wanted):
        moved = [jnp.zeros((slots, BLK), F32)] * 3
        for k in range(slots):
            same = wanted == keys[k]
            for part in range(3):
                moved[part] = moved[part] + jnp.where(same, blocks[k][part], 0.0)
        for b in range(node_blocks):
            same = wanted == (inner * node_blocks + b).astype(F32)
            for part in range(3):
                moved[part] = moved[part] - jnp.where(same, internal[part, b : b + 1], 0.0)
        return moved

    node_ids = lax.broadcasted_iota(jnp.int32, (node_blocks, BLK), 0)
    own_ids = (node_ids + inner * node_blocks).astype(F32)
    moved = summed(known[0][:slots])
    for part in range(3):
        total = -internal[part]
        for k in range(slots):
            total = total + jnp.where(own_ids == keys[k], blocks[k][part], 0.0)
        mine[part * node_blocks : (part + 1) * node_blocks] = total
        start = 3 * node_blocks + part * slots
        mine[start : start + slots] = moved[part]
    for k in range(slots):
        start = 3 * (node_blocks + slots) + k
        mine[start : start + 1] = keys[k]

    table = []
    for ref in known:
        table += [ref[k * slots : (k + 1) * slots] for k in range(ref.shape[0] // slots)]
    place_ids = lax.broadcasted_iota(jnp.int32, (8, BLK), 0).astype(F32)
    for step, message in enumerate(messages, 1):
        dest = partner_of(inner, step, count)
        moved = summed(table[step])
        low = (dest * node_blocks).astype(F32)
        before = jnp.zeros((1, BLK), F32)
        chosen = [jnp.zeros((8, BLK), F32)] * 3
        nodes = jnp.full((8, BLK), -1.0, F32)
        for k in range(slots):
            named = (keys[k] >= low) & (keys[k] < low + node_blocks)
            here = named & (place_ids == before)
            for part in range(3):
                chosen[part] = jnp.where(here, blocks[k][part], chosen[part])
            nodes = jnp.where(here, keys[k], nodes)
            before = before + jnp.where(named, 1.0, 0.0)
        for part in range(3):
            message[part * slots : (part + 1) * slots, 0] = moved[part]
            at = 3 * slots + part * CAP
            message[at : at + CAP, 0] = chosen[part][:CAP]
        at = 3 * slots + 3 * CAP
        message[at : at + CAP, 0] = nodes[:CAP]


def element_kernel(
    elements, displacement, next_nodes, shape_inverse, stiffness, low_ids, high_ids, forces, shapes,
    numbers, corners,
):
    node_dev = displacement.shape[1]
    node_blocks = node_dev // BLK
    runs = elements.shape[1] // BLK
    for j in range(runs):
        lanes = slice(j * BLK, (j + 1) * BLK)
        for row in range(3):
            numbers[row, j : j + 1] = elements[row : row + 1, lanes]
            shapes[row, j : j + 1] = shape_inverse[row : row + 1, lanes]
    for row in range(3):
        low_ids[row] = (numbers[row] & (BLK - 1)).astype(F32)
        high_ids[row] = (numbers[row] >> 7).astype(F32)

    def gather(group, carry):
        rows = pl.ds(pl.multiple_of(group * 8, 8), 8)
        low = [numbers[corner, rows] & (BLK - 1) for corner in range(3)]
        high = [numbers[corner, rows] >> 7 for corner in range(3)]
        for corner in range(3):
            nodes = [jnp.zeros((8, BLK), F32)] * 3
            for block in range(2 * node_blocks):
                source = displacement if block < node_blocks else next_nodes
                start = (block % node_blocks) * BLK
                here = high[corner] == block
                for part in range(3):
                    row = source[part : part + 1, start : start + BLK]
                    picked = jnp.take_along_axis(
                        jnp.broadcast_to(row, (8, BLK)),
                        low[corner],
                        axis=1,
                        mode="promise_in_bounds",
                    )
                    nodes[part] = jnp.where(here, picked, nodes[part])
            for part in range(3):
                corners[corner, part, rows] = nodes[part]
        return carry

    lax.fori_loop(0, runs // 8, gather, 0)

    first, second, third = [[corners[c, p] for p in range(3)] for c in range(3)]
    diag_a = shapes[0]
    skew_b = shapes[1]
    diag_c = shapes[2]
    stiff = stiffness[...]
    edge_one = [second[p] - first[p] for p in range(3)]
    edge_two = [third[p] - first[p] for p in range(3)]
    one = [diag_a * edge_one[p] for p in range(3)]
    two = [skew_b * edge_one[p] + diag_c * edge_two[p] for p in range(3)]
    one[0] = one[0] + 1.0
    two[1] = two[1] + 1.0
    aa = one[0] * one[0] + one[1] * one[1] + one[2] * one[2]
    ab = one[0] * two[0] + one[1] * two[1] + one[2] * two[2]
    bb = two[0] * two[0] + two[1] * two[1] + two[2] * two[2]
    determinant = aa * bb - ab * ab
    scale = 1.0 / determinant
    inverse_aa = bb * scale
    inverse_ab = -ab * scale
    inverse_bb = aa * scale
    pressure = LAME_RATIO * (0.5 * jnp.log(determinant))
    for p in range(3):
        pulled_one = one[p] * inverse_aa + two[p] * inverse_ab
        pulled_two = one[p] * inverse_ab + two[p] * inverse_bb
        stress_one = stiff * (one[p] - pulled_one + pressure * pulled_one)
        stress_two = stiff * (two[p] - pulled_two + pressure * pulled_two)
        force_one = diag_a * stress_one + skew_b * stress_two
        force_two = diag_c * stress_two
        for corner, force in enumerate((-(force_one + force_two), force_one, force_two)):
            rest = force
            for part in range(PIECES):
                piece = rest.astype(jnp.bfloat16).astype(F32)
                rest = rest - piece
                forces[part * 3 + p, corner] = piece


def spread_kernel(low_ids, high_ids, forces, own, other):
    runs = low_ids.shape[1]
    parts, rows, length = own.shape
    pieces = length // BLK
    node_blocks = pieces * rows
    slots = 2 * node_blocks
    kind = jnp.bfloat16
    tile = 16
    slot_ids = lax.broadcasted_iota(jnp.int32, (slots, BLK), 0).astype(F32).astype(kind)
    lane_ids = lax.broadcasted_iota(jnp.int32, (BLK, BLK), 0).astype(F32).astype(kind)
    ones = jnp.ones((BLK, BLK), kind)
    none = jnp.zeros((BLK, BLK), kind)
    blank = jnp.zeros((slots, BLK), kind)

    def tall_row(row, count):
        block = jnp.broadcast_to(row, (tile, BLK)).astype(kind)
        return jnp.concatenate([block] * (count // tile), axis=0)

    total = None
    for corner in range(3):
        for first in range(0, runs, STEP):
            left = [[] for _ in range(parts * PIECES)]
            right = []
            for j in range(first, min(first + STEP, runs)):
                row = slice(j, j + 1)
                here = slot_ids == tall_row(high_ids[corner, row], slots)
                there = lane_ids == tall_row(low_ids[corner, row], BLK)
                right.append(jnp.where(there, ones, none))
                for part in range(parts * PIECES):
                    left[part].append(
                        jnp.where(here, tall_row(forces[part, corner, row], slots), blank)
                    )
            tall = jnp.concatenate([jnp.concatenate(part, axis=1) for part in left], axis=0)
            wide = jnp.concatenate(right, axis=1)
            product = lax.dot_general(
                tall, wide, (((1,), (1,)), ((), ())), preferred_element_type=F32
            )
            total = product if total is None else total + product
    for p in range(parts):
        summed = total[p * slots : (p + 1) * slots]
        for part in range(1, PIECES):
            start = (parts * part + p) * slots
            summed = summed + total[start : start + slots]
        for out, first in ((own, 0), (other, node_blocks)):
            for piece in range(pieces):
                at = first + piece * rows
                out[p, :, piece * BLK : (piece + 1) * BLK] = summed[at : at + rows]


def store_kernel(values, out_hbm, sem):
    store = pltpu.make_async_copy(values, out_hbm, sem)
    store.start()
    store.wait()


def final_kernel(mine, *refs):
    messages, (residual, motion) = refs[:-2], refs[-2:]
    slots = motion.shape[1]
    node_blocks = residual.shape[1] // BLK
    inner = lax.axis_index("inner")
    node_ids = lax.broadcasted_iota(jnp.int32, (node_blocks, BLK), 0)
    own_ids = (node_ids + inner * node_blocks).astype(F32)
    total = [mine[p * node_blocks : (p + 1) * node_blocks] for p in range(3)]
    start = 3 * node_blocks
    moved = [mine[start + p * slots : start + (p + 1) * slots] for p in range(3)]
    live = mine[start + 3 * slots : start + 4 * slots] >= 0.0
    for message in messages:
        for place in range(CAP):
            here = own_ids == message[3 * slots + 3 * CAP + place]
            for part in range(3):
                row = message[3 * slots + part * CAP + place]
                total[part] = total[part] + jnp.where(here, row, 0.0)
        for part in range(3):
            moved[part] = moved[part] + message[part * slots : (part + 1) * slots, 0]
    for part in range(3):
        for b in range(node_blocks):
            residual[part : part + 1, b * BLK : (b + 1) * BLK] = total[part][b : b + 1]
        motion[part] = jnp.where(live, COMPLIANCE * moved[part], 0.0)


def call(kernel, outs, operands, spaces, scratch=(), out_spaces=None, micros=1.0, aliases=None):
    spec = lambda space: pl.BlockSpec(memory_space=space)
    out_spaces = out_spaces or (pltpu.VMEM,) * len(outs)
    return pl.pallas_call(
        kernel,
        out_shape=outs,
        in_specs=[spec(space) for space in spaces],
        out_specs=tuple(spec(space) for space in out_spaces),
        scratch_shapes=list(scratch),
        input_output_aliases=aliases or {},
        compiler_params=pltpu.CompilerParams(vmem_limit_bytes=VMEM_BYTES),
        cost_estimate=pl.CostEstimate(
            flops=0, bytes_accessed=int(micros * 3.6e6), transcendentals=0
        ),
    )(*operands)


def in_pairs(count):
    return count > 1 and count & (count - 1) == 0


def partner_of(at, step, count):
    return at ^ step if in_pairs(count) else (at + step) % count


def exchange(block, axis, step):
    count = lax.axis_size(axis)
    return lax.ppermute(block, axis, [(i, partner_of(i, step, count)) for i in range(count)])


def all_keys(own, known, axis):
    count = lax.axis_size(axis)
    if not in_pairs(count):
        return [own] + [exchange(own, axis, count - step) for step in range(1, count)]
    tables = [known]
    reach = 2
    while reach < count:
        joined = tables[0] if len(tables) == 1 else jnp.concatenate(tables, axis=0)
        tables.append(exchange(joined, axis, reach))
        reach *= 2
    return tables


def around(block, axis, step):
    count = lax.axis_size(axis)
    return lax.ppermute(block, axis, [(i, (i + step) % count) for i in range(count)])


def swap(near, far, axis, beside):
    count, others = lax.axis_size(axis), lax.axis_size(beside)
    routes = []
    for start in (0, 1):
        route = []
        for other in range(others):
            for i in range(count):
                j = i + 1 if i % 2 == start else i - 1
                to = other
                if not 0 <= j < count:
                    j = i
                    to = other ^ 1 if others % 2 == 0 else other
                route.append((other * count + i, to * count + j))
        routes.append(route)
    axes = (beside, axis)
    return lax.ppermute(near, axes, routes[0]), lax.ppermute(far, axes, routes[1])


def shards(
    populations,
    relaxation,
    node_flags,
    displacement,
    elements,
    shape_inverse,
    stiffness,
    block_source,
    block_target,
    block_node,
    block_count,
):
    planes, rows, length = populations.shape[1:]
    half = length // BLK
    node_dev = displacement.shape[1]
    node_blocks = node_dev // BLK
    runs = stiffness.shape[0] // BLK
    slots = block_source.shape[2]
    count = lax.axis_size("inner")
    shape = lambda *dims: jax.ShapeDtypeStruct(dims, F32)
    whole = shape(*populations.shape)
    vmem, hbm, smem = pltpu.VMEM, pltpu.HBM, pltpu.SMEM

    next_nodes = around(displacement, "slab", -1)
    room = -(-slots // (planes * half))
    face_y = shape(max(SLOTS + room, PADDED_SLOTS), planes, length)
    face_x = shape(SLOTS, rows, length)
    pin = lambda block: pltpu.with_memory_space_constraint(block, hbm)
    whole_like = lambda block: jax.ShapeDtypeStruct(block.shape, block.dtype)
    shell = (displacement, elements, shape_inverse, stiffness.reshape(runs, BLK))
    c1, fixed, far, near, own_nodes, corners, inverses, stiff, own_keys = call(
        first_kernel,
        (
            whole,
            shape(2, planes, rows, length),
            face_y,
            face_y,
            *(whole_like(block) for block in shell),
            shape(slots, BLK),
        ),
        tuple(
            pin(block)
            for block in (populations, relaxation, node_flags, *shell, block_target, block_node)
        ),
        (hbm,) * 9,
        scratch=(
            pltpu.VMEM((planes, Q, rows, length), F32),
            pltpu.VMEM((planes, rows, length), F32),
            pltpu.VMEM((planes, rows, length), jnp.int32),
            pltpu.SMEM(block_target.shape, jnp.int32),
            pltpu.SMEM(block_node.shape, jnp.int32),
            pltpu.SemaphoreType.DMA((planes + 8,)),
        ),
        micros=1.5,
    )
    near_y, far_y = swap(near, far, "inner", "slab")
    numbers = shape(3, runs, BLK)
    low_ids, high_ids, forces = call(
        element_kernel,
        (numbers, numbers, shape(3 * PIECES, 3, runs, BLK)),
        (corners, own_nodes, next_nodes, inverses, stiff),
        (vmem,) * 5,
        scratch=(
            pltpu.VMEM((3, runs, BLK), F32),
            pltpu.VMEM((3, runs, BLK), jnp.int32),
            pltpu.VMEM((3, 3, runs, BLK), F32),
        ),
        micros=0.001,
    )
    far, near = call(
        slab_face_kernel, (face_x, face_x), (c1, fixed, low_ids), (vmem,) * 3, micros=0.001
    )
    near_x, far_x = swap(near, far, "slab", "group")
    nodal = shape(3, node_blocks // half, length)
    own, other = call(
        spread_kernel,
        (nodal, nodal),
        (low_ids, high_ids, forces),
        (vmem,) * 3,
        micros=0.001,
    )
    corner = shape(CORNER_SLOTS, rows, length)
    far, near, known = call(
        corner_kernel,
        (corner, corner, shape(2 * slots, BLK)),
        (far_y, near_y, other, own_keys),
        (vmem,) * 4,
        scratch=(pltpu.VMEM((2, SLOTS, planes, length), F32),),
        micros=0.3,
    )
    near_c, far_c = swap(near, far, "slab", "group")
    wide = planes + 4
    walls_shape = shape(2, SLOTS, wide, length)
    second_shape = shape(Q, planes + 2, rows, length)
    extended, walls, crossing, second, ends = call(
        inside_kernel,
        (
            shape(Q, wide, rows, length),
            walls_shape,
            shape(2, 5, wide, length),
            second_shape,
            shape(2, 2, rows, length),
        ),
        (c1, fixed, far_y, near_y, far_x, near_x),
        (vmem,) * 6,
        scratch=(
            pltpu.VMEM((2, SLOTS, planes, length), F32),
            pltpu.VMEM((2, SLOTS, rows, length), F32),
        ),
        micros=0.8,
    )
    tables = all_keys(own_keys, known, "inner")
    first = 2 + len(tables)
    line = shape(3 * slots + 4 * CAP, 1, BLK)
    outs = call(
        functools.partial(second_kernel, count, len(tables)),
        (
            whole,
            shape(3 * node_blocks + 4 * slots, BLK),
            *([line] * (count - 1)),
            walls_shape,
            second_shape,
        ),
        (
            pin(block_source),
            block_count,
            *tables,
            far_c,
            near_c,
            fixed,
            extended,
            crossing,
            ends,
            own,
            walls,
            second,
        ),
        (hbm,) + (vmem,) * (first + 8),
        aliases={first + 7: 1 + count, first + 8: 2 + count},
        scratch=(
            pltpu.VMEM((2, CORNER_SLOTS, rows, length), F32),
            pltpu.VMEM((2, 5, wide, length), F32),
            pltpu.VMEM((planes * half, 3, rows, BLK), F32),
            pltpu.VMEM((3, node_blocks, BLK), F32),
            pltpu.SMEM(block_source.shape, jnp.int32),
            pltpu.SemaphoreType.DMA(()),
        ),
        micros=1.5,
    )
    values, mine = outs[:2]
    arrived = [exchange(outs[1 + step], "inner", step) for step in range(count - 1, 0, -1)]
    (populations_out,) = call(
        store_kernel,
        (whole,),
        (values,),
        (vmem,),
        out_spaces=(hbm,),
        scratch=(pltpu.SemaphoreType.DMA(()),),
        micros=1.0,
    )
    residual, motion = call(
        final_kernel,
        (shape(3, node_dev), shape(3, slots, BLK)),
        (mine, *arrived),
        (vmem,) * count,
        micros=0.8,
    )
    return populations_out, residual, motion.transpose(1, 0, 2)[None, None]


def solution(mesh):
    return jax.shard_map(
        shards,
        mesh=mesh,
        in_specs=(
            P(None, ("group", "slab"), "inner", None),
            P(("group", "slab"), "inner", None),
            P(("group", "slab"), "inner", None),
            P(None, ("group", "slab", "inner")),
            P(None, ("group", "slab", "inner")),
            P(None, ("group", "slab", "inner")),
            P(("group", "slab", "inner")),
            P(("group", "slab"), "inner", None),
            P(("group", "slab"), "inner", None),
            P(("group", "slab"), "inner", None),
            P(("group", "slab"), "inner"),
        ),
        out_specs=(
            P(None, ("group", "slab"), "inner", None),
            P(None, ("group", "slab", "inner")),
            P(("group", "slab"), "inner", None, None, None),
        ),
        check_vma=False,
    )
```

```python
import functools

import jax
import jax.numpy as jnp
from jax import lax
from jax.experimental import pallas as pl
from jax.experimental.pallas import tpu as pltpu
from jax.sharding import PartitionSpec as P

BLK = 128
VELOCITIES = (
    (0, 0, 0),
    (1, 0, 0),
    (-1, 0, 0),
    (0, 1, 0),
    (0, -1, 0),
    (0, 0, 1),
    (0, 0, -1),
    (1, 1, 0),
    (-1, -1, 0),
    (1, -1, 0),
    (-1, 1, 0),
    (1, 0, 1),
    (-1, 0, -1),
    (1, 0, -1),
    (-1, 0, 1),
    (0, 1, 1),
    (0, -1, -1),
    (0, 1, -1),
    (0, -1, 1),
)
WEIGHTS = (1.0 / 3.0,) + (1.0 / 18.0,) * 6 + (1.0 / 36.0,) * 12
OPPOSITE = (0, 2, 1, 4, 3, 6, 5, 8, 7, 10, 9, 12, 11, 14, 13, 16, 15, 18, 17)
INLET_SPEED = 0.04
LOAD_SCALE = 25.0
COMPLIANCE = 0.5
LAME_RATIO = 2.0
Q = 19
FLAG_SLOT = 19
RATE_SLOT = 20
SLOTS = 21
PADDED_SLOTS = 24
FORCE_SLOT = 6
CORNER_SLOTS = FORCE_SLOT + 3
PIECES = 2
CAP = 3
STEP = 4
F32 = jnp.float32
VMEM_BYTES = 48 * 1024 * 1024


def moments(values):
    sums = [values[q] + values[q + 1] for q in range(1, Q, 2)]
    diffs = [values[q] - values[q + 1] for q in range(1, Q, 2)]
    density = values[0]
    for term in sums:
        density = density + term
    flows = []
    for axis in range(3):
        total = None
        for k, q in enumerate(range(1, Q, 2)):
            factor = VELOCITIES[q][axis]
            if factor == 0:
                continue
            if total is None:
                total = diffs[k] if factor > 0 else -diffs[k]
            else:
                total = total + diffs[k] if factor > 0 else total - diffs[k]
        flows.append(total)
    return density, flows[0], flows[1], flows[2]


def collide(values, rate, kind):
    density, flow_x, flow_y, flow_z = moments(values)
    inverse = 1.0 / density
    wall = kind == 1
    inlet = kind == 2
    fluid = kind == 0
    vel = (
        jnp.where(inlet, INLET_SPEED, flow_x * inverse),
        jnp.where(inlet, 0.0, flow_y * inverse),
        jnp.where(inlet, 0.0, flow_z * inverse),
    )
    scale = jnp.where(fluid, density, 1.0)
    rate = jnp.where(fluid, rate, 1.0)
    base = 1.0 - 1.5 * (vel[0] * vel[0] + vel[1] * vel[1] + vel[2] * vel[2])
    weighted = {w: w * scale for w in set(WEIGHTS)}
    out = [None] * Q
    relaxed = values[0] + rate * (weighted[WEIGHTS[0]] * base - values[0])
    out[0] = jnp.where(wall, values[0], relaxed)
    for q in range(1, Q, 2):
        project = None
        for factor, component in zip(VELOCITIES[q], vel):
            if factor == 0:
                continue
            if project is None:
                project = component
            else:
                project = project + component if factor > 0 else project - component
        even = base + 4.5 * (project * project)
        odd = 3.0 * project
        w = weighted[WEIGHTS[q]]
        forward = values[q] + rate * (w * (even + odd) - values[q])
        backward = values[q + 1] + rate * (w * (even - odd) - values[q + 1])
        out[q] = jnp.where(wall, values[q + 1], forward)
        out[q + 1] = jnp.where(wall, values[q], backward)
    return out


def roll_by(block, step, axis):
    if step == 0:
        return block
    return pltpu.roll(block, step % block.shape[axis], axis)


def face_slots(axis, sign):
    picks = []
    for q in range(Q):
        if VELOCITIES[q][axis] * sign >= 0:
            picks.append((q, 0))
        else:
            picks.append((OPPOSITE[q], 1))
    return picks


def mirror(q, axis):
    flipped = tuple(-c if k == axis else c for k, c in enumerate(VELOCITIES[q]))
    return VELOCITIES.index(flipped)


def corner_rows(sign_x, sign_y):
    rows = []
    for q, depth in face_slots(0, sign_x):
        if VELOCITIES[q][1] * sign_y >= 0:
            rows.append((q, depth))
        else:
            rows.append((OPPOSITE[mirror(q, 1)], depth))
    return rows


def first_kernel(
    pops_hbm,
    rate_hbm,
    flags_hbm,
    displacement_hbm,
    elements_hbm,
    shape_hbm,
    stiffness_hbm,
    block_target_hbm,
    block_node_hbm,
    c1,
    fixed,
    far,
    near,
    displacement,
    elements,
    shape_inverse,
    stiffness,
    keys,
    pops,
    rate,
    flags,
    block_target,
    block_node,
    sems,
):
    planes, rows = c1.shape[1], c1.shape[2]
    copies = [
        pltpu.make_async_copy(rate_hbm, rate, sems.at[planes]),
        pltpu.make_async_copy(flags_hbm, flags, sems.at[planes + 1]),
    ]
    loads = [
        pltpu.make_async_copy(pops_hbm.at[:, x], pops.at[x], sems.at[x]) for x in range(planes)
    ]
    shell = [
        pltpu.make_async_copy(source, target, sems.at[planes + 2 + k])
        for k, (source, target) in enumerate(
            (
                (displacement_hbm, displacement),
                (elements_hbm, elements),
                (shape_hbm, shape_inverse),
                (stiffness_hbm, stiffness),
                (block_target_hbm, block_target),
                (block_node_hbm, block_node),
            )
        )
    ]
    for copy in loads[:1] + copies + loads[1:] + shell:
        copy.start()
    for copy in copies:
        copy.wait()

    def plane(x, carry):
        pltpu.make_async_copy(pops_hbm.at[:, x], pops.at[x], sems.at[x]).wait()
        kind = flags[x]
        values = [pops[x, q] for q in range(Q)]
        result = collide(values, rate[x], kind)
        for q in range(Q):
            c1[q, x] = roll_by(result[q], VELOCITIES[q][2], 1)
        fixed[0, x] = kind.astype(F32)
        fixed[1, x] = rate[x]
        return carry

    lax.fori_loop(0, planes, plane, 0)

    def pack(out, sign, outside):
        def line(x, carry):
            for slot, (q, depth) in enumerate(face_slots(1, sign)):
                y = rows - 1 - depth if sign > 0 else depth
                out[slot, pl.ds(x, 1)] = c1[q, x, y : y + 1]
            y = rows - 1 if sign > 0 else 0
            for k, slot in enumerate((FLAG_SLOT, RATE_SLOT)):
                out[slot, pl.ds(x, 1)] = fixed[k, x, y : y + 1]
            return carry

        lax.fori_loop(0, planes, line, 0)
        for slot in range(SLOTS, out.shape[0]):
            out[slot] = jnp.zeros(out.shape[1:], F32)
        clear_outside(out, outside)

    pack_pair(pack, "inner", near, far)
    for copy in shell:
        copy.wait()
    node_blocks = displacement.shape[1] // BLK
    for k in range(keys.shape[0]):
        key = block_target[0, 0, k] * node_blocks + block_node[0, 0, k]
        line = jnp.broadcast_to(key, (1, BLK)).astype(F32)
        keys[k : k + 1] = line
        slot, row, lanes = key_place(near, k)
        near[slot, row, lanes] = line


def key_place(face, k):
    planes, pieces = face.shape[1], face.shape[2] // BLK
    row, piece = divmod(k, pieces)
    slot, row = divmod(row, planes)
    return SLOTS + slot, slice(row, row + 1), slice(piece * BLK, (piece + 1) * BLK)


def clear_outside(out, outside):
    @pl.when(outside)
    def _():
        out[...] = jnp.zeros(out.shape, F32)


def pack_pair(pack, axis, near, far):
    at = lax.axis_index(axis)
    even = lax.rem(at, 2) == 0
    first, last = at == 0, at == lax.axis_size(axis) - 1

    @pl.when(even)
    def _():
        pack(near, 1, last)
        pack(far, -1, first)

    @pl.when(jnp.logical_not(even))
    def _():
        pack(near, -1, first)
        pack(far, 1, last)


def slab_face_kernel(c1, fixed, numbers, far, near):
    del numbers
    planes = c1.shape[1]

    def pack(out, sign, outside):
        for slot, (q, depth) in enumerate(face_slots(0, sign)):
            out[slot] = c1[q, planes - 1 - depth if sign > 0 else depth]
        end = planes - 1 if sign > 0 else 0
        out[FLAG_SLOT] = fixed[0, end]
        out[RATE_SLOT] = fixed[1, end]
        clear_outside(out, outside)

    pack_pair(pack, "slab", near, far)


def gather_both(near, far, both, axis):
    odd = lax.rem(lax.axis_index(axis), 2)
    for slot in range(both.shape[1]):
        both[1 - odd, slot] = near[slot]
        both[odd, slot] = far[slot]


def corner_kernel(far_y, near_y, other, keys, far, near, known, both):
    planes = near_y.shape[1]
    gather_both(near_y, far_y, both, "inner")

    def pack(out, sign, outside):
        for side, sign_y in enumerate((1, -1)):
            picks = corner_rows(sign, sign_y) + [(FLAG_SLOT, 0), (RATE_SLOT, 0)]
            for row, (slot, depth) in enumerate(picks):
                x = planes - 1 - depth if sign > 0 else depth
                at = 3 * side + row // 8
                out[at, row % 8 : row % 8 + 1] = both[side, slot, x : x + 1]
        for part in range(3):
            out[FORCE_SLOT + part] = other[part]
        clear_outside(out, outside)

    pack_pair(pack, "slab", near, far)
    slots = keys.shape[0]
    known[:slots] = keys[...]
    for k in range(slots):
        slot, row, lanes = key_place(near_y, k)
        known[slots + k : slots + k + 1] = near_y[slot, row, lanes]


def with_edge(block, step_y, edge):
    rows = block.shape[0]
    sub = lax.broadcasted_iota(jnp.int32, block.shape, 0)
    if step_y > 0:
        return jnp.where(sub == 0, edge, roll_by(block, 1, 0))
    return jnp.where(sub == rows - 1, edge, roll_by(block, -1, 0))


def store_plane(extended, walls, second, at, rate, kind):
    values = []
    for q in range(Q):
        step_x, step_y, _ = VELOCITIES[q]
        block = extended[q, at + 1 - step_x]
        if step_y != 0:
            edge = walls[0 if step_y > 0 else 1, q, pl.ds(at + 1 - step_x, 1)]
            block = with_edge(block, step_y, edge)
        values.append(block)
    result = collide(values, rate, kind)
    for q in range(Q):
        second[q, at] = roll_by(result[q], VELOCITIES[q][2], 1)


def inside_kernel(
    c1,
    fixed,
    far_y,
    near_y,
    far_x,
    near_x,
    extended,
    walls,
    crossing,
    second,
    ends,
    both_y,
    both_x,
):
    planes, rows, _ = c1.shape[1:]
    wide = planes + 4
    gather_both(near_y, far_y, both_y, "inner")
    gather_both(near_x, far_x, both_x, "slab")
    for q in range(Q):
        for x in range(planes):
            extended[q, x + 2] = c1[q, x]
        extended[q, 1] = both_x[0, q]
        extended[q, planes + 2] = both_x[1, q]
        if VELOCITIES[q][0] > 0:
            extended[q, 0] = both_x[0, OPPOSITE[q]]
        if VELOCITIES[q][0] < 0:
            extended[q, planes + 3] = both_x[1, OPPOSITE[q]]
    for end in range(2):
        ends[end, 0] = both_x[end, FLAG_SLOT]
        ends[end, 1] = both_x[end, RATE_SLOT]

    for side, sign in enumerate((1, -1)):
        y = 0 if sign > 0 else rows - 1
        for slot in range(SLOTS):
            walls[side, slot, 2 : planes + 2] = both_y[side, slot]
        place = 0
        for q in range(Q):
            if VELOCITIES[q][1] != -sign:
                continue
            for x in range(wide):
                crossing[side, place, x : x + 1] = extended[q, x, y : y + 1]
            place += 1

    def inside_plane(x, carry):
        store_plane(extended, walls, second, x + 1, fixed[1, x], fixed[0, x])
        return carry

    lax.fori_loop(1, planes - 1, inside_plane, 0)


def second_kernel(
    block_source_hbm,
    far,
    near,
    fixed,
    extended,
    crossing,
    ends,
    internal_own,
    walls_in,
    second_in,
    out,
    blocks,
    internal,
    walls,
    second,
    both,
    edges,
    loads,
    block_source,
    sem,
):
    del walls_in, second_in
    copy = pltpu.make_async_copy(block_source_hbm, block_source, sem)
    copy.start()
    planes, rows, length = out.shape[1:]
    half = length // BLK
    slots = block_source.shape[2]
    wide = planes + 4
    slab = lax.axis_index("slab")
    inner = lax.axis_index("inner")
    slab_end = lax.axis_size("slab") - 1
    inner_end = lax.axis_size("inner") - 1
    gather_both(near, far, both, "slab")

    for side, sign in enumerate((1, -1)):
        for end, sign_x in enumerate((1, -1)):
            for row, (slot, depth) in enumerate(corner_rows(sign_x, sign)):
                at = (1 - depth) if sign_x > 0 else planes + 2 + depth
                source = 3 * side + row // 8
                walls[side, slot, at : at + 1] = both[end, source, row % 8 : row % 8 + 1]
            at = 1 if sign_x > 0 else planes + 2
            for row in (FLAG_SLOT, RATE_SLOT):
                source = 3 * side + row // 8
                walls[side, row, at : at + 1] = both[end, source, row % 8 : row % 8 + 1]

    def edge_planes(end, carry):
        x = end * (planes - 1)
        store_plane(extended, walls, second, x + 1, fixed[1, x], fixed[0, x])
        store_plane(extended, walls, second, end * (planes + 1), ends[end, 1], ends[end, 0])
        return carry

    lax.fori_loop(0, 2, edge_planes, 0)

    @pl.when(slab == 0)
    def _():
        for q in range(Q):
            if VELOCITIES[q][0] > 0:
                second[q, 0] = jnp.zeros((rows, length), F32)

    @pl.when(slab == slab_end)
    def _():
        for q in range(Q):
            if VELOCITIES[q][0] < 0:
                second[q, planes + 1] = jnp.zeros((rows, length), F32)

    across = lax.broadcasted_iota(jnp.int32, (wide, length), 0)
    hidden = ((across <= 1) & (slab == 0)) | ((across >= planes + 2) & (slab == slab_end))
    for side, sign, outside in ((0, 1, inner == 0), (1, -1, inner == inner_end)):
        values = []
        place = 0
        for q in range(Q):
            step_x, step_y, _ = VELOCITIES[q]
            if step_y == 0:
                block = walls[side, q]
            elif step_y == sign:
                block = walls[side, OPPOSITE[q]]
            else:
                block = crossing[side, place]
                place += 1
            values.append(roll_by(block, step_x, 0))
        result = collide(values, walls[side, RATE_SLOT], walls[side, FLAG_SLOT])
        place = 0
        for q in range(Q):
            if VELOCITIES[q][1] == sign:
                kept = jnp.where(hidden | outside, 0.0, result[q])
                edges[side, place] = roll_by(kept, VELOCITIES[q][2], 1)
                place += 1

    def plane_two(x, carry):
        values = []
        places = {1: 0, -1: 0}
        for q in range(Q):
            step_x, step_y, _ = VELOCITIES[q]
            block = second[q, x + 1 - step_x]
            if step_y != 0:
                edge = edges[0 if step_y > 0 else 1, places[step_y], pl.ds(x + 2 - step_x, 1)]
                places[step_y] += 1
                block = with_edge(block, step_y, edge)
            values.append(block)
            out[q, x] = block
        density, flow_x, flow_y, flow_z = moments(values)
        parts = (
            LOAD_SCALE * flow_x,
            LOAD_SCALE * (flow_y + (density - 1.0) / 3.0),
            LOAD_SCALE * flow_z,
        )
        for part in range(3):
            for piece in range(half):
                loads[x * half + piece, part] = parts[part][:, piece * BLK : (piece + 1) * BLK]
        return carry

    lax.fori_loop(0, planes, plane_two, 0)

    node_blocks = internal_own.shape[1] * half
    for part in range(3):
        for piece in range(half):
            at = piece * rows
            lanes = slice(piece * BLK, (piece + 1) * BLK)
            internal[part, at : at + rows] = (
                internal_own[part, :, lanes] + both[0, FORCE_SLOT + part, :, lanes]
            )
    copy.wait()
    for k in range(slots):
        run = block_source[0, 0, k]
        x = run // (rows * half)
        left = run - x * (rows * half)
        y = left // half
        piece = left - y * half
        for part in range(3):
            row = 3 * k + part
            blocks[row : row + 1] = loads[x * half + piece, part, pl.ds(y, 1)]


def message_kernel(count, tables, block_count, *refs):
    known = refs[:tables]
    block_rows, internal, mine = refs[tables : tables + 3]
    messages = refs[tables + 3 :]
    slots = block_rows.shape[0] // 3
    node_blocks = internal.shape[1]
    inner = lax.axis_index("inner")
    live = jnp.broadcast_to(block_count[...], (1, BLK))
    blocks, keys = [], []
    for k in range(slots):
        blocks.append([block_rows[3 * k + part : 3 * k + part + 1] for part in range(3)])
        keys.append(jnp.where(live > k, known[0][k : k + 1], -1.0))

    def summed(wanted):
        moved = [jnp.zeros((slots, BLK), F32)] * 3
        for k in range(slots):
            same = wanted == keys[k]
            for part in range(3):
                moved[part] = moved[part] + jnp.where(same, blocks[k][part], 0.0)
        for b in range(node_blocks):
            same = wanted == (inner * node_blocks + b).astype(F32)
            for part in range(3):
                moved[part] = moved[part] - jnp.where(same, internal[part, b : b + 1], 0.0)
        return moved

    node_ids = lax.broadcasted_iota(jnp.int32, (node_blocks, BLK), 0)
    own_ids = (node_ids + inner * node_blocks).astype(F32)
    moved = summed(known[0][:slots])
    for part in range(3):
        total = -internal[part]
        for k in range(slots):
            total = total + jnp.where(own_ids == keys[k], blocks[k][part], 0.0)
        mine[part * node_blocks : (part + 1) * node_blocks] = total
        start = 3 * node_blocks + part * slots
        mine[start : start + slots] = moved[part]
    for k in range(slots):
        start = 3 * (node_blocks + slots) + k
        mine[start : start + 1] = keys[k]

    table = []
    for ref in known:
        table += [ref[k * slots : (k + 1) * slots] for k in range(ref.shape[0] // slots)]
    place_ids = lax.broadcasted_iota(jnp.int32, (8, BLK), 0).astype(F32)
    for step, message in enumerate(messages, 1):
        dest = partner_of(inner, step, count)
        moved = summed(table[step])
        low = (dest * node_blocks).astype(F32)
        before = jnp.zeros((1, BLK), F32)
        chosen = [jnp.zeros((8, BLK), F32)] * 3
        nodes = jnp.full((8, BLK), -1.0, F32)
        for k in range(slots):
            named = (keys[k] >= low) & (keys[k] < low + node_blocks)
            here = named & (place_ids == before)
            for part in range(3):
                chosen[part] = jnp.where(here, blocks[k][part], chosen[part])
            nodes = jnp.where(here, keys[k], nodes)
            before = before + jnp.where(named, 1.0, 0.0)
        for part in range(3):
            message[part * slots : (part + 1) * slots, 0] = moved[part]
            at = 3 * slots + part * CAP
            message[at : at + CAP, 0] = chosen[part][:CAP]
        at = 3 * slots + 3 * CAP
        message[at : at + CAP, 0] = nodes[:CAP]


def element_kernel(
    elements, displacement, next_nodes, shape_inverse, stiffness, low_ids, high_ids, forces, shapes,
    numbers, corners,
):
    node_dev = displacement.shape[1]
    node_blocks = node_dev // BLK
    runs = elements.shape[1] // BLK
    for j in range(runs):
        lanes = slice(j * BLK, (j + 1) * BLK)
        for row in range(3):
            numbers[row, j : j + 1] = elements[row : row + 1, lanes]
            shapes[row, j : j + 1] = shape_inverse[row : row + 1, lanes]
    for row in range(3):
        low_ids[row] = (numbers[row] & (BLK - 1)).astype(F32)
        high_ids[row] = (numbers[row] >> 7).astype(F32)

    def gather(group, carry):
        rows = pl.ds(pl.multiple_of(group * 8, 8), 8)
        low = [numbers[corner, rows] & (BLK - 1) for corner in range(3)]
        high = [numbers[corner, rows] >> 7 for corner in range(3)]
        for corner in range(3):
            nodes = [jnp.zeros((8, BLK), F32)] * 3
            for block in range(2 * node_blocks):
                source = displacement if block < node_blocks else next_nodes
                start = (block % node_blocks) * BLK
                here = high[corner] == block
                for part in range(3):
                    row = source[part : part + 1, start : start + BLK]
                    picked = jnp.take_along_axis(
                        jnp.broadcast_to(row, (8, BLK)),
                        low[corner],
                        axis=1,
                        mode="promise_in_bounds",
                    )
                    nodes[part] = jnp.where(here, picked, nodes[part])
            for part in range(3):
                corners[corner, part, rows] = nodes[part]
        return carry

    lax.fori_loop(0, runs // 8, gather, 0)

    first, second, third = [[corners[c, p] for p in range(3)] for c in range(3)]
    diag_a = shapes[0]
    skew_b = shapes[1]
    diag_c = shapes[2]
    stiff = stiffness[...]
    edge_one = [second[p] - first[p] for p in range(3)]
    edge_two = [third[p] - first[p] for p in range(3)]
    one = [diag_a * edge_one[p] for p in range(3)]
    two = [skew_b * edge_one[p] + diag_c * edge_two[p] for p in range(3)]
    one[0] = one[0] + 1.0
    two[1] = two[1] + 1.0
    aa = one[0] * one[0] + one[1] * one[1] + one[2] * one[2]
    ab = one[0] * two[0] + one[1] * two[1] + one[2] * two[2]
    bb = two[0] * two[0] + two[1] * two[1] + two[2] * two[2]
    determinant = aa * bb - ab * ab
    scale = 1.0 / determinant
    inverse_aa = bb * scale
    inverse_ab = -ab * scale
    inverse_bb = aa * scale
    pressure = LAME_RATIO * (0.5 * jnp.log(determinant))
    for p in range(3):
        pulled_one = one[p] * inverse_aa + two[p] * inverse_ab
        pulled_two = one[p] * inverse_ab + two[p] * inverse_bb
        stress_one = stiff * (one[p] - pulled_one + pressure * pulled_one)
        stress_two = stiff * (two[p] - pulled_two + pressure * pulled_two)
        force_one = diag_a * stress_one + skew_b * stress_two
        force_two = diag_c * stress_two
        for corner, force in enumerate((-(force_one + force_two), force_one, force_two)):
            rest = force
            for part in range(PIECES):
                piece = rest.astype(jnp.bfloat16).astype(F32)
                rest = rest - piece
                forces[part * 3 + p, corner] = piece


def spread_kernel(low_ids, high_ids, forces, own, other):
    runs = low_ids.shape[1]
    parts, rows, length = own.shape
    pieces = length // BLK
    node_blocks = pieces * rows
    slots = 2 * node_blocks
    kind = jnp.bfloat16
    tile = 16
    slot_ids = lax.broadcasted_iota(jnp.int32, (slots, BLK), 0).astype(F32).astype(kind)
    lane_ids = lax.broadcasted_iota(jnp.int32, (BLK, BLK), 0).astype(F32).astype(kind)
    ones = jnp.ones((BLK, BLK), kind)
    none = jnp.zeros((BLK, BLK), kind)
    blank = jnp.zeros((slots, BLK), kind)

    def tall_row(row, count):
        block = jnp.broadcast_to(row, (tile, BLK)).astype(kind)
        return jnp.concatenate([block] * (count // tile), axis=0)

    total = None
    for corner in range(3):
        for first in range(0, runs, STEP):
            left = [[] for _ in range(parts * PIECES)]
            right = []
            for j in range(first, min(first + STEP, runs)):
                row = slice(j, j + 1)
                here = slot_ids == tall_row(high_ids[corner, row], slots)
                there = lane_ids == tall_row(low_ids[corner, row], BLK)
                right.append(jnp.where(there, ones, none))
                for part in range(parts * PIECES):
                    left[part].append(
                        jnp.where(here, tall_row(forces[part, corner, row], slots), blank)
                    )
            tall = jnp.concatenate([jnp.concatenate(part, axis=1) for part in left], axis=0)
            wide = jnp.concatenate(right, axis=1)
            product = lax.dot_general(
                tall, wide, (((1,), (1,)), ((), ())), preferred_element_type=F32
            )
            total = product if total is None else total + product
    for p in range(parts):
        summed = total[p * slots : (p + 1) * slots]
        for part in range(1, PIECES):
            start = (parts * part + p) * slots
            summed = summed + total[start : start + slots]
        for out, first in ((own, 0), (other, node_blocks)):
            for piece in range(pieces):
                at = first + piece * rows
                out[p, :, piece * BLK : (piece + 1) * BLK] = summed[at : at + rows]


def store_kernel(values, out_hbm, sem):
    store = pltpu.make_async_copy(values, out_hbm, sem)
    store.start()
    store.wait()


def final_kernel(mine, *refs):
    messages, (residual, motion) = refs[:-2], refs[-2:]
    slots = motion.shape[1]
    node_blocks = residual.shape[1] // BLK
    inner = lax.axis_index("inner")
    node_ids = lax.broadcasted_iota(jnp.int32, (node_blocks, BLK), 0)
    own_ids = (node_ids + inner * node_blocks).astype(F32)
    total = [mine[p * node_blocks : (p + 1) * node_blocks] for p in range(3)]
    start = 3 * node_blocks
    moved = [mine[start + p * slots : start + (p + 1) * slots] for p in range(3)]
    live = mine[start + 3 * slots : start + 4 * slots] >= 0.0
    for message in messages:
        for place in range(CAP):
            here = own_ids == message[3 * slots + 3 * CAP + place]
            for part in range(3):
                row = message[3 * slots + part * CAP + place]
                total[part] = total[part] + jnp.where(here, row, 0.0)
        for part in range(3):
            moved[part] = moved[part] + message[part * slots : (part + 1) * slots, 0]
    for part in range(3):
        for b in range(node_blocks):
            residual[part : part + 1, b * BLK : (b + 1) * BLK] = total[part][b : b + 1]
        motion[part] = jnp.where(live, COMPLIANCE * moved[part], 0.0)


def call(kernel, outs, operands, spaces, scratch=(), out_spaces=None, micros=1.0, aliases=None):
    spec = lambda space: pl.BlockSpec(memory_space=space)
    out_spaces = out_spaces or (pltpu.VMEM,) * len(outs)
    return pl.pallas_call(
        kernel,
        out_shape=outs,
        in_specs=[spec(space) for space in spaces],
        out_specs=tuple(spec(space) for space in out_spaces),
        scratch_shapes=list(scratch),
        input_output_aliases=aliases or {},
        compiler_params=pltpu.CompilerParams(vmem_limit_bytes=VMEM_BYTES),
        cost_estimate=pl.CostEstimate(
            flops=0, bytes_accessed=int(micros * 3.6e6), transcendentals=0
        ),
    )(*operands)


def in_pairs(count):
    return count > 1 and count & (count - 1) == 0


def partner_of(at, step, count):
    return at ^ step if in_pairs(count) else (at + step) % count


def exchange(block, axis, step):
    count = lax.axis_size(axis)
    return lax.ppermute(block, axis, [(i, partner_of(i, step, count)) for i in range(count)])


def all_keys(own, known, axis):
    count = lax.axis_size(axis)
    if not in_pairs(count):
        return [own] + [exchange(own, axis, count - step) for step in range(1, count)]
    tables = [known]
    reach = 2
    while reach < count:
        joined = tables[0] if len(tables) == 1 else jnp.concatenate(tables, axis=0)
        tables.append(exchange(joined, axis, reach))
        reach *= 2
    return tables


def around(block, axis, step):
    count = lax.axis_size(axis)
    return lax.ppermute(block, axis, [(i, (i + step) % count) for i in range(count)])


def swap(near, far, axis, beside):
    count, others = lax.axis_size(axis), lax.axis_size(beside)
    routes = []
    for start in (0, 1):
        route = []
        for other in range(others):
            for i in range(count):
                j = i + 1 if i % 2 == start else i - 1
                to = other
                if not 0 <= j < count:
                    j = i
                    to = other ^ 1 if others % 2 == 0 else other
                route.append((other * count + i, to * count + j))
        routes.append(route)
    axes = (beside, axis)
    return lax.ppermute(near, axes, routes[0]), lax.ppermute(far, axes, routes[1])


def shards(
    populations,
    relaxation,
    node_flags,
    displacement,
    elements,
    shape_inverse,
    stiffness,
    block_source,
    block_target,
    block_node,
    block_count,
):
    planes, rows, length = populations.shape[1:]
    half = length // BLK
    node_dev = displacement.shape[1]
    node_blocks = node_dev // BLK
    runs = stiffness.shape[0] // BLK
    slots = block_source.shape[2]
    count = lax.axis_size("inner")
    shape = lambda *dims: jax.ShapeDtypeStruct(dims, F32)
    whole = shape(*populations.shape)
    vmem, hbm, smem = pltpu.VMEM, pltpu.HBM, pltpu.SMEM

    next_nodes = around(displacement, "slab", -1)
    room = -(-slots // (planes * half))
    face_y = shape(max(SLOTS + room, PADDED_SLOTS), planes, length)
    face_x = shape(SLOTS, rows, length)
    pin = lambda block: pltpu.with_memory_space_constraint(block, hbm)
    whole_like = lambda block: jax.ShapeDtypeStruct(block.shape, block.dtype)
    shell = (displacement, elements, shape_inverse, stiffness.reshape(runs, BLK))
    c1, fixed, far, near, own_nodes, corners, inverses, stiff, own_keys = call(
        first_kernel,
        (
            whole,
            shape(2, planes, rows, length),
            face_y,
            face_y,
            *(whole_like(block) for block in shell),
            shape(slots, BLK),
        ),
        tuple(
            pin(block)
            for block in (populations, relaxation, node_flags, *shell, block_target, block_node)
        ),
        (hbm,) * 9,
        scratch=(
            pltpu.VMEM((planes, Q, rows, length), F32),
            pltpu.VMEM((planes, rows, length), F32),
            pltpu.VMEM((planes, rows, length), jnp.int32),
            pltpu.SMEM(block_target.shape, jnp.int32),
            pltpu.SMEM(block_node.shape, jnp.int32),
            pltpu.SemaphoreType.DMA((planes + 8,)),
        ),
        micros=1.5,
    )
    near_y, far_y = swap(near, far, "inner", "slab")
    numbers = shape(3, runs, BLK)
    low_ids, high_ids, forces = call(
        element_kernel,
        (numbers, numbers, shape(3 * PIECES, 3, runs, BLK)),
        (corners, own_nodes, next_nodes, inverses, stiff),
        (vmem,) * 5,
        scratch=(
            pltpu.VMEM((3, runs, BLK), F32),
            pltpu.VMEM((3, runs, BLK), jnp.int32),
            pltpu.VMEM((3, 3, runs, BLK), F32),
        ),
        micros=0.001,
    )
    far, near = call(
        slab_face_kernel, (face_x, face_x), (c1, fixed, low_ids), (vmem,) * 3, micros=0.001
    )
    near_x, far_x = swap(near, far, "slab", "group")
    nodal = shape(3, node_blocks // half, length)
    own, other = call(
        spread_kernel,
        (nodal, nodal),
        (low_ids, high_ids, forces),
        (vmem,) * 3,
        micros=0.001,
    )
    corner = shape(CORNER_SLOTS, rows, length)
    far, near, known = call(
        corner_kernel,
        (corner, corner, shape(2 * slots, BLK)),
        (far_y, near_y, other, own_keys),
        (vmem,) * 4,
        scratch=(pltpu.VMEM((2, SLOTS, planes, length), F32),),
        micros=0.3,
    )
    near_c, far_c = swap(near, far, "slab", "group")
    wide = planes + 4
    walls_shape = shape(2, SLOTS, wide, length)
    second_shape = shape(Q, planes + 2, rows, length)
    extended, walls, crossing, second, ends = call(
        inside_kernel,
        (
            shape(Q, wide, rows, length),
            walls_shape,
            shape(2, 5, wide, length),
            second_shape,
            shape(2, 2, rows, length),
        ),
        (c1, fixed, far_y, near_y, far_x, near_x),
        (vmem,) * 6,
        scratch=(
            pltpu.VMEM((2, SLOTS, planes, length), F32),
            pltpu.VMEM((2, SLOTS, rows, length), F32),
        ),
        micros=0.8,
    )
    tables = all_keys(own_keys, known, "inner")
    values, blocks, internal, _, _ = call(
        second_kernel,
        (whole, shape(3 * slots, BLK), shape(3, node_blocks, BLK), walls_shape, second_shape),
        (
            pin(block_source),
            far_c,
            near_c,
            fixed,
            extended,
            crossing,
            ends,
            own,
            walls,
            second,
        ),
        (hbm,) + (vmem,) * 9,
        aliases={8: 3, 9: 4},
        scratch=(
            pltpu.VMEM((2, CORNER_SLOTS, rows, length), F32),
            pltpu.VMEM((2, 5, wide, length), F32),
            pltpu.VMEM((planes * half, 3, rows, BLK), F32),
            pltpu.SMEM(block_source.shape, jnp.int32),
            pltpu.SemaphoreType.DMA(()),
        ),
        micros=1.5,
    )
    line = shape(3 * slots + 4 * CAP, 1, BLK)
    mine, *outgoing = call(
        functools.partial(message_kernel, count, len(tables)),
        (shape(3 * node_blocks + 4 * slots, BLK), *([line] * (count - 1))),
        (block_count, *tables, blocks, internal),
        (vmem,) * (len(tables) + 3),
        micros=0.3,
    )
    arrived = [exchange(outgoing[step - 1], "inner", step) for step in range(count - 1, 0, -1)]
    (populations_out,) = call(
        store_kernel,
        (whole,),
        (values,),
        (vmem,),
        out_spaces=(hbm,),
        scratch=(pltpu.SemaphoreType.DMA(()),),
        micros=1.0,
    )
    residual, motion = call(
        final_kernel,
        (shape(3, node_dev), shape(3, slots, BLK)),
        (mine, *arrived),
        (vmem,) * count,
        micros=0.8,
    )
    return populations_out, residual, motion.transpose(1, 0, 2)[None, None]


def solution(mesh):
    return jax.shard_map(
        shards,
        mesh=mesh,
        in_specs=(
            P(None, ("group", "slab"), "inner", None),
            P(("group", "slab"), "inner", None),
            P(("group", "slab"), "inner", None),
            P(None, ("group", "slab", "inner")),
            P(None, ("group", "slab", "inner")),
            P(None, ("group", "slab", "inner")),
            P(("group", "slab", "inner")),
            P(("group", "slab"), "inner", None),
            P(("group", "slab"), "inner", None),
            P(("group", "slab"), "inner", None),
            P(("group", "slab"), "inner"),
        ),
        out_specs=(
            P(None, ("group", "slab"), "inner", None),
            P(None, ("group", "slab", "inner")),
            P(("group", "slab"), "inner", None, None, None),
        ),
        check_vma=False,
    )
```

```python
import functools

import jax
import jax.numpy as jnp
from jax import lax
from jax.experimental import pallas as pl
from jax.experimental.pallas import tpu as pltpu
from jax.sharding import PartitionSpec as P

BLK = 128
VELOCITIES = (
    (0, 0, 0),
    (1, 0, 0),
    (-1, 0, 0),
    (0, 1, 0),
    (0, -1, 0),
    (0, 0, 1),
    (0, 0, -1),
    (1, 1, 0),
    (-1, -1, 0),
    (1, -1, 0),
    (-1, 1, 0),
    (1, 0, 1),
    (-1, 0, -1),
    (1, 0, -1),
    (-1, 0, 1),
    (0, 1, 1),
    (0, -1, -1),
    (0, 1, -1),
    (0, -1, 1),
)
WEIGHTS = (1.0 / 3.0,) + (1.0 / 18.0,) * 6 + (1.0 / 36.0,) * 12
OPPOSITE = (0, 2, 1, 4, 3, 6, 5, 8, 7, 10, 9, 12, 11, 14, 13, 16, 15, 18, 17)
INLET_SPEED = 0.04
LOAD_SCALE = 25.0
COMPLIANCE = 0.5
LAME_RATIO = 2.0
Q = 19
FLAG_SLOT = 19
RATE_SLOT = 20
SLOTS = 21
SIDE_SLOTS = 24
FORCE_SLOT = 6
CORNER_SLOTS = FORCE_SLOT + 3
PIECES = 2
STEP = 4
F32 = jnp.float32
VMEM_BYTES = 48 * 1024 * 1024


def tree_sum(terms):
    terms = list(terms)
    while len(terms) > 1:
        pairs = [terms[k] + terms[k + 1] for k in range(0, len(terms) - 1, 2)]
        terms = pairs + terms[len(terms) - len(terms) % 2 :]
    return terms[0]


def moments(values):
    sums = [values[q] + values[q + 1] for q in range(1, Q, 2)]
    diffs = [values[q] - values[q + 1] for q in range(1, Q, 2)]
    density = tree_sum([values[0]] + sums)
    flows = []
    for axis in range(3):
        total = None
        for k, q in enumerate(range(1, Q, 2)):
            factor = VELOCITIES[q][axis]
            if factor == 0:
                continue
            if total is None:
                total = diffs[k] if factor > 0 else -diffs[k]
            else:
                total = total + diffs[k] if factor > 0 else total - diffs[k]
        flows.append(total)
    return density, flows[0], flows[1], flows[2]


def collide(values, rate, kind):
    density, flow_x, flow_y, flow_z = moments(values)
    inverse = 1.0 / density
    wall = kind == 1
    inlet = kind == 2
    fluid = kind == 0
    vel = (
        jnp.where(inlet, INLET_SPEED, flow_x * inverse),
        jnp.where(inlet, 0.0, flow_y * inverse),
        jnp.where(inlet, 0.0, flow_z * inverse),
    )
    scale = jnp.where(fluid, density, 1.0)
    rate = jnp.where(fluid, rate, 1.0)
    base = 1.0 - 1.5 * (vel[0] * vel[0] + vel[1] * vel[1] + vel[2] * vel[2])
    weighted = {w: w * scale for w in set(WEIGHTS)}
    out = [None] * Q
    relaxed = values[0] + rate * (weighted[WEIGHTS[0]] * base - values[0])
    out[0] = jnp.where(wall, values[0], relaxed)
    for q in range(1, Q, 2):
        project = None
        for factor, component in zip(VELOCITIES[q], vel):
            if factor == 0:
                continue
            if project is None:
                project = component
            else:
                project = project + component if factor > 0 else project - component
        even = base + 4.5 * (project * project)
        odd = 3.0 * project
        w = weighted[WEIGHTS[q]]
        forward = values[q] + rate * (w * (even + odd) - values[q])
        backward = values[q + 1] + rate * (w * (even - odd) - values[q + 1])
        out[q] = jnp.where(wall, values[q + 1], forward)
        out[q + 1] = jnp.where(wall, values[q], backward)
    return out


def roll_by(block, step, axis):
    if step == 0:
        return block
    return pltpu.roll(block, step % block.shape[axis], axis)


def face_slots(axis, sign):
    picks = []
    for q in range(Q):
        if VELOCITIES[q][axis] * sign >= 0:
            picks.append((q, 0))
        else:
            picks.append((OPPOSITE[q], 1))
    return picks


def mirror(q, axis):
    flipped = tuple(-c if k == axis else c for k, c in enumerate(VELOCITIES[q]))
    return VELOCITIES.index(flipped)


def corner_rows(sign_x, sign_y):
    rows = []
    for q, depth in face_slots(0, sign_x):
        if VELOCITIES[q][1] * sign_y >= 0:
            rows.append((q, depth))
        else:
            rows.append((OPPOSITE[mirror(q, 1)], depth))
    return rows


def first_kernel(
    pops_hbm,
    rate_hbm,
    flags_hbm,
    displacement_hbm,
    elements_hbm,
    shape_hbm,
    stiffness_hbm,
    c1,
    fixed,
    far,
    near,
    displacement,
    elements,
    shape_inverse,
    stiffness,
    pops,
    rate,
    flags,
    sems,
):
    planes, rows = c1.shape[1], c1.shape[2]
    copies = [
        pltpu.make_async_copy(rate_hbm, rate, sems.at[planes]),
        pltpu.make_async_copy(flags_hbm, flags, sems.at[planes + 1]),
    ]
    loads = [
        pltpu.make_async_copy(pops_hbm.at[:, x], pops.at[x], sems.at[x]) for x in range(planes)
    ]
    shell = [
        pltpu.make_async_copy(source, target, sems.at[planes + 2 + k])
        for k, (source, target) in enumerate(
            (
                (displacement_hbm, displacement),
                (elements_hbm, elements),
                (shape_hbm, shape_inverse),
                (stiffness_hbm, stiffness),
            )
        )
    ]
    for copy in loads[:1] + copies + loads[1:] + shell:
        copy.start()
    for copy in copies:
        copy.wait()

    def plane(x, carry):
        pltpu.make_async_copy(pops_hbm.at[:, x], pops.at[x], sems.at[x]).wait()
        kind = flags[x]
        values = [pops[x, q] for q in range(Q)]
        result = collide(values, rate[x], kind)
        for q in range(Q):
            c1[q, x] = roll_by(result[q], VELOCITIES[q][2], 1)
        fixed[0, x] = kind.astype(F32)
        fixed[1, x] = rate[x]
        return carry

    lax.fori_loop(0, planes, plane, 0, unroll=2)

    def pack(out, sign, outside):
        def line(x, carry):
            for slot, (q, depth) in enumerate(face_slots(1, sign)):
                y = rows - 1 - depth if sign > 0 else depth
                out[slot, pl.ds(x, 1)] = c1[q, x, y : y + 1]
            y = rows - 1 if sign > 0 else 0
            for k, slot in enumerate((FLAG_SLOT, RATE_SLOT)):
                out[slot, pl.ds(x, 1)] = fixed[k, x, y : y + 1]
            return carry

        lax.fori_loop(0, planes, line, 0)
        for slot in range(SLOTS, SIDE_SLOTS):
            out[slot] = jnp.zeros(out.shape[1:], F32)
        clear_outside(out, outside)

    pack_pair(pack, "inner", near, far)
    for copy in shell:
        copy.wait()


def clear_outside(out, outside):
    @pl.when(outside)
    def _():
        out[...] = jnp.zeros(out.shape, F32)


def pack_pair(pack, axis, near, far):
    at = lax.axis_index(axis)
    even = lax.rem(at, 2) == 0
    first, last = at == 0, at == lax.axis_size(axis) - 1

    @pl.when(even)
    def _():
        pack(near, 1, last)
        pack(far, -1, first)

    @pl.when(jnp.logical_not(even))
    def _():
        pack(near, -1, first)
        pack(far, 1, last)


def slab_face_kernel(c1, fixed, numbers, far, near):
    del numbers
    planes = c1.shape[1]

    def pack(out, sign, outside):
        for slot, (q, depth) in enumerate(face_slots(0, sign)):
            out[slot] = c1[q, planes - 1 - depth if sign > 0 else depth]
        end = planes - 1 if sign > 0 else 0
        out[FLAG_SLOT] = fixed[0, end]
        out[RATE_SLOT] = fixed[1, end]
        clear_outside(out, outside)

    pack_pair(pack, "slab", near, far)


def gather_both(near, far, both, axis):
    odd = lax.rem(lax.axis_index(axis), 2)
    for slot in range(both.shape[1]):
        both[1 - odd, slot] = near[slot]
        both[odd, slot] = far[slot]


def corner_kernel(far_y, near_y, other, far, near, both):
    planes = near_y.shape[1]
    gather_both(near_y, far_y, both, "inner")

    def pack(out, sign, outside):
        for side, sign_y in enumerate((1, -1)):
            picks = corner_rows(sign, sign_y) + [(FLAG_SLOT, 0), (RATE_SLOT, 0)]
            for row, (slot, depth) in enumerate(picks):
                x = planes - 1 - depth if sign > 0 else depth
                at = 3 * side + row // 8
                out[at, row % 8 : row % 8 + 1] = both[side, slot, x : x + 1]
        for part in range(3):
            out[FORCE_SLOT + part] = other[part]
        clear_outside(out, outside)

    pack_pair(pack, "slab", near, far)


def with_edge(block, step_y, edge):
    rows = block.shape[0]
    sub = lax.broadcasted_iota(jnp.int32, block.shape, 0)
    if step_y > 0:
        return jnp.where(sub == 0, edge, roll_by(block, 1, 0))
    return jnp.where(sub == rows - 1, edge, roll_by(block, -1, 0))


def store_plane(extended, walls, second, at, rate, kind):
    values = []
    for q in range(Q):
        step_x, step_y, _ = VELOCITIES[q]
        block = extended[q, at + 1 - step_x]
        if step_y != 0:
            edge = walls[0 if step_y > 0 else 1, q, pl.ds(at + 1 - step_x, 1)]
            block = with_edge(block, step_y, edge)
        values.append(block)
    result = collide(values, rate, kind)
    for q in range(Q):
        second[q, at] = roll_by(result[q], VELOCITIES[q][2], 1)


def inside_kernel(
    c1,
    fixed,
    far_y,
    near_y,
    far_x,
    near_x,
    extended,
    walls,
    crossing,
    second,
    ends,
    both_y,
    both_x,
):
    planes, rows, _ = c1.shape[1:]
    wide = planes + 4
    gather_both(near_y, far_y, both_y, "inner")
    gather_both(near_x, far_x, both_x, "slab")
    for q in range(Q):
        for x in range(planes):
            extended[q, x + 2] = c1[q, x]
        extended[q, 1] = both_x[0, q]
        extended[q, planes + 2] = both_x[1, q]
        if VELOCITIES[q][0] > 0:
            extended[q, 0] = both_x[0, OPPOSITE[q]]
        if VELOCITIES[q][0] < 0:
            extended[q, planes + 3] = both_x[1, OPPOSITE[q]]
    for end in range(2):
        ends[end, 0] = both_x[end, FLAG_SLOT]
        ends[end, 1] = both_x[end, RATE_SLOT]

    for side, sign in enumerate((1, -1)):
        y = 0 if sign > 0 else rows - 1
        for slot in range(SLOTS):
            walls[side, slot, 2 : planes + 2] = both_y[side, slot]
        place = 0
        for q in range(Q):
            if VELOCITIES[q][1] != -sign:
                continue
            for x in range(wide):
                crossing[side, place, x : x + 1] = extended[q, x, y : y + 1]
            place += 1

    def inside_plane(x, carry):
        store_plane(extended, walls, second, x + 1, fixed[1, x], fixed[0, x])
        return carry

    lax.fori_loop(1, planes - 1, inside_plane, 0, unroll=2)


def second_kernel(
    block_source_hbm,
    block_target_hbm,
    block_node_hbm,
    block_count,
    far,
    near,
    fixed,
    extended,
    crossing,
    ends,
    internal_own,
    walls_in,
    second_in,
    out,
    message,
    walls,
    second,
    both,
    edges,
    loads,
    block_source,
    block_target,
    block_node,
    sems,
):
    del walls_in, second_in
    copies = [
        pltpu.make_async_copy(block_source_hbm, block_source, sems.at[0]),
        pltpu.make_async_copy(block_target_hbm, block_target, sems.at[1]),
        pltpu.make_async_copy(block_node_hbm, block_node, sems.at[2]),
    ]
    for copy in copies:
        copy.start()
    planes, rows, length = out.shape[1:]
    half = length // BLK
    slots = block_source.shape[2]
    wide = planes + 4
    slab = lax.axis_index("slab")
    inner = lax.axis_index("inner")
    slab_end = lax.axis_size("slab") - 1
    inner_end = lax.axis_size("inner") - 1
    gather_both(near, far, both, "slab")

    for side, sign in enumerate((1, -1)):
        for end, sign_x in enumerate((1, -1)):
            for row, (slot, depth) in enumerate(corner_rows(sign_x, sign)):
                at = (1 - depth) if sign_x > 0 else planes + 2 + depth
                source = 3 * side + row // 8
                walls[side, slot, at : at + 1] = both[end, source, row % 8 : row % 8 + 1]
            at = 1 if sign_x > 0 else planes + 2
            for row in (FLAG_SLOT, RATE_SLOT):
                source = 3 * side + row // 8
                walls[side, row, at : at + 1] = both[end, source, row % 8 : row % 8 + 1]

    def edge_planes(end, carry):
        x = end * (planes - 1)
        store_plane(extended, walls, second, x + 1, fixed[1, x], fixed[0, x])
        store_plane(extended, walls, second, end * (planes + 1), ends[end, 1], ends[end, 0])
        return carry

    lax.fori_loop(0, 2, edge_planes, 0)

    @pl.when(slab == 0)
    def _():
        for q in range(Q):
            if VELOCITIES[q][0] > 0:
                second[q, 0] = jnp.zeros((rows, length), F32)

    @pl.when(slab == slab_end)
    def _():
        for q in range(Q):
            if VELOCITIES[q][0] < 0:
                second[q, planes + 1] = jnp.zeros((rows, length), F32)

    across = lax.broadcasted_iota(jnp.int32, (wide, length), 0)
    hidden = ((across <= 1) & (slab == 0)) | ((across >= planes + 2) & (slab == slab_end))
    for side, sign, outside in ((0, 1, inner == 0), (1, -1, inner == inner_end)):
        values = []
        place = 0
        for q in range(Q):
            step_x, step_y, _ = VELOCITIES[q]
            if step_y == 0:
                block = walls[side, q]
            elif step_y == sign:
                block = walls[side, OPPOSITE[q]]
            else:
                block = crossing[side, place]
                place += 1
            values.append(roll_by(block, step_x, 0))
        result = collide(values, walls[side, RATE_SLOT], walls[side, FLAG_SLOT])
        place = 0
        for q in range(Q):
            if VELOCITIES[q][1] == sign:
                kept = jnp.where(hidden | outside, 0.0, result[q])
                edges[side, place] = roll_by(kept, VELOCITIES[q][2], 1)
                place += 1

    def plane_two(x, carry):
        values = []
        places = {1: 0, -1: 0}
        for q in range(Q):
            step_x, step_y, _ = VELOCITIES[q]
            block = second[q, x + 1 - step_x]
            if step_y != 0:
                edge = edges[0 if step_y > 0 else 1, places[step_y], pl.ds(x + 2 - step_x, 1)]
                places[step_y] += 1
                block = with_edge(block, step_y, edge)
            values.append(block)
            out[q, x] = block
        density, flow_x, flow_y, flow_z = moments(values)
        parts = (
            LOAD_SCALE * flow_x,
            LOAD_SCALE * (flow_y + (density - 1.0) / 3.0),
            LOAD_SCALE * flow_z,
        )
        for part in range(3):
            for piece in range(half):
                loads[x * half + piece, part] = parts[part][:, piece * BLK : (piece + 1) * BLK]
        return carry

    lax.fori_loop(0, planes, plane_two, 0, unroll=2)

    for copy in copies:
        copy.wait()
    node_blocks = internal_own.shape[1] * half
    live = jnp.broadcast_to(block_count[...], (1, BLK))
    lanes_of = lax.broadcasted_iota(jnp.int32, (1, BLK), 1) // (BLK // slots)
    all_keys = jnp.full((1, BLK), -1, jnp.int32)
    for k in range(slots):
        run = block_source[0, 0, k]
        x = run // (rows * half)
        left = run - x * (rows * half)
        y = left // half
        piece = left - y * half
        for part in range(3):
            message[3 * k + part] = loads[x * half + piece, part, pl.ds(y, 1)]
        key = block_target[0, 0, k] * node_blocks + block_node[0, 0, k]
        all_keys = jnp.where((lanes_of == k) & (live > k), key, all_keys)
    message[3 * slots] = all_keys.astype(F32)
    for part in range(3):
        start = 3 * slots + 1 + part * node_blocks
        for piece in range(half):
            at = piece * rows
            lanes = slice(piece * BLK, (piece + 1) * BLK)
            message[start + at : start + at + rows, 0] = (
                internal_own[part, :, lanes] + both[0, FORCE_SLOT + part, :, lanes]
            )


def element_kernel(
    elements, displacement, next_nodes, shape_inverse, stiffness, low_ids, high_ids, forces, shapes,
    numbers, corners,
):
    node_dev = displacement.shape[1]
    node_blocks = node_dev // BLK
    runs = elements.shape[1] // BLK
    for j in range(runs):
        lanes = slice(j * BLK, (j + 1) * BLK)
        for row in range(3):
            numbers[row, j : j + 1] = elements[row : row + 1, lanes]
            shapes[row, j : j + 1] = shape_inverse[row : row + 1, lanes]
    for row in range(3):
        low_ids[row] = (numbers[row] & (BLK - 1)).astype(F32)
        high_ids[row] = (numbers[row] >> 7).astype(F32)

    def gather(group, carry):
        rows = pl.ds(pl.multiple_of(group * 8, 8), 8)
        low = [numbers[corner, rows] & (BLK - 1) for corner in range(3)]
        high = [numbers[corner, rows] >> 7 for corner in range(3)]
        for corner in range(3):
            nodes = [jnp.zeros((8, BLK), F32)] * 3
            for block in range(2 * node_blocks):
                source = displacement if block < node_blocks else next_nodes
                start = (block % node_blocks) * BLK
                here = high[corner] == block
                for part in range(3):
                    row = source[part : part + 1, start : start + BLK]
                    picked = jnp.take_along_axis(
                        jnp.broadcast_to(row, (8, BLK)),
                        low[corner],
                        axis=1,
                        mode="promise_in_bounds",
                    )
                    nodes[part] = jnp.where(here, picked, nodes[part])
            for part in range(3):
                corners[corner, part, rows] = nodes[part]
        return carry

    lax.fori_loop(0, runs // 8, gather, 0)

    first, second, third = [[corners[c, p] for p in range(3)] for c in range(3)]
    diag_a = shapes[0]
    skew_b = shapes[1]
    diag_c = shapes[2]
    stiff = stiffness[...]
    edge_one = [second[p] - first[p] for p in range(3)]
    edge_two = [third[p] - first[p] for p in range(3)]
    one = [diag_a * edge_one[p] for p in range(3)]
    two = [skew_b * edge_one[p] + diag_c * edge_two[p] for p in range(3)]
    one[0] = one[0] + 1.0
    two[1] = two[1] + 1.0
    aa = one[0] * one[0] + one[1] * one[1] + one[2] * one[2]
    ab = one[0] * two[0] + one[1] * two[1] + one[2] * two[2]
    bb = two[0] * two[0] + two[1] * two[1] + two[2] * two[2]
    determinant = aa * bb - ab * ab
    scale = 1.0 / determinant
    inverse_aa = bb * scale
    inverse_ab = -ab * scale
    inverse_bb = aa * scale
    pressure = LAME_RATIO * (0.5 * jnp.log(determinant))
    for p in range(3):
        pulled_one = one[p] * inverse_aa + two[p] * inverse_ab
        pulled_two = one[p] * inverse_ab + two[p] * inverse_bb
        stress_one = stiff * (one[p] - pulled_one + pressure * pulled_one)
        stress_two = stiff * (two[p] - pulled_two + pressure * pulled_two)
        force_one = diag_a * stress_one + skew_b * stress_two
        force_two = diag_c * stress_two
        for corner, force in enumerate((-(force_one + force_two), force_one, force_two)):
            rest = force
            for part in range(PIECES):
                piece = rest.astype(jnp.bfloat16).astype(F32)
                rest = rest - piece
                forces[part * 3 + p, corner] = piece


def spread_kernel(base, low_ids, high_ids, forces, out):
    runs = low_ids.shape[1]
    parts, rows, length = out.shape
    pieces = length // BLK
    slots = pieces * rows
    kind = jnp.bfloat16
    tile = 16
    slot_ids = lax.broadcasted_iota(jnp.int32, (slots, BLK), 0).astype(F32) + base
    slot_ids = slot_ids.astype(kind)
    lane_ids = lax.broadcasted_iota(jnp.int32, (BLK, BLK), 0).astype(F32).astype(kind)
    ones = jnp.ones((BLK, BLK), kind)
    none = jnp.zeros((BLK, BLK), kind)
    blank = jnp.zeros((slots, BLK), kind)

    def tall_row(row, count):
        block = jnp.broadcast_to(row, (tile, BLK)).astype(kind)
        return jnp.concatenate([block] * (count // tile), axis=0)

    total = None
    for corner in range(3):
        for first in range(0, runs, STEP):
            left = [[] for _ in range(parts * PIECES)]
            right = []
            for j in range(first, min(first + STEP, runs)):
                row = slice(j, j + 1)
                here = slot_ids == tall_row(high_ids[corner, row], slots)
                there = lane_ids == tall_row(low_ids[corner, row], BLK)
                right.append(jnp.where(there, ones, none))
                for part in range(parts * PIECES):
                    left[part].append(
                        jnp.where(here, tall_row(forces[part, corner, row], slots), blank)
                    )
            tall = jnp.concatenate([jnp.concatenate(part, axis=1) for part in left], axis=0)
            wide = jnp.concatenate(right, axis=1)
            product = lax.dot_general(
                tall, wide, (((1,), (1,)), ((), ())), preferred_element_type=F32
            )
            total = product if total is None else total + product
    for p in range(parts):
        summed = total[p * slots : (p + 1) * slots]
        for part in range(1, PIECES):
            start = (parts * part + p) * slots
            summed = summed + total[start : start + slots]
        for piece in range(pieces):
            out[p, :, piece * BLK : (piece + 1) * BLK] = summed[piece * rows : (piece + 1) * rows]


def store_kernel(values, out_hbm, sem):
    store = pltpu.make_async_copy(values, out_hbm, sem)
    store.start()
    store.wait()


def final_kernel(count, *refs):
    messages = refs[:count]
    residual, motion, keys = refs[count:]
    slots = keys.shape[0]
    node_blocks = residual.shape[1] // BLK
    inner = lax.axis_index("inner")
    width = BLK // slots

    def key_of(message, k):
        return jnp.broadcast_to(message[3 * slots][:, k * width : k * width + 1], (1, BLK))

    mine = messages[0]
    for k in range(slots):
        keys[k : k + 1] = key_of(mine, k)
    wanted = keys[...]
    node_ids = lax.broadcasted_iota(jnp.int32, (node_blocks, BLK), 0)
    own_ids = (node_ids + inner * node_blocks).astype(F32)
    external = [[] for _ in range(3)]
    moved = [[] for _ in range(3)]
    for step, message in enumerate(messages):
        sender = partner_of(inner, step, count)
        named = [key_of(message, k) for k in range(slots)]
        here = [own_ids == key for key in named]
        same = [wanted == key for key in named]
        owned = [
            wanted == (sender * node_blocks + b).astype(F32) for b in range(node_blocks)
        ]
        for part in range(3):
            rows = [message[3 * k + part] for k in range(slots)]
            external[part].append(
                tree_sum([jnp.where(here[k], rows[k], 0.0) for k in range(slots)])
            )
            moved[part].append(
                tree_sum([jnp.where(same[k], rows[k], 0.0) for k in range(slots)])
            )
            at = 3 * slots + 1 + part * node_blocks
            moved[part].append(
                -tree_sum([jnp.where(owned[b], message[at + b], 0.0) for b in range(node_blocks)])
            )
    external = [tree_sum(terms) for terms in external]
    moved = [tree_sum(terms) for terms in moved]
    live = wanted >= 0.0
    for part in range(3):
        start = 3 * slots + 1 + part * node_blocks
        left = external[part] - mine[start : start + node_blocks, 0]
        for b in range(node_blocks):
            residual[part : part + 1, b * BLK : (b + 1) * BLK] = left[b : b + 1]
        motion[part] = jnp.where(live, COMPLIANCE * moved[part], 0.0)


def call(kernel, outs, operands, spaces, scratch=(), out_spaces=None, micros=1.0, aliases=None):
    spec = lambda space: pl.BlockSpec(memory_space=space)
    out_spaces = out_spaces or (pltpu.VMEM,) * len(outs)
    return pl.pallas_call(
        kernel,
        out_shape=outs,
        in_specs=[spec(space) for space in spaces],
        out_specs=tuple(spec(space) for space in out_spaces),
        scratch_shapes=list(scratch),
        input_output_aliases=aliases or {},
        compiler_params=pltpu.CompilerParams(vmem_limit_bytes=VMEM_BYTES),
        cost_estimate=pl.CostEstimate(
            flops=0, bytes_accessed=int(micros * 3.6e6), transcendentals=0
        ),
    )(*operands)


def partner_of(at, step, count):
    if count & (count - 1) == 0:
        return at ^ step
    return (at + count - step) % count


def exchange(block, axis, step):
    count = lax.axis_size(axis)
    return lax.ppermute(block, axis, [(partner_of(i, step, count), i) for i in range(count)])


def around(block, axis, step):
    count = lax.axis_size(axis)
    return lax.ppermute(block, axis, [(i, (i + step) % count) for i in range(count)])


def swap(near, far, axis, beside):
    count, others = lax.axis_size(axis), lax.axis_size(beside)
    routes = []
    for start in (0, 1):
        route = []
        for other in range(others):
            for i in range(count):
                j = i + 1 if i % 2 == start else i - 1
                to = other
                if not 0 <= j < count:
                    j = i
                    to = other ^ 1 if others % 2 == 0 else other
                route.append((other * count + i, to * count + j))
        routes.append(route)
    axes = (beside, axis)
    return lax.ppermute(near, axes, routes[0]), lax.ppermute(far, axes, routes[1])


def shards(
    populations,
    relaxation,
    node_flags,
    displacement,
    elements,
    shape_inverse,
    stiffness,
    block_source,
    block_target,
    block_node,
    block_count,
):
    planes, rows, length = populations.shape[1:]
    half = length // BLK
    node_dev = displacement.shape[1]
    node_blocks = node_dev // BLK
    runs = stiffness.shape[0] // BLK
    slots = block_source.shape[2]
    count = lax.axis_size("inner")
    shape = lambda *dims: jax.ShapeDtypeStruct(dims, F32)
    whole = shape(*populations.shape)
    vmem, hbm, smem = pltpu.VMEM, pltpu.HBM, pltpu.SMEM

    next_nodes = around(displacement, "slab", -1)
    face_y = shape(SIDE_SLOTS, planes, length)
    face_x = shape(SLOTS, rows, length)
    pin = lambda block: pltpu.with_memory_space_constraint(block, hbm)
    whole_like = lambda block: jax.ShapeDtypeStruct(block.shape, block.dtype)
    shell = (displacement, elements, shape_inverse, stiffness.reshape(runs, BLK))
    c1, fixed, far, near, own_nodes, corners, inverses, stiff = call(
        first_kernel,
        (
            whole,
            shape(2, planes, rows, length),
            face_y,
            face_y,
            *(whole_like(block) for block in shell),
        ),
        tuple(pin(block) for block in (populations, relaxation, node_flags, *shell)),
        (hbm,) * 7,
        scratch=(
            pltpu.VMEM((planes, Q, rows, length), F32),
            pltpu.VMEM((planes, rows, length), F32),
            pltpu.VMEM((planes, rows, length), jnp.int32),
            pltpu.SemaphoreType.DMA((planes + 6,)),
        ),
        micros=1.5,
    )
    near_y, far_y = swap(near, far, "inner", "slab")
    numbers = shape(3, runs, BLK)
    low_ids, high_ids, forces = call(
        element_kernel,
        (numbers, numbers, shape(3 * PIECES, 3, runs, BLK)),
        (corners, own_nodes, next_nodes, inverses, stiff),
        (vmem,) * 5,
        scratch=(
            pltpu.VMEM((3, runs, BLK), F32),
            pltpu.VMEM((3, runs, BLK), jnp.int32),
            pltpu.VMEM((3, 3, runs, BLK), F32),
        ),
        micros=0.001,
    )
    far, near = call(
        slab_face_kernel, (face_x, face_x), (c1, fixed, low_ids), (vmem,) * 3, micros=0.001
    )
    near_x, far_x = swap(near, far, "slab", "group")
    nodal = shape(3, node_blocks // half, length)
    (other,) = call(
        functools.partial(spread_kernel, node_blocks),
        (nodal,),
        (low_ids, high_ids, forces),
        (vmem,) * 3,
        micros=0.001,
    )
    corner = shape(CORNER_SLOTS, rows, length)
    far, near = call(
        corner_kernel,
        (corner, corner),
        (far_y, near_y, other),
        (vmem,) * 3,
        scratch=(pltpu.VMEM((2, SLOTS, planes, length), F32),),
        micros=0.3,
    )
    near_c, far_c = swap(near, far, "slab", "group")
    (own,) = call(
        functools.partial(spread_kernel, 0),
        (nodal,),
        (low_ids, high_ids, forces),
        (vmem,) * 3,
        micros=0.8,
    )
    wide = planes + 4
    walls_shape = shape(2, SLOTS, wide, length)
    second_shape = shape(Q, planes + 2, rows, length)
    extended, walls, crossing, second, ends = call(
        inside_kernel,
        (
            shape(Q, wide, rows, length),
            walls_shape,
            shape(2, 5, wide, length),
            second_shape,
            shape(2, 2, rows, length),
        ),
        (c1, fixed, far_y, near_y, far_x, near_x),
        (vmem,) * 6,
        scratch=(
            pltpu.VMEM((2, SLOTS, planes, length), F32),
            pltpu.VMEM((2, SLOTS, rows, length), F32),
        ),
        micros=0.8,
    )
    lines = 3 * slots + 1 + 3 * node_blocks
    values, message, _, _ = call(
        second_kernel,
        (whole, shape(lines, 1, BLK), walls_shape, second_shape),
        (
            pin(block_source),
            pin(block_target),
            pin(block_node),
            block_count,
            far_c,
            near_c,
            fixed,
            extended,
            crossing,
            ends,
            own,
            walls,
            second,
        ),
        (hbm,) * 3 + (vmem,) * 10,
        aliases={11: 2, 12: 3},
        scratch=(
            pltpu.VMEM((2, CORNER_SLOTS, rows, length), F32),
            pltpu.VMEM((2, 5, wide, length), F32),
            pltpu.VMEM((planes * half, 3, rows, BLK), F32),
            pltpu.SMEM(block_source.shape, jnp.int32),
            pltpu.SMEM(block_target.shape, jnp.int32),
            pltpu.SMEM(block_node.shape, jnp.int32),
            pltpu.SemaphoreType.DMA((3,)),
        ),
        micros=1.5,
    )
    messages = [message] + [exchange(message, "inner", step) for step in range(1, count)]
    (populations_out,) = call(
        store_kernel,
        (whole,),
        (values,),
        (vmem,),
        out_spaces=(hbm,),
        scratch=(pltpu.SemaphoreType.DMA(()),),
        micros=1.0,
    )
    residual, motion = call(
        functools.partial(final_kernel, count),
        (shape(3, node_dev), shape(3, slots, BLK)),
        messages,
        (vmem,) * count,
        scratch=(pltpu.VMEM((slots, BLK), F32),),
        micros=0.8,
    )
    return populations_out, residual, motion.transpose(1, 0, 2)[None, None]


def solution(mesh):
    return jax.shard_map(
        shards,
        mesh=mesh,
        in_specs=(
            P(None, ("group", "slab"), "inner", None),
            P(("group", "slab"), "inner", None),
            P(("group", "slab"), "inner", None),
            P(None, ("group", "slab", "inner")),
            P(None, ("group", "slab", "inner")),
            P(None, ("group", "slab", "inner")),
            P(("group", "slab", "inner")),
            P(("group", "slab"), "inner", None),
            P(("group", "slab"), "inner", None),
            P(("group", "slab"), "inner", None),
            P(("group", "slab"), "inner"),
        ),
        out_specs=(
            P(None, ("group", "slab"), "inner", None),
            P(None, ("group", "slab", "inner")),
            P(("group", "slab"), "inner", None, None, None),
        ),
        check_vma=False,
    )
```

```python
import functools

import jax
import jax.numpy as jnp
from jax import lax
from jax.experimental import pallas as pl
from jax.experimental.pallas import tpu as pltpu
from jax.sharding import PartitionSpec as P

BLK = 128
VELOCITIES = (
    (0, 0, 0),
    (1, 0, 0),
    (-1, 0, 0),
    (0, 1, 0),
    (0, -1, 0),
    (0, 0, 1),
    (0, 0, -1),
    (1, 1, 0),
    (-1, -1, 0),
    (1, -1, 0),
    (-1, 1, 0),
    (1, 0, 1),
    (-1, 0, -1),
    (1, 0, -1),
    (-1, 0, 1),
    (0, 1, 1),
    (0, -1, -1),
    (0, 1, -1),
    (0, -1, 1),
)
WEIGHTS = (1.0 / 3.0,) + (1.0 / 18.0,) * 6 + (1.0 / 36.0,) * 12
OPPOSITE = (0, 2, 1, 4, 3, 6, 5, 8, 7, 10, 9, 12, 11, 14, 13, 16, 15, 18, 17)
INLET_SPEED = 0.04
LOAD_SCALE = 25.0
COMPLIANCE = 0.5
LAME_RATIO = 2.0
Q = 19
FLAG_SLOT = 19
RATE_SLOT = 20
SLOTS = 21
SIDE_SLOTS = 24
FORCE_SLOT = 6
CORNER_SLOTS = FORCE_SLOT + 3
PIECES = 2
STEP = 4
F32 = jnp.float32
VMEM_BYTES = 48 * 1024 * 1024


def tree_sum(terms):
    terms = list(terms)
    while len(terms) > 1:
        pairs = [terms[k] + terms[k + 1] for k in range(0, len(terms) - 1, 2)]
        terms = pairs + terms[len(terms) - len(terms) % 2 :]
    return terms[0]


def moments(values):
    sums = [values[q] + values[q + 1] for q in range(1, Q, 2)]
    diffs = [values[q] - values[q + 1] for q in range(1, Q, 2)]
    density = tree_sum([values[0]] + sums)
    flows = []
    for axis in range(3):
        total = None
        for k, q in enumerate(range(1, Q, 2)):
            factor = VELOCITIES[q][axis]
            if factor == 0:
                continue
            if total is None:
                total = diffs[k] if factor > 0 else -diffs[k]
            else:
                total = total + diffs[k] if factor > 0 else total - diffs[k]
        flows.append(total)
    return density, flows[0], flows[1], flows[2]


def collide(values, rate, kind):
    density, flow_x, flow_y, flow_z = moments(values)
    inverse = 1.0 / density
    wall = kind == 1
    inlet = kind == 2
    fluid = kind == 0
    vel = (
        jnp.where(inlet, INLET_SPEED, flow_x * inverse),
        jnp.where(inlet, 0.0, flow_y * inverse),
        jnp.where(inlet, 0.0, flow_z * inverse),
    )
    scale = jnp.where(fluid, density, 1.0)
    rate = jnp.where(fluid, rate, 1.0)
    base = 1.0 - 1.5 * (vel[0] * vel[0] + vel[1] * vel[1] + vel[2] * vel[2])
    weighted = {w: w * scale for w in set(WEIGHTS)}
    out = [None] * Q
    relaxed = values[0] + rate * (weighted[WEIGHTS[0]] * base - values[0])
    out[0] = jnp.where(wall, values[0], relaxed)
    for q in range(1, Q, 2):
        project = None
        for factor, component in zip(VELOCITIES[q], vel):
            if factor == 0:
                continue
            if project is None:
                project = component
            else:
                project = project + component if factor > 0 else project - component
        even = base + 4.5 * (project * project)
        odd = 3.0 * project
        w = weighted[WEIGHTS[q]]
        forward = values[q] + rate * (w * (even + odd) - values[q])
        backward = values[q + 1] + rate * (w * (even - odd) - values[q + 1])
        out[q] = jnp.where(wall, values[q + 1], forward)
        out[q + 1] = jnp.where(wall, values[q], backward)
    return out


def roll_by(block, step, axis):
    if step == 0:
        return block
    return pltpu.roll(block, step % block.shape[axis], axis)


def face_slots(axis, sign):
    picks = []
    for q in range(Q):
        if VELOCITIES[q][axis] * sign >= 0:
            picks.append((q, 0))
        else:
            picks.append((OPPOSITE[q], 1))
    return picks


def mirror(q, axis):
    flipped = tuple(-c if k == axis else c for k, c in enumerate(VELOCITIES[q]))
    return VELOCITIES.index(flipped)


def corner_rows(sign_x, sign_y):
    rows = []
    for q, depth in face_slots(0, sign_x):
        if VELOCITIES[q][1] * sign_y >= 0:
            rows.append((q, depth))
        else:
            rows.append((OPPOSITE[mirror(q, 1)], depth))
    return rows


def first_kernel(
    pops_hbm,
    rate_hbm,
    flags_hbm,
    displacement_hbm,
    elements_hbm,
    shape_hbm,
    stiffness_hbm,
    c1,
    fixed,
    near,
    far,
    displacement,
    elements,
    shape_inverse,
    stiffness,
    pops,
    rate,
    flags,
    sems,
):
    planes, rows = c1.shape[1], c1.shape[2]
    copies = [
        pltpu.make_async_copy(rate_hbm, rate, sems.at[planes]),
        pltpu.make_async_copy(flags_hbm, flags, sems.at[planes + 1]),
    ]
    loads = [
        pltpu.make_async_copy(pops_hbm.at[:, x], pops.at[x], sems.at[x]) for x in range(planes)
    ]
    shell = [
        pltpu.make_async_copy(source, target, sems.at[planes + 2 + k])
        for k, (source, target) in enumerate(
            (
                (displacement_hbm, displacement),
                (elements_hbm, elements),
                (shape_hbm, shape_inverse),
                (stiffness_hbm, stiffness),
            )
        )
    ]
    for copy in loads[:1] + copies + loads[1:] + shell:
        copy.start()
    for copy in copies:
        copy.wait()

    def plane(x, carry):
        pltpu.make_async_copy(pops_hbm.at[:, x], pops.at[x], sems.at[x]).wait()
        kind = flags[x]
        values = [pops[x, q] for q in range(Q)]
        result = collide(values, rate[x], kind)
        for q in range(Q):
            c1[q, x] = roll_by(result[q], VELOCITIES[q][2], 1)
        fixed[0, x] = kind.astype(F32)
        fixed[1, x] = rate[x]
        return carry

    lax.fori_loop(0, planes, plane, 0, unroll=2)

    def pack(out, sign, outside):
        def line(x, carry):
            for slot, (q, depth) in enumerate(face_slots(1, sign)):
                y = rows - 1 - depth if sign > 0 else depth
                out[slot, pl.ds(x, 1)] = c1[q, x, y : y + 1]
            y = rows - 1 if sign > 0 else 0
            for k, slot in enumerate((FLAG_SLOT, RATE_SLOT)):
                out[slot, pl.ds(x, 1)] = fixed[k, x, y : y + 1]
            return carry

        lax.fori_loop(0, planes, line, 0)
        for slot in range(SLOTS, SIDE_SLOTS):
            out[slot] = jnp.zeros(out.shape[1:], F32)
        clear_outside(out, outside)

    pack_pair(pack, "inner", near, far)
    for copy in shell:
        copy.wait()


def clear_outside(out, outside):
    @pl.when(outside)
    def _():
        out[...] = jnp.zeros(out.shape, F32)


def pack_pair(pack, axis, near, far):
    at = lax.axis_index(axis)
    even = lax.rem(at, 2) == 0
    first, last = at == 0, at == lax.axis_size(axis) - 1

    @pl.when(even)
    def _():
        pack(near, 1, last)
        pack(far, -1, first)

    @pl.when(jnp.logical_not(even))
    def _():
        pack(near, -1, first)
        pack(far, 1, last)


def slab_face_kernel(c1, fixed, numbers, near, far):
    del numbers
    planes = c1.shape[1]

    def pack(out, sign, outside):
        for slot, (q, depth) in enumerate(face_slots(0, sign)):
            out[slot] = c1[q, planes - 1 - depth if sign > 0 else depth]
        end = planes - 1 if sign > 0 else 0
        out[FLAG_SLOT] = fixed[0, end]
        out[RATE_SLOT] = fixed[1, end]
        clear_outside(out, outside)

    pack_pair(pack, "slab", near, far)


def gather_both(near, far, both, axis):
    odd = lax.rem(lax.axis_index(axis), 2)
    for slot in range(both.shape[1]):
        both[1 - odd, slot] = near[slot]
        both[odd, slot] = far[slot]


def corner_kernel(near_y, far_y, other, near, far, both):
    planes = near_y.shape[1]
    gather_both(near_y, far_y, both, "inner")

    def pack(out, sign, outside):
        for side, sign_y in enumerate((1, -1)):
            picks = corner_rows(sign, sign_y) + [(FLAG_SLOT, 0), (RATE_SLOT, 0)]
            for row, (slot, depth) in enumerate(picks):
                x = planes - 1 - depth if sign > 0 else depth
                at = 3 * side + row // 8
                out[at, row % 8 : row % 8 + 1] = both[side, slot, x : x + 1]
        for part in range(3):
            out[FORCE_SLOT + part] = other[part]
        clear_outside(out, outside)

    pack_pair(pack, "slab", near, far)


def with_edge(block, step_y, edge):
    rows = block.shape[0]
    sub = lax.broadcasted_iota(jnp.int32, block.shape, 0)
    if step_y > 0:
        return jnp.where(sub == 0, edge, roll_by(block, 1, 0))
    return jnp.where(sub == rows - 1, edge, roll_by(block, -1, 0))


def store_plane(extended, walls, second, at, rate, kind):
    values = []
    for q in range(Q):
        step_x, step_y, _ = VELOCITIES[q]
        block = extended[q, at + 1 - step_x]
        if step_y != 0:
            edge = walls[0 if step_y > 0 else 1, q, pl.ds(at + 1 - step_x, 1)]
            block = with_edge(block, step_y, edge)
        values.append(block)
    result = collide(values, rate, kind)
    for q in range(Q):
        second[q, at] = roll_by(result[q], VELOCITIES[q][2], 1)


def inside_kernel(
    c1,
    fixed,
    near_y,
    far_y,
    near_x,
    far_x,
    extended,
    walls,
    crossing,
    second,
    ends,
    both_y,
    both_x,
):
    planes, rows, _ = c1.shape[1:]
    wide = planes + 4
    gather_both(near_y, far_y, both_y, "inner")
    gather_both(near_x, far_x, both_x, "slab")
    for q in range(Q):
        for x in range(planes):
            extended[q, x + 2] = c1[q, x]
        extended[q, 1] = both_x[0, q]
        extended[q, planes + 2] = both_x[1, q]
        if VELOCITIES[q][0] > 0:
            extended[q, 0] = both_x[0, OPPOSITE[q]]
        if VELOCITIES[q][0] < 0:
            extended[q, planes + 3] = both_x[1, OPPOSITE[q]]
    for end in range(2):
        ends[end, 0] = both_x[end, FLAG_SLOT]
        ends[end, 1] = both_x[end, RATE_SLOT]

    for side, sign in enumerate((1, -1)):
        y = 0 if sign > 0 else rows - 1
        for slot in range(SLOTS):
            walls[side, slot, 2 : planes + 2] = both_y[side, slot]
        place = 0
        for q in range(Q):
            if VELOCITIES[q][1] != -sign:
                continue
            for x in range(wide):
                crossing[side, place, x : x + 1] = extended[q, x, y : y + 1]
            place += 1

    def inside_plane(x, carry):
        store_plane(extended, walls, second, x + 1, fixed[1, x], fixed[0, x])
        return carry

    lax.fori_loop(1, planes - 1, inside_plane, 0, unroll=2)


def second_kernel(
    block_source_hbm,
    block_target_hbm,
    block_node_hbm,
    block_count,
    near,
    far,
    fixed,
    extended,
    crossing,
    ends,
    internal_own,
    walls_in,
    second_in,
    out,
    message,
    walls,
    second,
    both,
    edges,
    loads,
    block_source,
    block_target,
    block_node,
    sems,
):
    del walls_in, second_in
    copies = [
        pltpu.make_async_copy(block_source_hbm, block_source, sems.at[0]),
        pltpu.make_async_copy(block_target_hbm, block_target, sems.at[1]),
        pltpu.make_async_copy(block_node_hbm, block_node, sems.at[2]),
    ]
    for copy in copies:
        copy.start()
    planes, rows, length = out.shape[1:]
    half = length // BLK
    slots = block_source.shape[2]
    wide = planes + 4
    slab = lax.axis_index("slab")
    inner = lax.axis_index("inner")
    slab_end = lax.axis_size("slab") - 1
    inner_end = lax.axis_size("inner") - 1
    gather_both(near, far, both, "slab")

    for side, sign in enumerate((1, -1)):
        for end, sign_x in enumerate((1, -1)):
            for row, (slot, depth) in enumerate(corner_rows(sign_x, sign)):
                at = (1 - depth) if sign_x > 0 else planes + 2 + depth
                source = 3 * side + row // 8
                walls[side, slot, at : at + 1] = both[end, source, row % 8 : row % 8 + 1]
            at = 1 if sign_x > 0 else planes + 2
            for row in (FLAG_SLOT, RATE_SLOT):
                source = 3 * side + row // 8
                walls[side, row, at : at + 1] = both[end, source, row % 8 : row % 8 + 1]

    def edge_planes(end, carry):
        x = end * (planes - 1)
        store_plane(extended, walls, second, x + 1, fixed[1, x], fixed[0, x])
        store_plane(extended, walls, second, end * (planes + 1), ends[end, 1], ends[end, 0])
        return carry

    lax.fori_loop(0, 2, edge_planes, 0)

    @pl.when(slab == 0)
    def _():
        for q in range(Q):
            if VELOCITIES[q][0] > 0:
                second[q, 0] = jnp.zeros((rows, length), F32)

    @pl.when(slab == slab_end)
    def _():
        for q in range(Q):
            if VELOCITIES[q][0] < 0:
                second[q, planes + 1] = jnp.zeros((rows, length), F32)

    across = lax.broadcasted_iota(jnp.int32, (wide, length), 0)
    hidden = ((across <= 1) & (slab == 0)) | ((across >= planes + 2) & (slab == slab_end))
    for side, sign, outside in ((0, 1, inner == 0), (1, -1, inner == inner_end)):
        values = []
        place = 0
        for q in range(Q):
            step_x, step_y, _ = VELOCITIES[q]
            if step_y == 0:
                block = walls[side, q]
            elif step_y == sign:
                block = walls[side, OPPOSITE[q]]
            else:
                block = crossing[side, place]
                place += 1
            values.append(roll_by(block, step_x, 0))
        result = collide(values, walls[side, RATE_SLOT], walls[side, FLAG_SLOT])
        place = 0
        for q in range(Q):
            if VELOCITIES[q][1] == sign:
                kept = jnp.where(hidden | outside, 0.0, result[q])
                edges[side, place] = roll_by(kept, VELOCITIES[q][2], 1)
                place += 1

    def plane_two(x, carry):
        values = []
        places = {1: 0, -1: 0}
        for q in range(Q):
            step_x, step_y, _ = VELOCITIES[q]
            block = second[q, x + 1 - step_x]
            if step_y != 0:
                edge = edges[0 if step_y > 0 else 1, places[step_y], pl.ds(x + 2 - step_x, 1)]
                places[step_y] += 1
                block = with_edge(block, step_y, edge)
            values.append(block)
            out[q, x] = block
        density, flow_x, flow_y, flow_z = moments(values)
        parts = (
            LOAD_SCALE * flow_x,
            LOAD_SCALE * (flow_y + (density - 1.0) / 3.0),
            LOAD_SCALE * flow_z,
        )
        for part in range(3):
            for piece in range(half):
                loads[x * half + piece, part] = parts[part][:, piece * BLK : (piece + 1) * BLK]
        return carry

    lax.fori_loop(0, planes, plane_two, 0, unroll=2)

    for copy in copies:
        copy.wait()
    node_blocks = internal_own.shape[1] * half
    live = jnp.broadcast_to(block_count[...], (1, BLK))
    lanes_of = lax.broadcasted_iota(jnp.int32, (1, BLK), 1) // (BLK // slots)
    all_keys = jnp.full((1, BLK), -1, jnp.int32)
    for k in range(slots):
        run = block_source[0, 0, k]
        x = run // (rows * half)
        left = run - x * (rows * half)
        y = left // half
        piece = left - y * half
        for part in range(3):
            message[3 * k + part] = loads[x * half + piece, part, pl.ds(y, 1)]
        key = block_target[0, 0, k] * node_blocks + block_node[0, 0, k]
        all_keys = jnp.where((lanes_of == k) & (live > k), key, all_keys)
    message[3 * slots] = all_keys.astype(F32)
    for part in range(3):
        start = 3 * slots + 1 + part * node_blocks
        for piece in range(half):
            at = piece * rows
            lanes = slice(piece * BLK, (piece + 1) * BLK)
            message[start + at : start + at + rows, 0] = (
                internal_own[part, :, lanes] + both[0, FORCE_SLOT + part, :, lanes]
            )


def element_kernel(
    elements, displacement, next_nodes, shape_inverse, stiffness, low_ids, high_ids, forces, shapes,
    numbers, corners,
):
    node_dev = displacement.shape[1]
    node_blocks = node_dev // BLK
    runs = elements.shape[1] // BLK
    for j in range(runs):
        lanes = slice(j * BLK, (j + 1) * BLK)
        for row in range(3):
            numbers[row, j : j + 1] = elements[row : row + 1, lanes]
            shapes[row, j : j + 1] = shape_inverse[row : row + 1, lanes]
    for row in range(3):
        low_ids[row] = (numbers[row] & (BLK - 1)).astype(F32)
        high_ids[row] = (numbers[row] >> 7).astype(F32)

    def gather(group, carry):
        rows = pl.ds(pl.multiple_of(group * 8, 8), 8)
        low = [numbers[corner, rows] & (BLK - 1) for corner in range(3)]
        high = [numbers[corner, rows] >> 7 for corner in range(3)]
        for corner in range(3):
            nodes = [jnp.zeros((8, BLK), F32)] * 3
            for block in range(2 * node_blocks):
                source = displacement if block < node_blocks else next_nodes
                start = (block % node_blocks) * BLK
                here = high[corner] == block
                for part in range(3):
                    row = source[part : part + 1, start : start + BLK]
                    picked = jnp.take_along_axis(
                        jnp.broadcast_to(row, (8, BLK)),
                        low[corner],
                        axis=1,
                        mode="promise_in_bounds",
                    )
                    nodes[part] = jnp.where(here, picked, nodes[part])
            for part in range(3):
                corners[corner, part, rows] = nodes[part]
        return carry

    lax.fori_loop(0, runs // 8, gather, 0)

    first, second, third = [[corners[c, p] for p in range(3)] for c in range(3)]
    diag_a = shapes[0]
    skew_b = shapes[1]
    diag_c = shapes[2]
    stiff = stiffness[...]
    edge_one = [second[p] - first[p] for p in range(3)]
    edge_two = [third[p] - first[p] for p in range(3)]
    one = [diag_a * edge_one[p] for p in range(3)]
    two = [skew_b * edge_one[p] + diag_c * edge_two[p] for p in range(3)]
    one[0] = one[0] + 1.0
    two[1] = two[1] + 1.0
    aa = one[0] * one[0] + one[1] * one[1] + one[2] * one[2]
    ab = one[0] * two[0] + one[1] * two[1] + one[2] * two[2]
    bb = two[0] * two[0] + two[1] * two[1] + two[2] * two[2]
    determinant = aa * bb - ab * ab
    scale = 1.0 / determinant
    inverse_aa = bb * scale
    inverse_ab = -ab * scale
    inverse_bb = aa * scale
    pressure = LAME_RATIO * (0.5 * jnp.log(determinant))
    for p in range(3):
        pulled_one = one[p] * inverse_aa + two[p] * inverse_ab
        pulled_two = one[p] * inverse_ab + two[p] * inverse_bb
        stress_one = stiff * (one[p] - pulled_one + pressure * pulled_one)
        stress_two = stiff * (two[p] - pulled_two + pressure * pulled_two)
        force_one = diag_a * stress_one + skew_b * stress_two
        force_two = diag_c * stress_two
        for corner, force in enumerate((-(force_one + force_two), force_one, force_two)):
            rest = force
            for part in range(PIECES):
                piece = rest.astype(jnp.bfloat16).astype(F32)
                rest = rest - piece
                forces[part * 3 + p, corner] = piece


def spread_kernel(base, low_ids, high_ids, forces, out):
    runs = low_ids.shape[1]
    parts, rows, length = out.shape
    pieces = length // BLK
    slots = pieces * rows
    kind = jnp.bfloat16
    tile = 16
    slot_ids = lax.broadcasted_iota(jnp.int32, (slots, BLK), 0).astype(F32) + base
    slot_ids = slot_ids.astype(kind)
    lane_ids = lax.broadcasted_iota(jnp.int32, (BLK, BLK), 0).astype(F32).astype(kind)
    ones = jnp.ones((BLK, BLK), kind)
    none = jnp.zeros((BLK, BLK), kind)
    blank = jnp.zeros((slots, BLK), kind)

    def tall_row(row, count):
        block = jnp.broadcast_to(row, (tile, BLK)).astype(kind)
        return jnp.concatenate([block] * (count // tile), axis=0)

    total = None
    for corner in range(3):
        for first in range(0, runs, STEP):
            left = [[] for _ in range(parts * PIECES)]
            right = []
            for j in range(first, min(first + STEP, runs)):
                row = slice(j, j + 1)
                here = slot_ids == tall_row(high_ids[corner, row], slots)
                there = lane_ids == tall_row(low_ids[corner, row], BLK)
                right.append(jnp.where(there, ones, none))
                for part in range(parts * PIECES):
                    left[part].append(
                        jnp.where(here, tall_row(forces[part, corner, row], slots), blank)
                    )
            tall = jnp.concatenate([jnp.concatenate(part, axis=1) for part in left], axis=0)
            wide = jnp.concatenate(right, axis=1)
            product = lax.dot_general(
                tall, wide, (((1,), (1,)), ((), ())), preferred_element_type=F32
            )
            total = product if total is None else total + product
    for p in range(parts):
        summed = total[p * slots : (p + 1) * slots]
        for part in range(1, PIECES):
            start = (parts * part + p) * slots
            summed = summed + total[start : start + slots]
        for piece in range(pieces):
            out[p, :, piece * BLK : (piece + 1) * BLK] = summed[piece * rows : (piece + 1) * rows]


def store_kernel(values, out_hbm, sem):
    store = pltpu.make_async_copy(values, out_hbm, sem)
    store.start()
    store.wait()


def sum_messages(messages, senders, wanted, node_blocks):
    slots = wanted.shape[0]
    own_ids = lax.broadcasted_iota(jnp.int32, (node_blocks, BLK), 0)
    own_ids = (own_ids + lax.axis_index("inner") * node_blocks).astype(F32)
    external = [[] for _ in range(3)]
    moved = [[] for _ in range(3)]
    for message, sender in zip(messages, senders):
        named = [key_of(message, k, slots) for k in range(slots)]
        here = [own_ids == key for key in named]
        same = [wanted == key for key in named]
        owned = [wanted == (sender * node_blocks + b).astype(F32) for b in range(node_blocks)]
        for part in range(3):
            rows = [message[3 * k + part] for k in range(slots)]
            at = 3 * slots + 1 + part * node_blocks
            inside = [message[at + b] for b in range(node_blocks)]
            external[part].append(tree_sum([jnp.where(m, r, 0.0) for m, r in zip(here, rows)]))
            moved[part].append(tree_sum([jnp.where(m, r, 0.0) for m, r in zip(same, rows)]))
            moved[part].append(-tree_sum([jnp.where(m, r, 0.0) for m, r in zip(owned, inside)]))
    return [tree_sum(terms) for terms in external], [tree_sum(terms) for terms in moved]


def key_of(message, k, slots):
    width = BLK // slots
    return jnp.broadcast_to(message[3 * slots][:, k * width : k * width + 1], (1, BLK))


def early_kernel(count, *refs):
    messages = refs[:-3]
    total, moved, keys = refs[-3:]
    slots, node_blocks = keys.shape[0], total.shape[1]
    inner = lax.axis_index("inner")
    for k in range(slots):
        keys[k : k + 1] = key_of(messages[0], k, slots)
    steps = [0] + list(range(count - 1, 1, -1))
    senders = [partner_of(inner, step, count) for step in steps]
    external, forces = sum_messages(messages, senders, keys[...], node_blocks)
    for part in range(3):
        start = 3 * slots + 1 + part * node_blocks
        total[part] = external[part] - messages[0][start : start + node_blocks, 0]
        moved[part] = forces[part]


def final_kernel(count, message, total, moved, keys, residual, motion):
    node_blocks = total.shape[1]
    wanted = keys[...]
    sender = partner_of(lax.axis_index("inner"), 1, count)
    external, forces = sum_messages([message], [sender], wanted, node_blocks)
    live = wanted >= 0.0
    for part in range(3):
        left = total[part] + external[part]
        for b in range(node_blocks):
            residual[part : part + 1, b * BLK : (b + 1) * BLK] = left[b : b + 1]
        motion[part] = jnp.where(live, COMPLIANCE * (moved[part] + forces[part]), 0.0)


def call(kernel, outs, operands, spaces, scratch=(), out_spaces=None, micros=1.0, aliases=None):
    spec = lambda space: pl.BlockSpec(memory_space=space)
    out_spaces = out_spaces or (pltpu.VMEM,) * len(outs)
    return pl.pallas_call(
        kernel,
        out_shape=outs,
        in_specs=[spec(space) for space in spaces],
        out_specs=tuple(spec(space) for space in out_spaces),
        scratch_shapes=list(scratch),
        input_output_aliases=aliases or {},
        compiler_params=pltpu.CompilerParams(vmem_limit_bytes=VMEM_BYTES),
        cost_estimate=pl.CostEstimate(
            flops=0, bytes_accessed=int(micros * 3.6e6), transcendentals=0
        ),
    )(*operands)


def partner_of(at, step, count):
    if count & (count - 1) == 0:
        return at ^ step
    return (at + count - step) % count


def exchange(block, axis, step):
    count = lax.axis_size(axis)
    return lax.ppermute(block, axis, [(partner_of(i, step, count), i) for i in range(count)])


def around(block, axis, step):
    count = lax.axis_size(axis)
    return lax.ppermute(block, axis, [(i, (i + step) % count) for i in range(count)])


def swap(near, far, axis, beside):
    count, others = lax.axis_size(axis), lax.axis_size(beside)
    routes = []
    for start in (0, 1):
        route = []
        for other in range(others):
            for i in range(count):
                j = i + 1 if i % 2 == start else i - 1
                to = other
                if not 0 <= j < count:
                    j = i
                    to = other ^ 1 if others % 2 == 0 else other
                route.append((other * count + i, to * count + j))
        routes.append(route)
    axes = (beside, axis)
    return lax.ppermute(near, axes, routes[0]), lax.ppermute(far, axes, routes[1])


def shards(
    populations,
    relaxation,
    node_flags,
    displacement,
    elements,
    shape_inverse,
    stiffness,
    block_source,
    block_target,
    block_node,
    block_count,
):
    planes, rows, length = populations.shape[1:]
    half = length // BLK
    node_dev = displacement.shape[1]
    node_blocks = node_dev // BLK
    runs = stiffness.shape[0] // BLK
    slots = block_source.shape[2]
    count = lax.axis_size("inner")
    shape = lambda *dims: jax.ShapeDtypeStruct(dims, F32)
    whole = shape(*populations.shape)
    vmem, hbm, smem = pltpu.VMEM, pltpu.HBM, pltpu.SMEM

    next_nodes = around(displacement, "slab", -1)
    face_y = shape(SIDE_SLOTS, planes, length)
    face_x = shape(SLOTS, rows, length)
    pin = lambda block: pltpu.with_memory_space_constraint(block, hbm)
    whole_like = lambda block: jax.ShapeDtypeStruct(block.shape, block.dtype)
    shell = (displacement, elements, shape_inverse, stiffness.reshape(runs, BLK))
    c1, fixed, near, far, own_nodes, corners, inverses, stiff = call(
        first_kernel,
        (
            whole,
            shape(2, planes, rows, length),
            face_y,
            face_y,
            *(whole_like(block) for block in shell),
        ),
        tuple(pin(block) for block in (populations, relaxation, node_flags, *shell)),
        (hbm,) * 7,
        scratch=(
            pltpu.VMEM((planes, Q, rows, length), F32),
            pltpu.VMEM((planes, rows, length), F32),
            pltpu.VMEM((planes, rows, length), jnp.int32),
            pltpu.SemaphoreType.DMA((planes + 6,)),
        ),
        micros=1.5,
    )
    near_y, far_y = swap(near, far, "inner", "slab")
    numbers = shape(3, runs, BLK)
    low_ids, high_ids, forces = call(
        element_kernel,
        (numbers, numbers, shape(3 * PIECES, 3, runs, BLK)),
        (corners, own_nodes, next_nodes, inverses, stiff),
        (vmem,) * 5,
        scratch=(
            pltpu.VMEM((3, runs, BLK), F32),
            pltpu.VMEM((3, runs, BLK), jnp.int32),
            pltpu.VMEM((3, 3, runs, BLK), F32),
        ),
        micros=0.001,
    )
    near, far = call(
        slab_face_kernel, (face_x, face_x), (c1, fixed, low_ids), (vmem,) * 3, micros=0.001
    )
    near_x, far_x = swap(near, far, "slab", "group")
    nodal = shape(3, node_blocks // half, length)
    (other,) = call(
        functools.partial(spread_kernel, node_blocks),
        (nodal,),
        (low_ids, high_ids, forces),
        (vmem,) * 3,
        micros=0.001,
    )
    corner = shape(CORNER_SLOTS, rows, length)
    near, far = call(
        corner_kernel,
        (corner, corner),
        (near_y, far_y, other),
        (vmem,) * 3,
        scratch=(pltpu.VMEM((2, SLOTS, planes, length), F32),),
        micros=0.3,
    )
    near_c, far_c = swap(near, far, "slab", "group")
    (own,) = call(
        functools.partial(spread_kernel, 0),
        (nodal,),
        (low_ids, high_ids, forces),
        (vmem,) * 3,
        micros=0.8,
    )
    wide = planes + 4
    walls_shape = shape(2, SLOTS, wide, length)
    second_shape = shape(Q, planes + 2, rows, length)
    extended, walls, crossing, second, ends = call(
        inside_kernel,
        (
            shape(Q, wide, rows, length),
            walls_shape,
            shape(2, 5, wide, length),
            second_shape,
            shape(2, 2, rows, length),
        ),
        (c1, fixed, near_y, far_y, near_x, far_x),
        (vmem,) * 6,
        scratch=(
            pltpu.VMEM((2, SLOTS, planes, length), F32),
            pltpu.VMEM((2, SLOTS, rows, length), F32),
        ),
        micros=0.8,
    )
    lines = 3 * slots + 1 + 3 * node_blocks
    values, message, _, _ = call(
        second_kernel,
        (whole, shape(lines, 1, BLK), walls_shape, second_shape),
        (
            pin(block_source),
            pin(block_target),
            pin(block_node),
            block_count,
            near_c,
            far_c,
            fixed,
            extended,
            crossing,
            ends,
            own,
            walls,
            second,
        ),
        (hbm,) * 3 + (vmem,) * 10,
        aliases={11: 2, 12: 3},
        scratch=(
            pltpu.VMEM((2, CORNER_SLOTS, rows, length), F32),
            pltpu.VMEM((2, 5, wide, length), F32),
            pltpu.VMEM((planes * half, 3, rows, BLK), F32),
            pltpu.SMEM(block_source.shape, jnp.int32),
            pltpu.SMEM(block_target.shape, jnp.int32),
            pltpu.SMEM(block_node.shape, jnp.int32),
            pltpu.SemaphoreType.DMA((3,)),
        ),
        micros=1.5,
    )
    messages = [message] + [exchange(message, "inner", step) for step in range(1, count)]
    (populations_out,) = call(
        store_kernel,
        (whole,),
        (values,),
        (vmem,),
        out_spaces=(hbm,),
        scratch=(pltpu.SemaphoreType.DMA(()),),
        micros=1.0,
    )
    total, moved, keys = call(
        functools.partial(early_kernel, count),
        (shape(3, node_blocks, BLK), shape(3, slots, BLK), shape(slots, BLK)),
        (messages[0], *messages[:1:-1]),
        (vmem,) * (count - 1),
        micros=0.4,
    )
    residual, motion = call(
        functools.partial(final_kernel, count),
        (shape(3, node_dev), shape(3, slots, BLK)),
        (messages[1], total, moved, keys),
        (vmem,) * 4,
        micros=0.5,
    )
    return populations_out, residual, motion.transpose(1, 0, 2)[None, None]


def solution(mesh):
    return jax.shard_map(
        shards,
        mesh=mesh,
        in_specs=(
            P(None, ("group", "slab"), "inner", None),
            P(("group", "slab"), "inner", None),
            P(("group", "slab"), "inner", None),
            P(None, ("group", "slab", "inner")),
            P(None, ("group", "slab", "inner")),
            P(None, ("group", "slab", "inner")),
            P(("group", "slab", "inner")),
            P(("group", "slab"), "inner", None),
            P(("group", "slab"), "inner", None),
            P(("group", "slab"), "inner", None),
            P(("group", "slab"), "inner"),
        ),
        out_specs=(
            P(None, ("group", "slab"), "inner", None),
            P(None, ("group", "slab", "inner")),
            P(("group", "slab"), "inner", None, None, None),
        ),
        check_vma=False,
    )
```

```python
import functools

import jax
import jax.numpy as jnp
from jax import lax
from jax.experimental import pallas as pl
from jax.experimental.pallas import tpu as pltpu
from jax.sharding import PartitionSpec as P

BLK = 128
VELOCITIES = (
    (0, 0, 0),
    (1, 0, 0),
    (-1, 0, 0),
    (0, 1, 0),
    (0, -1, 0),
    (0, 0, 1),
    (0, 0, -1),
    (1, 1, 0),
    (-1, -1, 0),
    (1, -1, 0),
    (-1, 1, 0),
    (1, 0, 1),
    (-1, 0, -1),
    (1, 0, -1),
    (-1, 0, 1),
    (0, 1, 1),
    (0, -1, -1),
    (0, 1, -1),
    (0, -1, 1),
)
WEIGHTS = (1.0 / 3.0,) + (1.0 / 18.0,) * 6 + (1.0 / 36.0,) * 12
OPPOSITE = (0, 2, 1, 4, 3, 6, 5, 8, 7, 10, 9, 12, 11, 14, 13, 16, 15, 18, 17)
INLET_SPEED = 0.04
LOAD_SCALE = 25.0
COMPLIANCE = 0.5
LAME_RATIO = 2.0
Q = 19
FLAG_SLOT = 19
RATE_SLOT = 20
SLOTS = 21
SIDE_SLOTS = 24
FORCE_SLOT = 6
CORNER_SLOTS = FORCE_SLOT + 3
PIECES = 2
STEP = 4
F32 = jnp.float32
VMEM_BYTES = 48 * 1024 * 1024


def tree_sum(terms):
    terms = list(terms)
    while len(terms) > 1:
        pairs = [terms[k] + terms[k + 1] for k in range(0, len(terms) - 1, 2)]
        terms = pairs + terms[len(terms) - len(terms) % 2 :]
    return terms[0]


def moments(values):
    sums = [values[q] + values[q + 1] for q in range(1, Q, 2)]
    diffs = [values[q] - values[q + 1] for q in range(1, Q, 2)]
    density = tree_sum([values[0]] + sums)
    flows = []
    for axis in range(3):
        total = None
        for k, q in enumerate(range(1, Q, 2)):
            factor = VELOCITIES[q][axis]
            if factor == 0:
                continue
            if total is None:
                total = diffs[k] if factor > 0 else -diffs[k]
            else:
                total = total + diffs[k] if factor > 0 else total - diffs[k]
        flows.append(total)
    return density, flows[0], flows[1], flows[2]


def collide(values, rate, kind):
    density, flow_x, flow_y, flow_z = moments(values)
    inverse = 1.0 / density
    wall = kind == 1
    inlet = kind == 2
    fluid = kind == 0
    vel = (
        jnp.where(inlet, INLET_SPEED, flow_x * inverse),
        jnp.where(inlet, 0.0, flow_y * inverse),
        jnp.where(inlet, 0.0, flow_z * inverse),
    )
    scale = jnp.where(fluid, density, 1.0)
    rate = jnp.where(fluid, rate, 1.0)
    base = 1.0 - 1.5 * (vel[0] * vel[0] + vel[1] * vel[1] + vel[2] * vel[2])
    weighted = {w: w * scale for w in set(WEIGHTS)}
    out = [None] * Q
    relaxed = values[0] + rate * (weighted[WEIGHTS[0]] * base - values[0])
    out[0] = jnp.where(wall, values[0], relaxed)
    for q in range(1, Q, 2):
        project = None
        for factor, component in zip(VELOCITIES[q], vel):
            if factor == 0:
                continue
            if project is None:
                project = component
            else:
                project = project + component if factor > 0 else project - component
        even = base + 4.5 * (project * project)
        odd = 3.0 * project
        w = weighted[WEIGHTS[q]]
        forward = values[q] + rate * (w * (even + odd) - values[q])
        backward = values[q + 1] + rate * (w * (even - odd) - values[q + 1])
        out[q] = jnp.where(wall, values[q + 1], forward)
        out[q + 1] = jnp.where(wall, values[q], backward)
    return out


def roll_by(block, step, axis):
    if step == 0:
        return block
    return pltpu.roll(block, step % block.shape[axis], axis)


def face_slots(axis, sign):
    picks = []
    for q in range(Q):
        if VELOCITIES[q][axis] * sign >= 0:
            picks.append((q, 0))
        else:
            picks.append((OPPOSITE[q], 1))
    return picks


def mirror(q, axis):
    flipped = tuple(-c if k == axis else c for k, c in enumerate(VELOCITIES[q]))
    return VELOCITIES.index(flipped)


def corner_rows(sign_x, sign_y):
    rows = []
    for q, depth in face_slots(0, sign_x):
        if VELOCITIES[q][1] * sign_y >= 0:
            rows.append((q, depth))
        else:
            rows.append((OPPOSITE[mirror(q, 1)], depth))
    return rows


def first_kernel(
    pops_hbm,
    rate_hbm,
    flags_hbm,
    displacement_hbm,
    elements_hbm,
    shape_hbm,
    stiffness_hbm,
    c1,
    fixed,
    far,
    near,
    displacement,
    elements,
    shape_inverse,
    stiffness,
    pops,
    rate,
    flags,
    sems,
):
    planes, rows = c1.shape[1], c1.shape[2]
    copies = [
        pltpu.make_async_copy(rate_hbm, rate, sems.at[planes]),
        pltpu.make_async_copy(flags_hbm, flags, sems.at[planes + 1]),
    ]
    loads = [
        pltpu.make_async_copy(pops_hbm.at[:, x], pops.at[x], sems.at[x]) for x in range(planes)
    ]
    shell = [
        pltpu.make_async_copy(source, target, sems.at[planes + 2 + k])
        for k, (source, target) in enumerate(
            (
                (displacement_hbm, displacement),
                (elements_hbm, elements),
                (shape_hbm, shape_inverse),
                (stiffness_hbm, stiffness),
            )
        )
    ]
    for copy in loads[:1] + copies + loads[1:] + shell:
        copy.start()
    for copy in copies:
        copy.wait()

    def plane(x, carry):
        pltpu.make_async_copy(pops_hbm.at[:, x], pops.at[x], sems.at[x]).wait()
        kind = flags[x]
        values = [pops[x, q] for q in range(Q)]
        result = collide(values, rate[x], kind)
        for q in range(Q):
            c1[q, x] = roll_by(result[q], VELOCITIES[q][2], 1)
        fixed[0, x] = kind.astype(F32)
        fixed[1, x] = rate[x]
        return carry

    lax.fori_loop(0, planes, plane, 0, unroll=2)

    def pack(out, sign, outside):
        def line(x, carry):
            for slot, (q, depth) in enumerate(face_slots(1, sign)):
                y = rows - 1 - depth if sign > 0 else depth
                out[slot, pl.ds(x, 1)] = c1[q, x, y : y + 1]
            y = rows - 1 if sign > 0 else 0
            for k, slot in enumerate((FLAG_SLOT, RATE_SLOT)):
                out[slot, pl.ds(x, 1)] = fixed[k, x, y : y + 1]
            return carry

        lax.fori_loop(0, planes, line, 0)
        for slot in range(SLOTS, SIDE_SLOTS):
            out[slot] = jnp.zeros(out.shape[1:], F32)
        clear_outside(out, outside)

    pack_pair(pack, "inner", near, far)
    for copy in shell:
        copy.wait()


def clear_outside(out, outside):
    @pl.when(outside)
    def _():
        out[...] = jnp.zeros(out.shape, F32)


def pack_pair(pack, axis, near, far):
    at = lax.axis_index(axis)
    even = lax.rem(at, 2) == 0
    first, last = at == 0, at == lax.axis_size(axis) - 1

    @pl.when(even)
    def _():
        pack(near, 1, last)
        pack(far, -1, first)

    @pl.when(jnp.logical_not(even))
    def _():
        pack(near, -1, first)
        pack(far, 1, last)


def slab_face_kernel(c1, fixed, numbers, far, near):
    del numbers
    planes = c1.shape[1]

    def pack(out, sign, outside):
        for slot, (q, depth) in enumerate(face_slots(0, sign)):
            out[slot] = c1[q, planes - 1 - depth if sign > 0 else depth]
        end = planes - 1 if sign > 0 else 0
        out[FLAG_SLOT] = fixed[0, end]
        out[RATE_SLOT] = fixed[1, end]
        clear_outside(out, outside)

    pack_pair(pack, "slab", near, far)


def gather_both(near, far, both, axis):
    odd = lax.rem(lax.axis_index(axis), 2)
    for slot in range(both.shape[1]):
        both[1 - odd, slot] = near[slot]
        both[odd, slot] = far[slot]


def corner_kernel(far_y, near_y, other, far, near, both):
    planes = near_y.shape[1]
    gather_both(near_y, far_y, both, "inner")

    def pack(out, sign, outside):
        for side, sign_y in enumerate((1, -1)):
            picks = corner_rows(sign, sign_y) + [(FLAG_SLOT, 0), (RATE_SLOT, 0)]
            for row, (slot, depth) in enumerate(picks):
                x = planes - 1 - depth if sign > 0 else depth
                at = 3 * side + row // 8
                out[at, row % 8 : row % 8 + 1] = both[side, slot, x : x + 1]
        for part in range(3):
            out[FORCE_SLOT + part] = other[part]
        clear_outside(out, outside)

    pack_pair(pack, "slab", near, far)


def with_edge(block, step_y, edge):
    rows = block.shape[0]
    sub = lax.broadcasted_iota(jnp.int32, block.shape, 0)
    if step_y > 0:
        return jnp.where(sub == 0, edge, roll_by(block, 1, 0))
    return jnp.where(sub == rows - 1, edge, roll_by(block, -1, 0))


def store_plane(extended, walls, second, at, rate, kind):
    values = []
    for q in range(Q):
        step_x, step_y, _ = VELOCITIES[q]
        block = extended[q, at + 1 - step_x]
        if step_y != 0:
            edge = walls[0 if step_y > 0 else 1, q, pl.ds(at + 1 - step_x, 1)]
            block = with_edge(block, step_y, edge)
        values.append(block)
    result = collide(values, rate, kind)
    for q in range(Q):
        second[q, at] = roll_by(result[q], VELOCITIES[q][2], 1)


def inside_kernel(
    c1,
    fixed,
    far_y,
    near_y,
    far_x,
    near_x,
    extended,
    walls,
    crossing,
    second,
    ends,
    both_y,
    both_x,
):
    planes, rows, _ = c1.shape[1:]
    wide = planes + 4
    gather_both(near_y, far_y, both_y, "inner")
    gather_both(near_x, far_x, both_x, "slab")
    for q in range(Q):
        for x in range(planes):
            extended[q, x + 2] = c1[q, x]
        extended[q, 1] = both_x[0, q]
        extended[q, planes + 2] = both_x[1, q]
        if VELOCITIES[q][0] > 0:
            extended[q, 0] = both_x[0, OPPOSITE[q]]
        if VELOCITIES[q][0] < 0:
            extended[q, planes + 3] = both_x[1, OPPOSITE[q]]
    for end in range(2):
        ends[end, 0] = both_x[end, FLAG_SLOT]
        ends[end, 1] = both_x[end, RATE_SLOT]

    for side, sign in enumerate((1, -1)):
        y = 0 if sign > 0 else rows - 1
        for slot in range(SLOTS):
            walls[side, slot, 2 : planes + 2] = both_y[side, slot]
        place = 0
        for q in range(Q):
            if VELOCITIES[q][1] != -sign:
                continue
            for x in range(wide):
                crossing[side, place, x : x + 1] = extended[q, x, y : y + 1]
            place += 1

    def inside_plane(x, carry):
        store_plane(extended, walls, second, x + 1, fixed[1, x], fixed[0, x])
        return carry

    lax.fori_loop(1, planes - 1, inside_plane, 0, unroll=2)


def second_kernel(
    block_source_hbm,
    block_target_hbm,
    block_node_hbm,
    block_count,
    far,
    near,
    fixed,
    extended,
    crossing,
    ends,
    internal_own,
    walls_in,
    second_in,
    out,
    message,
    walls,
    second,
    both,
    edges,
    loads,
    block_source,
    block_target,
    block_node,
    sems,
):
    del walls_in, second_in
    copies = [
        pltpu.make_async_copy(block_source_hbm, block_source, sems.at[0]),
        pltpu.make_async_copy(block_target_hbm, block_target, sems.at[1]),
        pltpu.make_async_copy(block_node_hbm, block_node, sems.at[2]),
    ]
    for copy in copies:
        copy.start()
    planes, rows, length = out.shape[1:]
    half = length // BLK
    slots = block_source.shape[2]
    wide = planes + 4
    slab = lax.axis_index("slab")
    inner = lax.axis_index("inner")
    slab_end = lax.axis_size("slab") - 1
    inner_end = lax.axis_size("inner") - 1
    gather_both(near, far, both, "slab")

    for side, sign in enumerate((1, -1)):
        for end, sign_x in enumerate((1, -1)):
            for row, (slot, depth) in enumerate(corner_rows(sign_x, sign)):
                at = (1 - depth) if sign_x > 0 else planes + 2 + depth
                source = 3 * side + row // 8
                walls[side, slot, at : at + 1] = both[end, source, row % 8 : row % 8 + 1]
            at = 1 if sign_x > 0 else planes + 2
            for row in (FLAG_SLOT, RATE_SLOT):
                source = 3 * side + row // 8
                walls[side, row, at : at + 1] = both[end, source, row % 8 : row % 8 + 1]

    def edge_planes(end, carry):
        x = end * (planes - 1)
        store_plane(extended, walls, second, x + 1, fixed[1, x], fixed[0, x])
        store_plane(extended, walls, second, end * (planes + 1), ends[end, 1], ends[end, 0])
        return carry

    lax.fori_loop(0, 2, edge_planes, 0)

    @pl.when(slab == 0)
    def _():
        for q in range(Q):
            if VELOCITIES[q][0] > 0:
                second[q, 0] = jnp.zeros((rows, length), F32)

    @pl.when(slab == slab_end)
    def _():
        for q in range(Q):
            if VELOCITIES[q][0] < 0:
                second[q, planes + 1] = jnp.zeros((rows, length), F32)

    across = lax.broadcasted_iota(jnp.int32, (wide, length), 0)
    hidden = ((across <= 1) & (slab == 0)) | ((across >= planes + 2) & (slab == slab_end))
    for side, sign, outside in ((0, 1, inner == 0), (1, -1, inner == inner_end)):
        values = []
        place = 0
        for q in range(Q):
            step_x, step_y, _ = VELOCITIES[q]
            if step_y == 0:
                block = walls[side, q]
            elif step_y == sign:
                block = walls[side, OPPOSITE[q]]
            else:
                block = crossing[side, place]
                place += 1
            values.append(roll_by(block, step_x, 0))
        result = collide(values, walls[side, RATE_SLOT], walls[side, FLAG_SLOT])
        place = 0
        for q in range(Q):
            if VELOCITIES[q][1] == sign:
                kept = jnp.where(hidden | outside, 0.0, result[q])
                edges[side, place] = roll_by(kept, VELOCITIES[q][2], 1)
                place += 1

    def plane_two(x, carry):
        values = []
        places = {1: 0, -1: 0}
        for q in range(Q):
            step_x, step_y, _ = VELOCITIES[q]
            block = second[q, x + 1 - step_x]
            if step_y != 0:
                edge = edges[0 if step_y > 0 else 1, places[step_y], pl.ds(x + 2 - step_x, 1)]
                places[step_y] += 1
                block = with_edge(block, step_y, edge)
            values.append(block)
            out[q, x] = block
        density, flow_x, flow_y, flow_z = moments(values)
        parts = (
            LOAD_SCALE * flow_x,
            LOAD_SCALE * (flow_y + (density - 1.0) / 3.0),
            LOAD_SCALE * flow_z,
        )
        for part in range(3):
            for piece in range(half):
                loads[x * half + piece, part] = parts[part][:, piece * BLK : (piece + 1) * BLK]
        return carry

    lax.fori_loop(0, planes, plane_two, 0, unroll=2)

    for copy in copies:
        copy.wait()
    node_blocks = internal_own.shape[1] * half
    live = jnp.broadcast_to(block_count[...], (1, BLK))
    lanes_of = lax.broadcasted_iota(jnp.int32, (1, BLK), 1) // (BLK // slots)
    all_keys = jnp.full((1, BLK), -1, jnp.int32)
    for k in range(slots):
        run = block_source[0, 0, k]
        x = run // (rows * half)
        left = run - x * (rows * half)
        y = left // half
        piece = left - y * half
        for part in range(3):
            message[3 * k + part] = loads[x * half + piece, part, pl.ds(y, 1)]
        key = block_target[0, 0, k] * node_blocks + block_node[0, 0, k]
        all_keys = jnp.where((lanes_of == k) & (live > k), key, all_keys)
    message[3 * slots] = all_keys.astype(F32)
    for part in range(3):
        start = 3 * slots + 1 + part * node_blocks
        for piece in range(half):
            at = piece * rows
            lanes = slice(piece * BLK, (piece + 1) * BLK)
            message[start + at : start + at + rows, 0] = (
                internal_own[part, :, lanes] + both[0, FORCE_SLOT + part, :, lanes]
            )


def element_kernel(
    elements, displacement, next_nodes, shape_inverse, stiffness, low_ids, high_ids, forces, shapes,
    numbers, corners,
):
    node_dev = displacement.shape[1]
    node_blocks = node_dev // BLK
    runs = elements.shape[1] // BLK
    for j in range(runs):
        lanes = slice(j * BLK, (j + 1) * BLK)
        for row in range(3):
            numbers[row, j : j + 1] = elements[row : row + 1, lanes]
            shapes[row, j : j + 1] = shape_inverse[row : row + 1, lanes]
    for row in range(3):
        low_ids[row] = (numbers[row] & (BLK - 1)).astype(F32)
        high_ids[row] = (numbers[row] >> 7).astype(F32)

    def gather(group, carry):
        rows = pl.ds(pl.multiple_of(group * 8, 8), 8)
        low = [numbers[corner, rows] & (BLK - 1) for corner in range(3)]
        high = [numbers[corner, rows] >> 7 for corner in range(3)]
        for corner in range(3):
            nodes = [jnp.zeros((8, BLK), F32)] * 3
            for block in range(2 * node_blocks):
                source = displacement if block < node_blocks else next_nodes
                start = (block % node_blocks) * BLK
                here = high[corner] == block
                for part in range(3):
                    row = source[part : part + 1, start : start + BLK]
                    picked = jnp.take_along_axis(
                        jnp.broadcast_to(row, (8, BLK)),
                        low[corner],
                        axis=1,
                        mode="promise_in_bounds",
                    )
                    nodes[part] = jnp.where(here, picked, nodes[part])
            for part in range(3):
                corners[corner, part, rows] = nodes[part]
        return carry

    lax.fori_loop(0, runs // 8, gather, 0)

    first, second, third = [[corners[c, p] for p in range(3)] for c in range(3)]
    diag_a = shapes[0]
    skew_b = shapes[1]
    diag_c = shapes[2]
    stiff = stiffness[...]
    edge_one = [second[p] - first[p] for p in range(3)]
    edge_two = [third[p] - first[p] for p in range(3)]
    one = [diag_a * edge_one[p] for p in range(3)]
    two = [skew_b * edge_one[p] + diag_c * edge_two[p] for p in range(3)]
    one[0] = one[0] + 1.0
    two[1] = two[1] + 1.0
    aa = one[0] * one[0] + one[1] * one[1] + one[2] * one[2]
    ab = one[0] * two[0] + one[1] * two[1] + one[2] * two[2]
    bb = two[0] * two[0] + two[1] * two[1] + two[2] * two[2]
    determinant = aa * bb - ab * ab
    scale = 1.0 / determinant
    inverse_aa = bb * scale
    inverse_ab = -ab * scale
    inverse_bb = aa * scale
    pressure = LAME_RATIO * (0.5 * jnp.log(determinant))
    for p in range(3):
        pulled_one = one[p] * inverse_aa + two[p] * inverse_ab
        pulled_two = one[p] * inverse_ab + two[p] * inverse_bb
        stress_one = stiff * (one[p] - pulled_one + pressure * pulled_one)
        stress_two = stiff * (two[p] - pulled_two + pressure * pulled_two)
        force_one = diag_a * stress_one + skew_b * stress_two
        force_two = diag_c * stress_two
        for corner, force in enumerate((-(force_one + force_two), force_one, force_two)):
            rest = force
            for part in range(PIECES):
                piece = rest.astype(jnp.bfloat16).astype(F32)
                rest = rest - piece
                forces[part * 3 + p, corner] = piece


def spread_kernel(base, low_ids, high_ids, forces, out):
    runs = low_ids.shape[1]
    parts, rows, length = out.shape
    pieces = length // BLK
    slots = pieces * rows
    kind = jnp.bfloat16
    tile = 16
    slot_ids = lax.broadcasted_iota(jnp.int32, (slots, BLK), 0).astype(F32) + base
    slot_ids = slot_ids.astype(kind)
    lane_ids = lax.broadcasted_iota(jnp.int32, (BLK, BLK), 0).astype(F32).astype(kind)
    ones = jnp.ones((BLK, BLK), kind)
    none = jnp.zeros((BLK, BLK), kind)
    blank = jnp.zeros((slots, BLK), kind)

    def tall_row(row, count):
        block = jnp.broadcast_to(row, (tile, BLK)).astype(kind)
        return jnp.concatenate([block] * (count // tile), axis=0)

    total = None
    for corner in range(3):
        for first in range(0, runs, STEP):
            left = [[] for _ in range(parts * PIECES)]
            right = []
            for j in range(first, min(first + STEP, runs)):
                row = slice(j, j + 1)
                here = slot_ids == tall_row(high_ids[corner, row], slots)
                there = lane_ids == tall_row(low_ids[corner, row], BLK)
                right.append(jnp.where(there, ones, none))
                for part in range(parts * PIECES):
                    left[part].append(
                        jnp.where(here, tall_row(forces[part, corner, row], slots), blank)
                    )
            tall = jnp.concatenate([jnp.concatenate(part, axis=1) for part in left], axis=0)
            wide = jnp.concatenate(right, axis=1)
            product = lax.dot_general(
                tall, wide, (((1,), (1,)), ((), ())), preferred_element_type=F32
            )
            total = product if total is None else total + product
    for p in range(parts):
        summed = total[p * slots : (p + 1) * slots]
        for part in range(1, PIECES):
            start = (parts * part + p) * slots
            summed = summed + total[start : start + slots]
        for piece in range(pieces):
            out[p, :, piece * BLK : (piece + 1) * BLK] = summed[piece * rows : (piece + 1) * rows]


def store_kernel(values, out_hbm, sem):
    store = pltpu.make_async_copy(values, out_hbm, sem)
    store.start()
    store.wait()


def sum_messages(messages, senders, wanted, node_blocks):
    slots = wanted.shape[0]
    own_ids = lax.broadcasted_iota(jnp.int32, (node_blocks, BLK), 0)
    own_ids = (own_ids + lax.axis_index("inner") * node_blocks).astype(F32)
    external = [[] for _ in range(3)]
    moved = [[] for _ in range(3)]
    for message, sender in zip(messages, senders):
        named = [key_of(message, k, slots) for k in range(slots)]
        here = [own_ids == key for key in named]
        same = [wanted == key for key in named]
        owned = [wanted == (sender * node_blocks + b).astype(F32) for b in range(node_blocks)]
        for part in range(3):
            rows = [message[3 * k + part] for k in range(slots)]
            at = 3 * slots + 1 + part * node_blocks
            inside = [message[at + b] for b in range(node_blocks)]
            external[part].append(tree_sum([jnp.where(m, r, 0.0) for m, r in zip(here, rows)]))
            moved[part].append(tree_sum([jnp.where(m, r, 0.0) for m, r in zip(same, rows)]))
            moved[part].append(-tree_sum([jnp.where(m, r, 0.0) for m, r in zip(owned, inside)]))
    return [tree_sum(terms) for terms in external], [tree_sum(terms) for terms in moved]


def key_of(message, k, slots):
    width = BLK // slots
    return jnp.broadcast_to(message[3 * slots][:, k * width : k * width + 1], (1, BLK))


def early_kernel(count, *refs):
    messages = refs[:-3]
    total, moved, keys = refs[-3:]
    slots, node_blocks = keys.shape[0], total.shape[1]
    inner = lax.axis_index("inner")
    for k in range(slots):
        keys[k : k + 1] = key_of(messages[0], k, slots)
    steps = [0] + list(range(2, count))
    senders = [partner_of(inner, step, count) for step in steps]
    external, forces = sum_messages(messages, senders, keys[...], node_blocks)
    for part in range(3):
        start = 3 * slots + 1 + part * node_blocks
        total[part] = external[part] - messages[0][start : start + node_blocks, 0]
        moved[part] = forces[part]


def final_kernel(count, message, total, moved, keys, residual, motion):
    node_blocks = total.shape[1]
    wanted = keys[...]
    sender = partner_of(lax.axis_index("inner"), 1, count)
    external, forces = sum_messages([message], [sender], wanted, node_blocks)
    live = wanted >= 0.0
    for part in range(3):
        left = total[part] + external[part]
        for b in range(node_blocks):
            residual[part : part + 1, b * BLK : (b + 1) * BLK] = left[b : b + 1]
        motion[part] = jnp.where(live, COMPLIANCE * (moved[part] + forces[part]), 0.0)


def call(kernel, outs, operands, spaces, scratch=(), out_spaces=None, micros=1.0, aliases=None):
    spec = lambda space: pl.BlockSpec(memory_space=space)
    out_spaces = out_spaces or (pltpu.VMEM,) * len(outs)
    return pl.pallas_call(
        kernel,
        out_shape=outs,
        in_specs=[spec(space) for space in spaces],
        out_specs=tuple(spec(space) for space in out_spaces),
        scratch_shapes=list(scratch),
        input_output_aliases=aliases or {},
        compiler_params=pltpu.CompilerParams(vmem_limit_bytes=VMEM_BYTES),
        cost_estimate=pl.CostEstimate(
            flops=0, bytes_accessed=int(micros * 3.6e6), transcendentals=0
        ),
    )(*operands)


def partner_of(at, step, count):
    if count & (count - 1) == 0:
        return at ^ step
    return (at + count - step) % count


def exchange(block, axis, step):
    count = lax.axis_size(axis)
    return lax.ppermute(block, axis, [(partner_of(i, step, count), i) for i in range(count)])


def around(block, axis, step):
    count = lax.axis_size(axis)
    return lax.ppermute(block, axis, [(i, (i + step) % count) for i in range(count)])


def swap(near, far, axis, beside):
    count, others = lax.axis_size(axis), lax.axis_size(beside)
    routes = []
    for start in (0, 1):
        route = []
        for other in range(others):
            for i in range(count):
                j = i + 1 if i % 2 == start else i - 1
                to = other
                if not 0 <= j < count:
                    j = i
                    to = other ^ 1 if others % 2 == 0 else other
                route.append((other * count + i, to * count + j))
        routes.append(route)
    axes = (beside, axis)
    return lax.ppermute(near, axes, routes[0]), lax.ppermute(far, axes, routes[1])


def shards(
    populations,
    relaxation,
    node_flags,
    displacement,
    elements,
    shape_inverse,
    stiffness,
    block_source,
    block_target,
    block_node,
    block_count,
):
    planes, rows, length = populations.shape[1:]
    half = length // BLK
    node_dev = displacement.shape[1]
    node_blocks = node_dev // BLK
    runs = stiffness.shape[0] // BLK
    slots = block_source.shape[2]
    count = lax.axis_size("inner")
    shape = lambda *dims: jax.ShapeDtypeStruct(dims, F32)
    whole = shape(*populations.shape)
    vmem, hbm, smem = pltpu.VMEM, pltpu.HBM, pltpu.SMEM

    next_nodes = around(displacement, "slab", -1)
    face_y = shape(SIDE_SLOTS, planes, length)
    face_x = shape(SLOTS, rows, length)
    pin = lambda block: pltpu.with_memory_space_constraint(block, hbm)
    whole_like = lambda block: jax.ShapeDtypeStruct(block.shape, block.dtype)
    shell = (displacement, elements, shape_inverse, stiffness.reshape(runs, BLK))
    c1, fixed, far, near, own_nodes, corners, inverses, stiff = call(
        first_kernel,
        (
            whole,
            shape(2, planes, rows, length),
            face_y,
            face_y,
            *(whole_like(block) for block in shell),
        ),
        tuple(pin(block) for block in (populations, relaxation, node_flags, *shell)),
        (hbm,) * 7,
        scratch=(
            pltpu.VMEM((planes, Q, rows, length), F32),
            pltpu.VMEM((planes, rows, length), F32),
            pltpu.VMEM((planes, rows, length), jnp.int32),
            pltpu.SemaphoreType.DMA((planes + 6,)),
        ),
        micros=1.5,
    )
    near_y, far_y = swap(near, far, "inner", "slab")
    numbers = shape(3, runs, BLK)
    low_ids, high_ids, forces = call(
        element_kernel,
        (numbers, numbers, shape(3 * PIECES, 3, runs, BLK)),
        (corners, own_nodes, next_nodes, inverses, stiff),
        (vmem,) * 5,
        scratch=(
            pltpu.VMEM((3, runs, BLK), F32),
            pltpu.VMEM((3, runs, BLK), jnp.int32),
            pltpu.VMEM((3, 3, runs, BLK), F32),
        ),
        micros=0.001,
    )
    far, near = call(
        slab_face_kernel, (face_x, face_x), (c1, fixed, low_ids), (vmem,) * 3, micros=0.001
    )
    near_x, far_x = swap(near, far, "slab", "group")
    nodal = shape(3, node_blocks // half, length)
    (other,) = call(
        functools.partial(spread_kernel, node_blocks),
        (nodal,),
        (low_ids, high_ids, forces),
        (vmem,) * 3,
        micros=0.001,
    )
    corner = shape(CORNER_SLOTS, rows, length)
    far, near = call(
        corner_kernel,
        (corner, corner),
        (far_y, near_y, other),
        (vmem,) * 3,
        scratch=(pltpu.VMEM((2, SLOTS, planes, length), F32),),
        micros=0.3,
    )
    near_c, far_c = swap(near, far, "slab", "group")
    (own,) = call(
        functools.partial(spread_kernel, 0),
        (nodal,),
        (low_ids, high_ids, forces),
        (vmem,) * 3,
        micros=0.8,
    )
    wide = planes + 4
    walls_shape = shape(2, SLOTS, wide, length)
    second_shape = shape(Q, planes + 2, rows, length)
    extended, walls, crossing, second, ends = call(
        inside_kernel,
        (
            shape(Q, wide, rows, length),
            walls_shape,
            shape(2, 5, wide, length),
            second_shape,
            shape(2, 2, rows, length),
        ),
        (c1, fixed, far_y, near_y, far_x, near_x),
        (vmem,) * 6,
        scratch=(
            pltpu.VMEM((2, SLOTS, planes, length), F32),
            pltpu.VMEM((2, SLOTS, rows, length), F32),
        ),
        micros=0.8,
    )
    lines = 3 * slots + 1 + 3 * node_blocks
    values, message, _, _ = call(
        second_kernel,
        (whole, shape(lines, 1, BLK), walls_shape, second_shape),
        (
            pin(block_source),
            pin(block_target),
            pin(block_node),
            block_count,
            far_c,
            near_c,
            fixed,
            extended,
            crossing,
            ends,
            own,
            walls,
            second,
        ),
        (hbm,) * 3 + (vmem,) * 10,
        aliases={11: 2, 12: 3},
        scratch=(
            pltpu.VMEM((2, CORNER_SLOTS, rows, length), F32),
            pltpu.VMEM((2, 5, wide, length), F32),
            pltpu.VMEM((planes * half, 3, rows, BLK), F32),
            pltpu.SMEM(block_source.shape, jnp.int32),
            pltpu.SMEM(block_target.shape, jnp.int32),
            pltpu.SMEM(block_node.shape, jnp.int32),
            pltpu.SemaphoreType.DMA((3,)),
        ),
        micros=1.5,
    )
    messages = [message] + [exchange(message, "inner", step) for step in range(1, count)]
    (populations_out,) = call(
        store_kernel,
        (whole,),
        (values,),
        (vmem,),
        out_spaces=(hbm,),
        scratch=(pltpu.SemaphoreType.DMA(()),),
        micros=1.0,
    )
    total, moved, keys = call(
        functools.partial(early_kernel, count),
        (shape(3, node_blocks, BLK), shape(3, slots, BLK), shape(slots, BLK)),
        (messages[0], *messages[2:]),
        (vmem,) * (count - 1),
        micros=0.4,
    )
    residual, motion = call(
        functools.partial(final_kernel, count),
        (shape(3, node_dev), shape(3, slots, BLK)),
        (messages[1], total, moved, keys),
        (vmem,) * 4,
        micros=0.5,
    )
    return populations_out, residual, motion.transpose(1, 0, 2)[None, None]


def solution(mesh):
    return jax.shard_map(
        shards,
        mesh=mesh,
        in_specs=(
            P(None, ("group", "slab"), "inner", None),
            P(("group", "slab"), "inner", None),
            P(("group", "slab"), "inner", None),
            P(None, ("group", "slab", "inner")),
            P(None, ("group", "slab", "inner")),
            P(None, ("group", "slab", "inner")),
            P(("group", "slab", "inner")),
            P(("group", "slab"), "inner", None),
            P(("group", "slab"), "inner", None),
            P(("group", "slab"), "inner", None),
            P(("group", "slab"), "inner"),
        ),
        out_specs=(
            P(None, ("group", "slab"), "inner", None),
            P(None, ("group", "slab", "inner")),
            P(("group", "slab"), "inner", None, None, None),
        ),
        check_vma=False,
    )
```

```python
import functools

import jax
import jax.numpy as jnp
from jax import lax
from jax.experimental import pallas as pl
from jax.experimental.pallas import tpu as pltpu
from jax.sharding import PartitionSpec as P

BLK = 128
VELOCITIES = (
    (0, 0, 0),
    (1, 0, 0),
    (-1, 0, 0),
    (0, 1, 0),
    (0, -1, 0),
    (0, 0, 1),
    (0, 0, -1),
    (1, 1, 0),
    (-1, -1, 0),
    (1, -1, 0),
    (-1, 1, 0),
    (1, 0, 1),
    (-1, 0, -1),
    (1, 0, -1),
    (-1, 0, 1),
    (0, 1, 1),
    (0, -1, -1),
    (0, 1, -1),
    (0, -1, 1),
)
WEIGHTS = (1.0 / 3.0,) + (1.0 / 18.0,) * 6 + (1.0 / 36.0,) * 12
OPPOSITE = (0, 2, 1, 4, 3, 6, 5, 8, 7, 10, 9, 12, 11, 14, 13, 16, 15, 18, 17)
INLET_SPEED = 0.04
LOAD_SCALE = 25.0
COMPLIANCE = 0.5
LAME_RATIO = 2.0
Q = 19
FLAG_SLOT = 19
RATE_SLOT = 20
SLOTS = 21
SIDE_SLOTS = 24
FORCE_SLOT = 6
CORNER_SLOTS = FORCE_SLOT + 3
PIECES = 2
STEP = 4
F32 = jnp.float32
VMEM_BYTES = 48 * 1024 * 1024


def moments(values):
    sums = [values[q] + values[q + 1] for q in range(1, Q, 2)]
    diffs = [values[q] - values[q + 1] for q in range(1, Q, 2)]
    density = values[0]
    for term in sums:
        density = density + term
    flows = []
    for axis in range(3):
        total = None
        for k, q in enumerate(range(1, Q, 2)):
            factor = VELOCITIES[q][axis]
            if factor == 0:
                continue
            if total is None:
                total = diffs[k] if factor > 0 else -diffs[k]
            else:
                total = total + diffs[k] if factor > 0 else total - diffs[k]
        flows.append(total)
    return density, flows[0], flows[1], flows[2]


def collide(values, rate, kind):
    density, flow_x, flow_y, flow_z = moments(values)
    inverse = 1.0 / density
    wall = kind == 1
    inlet = kind == 2
    fluid = kind == 0
    vel = (
        jnp.where(inlet, INLET_SPEED, flow_x * inverse),
        jnp.where(inlet, 0.0, flow_y * inverse),
        jnp.where(inlet, 0.0, flow_z * inverse),
    )
    scale = jnp.where(fluid, density, 1.0)
    rate = jnp.where(fluid, rate, 1.0)
    base = 1.0 - 1.5 * (vel[0] * vel[0] + vel[1] * vel[1] + vel[2] * vel[2])
    weighted = {w: w * scale for w in set(WEIGHTS)}
    out = [None] * Q
    relaxed = values[0] + rate * (weighted[WEIGHTS[0]] * base - values[0])
    out[0] = jnp.where(wall, values[0], relaxed)
    for q in range(1, Q, 2):
        project = None
        for factor, component in zip(VELOCITIES[q], vel):
            if factor == 0:
                continue
            if project is None:
                project = component
            else:
                project = project + component if factor > 0 else project - component
        even = base + 4.5 * (project * project)
        odd = 3.0 * project
        w = weighted[WEIGHTS[q]]
        forward = values[q] + rate * (w * (even + odd) - values[q])
        backward = values[q + 1] + rate * (w * (even - odd) - values[q + 1])
        out[q] = jnp.where(wall, values[q + 1], forward)
        out[q + 1] = jnp.where(wall, values[q], backward)
    return out


def roll_by(block, step, axis):
    if step == 0:
        return block
    return pltpu.roll(block, step % block.shape[axis], axis)


def face_slots(axis, sign):
    picks = []
    for q in range(Q):
        if VELOCITIES[q][axis] * sign >= 0:
            picks.append((q, 0))
        else:
            picks.append((OPPOSITE[q], 1))
    return picks


def mirror(q, axis):
    flipped = tuple(-c if k == axis else c for k, c in enumerate(VELOCITIES[q]))
    return VELOCITIES.index(flipped)


def corner_rows(sign_x, sign_y):
    rows = []
    for q, depth in face_slots(0, sign_x):
        if VELOCITIES[q][1] * sign_y >= 0:
            rows.append((q, depth))
        else:
            rows.append((OPPOSITE[mirror(q, 1)], depth))
    return rows


def first_kernel(
    pops_hbm,
    rate_hbm,
    flags_hbm,
    displacement_hbm,
    elements_hbm,
    shape_hbm,
    stiffness_hbm,
    c1,
    fixed,
    far,
    near,
    displacement,
    elements,
    shape_inverse,
    stiffness,
    pops,
    rate,
    flags,
    sems,
):
    planes, rows = c1.shape[1], c1.shape[2]
    copies = [
        pltpu.make_async_copy(rate_hbm, rate, sems.at[planes]),
        pltpu.make_async_copy(flags_hbm, flags, sems.at[planes + 1]),
    ]
    loads = [
        pltpu.make_async_copy(pops_hbm.at[:, x], pops.at[x], sems.at[x]) for x in range(planes)
    ]
    shell = [
        pltpu.make_async_copy(source, target, sems.at[planes + 2 + k])
        for k, (source, target) in enumerate(
            (
                (displacement_hbm, displacement),
                (elements_hbm, elements),
                (shape_hbm, shape_inverse),
                (stiffness_hbm, stiffness),
            )
        )
    ]
    for copy in loads[:1] + copies + loads[1:] + shell:
        copy.start()
    for copy in copies:
        copy.wait()

    def plane(x, carry):
        pltpu.make_async_copy(pops_hbm.at[:, x], pops.at[x], sems.at[x]).wait()
        kind = flags[x]
        values = [pops[x, q] for q in range(Q)]
        result = collide(values, rate[x], kind)
        for q in range(Q):
            c1[q, x] = roll_by(result[q], VELOCITIES[q][2], 1)
        fixed[0, x] = kind.astype(F32)
        fixed[1, x] = rate[x]
        return carry

    lax.fori_loop(0, planes, plane, 0)

    def pack(out, sign, outside):
        def line(x, carry):
            for slot, (q, depth) in enumerate(face_slots(1, sign)):
                y = rows - 1 - depth if sign > 0 else depth
                out[slot, pl.ds(x, 1)] = c1[q, x, y : y + 1]
            y = rows - 1 if sign > 0 else 0
            for k, slot in enumerate((FLAG_SLOT, RATE_SLOT)):
                out[slot, pl.ds(x, 1)] = fixed[k, x, y : y + 1]
            return carry

        lax.fori_loop(0, planes, line, 0)
        for slot in range(SLOTS, SIDE_SLOTS):
            out[slot] = jnp.zeros(out.shape[1:], F32)
        clear_outside(out, outside)

    pack_pair(pack, "inner", near, far)
    for copy in shell:
        copy.wait()


def clear_outside(out, outside):
    @pl.when(outside)
    def _():
        out[...] = jnp.zeros(out.shape, F32)


def pack_pair(pack, axis, near, far):
    at = lax.axis_index(axis)
    even = lax.rem(at, 2) == 0
    first, last = at == 0, at == lax.axis_size(axis) - 1

    @pl.when(even)
    def _():
        pack(near, 1, last)
        pack(far, -1, first)

    @pl.when(jnp.logical_not(even))
    def _():
        pack(near, -1, first)
        pack(far, 1, last)


def slab_face_kernel(c1, fixed, numbers, far, near):
    del numbers
    planes = c1.shape[1]

    def pack(out, sign, outside):
        for slot, (q, depth) in enumerate(face_slots(0, sign)):
            out[slot] = c1[q, planes - 1 - depth if sign > 0 else depth]
        end = planes - 1 if sign > 0 else 0
        out[FLAG_SLOT] = fixed[0, end]
        out[RATE_SLOT] = fixed[1, end]
        clear_outside(out, outside)

    pack_pair(pack, "slab", near, far)


def gather_both(near, far, both, axis):
    odd = lax.rem(lax.axis_index(axis), 2)
    for slot in range(both.shape[1]):
        both[1 - odd, slot] = near[slot]
        both[odd, slot] = far[slot]


def corner_kernel(far_y, near_y, other, far, near, both):
    planes = near_y.shape[1]
    gather_both(near_y, far_y, both, "inner")

    def pack(out, sign, outside):
        for side, sign_y in enumerate((1, -1)):
            picks = corner_rows(sign, sign_y) + [(FLAG_SLOT, 0), (RATE_SLOT, 0)]
            for row, (slot, depth) in enumerate(picks):
                x = planes - 1 - depth if sign > 0 else depth
                at = 3 * side + row // 8
                out[at, row % 8 : row % 8 + 1] = both[side, slot, x : x + 1]
        for part in range(3):
            out[FORCE_SLOT + part] = other[part]
        clear_outside(out, outside)

    pack_pair(pack, "slab", near, far)


def with_edge(block, step_y, edge):
    rows = block.shape[0]
    sub = lax.broadcasted_iota(jnp.int32, block.shape, 0)
    if step_y > 0:
        return jnp.where(sub == 0, edge, roll_by(block, 1, 0))
    return jnp.where(sub == rows - 1, edge, roll_by(block, -1, 0))


def store_plane(extended, walls, second, at, rate, kind):
    values = []
    for q in range(Q):
        step_x, step_y, _ = VELOCITIES[q]
        block = extended[q, at + 1 - step_x]
        if step_y != 0:
            edge = walls[0 if step_y > 0 else 1, q, pl.ds(at + 1 - step_x, 1)]
            block = with_edge(block, step_y, edge)
        values.append(block)
    result = collide(values, rate, kind)
    for q in range(Q):
        second[q, at] = roll_by(result[q], VELOCITIES[q][2], 1)


def inside_kernel(
    c1,
    fixed,
    far_y,
    near_y,
    far_x,
    near_x,
    extended,
    walls,
    crossing,
    second,
    ends,
    both_y,
    both_x,
):
    planes, rows, _ = c1.shape[1:]
    wide = planes + 4
    gather_both(near_y, far_y, both_y, "inner")
    gather_both(near_x, far_x, both_x, "slab")
    for q in range(Q):
        for x in range(planes):
            extended[q, x + 2] = c1[q, x]
        extended[q, 1] = both_x[0, q]
        extended[q, planes + 2] = both_x[1, q]
        if VELOCITIES[q][0] > 0:
            extended[q, 0] = both_x[0, OPPOSITE[q]]
        if VELOCITIES[q][0] < 0:
            extended[q, planes + 3] = both_x[1, OPPOSITE[q]]
    for end in range(2):
        ends[end, 0] = both_x[end, FLAG_SLOT]
        ends[end, 1] = both_x[end, RATE_SLOT]

    for side, sign in enumerate((1, -1)):
        y = 0 if sign > 0 else rows - 1
        for slot in range(SLOTS):
            walls[side, slot, 2 : planes + 2] = both_y[side, slot]
        place = 0
        for q in range(Q):
            if VELOCITIES[q][1] != -sign:
                continue
            for x in range(wide):
                crossing[side, place, x : x + 1] = extended[q, x, y : y + 1]
            place += 1

    def inside_plane(x, carry):
        store_plane(extended, walls, second, x + 1, fixed[1, x], fixed[0, x])
        return carry

    lax.fori_loop(1, planes - 1, inside_plane, 0)


def second_kernel(
    block_source_hbm,
    block_target_hbm,
    block_node_hbm,
    block_count,
    far,
    near,
    fixed,
    extended,
    crossing,
    ends,
    internal_own,
    walls_in,
    second_in,
    out,
    message,
    walls,
    second,
    both,
    edges,
    loads,
    block_source,
    block_target,
    block_node,
    sems,
):
    del walls_in, second_in
    copies = [
        pltpu.make_async_copy(block_source_hbm, block_source, sems.at[0]),
        pltpu.make_async_copy(block_target_hbm, block_target, sems.at[1]),
        pltpu.make_async_copy(block_node_hbm, block_node, sems.at[2]),
    ]
    for copy in copies:
        copy.start()
    planes, rows, length = out.shape[1:]
    half = length // BLK
    slots = block_source.shape[2]
    wide = planes + 4
    slab = lax.axis_index("slab")
    inner = lax.axis_index("inner")
    slab_end = lax.axis_size("slab") - 1
    inner_end = lax.axis_size("inner") - 1
    gather_both(near, far, both, "slab")

    for side, sign in enumerate((1, -1)):
        for end, sign_x in enumerate((1, -1)):
            for row, (slot, depth) in enumerate(corner_rows(sign_x, sign)):
                at = (1 - depth) if sign_x > 0 else planes + 2 + depth
                source = 3 * side + row // 8
                walls[side, slot, at : at + 1] = both[end, source, row % 8 : row % 8 + 1]
            at = 1 if sign_x > 0 else planes + 2
            for row in (FLAG_SLOT, RATE_SLOT):
                source = 3 * side + row // 8
                walls[side, row, at : at + 1] = both[end, source, row % 8 : row % 8 + 1]

    def edge_planes(end, carry):
        x = end * (planes - 1)
        store_plane(extended, walls, second, x + 1, fixed[1, x], fixed[0, x])
        store_plane(extended, walls, second, end * (planes + 1), ends[end, 1], ends[end, 0])
        return carry

    lax.fori_loop(0, 2, edge_planes, 0)

    @pl.when(slab == 0)
    def _():
        for q in range(Q):
            if VELOCITIES[q][0] > 0:
                second[q, 0] = jnp.zeros((rows, length), F32)

    @pl.when(slab == slab_end)
    def _():
        for q in range(Q):
            if VELOCITIES[q][0] < 0:
                second[q, planes + 1] = jnp.zeros((rows, length), F32)

    across = lax.broadcasted_iota(jnp.int32, (wide, length), 0)
    hidden = ((across <= 1) & (slab == 0)) | ((across >= planes + 2) & (slab == slab_end))
    for side, sign, outside in ((0, 1, inner == 0), (1, -1, inner == inner_end)):
        values = []
        place = 0
        for q in range(Q):
            step_x, step_y, _ = VELOCITIES[q]
            if step_y == 0:
                block = walls[side, q]
            elif step_y == sign:
                block = walls[side, OPPOSITE[q]]
            else:
                block = crossing[side, place]
                place += 1
            values.append(roll_by(block, step_x, 0))
        result = collide(values, walls[side, RATE_SLOT], walls[side, FLAG_SLOT])
        place = 0
        for q in range(Q):
            if VELOCITIES[q][1] == sign:
                kept = jnp.where(hidden | outside, 0.0, result[q])
                edges[side, place] = roll_by(kept, VELOCITIES[q][2], 1)
                place += 1

    def plane_two(x, carry):
        values = []
        places = {1: 0, -1: 0}
        for q in range(Q):
            step_x, step_y, _ = VELOCITIES[q]
            block = second[q, x + 1 - step_x]
            if step_y != 0:
                edge = edges[0 if step_y > 0 else 1, places[step_y], pl.ds(x + 2 - step_x, 1)]
                places[step_y] += 1
                block = with_edge(block, step_y, edge)
            values.append(block)
            out[q, x] = block
        density, flow_x, flow_y, flow_z = moments(values)
        parts = (
            LOAD_SCALE * flow_x,
            LOAD_SCALE * (flow_y + (density - 1.0) / 3.0),
            LOAD_SCALE * flow_z,
        )
        for part in range(3):
            for piece in range(half):
                loads[x * half + piece, part] = parts[part][:, piece * BLK : (piece + 1) * BLK]
        return carry

    lax.fori_loop(0, planes, plane_two, 0)

    for copy in copies:
        copy.wait()
    node_blocks = internal_own.shape[1] * half
    live = jnp.broadcast_to(block_count[...], (1, BLK))
    lanes_of = lax.broadcasted_iota(jnp.int32, (1, BLK), 1) // (BLK // slots)
    all_keys = jnp.full((1, BLK), -1, jnp.int32)
    for k in range(slots):
        run = block_source[0, 0, k]
        x = run // (rows * half)
        left = run - x * (rows * half)
        y = left // half
        piece = left - y * half
        for part in range(3):
            message[3 * k + part] = loads[x * half + piece, part, pl.ds(y, 1)]
        key = block_target[0, 0, k] * node_blocks + block_node[0, 0, k]
        all_keys = jnp.where((lanes_of == k) & (live > k), key, all_keys)
    message[3 * slots] = all_keys.astype(F32)
    for part in range(3):
        start = 3 * slots + 1 + part * node_blocks
        for piece in range(half):
            at = piece * rows
            lanes = slice(piece * BLK, (piece + 1) * BLK)
            message[start + at : start + at + rows, 0] = (
                internal_own[part, :, lanes] + both[0, FORCE_SLOT + part, :, lanes]
            )


def element_kernel(
    elements, displacement, next_nodes, shape_inverse, stiffness, low_ids, high_ids, forces, shapes,
    numbers, corners,
):
    node_dev = displacement.shape[1]
    node_blocks = node_dev // BLK
    runs = elements.shape[1] // BLK
    for j in range(runs):
        lanes = slice(j * BLK, (j + 1) * BLK)
        for row in range(3):
            numbers[row, j : j + 1] = elements[row : row + 1, lanes]
            shapes[row, j : j + 1] = shape_inverse[row : row + 1, lanes]
    for row in range(3):
        low_ids[row] = (numbers[row] & (BLK - 1)).astype(F32)
        high_ids[row] = (numbers[row] >> 7).astype(F32)

    def gather(group, carry):
        rows = pl.ds(pl.multiple_of(group * 8, 8), 8)
        low = [numbers[corner, rows] & (BLK - 1) for corner in range(3)]
        high = [numbers[corner, rows] >> 7 for corner in range(3)]
        for corner in range(3):
            nodes = [jnp.zeros((8, BLK), F32)] * 3
            for block in range(2 * node_blocks):
                source = displacement if block < node_blocks else next_nodes
                start = (block % node_blocks) * BLK
                here = high[corner] == block
                for part in range(3):
                    row = source[part : part + 1, start : start + BLK]
                    picked = jnp.take_along_axis(
                        jnp.broadcast_to(row, (8, BLK)),
                        low[corner],
                        axis=1,
                        mode="promise_in_bounds",
                    )
                    nodes[part] = jnp.where(here, picked, nodes[part])
            for part in range(3):
                corners[corner, part, rows] = nodes[part]
        return carry

    lax.fori_loop(0, runs // 8, gather, 0, unroll=2)

    first, second, third = [[corners[c, p] for p in range(3)] for c in range(3)]
    diag_a = shapes[0]
    skew_b = shapes[1]
    diag_c = shapes[2]
    stiff = stiffness[...]
    edge_one = [second[p] - first[p] for p in range(3)]
    edge_two = [third[p] - first[p] for p in range(3)]
    one = [diag_a * edge_one[p] for p in range(3)]
    two = [skew_b * edge_one[p] + diag_c * edge_two[p] for p in range(3)]
    one[0] = one[0] + 1.0
    two[1] = two[1] + 1.0
    aa = one[0] * one[0] + one[1] * one[1] + one[2] * one[2]
    ab = one[0] * two[0] + one[1] * two[1] + one[2] * two[2]
    bb = two[0] * two[0] + two[1] * two[1] + two[2] * two[2]
    determinant = aa * bb - ab * ab
    scale = 1.0 / determinant
    inverse_aa = bb * scale
    inverse_ab = -ab * scale
    inverse_bb = aa * scale
    pressure = LAME_RATIO * (0.5 * jnp.log(determinant))
    for p in range(3):
        pulled_one = one[p] * inverse_aa + two[p] * inverse_ab
        pulled_two = one[p] * inverse_ab + two[p] * inverse_bb
        stress_one = stiff * (one[p] - pulled_one + pressure * pulled_one)
        stress_two = stiff * (two[p] - pulled_two + pressure * pulled_two)
        force_one = diag_a * stress_one + skew_b * stress_two
        force_two = diag_c * stress_two
        for corner, force in enumerate((-(force_one + force_two), force_one, force_two)):
            rest = force
            for part in range(PIECES):
                piece = rest.astype(jnp.bfloat16).astype(F32)
                rest = rest - piece
                forces[part * 3 + p, corner] = piece


def spread_kernel(base, low_ids, high_ids, forces, out):
    runs = low_ids.shape[1]
    parts, rows, length = out.shape
    pieces = length // BLK
    slots = pieces * rows
    kind = jnp.bfloat16
    tile = 16
    slot_ids = lax.broadcasted_iota(jnp.int32, (slots, BLK), 0).astype(F32) + base
    slot_ids = slot_ids.astype(kind)
    lane_ids = lax.broadcasted_iota(jnp.int32, (BLK, BLK), 0).astype(F32).astype(kind)
    ones = jnp.ones((BLK, BLK), kind)
    none = jnp.zeros((BLK, BLK), kind)
    blank = jnp.zeros((slots, BLK), kind)

    def tall_row(row, count):
        block = jnp.broadcast_to(row, (tile, BLK)).astype(kind)
        return jnp.concatenate([block] * (count // tile), axis=0)

    total = None
    for corner in range(3):
        for first in range(0, runs, STEP):
            left = [[] for _ in range(parts * PIECES)]
            right = []
            for j in range(first, min(first + STEP, runs)):
                row = slice(j, j + 1)
                here = slot_ids == tall_row(high_ids[corner, row], slots)
                there = lane_ids == tall_row(low_ids[corner, row], BLK)
                right.append(jnp.where(there, ones, none))
                for part in range(parts * PIECES):
                    left[part].append(
                        jnp.where(here, tall_row(forces[part, corner, row], slots), blank)
                    )
            tall = jnp.concatenate([jnp.concatenate(part, axis=1) for part in left], axis=0)
            wide = jnp.concatenate(right, axis=1)
            product = lax.dot_general(
                tall, wide, (((1,), (1,)), ((), ())), preferred_element_type=F32
            )
            total = product if total is None else total + product
    for p in range(parts):
        summed = total[p * slots : (p + 1) * slots]
        for part in range(1, PIECES):
            start = (parts * part + p) * slots
            summed = summed + total[start : start + slots]
        for piece in range(pieces):
            out[p, :, piece * BLK : (piece + 1) * BLK] = summed[piece * rows : (piece + 1) * rows]


def store_kernel(values, out_hbm, sem):
    store = pltpu.make_async_copy(values, out_hbm, sem)
    store.start()
    store.wait()


def final_kernel(count, *refs):
    messages = refs[:count]
    residual, motion, keys = refs[count:]
    slots = keys.shape[0]
    node_blocks = residual.shape[1] // BLK
    inner = lax.axis_index("inner")
    width = BLK // slots

    def key_of(message, k):
        return jnp.broadcast_to(message[3 * slots][:, k * width : k * width + 1], (1, BLK))

    mine = messages[0]
    for k in range(slots):
        keys[k : k + 1] = key_of(mine, k)
    wanted = keys[...]
    node_ids = lax.broadcasted_iota(jnp.int32, (node_blocks, BLK), 0)
    own_ids = (node_ids + inner * node_blocks).astype(F32)
    external = [jnp.zeros((node_blocks, BLK), F32)] * 3
    moved = [jnp.zeros((slots, BLK), F32)] * 3
    for message in messages:
        for k in range(slots):
            key = key_of(message, k)
            here = own_ids == key
            same = wanted == key
            for part in range(3):
                row = message[3 * k + part]
                external[part] = external[part] + jnp.where(here, row, 0.0)
                moved[part] = moved[part] + jnp.where(same, row, 0.0)
    for step, message in enumerate(messages):
        sender = partner_of(inner, step, count)
        for b in range(node_blocks):
            key = jnp.broadcast_to(sender * node_blocks + b, (1, BLK)).astype(F32)
            same = wanted == key
            for part in range(3):
                at = 3 * slots + 1 + part * node_blocks + b
                moved[part] = moved[part] - jnp.where(same, message[at], 0.0)
    live = wanted >= 0.0
    for part in range(3):
        start = 3 * slots + 1 + part * node_blocks
        left = external[part] - mine[start : start + node_blocks, 0]
        for b in range(node_blocks):
            residual[part : part + 1, b * BLK : (b + 1) * BLK] = left[b : b + 1]
        motion[part] = jnp.where(live, COMPLIANCE * moved[part], 0.0)


def call(kernel, outs, operands, spaces, scratch=(), out_spaces=None, micros=1.0, aliases=None):
    spec = lambda space: pl.BlockSpec(memory_space=space)
    out_spaces = out_spaces or (pltpu.VMEM,) * len(outs)
    return pl.pallas_call(
        kernel,
        out_shape=outs,
        in_specs=[spec(space) for space in spaces],
        out_specs=tuple(spec(space) for space in out_spaces),
        scratch_shapes=list(scratch),
        input_output_aliases=aliases or {},
        compiler_params=pltpu.CompilerParams(vmem_limit_bytes=VMEM_BYTES),
        cost_estimate=pl.CostEstimate(
            flops=0, bytes_accessed=int(micros * 3.6e6), transcendentals=0
        ),
    )(*operands)


def partner_of(at, step, count):
    if count & (count - 1) == 0:
        return at ^ step
    return (at + count - step) % count


def exchange(block, axis, step):
    count = lax.axis_size(axis)
    return lax.ppermute(block, axis, [(partner_of(i, step, count), i) for i in range(count)])


def around(block, axis, step):
    count = lax.axis_size(axis)
    return lax.ppermute(block, axis, [(i, (i + step) % count) for i in range(count)])


def swap(near, far, axis, beside):
    count, others = lax.axis_size(axis), lax.axis_size(beside)
    routes = []
    for start in (0, 1):
        route = []
        for other in range(others):
            for i in range(count):
                j = i + 1 if i % 2 == start else i - 1
                to = other
                if not 0 <= j < count:
                    j = i
                    to = other ^ 1 if others % 2 == 0 else other
                route.append((other * count + i, to * count + j))
        routes.append(route)
    axes = (beside, axis)
    return lax.ppermute(near, axes, routes[0]), lax.ppermute(far, axes, routes[1])


def shards(
    populations,
    relaxation,
    node_flags,
    displacement,
    elements,
    shape_inverse,
    stiffness,
    block_source,
    block_target,
    block_node,
    block_count,
):
    planes, rows, length = populations.shape[1:]
    half = length // BLK
    node_dev = displacement.shape[1]
    node_blocks = node_dev // BLK
    runs = stiffness.shape[0] // BLK
    slots = block_source.shape[2]
    count = lax.axis_size("inner")
    shape = lambda *dims: jax.ShapeDtypeStruct(dims, F32)
    whole = shape(*populations.shape)
    vmem, hbm, smem = pltpu.VMEM, pltpu.HBM, pltpu.SMEM

    next_nodes = around(displacement, "slab", -1)
    face_y = shape(SIDE_SLOTS, planes, length)
    face_x = shape(SLOTS, rows, length)
    pin = lambda block: pltpu.with_memory_space_constraint(block, hbm)
    whole_like = lambda block: jax.ShapeDtypeStruct(block.shape, block.dtype)
    shell = (displacement, elements, shape_inverse, stiffness.reshape(runs, BLK))
    c1, fixed, far, near, own_nodes, corners, inverses, stiff = call(
        first_kernel,
        (
            whole,
            shape(2, planes, rows, length),
            face_y,
            face_y,
            *(whole_like(block) for block in shell),
        ),
        tuple(pin(block) for block in (populations, relaxation, node_flags, *shell)),
        (hbm,) * 7,
        scratch=(
            pltpu.VMEM((planes, Q, rows, length), F32),
            pltpu.VMEM((planes, rows, length), F32),
            pltpu.VMEM((planes, rows, length), jnp.int32),
            pltpu.SemaphoreType.DMA((planes + 6,)),
        ),
        micros=1.5,
    )
    near_y, far_y = swap(near, far, "inner", "slab")
    numbers = shape(3, runs, BLK)
    low_ids, high_ids, forces = call(
        element_kernel,
        (numbers, numbers, shape(3 * PIECES, 3, runs, BLK)),
        (corners, own_nodes, next_nodes, inverses, stiff),
        (vmem,) * 5,
        scratch=(
            pltpu.VMEM((3, runs, BLK), F32),
            pltpu.VMEM((3, runs, BLK), jnp.int32),
            pltpu.VMEM((3, 3, runs, BLK), F32),
        ),
        micros=0.001,
    )
    far, near = call(
        slab_face_kernel, (face_x, face_x), (c1, fixed, low_ids), (vmem,) * 3, micros=0.001
    )
    near_x, far_x = swap(near, far, "slab", "group")
    nodal = shape(3, node_blocks // half, length)
    (other,) = call(
        functools.partial(spread_kernel, node_blocks),
        (nodal,),
        (low_ids, high_ids, forces),
        (vmem,) * 3,
        micros=0.001,
    )
    corner = shape(CORNER_SLOTS, rows, length)
    far, near = call(
        corner_kernel,
        (corner, corner),
        (far_y, near_y, other),
        (vmem,) * 3,
        scratch=(pltpu.VMEM((2, SLOTS, planes, length), F32),),
        micros=0.3,
    )
    near_c, far_c = swap(near, far, "slab", "group")
    (own,) = call(
        functools.partial(spread_kernel, 0),
        (nodal,),
        (low_ids, high_ids, forces),
        (vmem,) * 3,
        micros=0.8,
    )
    wide = planes + 4
    walls_shape = shape(2, SLOTS, wide, length)
    second_shape = shape(Q, planes + 2, rows, length)
    extended, walls, crossing, second, ends = call(
        inside_kernel,
        (
            shape(Q, wide, rows, length),
            walls_shape,
            shape(2, 5, wide, length),
            second_shape,
            shape(2, 2, rows, length),
        ),
        (c1, fixed, far_y, near_y, far_x, near_x),
        (vmem,) * 6,
        scratch=(
            pltpu.VMEM((2, SLOTS, planes, length), F32),
            pltpu.VMEM((2, SLOTS, rows, length), F32),
        ),
        micros=0.8,
    )
    lines = 3 * slots + 1 + 3 * node_blocks
    values, message, _, _ = call(
        second_kernel,
        (whole, shape(lines, 1, BLK), walls_shape, second_shape),
        (
            pin(block_source),
            pin(block_target),
            pin(block_node),
            block_count,
            far_c,
            near_c,
            fixed,
            extended,
            crossing,
            ends,
            own,
            walls,
            second,
        ),
        (hbm,) * 3 + (vmem,) * 10,
        aliases={11: 2, 12: 3},
        scratch=(
            pltpu.VMEM((2, CORNER_SLOTS, rows, length), F32),
            pltpu.VMEM((2, 5, wide, length), F32),
            pltpu.VMEM((planes * half, 3, rows, BLK), F32),
            pltpu.SMEM(block_source.shape, jnp.int32),
            pltpu.SMEM(block_target.shape, jnp.int32),
            pltpu.SMEM(block_node.shape, jnp.int32),
            pltpu.SemaphoreType.DMA((3,)),
        ),
        micros=1.5,
    )
    messages = [message] + [exchange(message, "inner", step) for step in range(1, count)]
    (populations_out,) = call(
        store_kernel,
        (whole,),
        (values,),
        (vmem,),
        out_spaces=(hbm,),
        scratch=(pltpu.SemaphoreType.DMA(()),),
        micros=1.0,
    )
    residual, motion = call(
        functools.partial(final_kernel, count),
        (shape(3, node_dev), shape(3, slots, BLK)),
        messages,
        (vmem,) * count,
        scratch=(pltpu.VMEM((slots, BLK), F32),),
        micros=0.8,
    )
    return populations_out, residual, motion.transpose(1, 0, 2)[None, None]


def solution(mesh):
    return jax.shard_map(
        shards,
        mesh=mesh,
        in_specs=(
            P(None, ("group", "slab"), "inner", None),
            P(("group", "slab"), "inner", None),
            P(("group", "slab"), "inner", None),
            P(None, ("group", "slab", "inner")),
            P(None, ("group", "slab", "inner")),
            P(None, ("group", "slab", "inner")),
            P(("group", "slab", "inner")),
            P(("group", "slab"), "inner", None),
            P(("group", "slab"), "inner", None),
            P(("group", "slab"), "inner", None),
            P(("group", "slab"), "inner"),
        ),
        out_specs=(
            P(None, ("group", "slab"), "inner", None),
            P(None, ("group", "slab", "inner")),
            P(("group", "slab"), "inner", None, None, None),
        ),
        check_vma=False,
    )
```

```python
import functools

import jax
import jax.numpy as jnp
from jax import lax
from jax.experimental import pallas as pl
from jax.experimental.pallas import tpu as pltpu
from jax.sharding import PartitionSpec as P

BLK = 128
VELOCITIES = (
    (0, 0, 0),
    (1, 0, 0),
    (-1, 0, 0),
    (0, 1, 0),
    (0, -1, 0),
    (0, 0, 1),
    (0, 0, -1),
    (1, 1, 0),
    (-1, -1, 0),
    (1, -1, 0),
    (-1, 1, 0),
    (1, 0, 1),
    (-1, 0, -1),
    (1, 0, -1),
    (-1, 0, 1),
    (0, 1, 1),
    (0, -1, -1),
    (0, 1, -1),
    (0, -1, 1),
)
WEIGHTS = (1.0 / 3.0,) + (1.0 / 18.0,) * 6 + (1.0 / 36.0,) * 12
OPPOSITE = (0, 2, 1, 4, 3, 6, 5, 8, 7, 10, 9, 12, 11, 14, 13, 16, 15, 18, 17)
INLET_SPEED = 0.04
LOAD_SCALE = 25.0
COMPLIANCE = 0.5
LAME_RATIO = 2.0
Q = 19
FLAG_SLOT = 19
RATE_SLOT = 20
SLOTS = 21
SIDE_SLOTS = 24
FORCE_SLOT = 6
CORNER_SLOTS = FORCE_SLOT + 3
PIECES = 2
STEP = 4
F32 = jnp.float32
VMEM_BYTES = 48 * 1024 * 1024


def moments(values):
    sums = [values[q] + values[q + 1] for q in range(1, Q, 2)]
    diffs = [values[q] - values[q + 1] for q in range(1, Q, 2)]
    density = values[0]
    for term in sums:
        density = density + term
    flows = []
    for axis in range(3):
        total = None
        for k, q in enumerate(range(1, Q, 2)):
            factor = VELOCITIES[q][axis]
            if factor == 0:
                continue
            if total is None:
                total = diffs[k] if factor > 0 else -diffs[k]
            else:
                total = total + diffs[k] if factor > 0 else total - diffs[k]
        flows.append(total)
    return density, flows[0], flows[1], flows[2]


def collide(values, rate, kind):
    density, flow_x, flow_y, flow_z = moments(values)
    inverse = 1.0 / density
    wall = kind == 1
    inlet = kind == 2
    fluid = kind == 0
    vel = (
        jnp.where(inlet, INLET_SPEED, flow_x * inverse),
        jnp.where(inlet, 0.0, flow_y * inverse),
        jnp.where(inlet, 0.0, flow_z * inverse),
    )
    scale = jnp.where(fluid, density, 1.0)
    rate = jnp.where(fluid, rate, 1.0)
    base = 1.0 - 1.5 * (vel[0] * vel[0] + vel[1] * vel[1] + vel[2] * vel[2])
    weighted = {w: w * scale for w in set(WEIGHTS)}
    out = [None] * Q
    relaxed = values[0] + rate * (weighted[WEIGHTS[0]] * base - values[0])
    out[0] = jnp.where(wall, values[0], relaxed)
    for q in range(1, Q, 2):
        project = None
        for factor, component in zip(VELOCITIES[q], vel):
            if factor == 0:
                continue
            if project is None:
                project = component
            else:
                project = project + component if factor > 0 else project - component
        even = base + 4.5 * (project * project)
        odd = 3.0 * project
        w = weighted[WEIGHTS[q]]
        forward = values[q] + rate * (w * (even + odd) - values[q])
        backward = values[q + 1] + rate * (w * (even - odd) - values[q + 1])
        out[q] = jnp.where(wall, values[q + 1], forward)
        out[q + 1] = jnp.where(wall, values[q], backward)
    return out


def roll_by(block, step, axis):
    if step == 0:
        return block
    return pltpu.roll(block, step % block.shape[axis], axis)


def face_slots(axis, sign):
    picks = []
    for q in range(Q):
        if VELOCITIES[q][axis] * sign >= 0:
            picks.append((q, 0))
        else:
            picks.append((OPPOSITE[q], 1))
    return picks


def mirror(q, axis):
    flipped = tuple(-c if k == axis else c for k, c in enumerate(VELOCITIES[q]))
    return VELOCITIES.index(flipped)


def corner_rows(sign_x, sign_y):
    rows = []
    for q, depth in face_slots(0, sign_x):
        if VELOCITIES[q][1] * sign_y >= 0:
            rows.append((q, depth))
        else:
            rows.append((OPPOSITE[mirror(q, 1)], depth))
    return rows


def first_kernel(
    pops_hbm,
    rate_hbm,
    flags_hbm,
    displacement_hbm,
    elements_hbm,
    shape_hbm,
    stiffness_hbm,
    c1,
    fixed,
    far,
    near,
    displacement,
    elements,
    shape_inverse,
    stiffness,
    pops,
    rate,
    flags,
    sems,
):
    planes, rows = c1.shape[1], c1.shape[2]
    copies = [
        pltpu.make_async_copy(rate_hbm, rate, sems.at[planes]),
        pltpu.make_async_copy(flags_hbm, flags, sems.at[planes + 1]),
    ]
    loads = [
        pltpu.make_async_copy(pops_hbm.at[:, x], pops.at[x], sems.at[x]) for x in range(planes)
    ]
    shell = [
        pltpu.make_async_copy(source, target, sems.at[planes + 2 + k])
        for k, (source, target) in enumerate(
            (
                (displacement_hbm, displacement),
                (elements_hbm, elements),
                (shape_hbm, shape_inverse),
                (stiffness_hbm, stiffness),
            )
        )
    ]
    for copy in loads[:1] + copies + loads[1:] + shell:
        copy.start()
    for copy in copies:
        copy.wait()

    def plane(x, carry):
        pltpu.make_async_copy(pops_hbm.at[:, x], pops.at[x], sems.at[x]).wait()
        kind = flags[x]
        values = [pops[x, q] for q in range(Q)]
        result = collide(values, rate[x], kind)
        for q in range(Q):
            c1[q, x] = roll_by(result[q], VELOCITIES[q][2], 1)
        fixed[0, x] = kind.astype(F32)
        fixed[1, x] = rate[x]
        return carry

    lax.fori_loop(0, planes, plane, 0)

    def pack(out, sign, outside):
        def line(x, carry):
            for slot, (q, depth) in enumerate(face_slots(1, sign)):
                y = rows - 1 - depth if sign > 0 else depth
                out[slot, pl.ds(x, 1)] = c1[q, x, y : y + 1]
            y = rows - 1 if sign > 0 else 0
            for k, slot in enumerate((FLAG_SLOT, RATE_SLOT)):
                out[slot, pl.ds(x, 1)] = fixed[k, x, y : y + 1]
            return carry

        lax.fori_loop(0, planes, line, 0)
        for slot in range(SLOTS, SIDE_SLOTS):
            out[slot] = jnp.zeros(out.shape[1:], F32)
        clear_outside(out, outside)

    pack_pair(pack, "inner", near, far)
    for copy in shell:
        copy.wait()


def clear_outside(out, outside):
    @pl.when(outside)
    def _():
        out[...] = jnp.zeros(out.shape, F32)


def pack_pair(pack, axis, near, far):
    at = lax.axis_index(axis)
    even = lax.rem(at, 2) == 0
    first, last = at == 0, at == lax.axis_size(axis) - 1

    @pl.when(even)
    def _():
        pack(near, 1, last)
        pack(far, -1, first)

    @pl.when(jnp.logical_not(even))
    def _():
        pack(near, -1, first)
        pack(far, 1, last)


def slab_face_kernel(c1, fixed, numbers, far, near):
    del numbers
    planes = c1.shape[1]

    def pack(out, sign, outside):
        for slot, (q, depth) in enumerate(face_slots(0, sign)):
            out[slot] = c1[q, planes - 1 - depth if sign > 0 else depth]
        end = planes - 1 if sign > 0 else 0
        out[FLAG_SLOT] = fixed[0, end]
        out[RATE_SLOT] = fixed[1, end]
        clear_outside(out, outside)

    pack_pair(pack, "slab", near, far)


def gather_both(near, far, both, axis):
    odd = lax.rem(lax.axis_index(axis), 2)
    for slot in range(both.shape[1]):
        both[1 - odd, slot] = near[slot]
        both[odd, slot] = far[slot]


def corner_kernel(far_y, near_y, other, far, near, both):
    planes = near_y.shape[1]
    gather_both(near_y, far_y, both, "inner")

    def pack(out, sign, outside):
        for side, sign_y in enumerate((1, -1)):
            picks = corner_rows(sign, sign_y) + [(FLAG_SLOT, 0), (RATE_SLOT, 0)]
            for row, (slot, depth) in enumerate(picks):
                x = planes - 1 - depth if sign > 0 else depth
                at = 3 * side + row // 8
                out[at, row % 8 : row % 8 + 1] = both[side, slot, x : x + 1]
        for part in range(3):
            out[FORCE_SLOT + part] = other[part]
        clear_outside(out, outside)

    pack_pair(pack, "slab", near, far)


def with_edge(block, step_y, edge):
    rows = block.shape[0]
    sub = lax.broadcasted_iota(jnp.int32, block.shape, 0)
    if step_y > 0:
        return jnp.where(sub == 0, edge, roll_by(block, 1, 0))
    return jnp.where(sub == rows - 1, edge, roll_by(block, -1, 0))


def store_plane(extended, walls, second, at, rate, kind):
    values = []
    for q in range(Q):
        step_x, step_y, _ = VELOCITIES[q]
        block = extended[q, at + 1 - step_x]
        if step_y != 0:
            edge = walls[0 if step_y > 0 else 1, q, pl.ds(at + 1 - step_x, 1)]
            block = with_edge(block, step_y, edge)
        values.append(block)
    result = collide(values, rate, kind)
    for q in range(Q):
        second[q, at] = roll_by(result[q], VELOCITIES[q][2], 1)


def inside_kernel(
    c1,
    fixed,
    far_y,
    near_y,
    far_x,
    near_x,
    extended,
    walls,
    crossing,
    second,
    ends,
    both_y,
    both_x,
):
    planes, rows, _ = c1.shape[1:]
    wide = planes + 4
    gather_both(near_y, far_y, both_y, "inner")
    gather_both(near_x, far_x, both_x, "slab")
    for q in range(Q):
        for x in range(planes):
            extended[q, x + 2] = c1[q, x]
        extended[q, 1] = both_x[0, q]
        extended[q, planes + 2] = both_x[1, q]
        if VELOCITIES[q][0] > 0:
            extended[q, 0] = both_x[0, OPPOSITE[q]]
        if VELOCITIES[q][0] < 0:
            extended[q, planes + 3] = both_x[1, OPPOSITE[q]]
    for end in range(2):
        ends[end, 0] = both_x[end, FLAG_SLOT]
        ends[end, 1] = both_x[end, RATE_SLOT]

    for side, sign in enumerate((1, -1)):
        y = 0 if sign > 0 else rows - 1
        for slot in range(SLOTS):
            walls[side, slot, 2 : planes + 2] = both_y[side, slot]
        place = 0
        for q in range(Q):
            if VELOCITIES[q][1] != -sign:
                continue
            for x in range(wide):
                crossing[side, place, x : x + 1] = extended[q, x, y : y + 1]
            place += 1

    def inside_plane(x, carry):
        store_plane(extended, walls, second, x + 1, fixed[1, x], fixed[0, x])
        return carry

    lax.fori_loop(1, planes - 1, inside_plane, 0)


def second_kernel(
    block_source_hbm,
    block_target_hbm,
    block_node_hbm,
    block_count,
    far,
    near,
    fixed,
    extended,
    crossing,
    ends,
    internal_own,
    walls_in,
    second_in,
    out,
    message,
    walls,
    second,
    both,
    edges,
    loads,
    block_source,
    block_target,
    block_node,
    sems,
):
    del walls_in, second_in
    copies = [
        pltpu.make_async_copy(block_source_hbm, block_source, sems.at[0]),
        pltpu.make_async_copy(block_target_hbm, block_target, sems.at[1]),
        pltpu.make_async_copy(block_node_hbm, block_node, sems.at[2]),
    ]
    for copy in copies:
        copy.start()
    planes, rows, length = out.shape[1:]
    half = length // BLK
    slots = block_source.shape[2]
    wide = planes + 4
    slab = lax.axis_index("slab")
    inner = lax.axis_index("inner")
    slab_end = lax.axis_size("slab") - 1
    inner_end = lax.axis_size("inner") - 1
    gather_both(near, far, both, "slab")

    for side, sign in enumerate((1, -1)):
        for end, sign_x in enumerate((1, -1)):
            for row, (slot, depth) in enumerate(corner_rows(sign_x, sign)):
                at = (1 - depth) if sign_x > 0 else planes + 2 + depth
                source = 3 * side + row // 8
                walls[side, slot, at : at + 1] = both[end, source, row % 8 : row % 8 + 1]
            at = 1 if sign_x > 0 else planes + 2
            for row in (FLAG_SLOT, RATE_SLOT):
                source = 3 * side + row // 8
                walls[side, row, at : at + 1] = both[end, source, row % 8 : row % 8 + 1]

    def edge_planes(end, carry):
        x = end * (planes - 1)
        store_plane(extended, walls, second, x + 1, fixed[1, x], fixed[0, x])
        store_plane(extended, walls, second, end * (planes + 1), ends[end, 1], ends[end, 0])
        return carry

    lax.fori_loop(0, 2, edge_planes, 0)

    @pl.when(slab == 0)
    def _():
        for q in range(Q):
            if VELOCITIES[q][0] > 0:
                second[q, 0] = jnp.zeros((rows, length), F32)

    @pl.when(slab == slab_end)
    def _():
        for q in range(Q):
            if VELOCITIES[q][0] < 0:
                second[q, planes + 1] = jnp.zeros((rows, length), F32)

    across = lax.broadcasted_iota(jnp.int32, (wide, length), 0)
    hidden = ((across <= 1) & (slab == 0)) | ((across >= planes + 2) & (slab == slab_end))
    for side, sign, outside in ((0, 1, inner == 0), (1, -1, inner == inner_end)):
        values = []
        place = 0
        for q in range(Q):
            step_x, step_y, _ = VELOCITIES[q]
            if step_y == 0:
                block = walls[side, q]
            elif step_y == sign:
                block = walls[side, OPPOSITE[q]]
            else:
                block = crossing[side, place]
                place += 1
            values.append(roll_by(block, step_x, 0))
        result = collide(values, walls[side, RATE_SLOT], walls[side, FLAG_SLOT])
        place = 0
        for q in range(Q):
            if VELOCITIES[q][1] == sign:
                kept = jnp.where(hidden | outside, 0.0, result[q])
                edges[side, place] = roll_by(kept, VELOCITIES[q][2], 1)
                place += 1

    def plane_two(x, carry):
        values = []
        places = {1: 0, -1: 0}
        for q in range(Q):
            step_x, step_y, _ = VELOCITIES[q]
            block = second[q, x + 1 - step_x]
            if step_y != 0:
                edge = edges[0 if step_y > 0 else 1, places[step_y], pl.ds(x + 2 - step_x, 1)]
                places[step_y] += 1
                block = with_edge(block, step_y, edge)
            values.append(block)
            out[q, x] = block
        density, flow_x, flow_y, flow_z = moments(values)
        parts = (
            LOAD_SCALE * flow_x,
            LOAD_SCALE * (flow_y + (density - 1.0) / 3.0),
            LOAD_SCALE * flow_z,
        )
        for part in range(3):
            for piece in range(half):
                loads[x * half + piece, part] = parts[part][:, piece * BLK : (piece + 1) * BLK]
        return carry

    lax.fori_loop(0, planes, plane_two, 0)

    for copy in copies:
        copy.wait()
    node_blocks = internal_own.shape[1] * half
    live = jnp.broadcast_to(block_count[...], (1, BLK))
    lanes_of = lax.broadcasted_iota(jnp.int32, (1, BLK), 1) // (BLK // slots)
    all_keys = jnp.full((1, BLK), -1, jnp.int32)
    for k in range(slots):
        run = block_source[0, 0, k]
        x = run // (rows * half)
        left = run - x * (rows * half)
        y = left // half
        piece = left - y * half
        for part in range(3):
            message[3 * k + part] = loads[x * half + piece, part, pl.ds(y, 1)]
        key = block_target[0, 0, k] * node_blocks + block_node[0, 0, k]
        all_keys = jnp.where((lanes_of == k) & (live > k), key, all_keys)
    message[3 * slots] = all_keys.astype(F32)
    for part in range(3):
        start = 3 * slots + 1 + part * node_blocks
        for piece in range(half):
            at = piece * rows
            lanes = slice(piece * BLK, (piece + 1) * BLK)
            message[start + at : start + at + rows, 0] = (
                internal_own[part, :, lanes] + both[0, FORCE_SLOT + part, :, lanes]
            )


def element_kernel(
    elements, displacement, next_nodes, shape_inverse, stiffness, low_ids, high_ids, forces, shapes,
    numbers, corners,
):
    node_dev = displacement.shape[1]
    node_blocks = node_dev // BLK
    runs = elements.shape[1] // BLK
    for j in range(runs):
        lanes = slice(j * BLK, (j + 1) * BLK)
        for row in range(3):
            numbers[row, j : j + 1] = elements[row : row + 1, lanes]
            shapes[row, j : j + 1] = shape_inverse[row : row + 1, lanes]
    for row in range(3):
        low_ids[row] = (numbers[row] & (BLK - 1)).astype(F32)
        high_ids[row] = (numbers[row] >> 7).astype(F32)

    def gather(group, carry):
        rows = pl.ds(pl.multiple_of(group * 8, 8), 8)
        low = [numbers[corner, rows] & (BLK - 1) for corner in range(3)]
        high = [numbers[corner, rows] >> 7 for corner in range(3)]
        for corner in range(3):
            nodes = [jnp.zeros((8, BLK), F32)] * 3
            for block in range(2 * node_blocks):
                source = displacement if block < node_blocks else next_nodes
                start = (block % node_blocks) * BLK
                here = high[corner] == block
                for part in range(3):
                    row = source[part : part + 1, start : start + BLK]
                    picked = jnp.take_along_axis(
                        jnp.broadcast_to(row, (8, BLK)),
                        low[corner],
                        axis=1,
                        mode="promise_in_bounds",
                    )
                    nodes[part] = jnp.where(here, picked, nodes[part])
            for part in range(3):
                corners[corner, part, rows] = nodes[part]
        return carry

    lax.fori_loop(0, runs // 8, gather, 0, unroll=4)

    first, second, third = [[corners[c, p] for p in range(3)] for c in range(3)]
    diag_a = shapes[0]
    skew_b = shapes[1]
    diag_c = shapes[2]
    stiff = stiffness[...]
    edge_one = [second[p] - first[p] for p in range(3)]
    edge_two = [third[p] - first[p] for p in range(3)]
    one = [diag_a * edge_one[p] for p in range(3)]
    two = [skew_b * edge_one[p] + diag_c * edge_two[p] for p in range(3)]
    one[0] = one[0] + 1.0
    two[1] = two[1] + 1.0
    aa = one[0] * one[0] + one[1] * one[1] + one[2] * one[2]
    ab = one[0] * two[0] + one[1] * two[1] + one[2] * two[2]
    bb = two[0] * two[0] + two[1] * two[1] + two[2] * two[2]
    determinant = aa * bb - ab * ab
    scale = 1.0 / determinant
    inverse_aa = bb * scale
    inverse_ab = -ab * scale
    inverse_bb = aa * scale
    pressure = LAME_RATIO * (0.5 * jnp.log(determinant))
    for p in range(3):
        pulled_one = one[p] * inverse_aa + two[p] * inverse_ab
        pulled_two = one[p] * inverse_ab + two[p] * inverse_bb
        stress_one = stiff * (one[p] - pulled_one + pressure * pulled_one)
        stress_two = stiff * (two[p] - pulled_two + pressure * pulled_two)
        force_one = diag_a * stress_one + skew_b * stress_two
        force_two = diag_c * stress_two
        for corner, force in enumerate((-(force_one + force_two), force_one, force_two)):
            rest = force
            for part in range(PIECES):
                piece = rest.astype(jnp.bfloat16).astype(F32)
                rest = rest - piece
                forces[part * 3 + p, corner] = piece


def spread_kernel(base, low_ids, high_ids, forces, out):
    runs = low_ids.shape[1]
    parts, rows, length = out.shape
    pieces = length // BLK
    slots = pieces * rows
    kind = jnp.bfloat16
    tile = 16
    slot_ids = lax.broadcasted_iota(jnp.int32, (slots, BLK), 0).astype(F32) + base
    slot_ids = slot_ids.astype(kind)
    lane_ids = lax.broadcasted_iota(jnp.int32, (BLK, BLK), 0).astype(F32).astype(kind)
    ones = jnp.ones((BLK, BLK), kind)
    none = jnp.zeros((BLK, BLK), kind)
    blank = jnp.zeros((slots, BLK), kind)

    def tall_row(row, count):
        block = jnp.broadcast_to(row, (tile, BLK)).astype(kind)
        return jnp.concatenate([block] * (count // tile), axis=0)

    total = None
    for corner in range(3):
        for first in range(0, runs, STEP):
            left = [[] for _ in range(parts * PIECES)]
            right = []
            for j in range(first, min(first + STEP, runs)):
                row = slice(j, j + 1)
                here = slot_ids == tall_row(high_ids[corner, row], slots)
                there = lane_ids == tall_row(low_ids[corner, row], BLK)
                right.append(jnp.where(there, ones, none))
                for part in range(parts * PIECES):
                    left[part].append(
                        jnp.where(here, tall_row(forces[part, corner, row], slots), blank)
                    )
            tall = jnp.concatenate([jnp.concatenate(part, axis=1) for part in left], axis=0)
            wide = jnp.concatenate(right, axis=1)
            product = lax.dot_general(
                tall, wide, (((1,), (1,)), ((), ())), preferred_element_type=F32
            )
            total = product if total is None else total + product
    for p in range(parts):
        summed = total[p * slots : (p + 1) * slots]
        for part in range(1, PIECES):
            start = (parts * part + p) * slots
            summed = summed + total[start : start + slots]
        for piece in range(pieces):
            out[p, :, piece * BLK : (piece + 1) * BLK] = summed[piece * rows : (piece + 1) * rows]


def store_kernel(values, out_hbm, sem):
    store = pltpu.make_async_copy(values, out_hbm, sem)
    store.start()
    store.wait()


def final_kernel(count, *refs):
    messages = refs[:count]
    residual, motion, keys = refs[count:]
    slots = keys.shape[0]
    node_blocks = residual.shape[1] // BLK
    inner = lax.axis_index("inner")
    width = BLK // slots

    def key_of(message, k):
        return jnp.broadcast_to(message[3 * slots][:, k * width : k * width + 1], (1, BLK))

    mine = messages[0]
    for k in range(slots):
        keys[k : k + 1] = key_of(mine, k)
    wanted = keys[...]
    node_ids = lax.broadcasted_iota(jnp.int32, (node_blocks, BLK), 0)
    own_ids = (node_ids + inner * node_blocks).astype(F32)
    external = [jnp.zeros((node_blocks, BLK), F32)] * 3
    moved = [jnp.zeros((slots, BLK), F32)] * 3
    for message in messages:
        for k in range(slots):
            key = key_of(message, k)
            here = own_ids == key
            same = wanted == key
            for part in range(3):
                row = message[3 * k + part]
                external[part] = external[part] + jnp.where(here, row, 0.0)
                moved[part] = moved[part] + jnp.where(same, row, 0.0)
    for step, message in enumerate(messages):
        sender = partner_of(inner, step, count)
        for b in range(node_blocks):
            key = jnp.broadcast_to(sender * node_blocks + b, (1, BLK)).astype(F32)
            same = wanted == key
            for part in range(3):
                at = 3 * slots + 1 + part * node_blocks + b
                moved[part] = moved[part] - jnp.where(same, message[at], 0.0)
    live = wanted >= 0.0
    for part in range(3):
        start = 3 * slots + 1 + part * node_blocks
        left = external[part] - mine[start : start + node_blocks, 0]
        for b in range(node_blocks):
            residual[part : part + 1, b * BLK : (b + 1) * BLK] = left[b : b + 1]
        motion[part] = jnp.where(live, COMPLIANCE * moved[part], 0.0)


def call(kernel, outs, operands, spaces, scratch=(), out_spaces=None, micros=1.0, aliases=None):
    spec = lambda space: pl.BlockSpec(memory_space=space)
    out_spaces = out_spaces or (pltpu.VMEM,) * len(outs)
    return pl.pallas_call(
        kernel,
        out_shape=outs,
        in_specs=[spec(space) for space in spaces],
        out_specs=tuple(spec(space) for space in out_spaces),
        scratch_shapes=list(scratch),
        input_output_aliases=aliases or {},
        compiler_params=pltpu.CompilerParams(vmem_limit_bytes=VMEM_BYTES),
        cost_estimate=pl.CostEstimate(
            flops=0, bytes_accessed=int(micros * 3.6e6), transcendentals=0
        ),
    )(*operands)


def partner_of(at, step, count):
    if count & (count - 1) == 0:
        return at ^ step
    return (at + count - step) % count


def exchange(block, axis, step):
    count = lax.axis_size(axis)
    return lax.ppermute(block, axis, [(partner_of(i, step, count), i) for i in range(count)])


def around(block, axis, step):
    count = lax.axis_size(axis)
    return lax.ppermute(block, axis, [(i, (i + step) % count) for i in range(count)])


def swap(near, far, axis, beside):
    count, others = lax.axis_size(axis), lax.axis_size(beside)
    routes = []
    for start in (0, 1):
        route = []
        for other in range(others):
            for i in range(count):
                j = i + 1 if i % 2 == start else i - 1
                to = other
                if not 0 <= j < count:
                    j = i
                    to = other ^ 1 if others % 2 == 0 else other
                route.append((other * count + i, to * count + j))
        routes.append(route)
    axes = (beside, axis)
    return lax.ppermute(near, axes, routes[0]), lax.ppermute(far, axes, routes[1])


def shards(
    populations,
    relaxation,
    node_flags,
    displacement,
    elements,
    shape_inverse,
    stiffness,
    block_source,
    block_target,
    block_node,
    block_count,
):
    planes, rows, length = populations.shape[1:]
    half = length // BLK
    node_dev = displacement.shape[1]
    node_blocks = node_dev // BLK
    runs = stiffness.shape[0] // BLK
    slots = block_source.shape[2]
    count = lax.axis_size("inner")
    shape = lambda *dims: jax.ShapeDtypeStruct(dims, F32)
    whole = shape(*populations.shape)
    vmem, hbm, smem = pltpu.VMEM, pltpu.HBM, pltpu.SMEM

    next_nodes = around(displacement, "slab", -1)
    face_y = shape(SIDE_SLOTS, planes, length)
    face_x = shape(SLOTS, rows, length)
    pin = lambda block: pltpu.with_memory_space_constraint(block, hbm)
    whole_like = lambda block: jax.ShapeDtypeStruct(block.shape, block.dtype)
    shell = (displacement, elements, shape_inverse, stiffness.reshape(runs, BLK))
    c1, fixed, far, near, own_nodes, corners, inverses, stiff = call(
        first_kernel,
        (
            whole,
            shape(2, planes, rows, length),
            face_y,
            face_y,
            *(whole_like(block) for block in shell),
        ),
        tuple(pin(block) for block in (populations, relaxation, node_flags, *shell)),
        (hbm,) * 7,
        scratch=(
            pltpu.VMEM((planes, Q, rows, length), F32),
            pltpu.VMEM((planes, rows, length), F32),
            pltpu.VMEM((planes, rows, length), jnp.int32),
            pltpu.SemaphoreType.DMA((planes + 6,)),
        ),
        micros=1.5,
    )
    near_y, far_y = swap(near, far, "inner", "slab")
    numbers = shape(3, runs, BLK)
    low_ids, high_ids, forces = call(
        element_kernel,
        (numbers, numbers, shape(3 * PIECES, 3, runs, BLK)),
        (corners, own_nodes, next_nodes, inverses, stiff),
        (vmem,) * 5,
        scratch=(
            pltpu.VMEM((3, runs, BLK), F32),
            pltpu.VMEM((3, runs, BLK), jnp.int32),
            pltpu.VMEM((3, 3, runs, BLK), F32),
        ),
        micros=0.001,
    )
    far, near = call(
        slab_face_kernel, (face_x, face_x), (c1, fixed, low_ids), (vmem,) * 3, micros=0.001
    )
    near_x, far_x = swap(near, far, "slab", "group")
    nodal = shape(3, node_blocks // half, length)
    (other,) = call(
        functools.partial(spread_kernel, node_blocks),
        (nodal,),
        (low_ids, high_ids, forces),
        (vmem,) * 3,
        micros=0.001,
    )
    corner = shape(CORNER_SLOTS, rows, length)
    far, near = call(
        corner_kernel,
        (corner, corner),
        (far_y, near_y, other),
        (vmem,) * 3,
        scratch=(pltpu.VMEM((2, SLOTS, planes, length), F32),),
        micros=0.3,
    )
    near_c, far_c = swap(near, far, "slab", "group")
    (own,) = call(
        functools.partial(spread_kernel, 0),
        (nodal,),
        (low_ids, high_ids, forces),
        (vmem,) * 3,
        micros=0.8,
    )
    wide = planes + 4
    walls_shape = shape(2, SLOTS, wide, length)
    second_shape = shape(Q, planes + 2, rows, length)
    extended, walls, crossing, second, ends = call(
        inside_kernel,
        (
            shape(Q, wide, rows, length),
            walls_shape,
            shape(2, 5, wide, length),
            second_shape,
            shape(2, 2, rows, length),
        ),
        (c1, fixed, far_y, near_y, far_x, near_x),
        (vmem,) * 6,
        scratch=(
            pltpu.VMEM((2, SLOTS, planes, length), F32),
            pltpu.VMEM((2, SLOTS, rows, length), F32),
        ),
        micros=0.8,
    )
    lines = 3 * slots + 1 + 3 * node_blocks
    values, message, _, _ = call(
        second_kernel,
        (whole, shape(lines, 1, BLK), walls_shape, second_shape),
        (
            pin(block_source),
            pin(block_target),
            pin(block_node),
            block_count,
            far_c,
            near_c,
            fixed,
            extended,
            crossing,
            ends,
            own,
            walls,
            second,
        ),
        (hbm,) * 3 + (vmem,) * 10,
        aliases={11: 2, 12: 3},
        scratch=(
            pltpu.VMEM((2, CORNER_SLOTS, rows, length), F32),
            pltpu.VMEM((2, 5, wide, length), F32),
            pltpu.VMEM((planes * half, 3, rows, BLK), F32),
            pltpu.SMEM(block_source.shape, jnp.int32),
            pltpu.SMEM(block_target.shape, jnp.int32),
            pltpu.SMEM(block_node.shape, jnp.int32),
            pltpu.SemaphoreType.DMA((3,)),
        ),
        micros=1.5,
    )
    messages = [message] + [exchange(message, "inner", step) for step in range(1, count)]
    (populations_out,) = call(
        store_kernel,
        (whole,),
        (values,),
        (vmem,),
        out_spaces=(hbm,),
        scratch=(pltpu.SemaphoreType.DMA(()),),
        micros=1.0,
    )
    residual, motion = call(
        functools.partial(final_kernel, count),
        (shape(3, node_dev), shape(3, slots, BLK)),
        messages,
        (vmem,) * count,
        scratch=(pltpu.VMEM((slots, BLK), F32),),
        micros=0.8,
    )
    return populations_out, residual, motion.transpose(1, 0, 2)[None, None]


def solution(mesh):
    return jax.shard_map(
        shards,
        mesh=mesh,
        in_specs=(
            P(None, ("group", "slab"), "inner", None),
            P(("group", "slab"), "inner", None),
            P(("group", "slab"), "inner", None),
            P(None, ("group", "slab", "inner")),
            P(None, ("group", "slab", "inner")),
            P(None, ("group", "slab", "inner")),
            P(("group", "slab", "inner")),
            P(("group", "slab"), "inner", None),
            P(("group", "slab"), "inner", None),
            P(("group", "slab"), "inner", None),
            P(("group", "slab"), "inner"),
        ),
        out_specs=(
            P(None, ("group", "slab"), "inner", None),
            P(None, ("group", "slab", "inner")),
            P(("group", "slab"), "inner", None, None, None),
        ),
        check_vma=False,
    )
```
